32 devices in a mesh: seq: 2 (over x), heads: 4 (over y, core), dp: 4 (over z).
Axes of the slice: x: 2, y: 2, z: 4, core: 2. Of those that a mesh axis runs over, the one named last changes fastest.
Arguments:
- activations: bfloat16 [1024, 8192], P(('dp', 'seq'), 'heads'), parts along dimension 0, may hold values from -6 to 6
- conv_taps: bfloat16 [4, 8192], P(None, 'heads'), may hold values from -3 to 3
- gate_in: bfloat16 [8192, 1024], P('heads', 'seq'), may hold values from -0.0625 to 0.0625
- gate_out: bfloat16 [1024, 8], replicated, may hold values from -0.59765625 to 0.59765625
- queries: bfloat16 [1024, 8192], P(('dp', 'seq'), 'heads'), parts along dimension 0, may hold values from -1000 to 1000, as said below
- key_vectors: bfloat16 [1024, 1024], P(('dp', 'seq'), 'heads'), parts along dimension 0, may hold values from -4 to 4, as said below
- value_vectors: bfloat16 [1024, 1024], P(('dp', 'seq'), 'heads'), parts along dimension 0, may hold values from -6 to 6
- segment_ids: int32 [1024], P('dp'), parts along dimension 0, may hold values from 0 to 3, never falling along the last dimension, each value on 1 to 128 neighbouring positions
Outputs:
- attended: bfloat16 [1024, 8192], P(('dp', 'seq'), 'heads'), parts along dimension 0
- key_mass: bfloat16 [8, 1024], P('heads', ('dp', 'seq')), parts along dimension 1
The draws below stay inside these ranges and needn't reach their ends.
There are 4 independent parts, one for each index of `dp`. The reference program is written for one: setup_inputs(seed, part) draws one part's arguments, and reference() takes and returns one part's arrays. A program takes and returns all parts, laid end to end along the dimension named above; an argument that names none is the same for every part. Nothing has to cross between parts.
Inputs may be any that keep to these rules, and one draw needn't show every extreme that they name: `queries`: finite. `key_vectors`: finite.
All inputs are finite; a program needn't handle non-finite values.
Results may differ from the reference program's by a relative error of at most 0.0056.
Values may be sent and summed in bfloat16 or wider, within the bound.
No kernel may reach another device: no remote copies, remote signals or barrier semaphores. Data moves between devices by JAX's collectives and lax.ppermute only.
A program may use at most 64 MiB of HBM per device.

```python
import math
import jax
import jax.numpy as jnp
import numpy as np
from jax import lax

MODEL_WIDTH = 8192
QUERY_HEADS = 64
KV_HEADS = 8
HEAD_DIM = 128
GATE_HIDDEN = 1024
CONV_TAPS = 4
SEQ_LEN = 256


def joint_draw(key):
    base_keys = jnp.clip(jax.random.normal(jax.random.fold_in(key, 21), (SEQ_LEN, KV_HEADS, HEAD_DIM), jnp.float32), -4.0, 4.0)
    base_queries = 1.5 * jnp.clip(jax.random.normal(jax.random.fold_in(key, 22), (SEQ_LEN, QUERY_HEADS, HEAD_DIM), jnp.float32), -4.0, 4.0)
    return (base_queries.reshape(SEQ_LEN, QUERY_HEADS * HEAD_DIM), base_keys.reshape(SEQ_LEN, KV_HEADS * HEAD_DIM))


def draw_queries(key, part):
    return joint_draw(key)[0].astype(jnp.bfloat16)


def draw_key_vectors(key, part):
    return joint_draw(key)[1].astype(jnp.bfloat16)


def block_scale(key, dims, pieces, least, high):
    factor_of = 1.0
    for axis_at, blocks in pieces:
        heights = jax.random.uniform(jax.random.fold_in(jax.random.fold_in(key, 6), axis_at), (blocks,), jnp.float32, least / len(pieces), high / len(pieces))
        factor_of = factor_of * jnp.repeat(jnp.exp(heights), dims[axis_at] // blocks).reshape((-1,) + (1,) * (len(dims) - 1 - axis_at))
    return factor_of


def split_up(amount, total, limit, skew):
    loads = [(1 << 20) // math.isqrt(grade ** skew) + 1 for grade in range(2, amount + 1)]
    rest, given = total - limit - (amount - 1), [1] * (amount - 1)
    while rest > 0:
        candidates = [i for i in range(amount - 1) if given[i] < limit]
        pool, left = sum([loads[i] for i in candidates]), rest
        for i in candidates:
            more = min(limit - given[i], max(1, left * loads[i] // pool), rest)
            given[i] = given[i] + more
            rest = rest - more
    return np.array([limit] + given)


def uneven(key, number_of, total, reach, lean):
    if number_of == 2:
        one = jax.random.randint(key, (), max(1, total - reach), min(reach, total - 1) + 1)
        return jnp.stack([one, total - one])
    sizes = jnp.asarray(split_up(number_of, total, reach, lean), jnp.int32)
    couples = (number_of - 1) // 2
    giver, sink = sizes[1:1 + 2 * couples:2], sizes[2:2 + 2 * couples:2]
    margin = jnp.minimum(giver - 1, reach - sink)
    moved = jax.random.randint(jax.random.fold_in(key, 1), (couples,), 0, 1 << 20) % (margin + 1)
    sizes = sizes.at[1:1 + 2 * couples:2].set(giver - moved).at[2:2 + 2 * couples:2].set(sink + moved)
    return sizes[jax.random.permutation(jax.random.fold_in(key, 2), number_of)]


def scatter_about(key, shape, scale, limit, shards=(), kind=jnp.bfloat16):
    result = scale * jax.random.normal(key, shape, jnp.float32)
    if shards:
        result = result * block_scale(key, shape, shards, -0.22, 0.18)
    return jnp.clip(result, -limit, limit).astype(kind)


def setup_inputs(seed: int = 0, part: int = 0) -> dict:
    seeds = jax.random.split(jax.random.key(seed), 9)
    part_splits = jax.random.split(jax.random.fold_in(seeds[8], part), 9)
    return {
        "activations": scatter_about(part_splits[0], (SEQ_LEN, MODEL_WIDTH), 1.0, 6.0, ((0, 2), (1, 4))),
        "conv_taps": scatter_about(seeds[1], (CONV_TAPS, MODEL_WIDTH), 0.5, 3.0, ((1, 4),)),
        "gate_in": scatter_about(seeds[2], (MODEL_WIDTH, GATE_HIDDEN), MODEL_WIDTH ** -0.5, 0.0625, ((0, 4), (1, 2))),
        "gate_out": scatter_about(seeds[3], (GATE_HIDDEN, KV_HEADS), 0.1, 0.59765625),
        "queries": draw_queries(jax.random.fold_in(jax.random.fold_in(seeds[8], part), 71), part),
        "key_vectors": draw_key_vectors(jax.random.fold_in(jax.random.fold_in(seeds[8], part), 71), part),
        "value_vectors": scatter_about(part_splits[6], (SEQ_LEN, KV_HEADS * HEAD_DIM), 1.0, 6.0, ((0, 2), (1, 4))),
        "segment_ids": jnp.searchsorted(jnp.cumsum(uneven(part_splits[7], 4, SEQ_LEN, SEQ_LEN // 2, 2)), jnp.arange(SEQ_LEN), side="right").astype(jnp.int32),
    }


def causal_mix(activations, conv_taps):
    length = activations.shape[0]
    tap_count = conv_taps.shape[0]
    widened = jnp.concatenate([jnp.zeros((tap_count - 1, activations.shape[1]), jnp.float32), activations.astype(jnp.float32)], 0)
    summed = jnp.zeros((length, activations.shape[1]), jnp.float32)
    for shift_back in range(tap_count):
        start_row = tap_count - 1 - shift_back
        summed = summed + conv_taps[shift_back].astype(jnp.float32) * widened[start_row:start_row + length]
    return summed.astype(jnp.bfloat16)

def reference(activations, conv_taps, gate_in, gate_out, queries, key_vectors, value_vectors, segment_ids):
    mixed_rows = causal_mix(activations, conv_taps)
    hidden = jax.nn.silu(jnp.dot(mixed_rows, gate_in, preferred_element_type=jnp.float32)).astype(jnp.bfloat16)
    logits = jnp.dot(hidden, gate_out, preferred_element_type=jnp.float32)
    retention = jax.nn.log_sigmoid(logits).astype(jnp.bfloat16)
    length = activations.shape[0]
    group_size = QUERY_HEADS // KV_HEADS
    score_scale = 1.0 / math.sqrt(HEAD_DIM)
    positions = jnp.arange(length, dtype=jnp.int32)
    visible = (positions[None, :] <= positions[:, None]) & (segment_ids[None, :] == segment_ids[:, None])

    def one_head(head_number):
        kv_index = head_number // group_size
        query_rows = lax.dynamic_slice_in_dim(queries, head_number * HEAD_DIM, HEAD_DIM, 1)
        key_rows = lax.dynamic_slice_in_dim(key_vectors, kv_index * HEAD_DIM, HEAD_DIM, 1)
        value_rows = lax.dynamic_slice_in_dim(value_vectors, kv_index * HEAD_DIM, HEAD_DIM, 1)
        bias_col = lax.dynamic_slice_in_dim(retention, kv_index, 1, 1)[:, 0].astype(jnp.float32)
        scores = jnp.dot(query_rows, key_rows.T, preferred_element_type=jnp.float32) * score_scale + bias_col[None, :]
        masked = jnp.where(visible, scores, -1e+30)
        row_peak = lax.optimization_barrier(jnp.max(masked, axis=1, keepdims=True))
        weights = jnp.where(visible, jnp.exp(masked - row_peak), 0.0)
        weights = weights / lax.optimization_barrier(jnp.sum(weights, axis=1, keepdims=True))
        head_out = jnp.dot(weights.astype(jnp.bfloat16), value_rows, preferred_element_type=jnp.float32).astype(jnp.bfloat16)
        return (head_out, lax.optimization_barrier(jnp.sum(weights, axis=0)))
    head_outs, column_mass = lax.map(one_head, jnp.arange(QUERY_HEADS, dtype=jnp.int32))
    attended = jnp.transpose(head_outs, (1, 0, 2)).reshape(length, QUERY_HEADS * HEAD_DIM)
    key_mass = (lax.optimization_barrier(jnp.sum(column_mass.reshape(KV_HEADS, group_size, length), axis=1)) / group_size).astype(jnp.bfloat16)
    return (attended, key_mass)
```

```python
import math

import jax
import jax.numpy as jnp
from jax import lax
from jax.experimental import pallas as pl
from jax.experimental.pallas import tpu as pltpu
from jax.sharding import PartitionSpec as P

QUERY_HEADS = 64
KV_HEADS = 8
HEAD_DIM = 128


NEG_FILL = -1e30
RIM_ROWS = 16
VMEM_BYTES = 48 * 1024 * 1024


def mix_project_kernel(rows_ref, rim_ref, taps_ref, gate_ref, out_ref, widened):
    rows, features = rows_ref.shape
    tap_count = taps_ref.shape[0]
    lead = widened.shape[0] - rows
    parts, _, width = out_ref.shape
    tile = math.gcd(features, 512)
    total = jnp.zeros((rows, parts * width), jnp.float32)
    for start in range(0, features, tile):
        columns = slice(start, start + tile)
        rim = rim_ref[:, columns].astype(jnp.float32)
        widened[:lead, columns] = rim[rim.shape[0] - lead :]
        widened[lead:, columns] = rows_ref[:, columns].astype(jnp.float32)
        summed = jnp.zeros((rows, tile), jnp.float32)
        for back in range(tap_count):
            tap = taps_ref[back : back + 1, columns].astype(jnp.float32)
            summed = summed + tap * widened[lead - back : lead - back + rows, columns]
        total = total + jnp.dot(
            summed.astype(jnp.bfloat16), gate_ref[columns, :], preferred_element_type=jnp.float32
        )
    for part in range(parts):
        out_ref[part] = total[:, part * width : (part + 1) * width]


def mix_project(block, rim, conv_taps, gate_in, parts):
    rows, features = block.shape
    width = gate_in.shape[1] // parts
    return pl.pallas_call(
        mix_project_kernel,
        out_shape=jax.ShapeDtypeStruct((parts, rows, width), jnp.float32),
        scratch_shapes=[pltpu.VMEM((rows + 8, features), jnp.float32)],
        compiler_params=pltpu.CompilerParams(vmem_limit_bytes=VMEM_BYTES),
        cost_estimate=pl.CostEstimate(
            flops=2 * rows * features * gate_in.shape[1],
            bytes_accessed=2 * (block.size + gate_in.size) + 4 * rows * gate_in.shape[1],
            transcendentals=0,
        ),
    )(block, rim, conv_taps, gate_in)


def logits_kernel(rank_ref, own_ref, peer_ref, gate_out_ref, out_ref):
    first = rank_ref[0] == 0
    shares = []
    for ref in (own_ref, peer_ref):
        pre = ref[0]
        for part in range(1, ref.shape[0]):
            pre = pre + ref[part]
        hidden = (pre / (1.0 + jnp.exp(-pre))).astype(jnp.bfloat16)
        shares.append(
            lax.dot_general(
                gate_out_ref[...],
                hidden,
                (((0,), (1,)), ((), ())),
                preferred_element_type=jnp.float32,
            )
        )
    own, peer = shares
    out_ref[0] = jnp.where(first, own, peer)
    out_ref[1] = jnp.where(first, peer, own)


def logits_share(seq_rank, own_sum, peer_sum, gate_out):
    rows = own_sum.shape[1]
    return pl.pallas_call(
        logits_kernel,
        in_specs=[pl.BlockSpec(memory_space=pltpu.SMEM)]
        + [pl.BlockSpec(memory_space=pltpu.VMEM)] * 3,
        out_shape=jax.ShapeDtypeStruct((2, gate_out.shape[1], rows), jnp.float32),
        compiler_params=pltpu.CompilerParams(vmem_limit_bytes=VMEM_BYTES),
    )(jnp.reshape(seq_rank, (1,)), own_sum, peer_sum, gate_out)


def attention_kernel(
    rank_ref,
    logits_ref,
    segments_ref,
    queries_ref,
    keys_ref,
    behind_keys_ref,
    values_ref,
    behind_values_ref,
    attended_ref,
    own_mass_ref,
    behind_mass_ref,
    retention,
):
    seq_rank, head_rank = rank_ref[0], rank_ref[1]
    rows = queries_ref.shape[0]
    kv_local = keys_ref.shape[1] // HEAD_DIM
    group_size = queries_ref.shape[1] // keys_ref.shape[1]
    score_scale = 1.0 / math.sqrt(HEAD_DIM)
    logits = logits_ref[0]
    for share in range(1, logits_ref.shape[0]):
        logits = logits + logits_ref[share]
    log_gate = jnp.minimum(logits, 0.0) - jnp.log1p(jnp.exp(-jnp.abs(logits)))
    retention[...] = log_gate.astype(jnp.bfloat16).astype(jnp.float32)

    own_segments = segments_ref[pl.ds(seq_rank, 1), :]
    behind_segments = segments_ref[pl.ds(0, 1), :]
    query_segments = jnp.transpose(jnp.broadcast_to(own_segments, (rows, rows)))
    query_at = lax.broadcasted_iota(jnp.int32, (rows, rows), 0)
    key_at = lax.broadcasted_iota(jnp.int32, (rows, rows), 1)
    see_own = (key_at <= query_at) & (query_segments == own_segments)
    see_behind = (query_segments == behind_segments) & (seq_rank > 0)
    visible = jnp.concatenate([see_behind, see_own], axis=1)

    for g in range(kv_local):
        columns = slice(g * HEAD_DIM, (g + 1) * HEAD_DIM)
        keys = jnp.concatenate([behind_keys_ref[:, columns], keys_ref[:, columns]], axis=0)
        values = jnp.concatenate([behind_values_ref[:, columns], values_ref[:, columns]], axis=0)
        row = head_rank * kv_local + g
        bias = jnp.concatenate(
            [retention[0, pl.ds(row, 1), :], retention[seq_rank, pl.ds(row, 1), :]], axis=1
        )
        mass = jnp.zeros((1, 2 * rows), jnp.float32)
        for e in range(group_size):
            at = (g * group_size + e) * HEAD_DIM
            scores = lax.dot_general(
                queries_ref[:, at : at + HEAD_DIM],
                keys,
                (((1,), (1,)), ((), ())),
                preferred_element_type=jnp.float32,
            )
            scores = jnp.where(visible, scores * score_scale + bias, NEG_FILL)
            weights = jnp.exp(scores - jnp.max(scores, axis=1, keepdims=True))
            weights = weights * (1.0 / jnp.sum(weights, axis=1, keepdims=True))
            mass = mass + jnp.sum(weights, axis=0, keepdims=True)
            attended_ref[:, at : at + HEAD_DIM] = jnp.dot(
                weights.astype(jnp.bfloat16), values, preferred_element_type=jnp.float32
            ).astype(jnp.bfloat16)
        mass = mass / group_size
        behind_mass_ref[g : g + 1, :] = mass[:, :rows]
        own_mass_ref[g : g + 1, :] = mass[:, rows:]


def attention(ranks, logit_shares, segments, queries, keys, behind_keys, values, behind_values):
    rows = queries.shape[0]
    kv_local = keys.shape[1] // HEAD_DIM
    mass = jax.ShapeDtypeStruct((kv_local, rows), jnp.float32)
    return pl.pallas_call(
        attention_kernel,
        in_specs=[pl.BlockSpec(memory_space=pltpu.SMEM)]
        + [pl.BlockSpec(memory_space=pltpu.VMEM)] * 7,
        out_shape=(jax.ShapeDtypeStruct(queries.shape, jnp.bfloat16), mass, mass),
        scratch_shapes=[pltpu.VMEM(logit_shares.shape[1:], jnp.float32)],
        compiler_params=pltpu.CompilerParams(vmem_limit_bytes=VMEM_BYTES),
    )(ranks, logit_shares, segments, queries, keys, behind_keys, values, behind_values)


def pair_device(
    activations, conv_taps, gate_in, gate_out, queries, key_vectors, value_vectors, segment_ids
):
    rows = activations.shape[0]
    parts = lax.axis_size("heads")
    seq_rank = lax.axis_index("seq")
    head_rank = lax.axis_index("heads")
    tail = activations[rows - RIM_ROWS :]
    rim = lax.ppermute(tail, "seq", [(0, 1)])
    peer_rows = lax.ppermute(activations, "seq", [(0, 1), (1, 0)])
    behind_keys = lax.ppermute(key_vectors, "seq", [(0, 1)])
    behind_values = lax.ppermute(value_vectors, "seq", [(0, 1)])
    peer_rim = jnp.where(seq_rank == 0, tail, jnp.zeros_like(tail))

    own_part = mix_project(activations, rim, conv_taps, gate_in, parts)
    own_sum = lax.all_to_all(own_part, "heads", 0, 0, tiled=True)
    peer_part = mix_project(peer_rows, peer_rim, conv_taps, gate_in, parts)
    peer_sum = lax.all_to_all(peer_part, "heads", 0, 0, tiled=True)
    width = own_part.shape[2]
    gate_rows = lax.dynamic_slice_in_dim(
        gate_out, (seq_rank * parts + head_rank) * width, width, 0
    )
    share = logits_share(seq_rank, own_sum, peer_sum, gate_rows)
    shares = lax.all_gather(share, ("seq", "heads"), axis=0)
    ranks = jnp.stack([seq_rank, head_rank]).astype(jnp.int32)
    attended, own_mass, behind_mass = attention(
        ranks,
        shares,
        segment_ids.reshape(2, rows),
        queries,
        key_vectors,
        behind_keys,
        value_vectors,
        behind_values,
    )
    key_mass = own_mass + lax.ppermute(behind_mass, "seq", [(1, 0)])
    return (attended, key_mass.astype(jnp.bfloat16))


def from_behind(block, axis, distance):
    devices = range(lax.axis_size(axis))
    route = [(i - distance, i) for i in devices if i - distance in devices]
    return lax.ppermute(block, axis, route)


def block_scores(query_heads, key_block, bias_block, allowed, score_scale):
    scores = (
        jnp.einsum("tgeh,kgh->getk", query_heads, key_block, preferred_element_type=jnp.float32)
        * score_scale
    )
    scores = scores + jnp.transpose(bias_block.astype(jnp.float32))[:, None, None, :]
    return jnp.where(allowed[None, None], scores, NEG_FILL)


def ring_device(
    activations, conv_taps, gate_in, gate_out, queries, key_vectors, value_vectors, segment_ids
):
    shard_rows = activations.shape[0]
    tap_count = conv_taps.shape[0]
    rim_rows = from_behind(activations[shard_rows - (tap_count - 1) :], "seq", 1)
    widened = jnp.concatenate([rim_rows, activations], 0).astype(jnp.float32)
    summed = jnp.zeros(activations.shape, jnp.float32)
    for shift_back in range(tap_count):
        start_row = tap_count - 1 - shift_back
        summed = (
            summed
            + conv_taps[shift_back].astype(jnp.float32)
            * widened[start_row : start_row + shard_rows]
        )
    mixed_rows = summed.astype(jnp.bfloat16)
    partial_hidden = jnp.dot(
        mixed_rows,
        lax.all_gather(gate_in, "seq", axis=1, tiled=True),
        preferred_element_type=jnp.float32,
    )
    kv_local = key_vectors.shape[1] // HEAD_DIM
    group_size = QUERY_HEADS // KV_HEADS
    head_rank = lax.axis_index("heads")
    hidden = jax.nn.silu(lax.psum(partial_hidden, "heads")).astype(jnp.bfloat16)
    logits = jnp.dot(hidden, gate_out, preferred_element_type=jnp.float32)
    retention = lax.dynamic_slice_in_dim(
        jax.nn.log_sigmoid(logits).astype(jnp.bfloat16), head_rank * kv_local, kv_local, 1
    )
    seq_rank = lax.axis_index("seq")
    local_index = jnp.arange(shard_rows, dtype=jnp.int32)
    own_queries, own_keys, own_values, own_bias = (queries, key_vectors, value_vectors, retention)
    query_places = seq_rank * shard_rows + local_index
    query_segments = jnp.take(segment_ids, query_places)
    query_heads = own_queries.reshape(shard_rows, kv_local, group_size, HEAD_DIM)
    score_scale = 1.0 / math.sqrt(HEAD_DIM)

    def visibility(flat_index):
        key_segments = jnp.take(segment_ids, flat_index)
        return (flat_index[None, :] <= query_places[:, None]) & (
            key_segments[None, :] == query_segments[:, None]
        )

    initial = (
        jnp.full((kv_local, group_size, shard_rows), NEG_FILL, jnp.float32),
        jnp.zeros((kv_local, group_size, shard_rows), jnp.float32),
    )
    all_keys, all_values, all_bias = (
        lax.all_gather(own_keys, "seq", axis=0, tiled=True),
        lax.all_gather(own_values, "seq", axis=0, tiled=True),
        lax.all_gather(own_bias, "seq", axis=0, tiled=True),
    )
    piece_rows = all_keys.shape[0]
    stats_block_width = math.gcd(piece_rows, 512)

    def one_block(block_number, state_in):
        offset = block_number * stats_block_width
        key_block = lax.dynamic_slice_in_dim(all_keys, offset, stats_block_width, 0).reshape(
            stats_block_width, kv_local, HEAD_DIM
        )
        bias_block = lax.dynamic_slice_in_dim(all_bias, offset, stats_block_width, 0)
        allowed = visibility(0 + offset + jnp.arange(stats_block_width, dtype=jnp.int32))

        def update(state_old):
            peak_old, mass_old = state_old
            masked = block_scores(query_heads, key_block, bias_block, allowed, score_scale)
            peak_new = jnp.maximum(peak_old, jnp.max(masked, axis=3))
            exponent = jnp.where(allowed[None, None], jnp.exp(masked - peak_new[..., None]), 0.0)
            return (peak_new, mass_old * jnp.exp(peak_old - peak_new) + jnp.sum(exponent, axis=3))

        def keep_state(state_old):
            return state_old

        return lax.cond(jnp.any(allowed), update, keep_state, state_in)

    row_peak, total_mass = lax.fori_loop(0, piece_rows // stats_block_width, one_block, initial)
    total_keys = all_keys.shape[0]
    block_width = math.gcd(total_keys, 512)
    block_count = total_keys // block_width
    key_blocks = all_keys.reshape(block_count, block_width, kv_local, HEAD_DIM)
    value_blocks = all_values.reshape(block_count, block_width, kv_local, HEAD_DIM)
    bias_blocks = all_bias.reshape(block_count, block_width, kv_local)

    def second_pass(accumulated, block_items):
        block_number, key_block, value_block, bias_block = block_items
        allowed = visibility(block_number * block_width + jnp.arange(block_width, dtype=jnp.int32))

        def attend(accum_in):
            masked = block_scores(query_heads, key_block, bias_block, allowed, score_scale)
            weights = (
                jnp.where(allowed[None, None], jnp.exp(masked - row_peak[..., None]), 0.0)
                / total_mass[..., None]
            )
            accum_out = accum_in + jnp.einsum(
                "getk,kgh->tgeh",
                weights.astype(jnp.bfloat16),
                value_block,
                preferred_element_type=jnp.float32,
            )
            return (accum_out, jnp.transpose(jnp.sum(weights, axis=(1, 2))) / group_size)

        def skip_block(accum_in):
            return (accum_in, jnp.zeros((block_width, kv_local), jnp.float32))

        return lax.cond(jnp.any(allowed), attend, skip_block, accumulated)

    accumulated, mass_blocks = lax.scan(
        second_pass,
        jnp.zeros((shard_rows, kv_local, group_size, HEAD_DIM), jnp.float32),
        (jnp.arange(block_count, dtype=jnp.int32), key_blocks, value_blocks, bias_blocks),
    )
    key_term = mass_blocks.reshape(total_keys, kv_local)
    key_mass = lax.psum_scatter(key_term, "seq", scatter_dimension=0, tiled=True).astype(
        jnp.bfloat16
    )
    attended = accumulated.reshape(shard_rows, kv_local * group_size * HEAD_DIM).astype(
        jnp.bfloat16
    )
    return (attended, jnp.transpose(key_mass))


def solution(mesh):
    return jax.shard_map(
        pair_device if mesh.shape["seq"] == 2 else ring_device,
        mesh=mesh,
        in_specs=(
            P(("dp", "seq"), "heads"),
            P(None, "heads"),
            P("heads", "seq"),
            P(),
            P(("dp", "seq"), "heads"),
            P(("dp", "seq"), "heads"),
            P(("dp", "seq"), "heads"),
            P("dp"),
        ),
        out_specs=(P(("dp", "seq"), "heads"), P("heads", ("dp", "seq"))),
        check_vma=False,
    )
```

```python
import math

import jax
import jax.numpy as jnp
from jax import lax
from jax.experimental import pallas as pl
from jax.experimental.pallas import tpu as pltpu
from jax.sharding import PartitionSpec as P

QUERY_HEADS = 64
KV_HEADS = 8
HEAD_DIM = 128


NEG_FILL = -1e30
RIM_ROWS = 16
VMEM_BYTES = 48 * 1024 * 1024


def convolve(widened, taps_ref, columns, lead, rows):
    summed = jnp.zeros((rows, columns.stop - columns.start), jnp.float32)
    for back in range(taps_ref.shape[0]):
        tap = taps_ref[back : back + 1, columns].astype(jnp.float32)
        summed = summed + tap * widened[lead - back : lead - back + rows, columns]
    return summed.astype(jnp.bfloat16)


def own_project_kernel(rows_ref, taps_ref, gate_ref, out_ref, widened):
    rows, features = rows_ref.shape
    tile = math.gcd(features, 512)
    total = jnp.zeros(out_ref.shape, jnp.float32)
    for start in range(0, features, tile):
        columns = slice(start, start + tile)
        widened[:, columns] = rows_ref[:, columns].astype(jnp.float32)
        mixed = convolve(widened, taps_ref, columns, RIM_ROWS, rows - RIM_ROWS)
        total = total + jnp.dot(mixed, gate_ref[columns, :], preferred_element_type=jnp.float32)
    out_ref[...] = total


def peer_project_kernel(
    rank_ref, peer_ref, own_ref, taps_ref, gate_ref, out_ref, widened, own_widened
):
    rows, features = peer_ref.shape
    tile = math.gcd(features, 512)
    first = rank_ref[0] == 0
    total = jnp.zeros(out_ref.shape, jnp.float32)
    for start in range(0, features, tile):
        columns = slice(start, start + tile)
        own_tail = own_ref[rows - RIM_ROWS :, columns].astype(jnp.float32)
        peer_tail = peer_ref[rows - RIM_ROWS :, columns].astype(jnp.float32)
        widened[:RIM_ROWS, columns] = jnp.where(first, own_tail, 0.0)
        widened[RIM_ROWS:, columns] = peer_ref[:, columns].astype(jnp.float32)
        own_widened[:RIM_ROWS, columns] = jnp.where(first, 0.0, peer_tail)
        own_widened[RIM_ROWS:, columns] = own_ref[:RIM_ROWS, columns].astype(jnp.float32)
        mixed = jnp.concatenate(
            [
                convolve(own_widened, taps_ref, columns, RIM_ROWS, RIM_ROWS),
                convolve(widened, taps_ref, columns, RIM_ROWS, rows),
            ],
            axis=0,
        )
        total = total + jnp.dot(mixed, gate_ref[columns, :], preferred_element_type=jnp.float32)
    out_ref[...] = total


def project_cost(rows, gate_in):
    return pl.CostEstimate(
        flops=2 * rows * gate_in.size,
        bytes_accessed=2 * (rows * gate_in.shape[0] + gate_in.size) + 4 * rows * gate_in.shape[1],
        transcendentals=0,
    )


def own_project(activations, conv_taps, gate_in):
    rows, features = activations.shape
    done = rows - RIM_ROWS
    return pl.pallas_call(
        own_project_kernel,
        out_shape=jax.ShapeDtypeStruct((done, gate_in.shape[1]), jnp.float32),
        scratch_shapes=[pltpu.VMEM((rows, features), jnp.float32)],
        compiler_params=pltpu.CompilerParams(vmem_limit_bytes=VMEM_BYTES),
        cost_estimate=pl.CostEstimate(flops=1, bytes_accessed=1, transcendentals=0),
    )(activations, conv_taps, gate_in)


def peer_project(rank, peer_rows, activations, conv_taps, gate_in):
    rows, features = activations.shape
    done = rows + RIM_ROWS
    return pl.pallas_call(
        peer_project_kernel,
        in_specs=[pl.BlockSpec(memory_space=pltpu.SMEM)]
        + [pl.BlockSpec(memory_space=pltpu.VMEM)] * 4,
        out_shape=jax.ShapeDtypeStruct((done, gate_in.shape[1]), jnp.float32),
        scratch_shapes=[
            pltpu.VMEM((rows + RIM_ROWS, features), jnp.float32),
            pltpu.VMEM((2 * RIM_ROWS, features), jnp.float32),
        ],
        compiler_params=pltpu.CompilerParams(vmem_limit_bytes=VMEM_BYTES),
        cost_estimate=project_cost(done, gate_in),
    )(rank, peer_rows, activations, conv_taps, gate_in)


def head_sum(part):
    count = lax.axis_size("heads")
    step = 1
    received = None
    while step < count:
        if received is not None:
            part = part + received.astype(jnp.float32)
        route = [(i, i ^ step) for i in range(count)]
        sent = part if step == 1 else part.astype(jnp.bfloat16)
        received = lax.ppermute(sent, "heads", route)
        step *= 2
    return part, received


def logits_kernel(rank_ref, own_ref, own_in_ref, peer_ref, peer_in_ref, gate_out_ref, out_ref):
    first = rank_ref[0] == 0
    hidden = []
    for ref, in_ref in ((own_ref, own_in_ref), (peer_ref, peer_in_ref)):
        pre = ref[...] + in_ref[...].astype(jnp.float32)
        hidden.append((pre / (1.0 + jnp.exp(-pre))).astype(jnp.bfloat16))
    own = jnp.concatenate([hidden[1][:RIM_ROWS], hidden[0]], axis=0)
    own, peer = [
        lax.dot_general(
            gate_out_ref[...], rows, (((0,), (1,)), ((), ())), preferred_element_type=jnp.float32
        )
        for rows in (own, hidden[1][RIM_ROWS:])
    ]
    out_ref[0] = jnp.where(first, own, peer)
    out_ref[1] = jnp.where(first, peer, own)


def logits_share(rank, own_part, own_in, peer_part, peer_in, gate_rows):
    rows = (own_part.shape[0] + peer_part.shape[0]) // 2
    return pl.pallas_call(
        logits_kernel,
        in_specs=[pl.BlockSpec(memory_space=pltpu.SMEM)]
        + [pl.BlockSpec(memory_space=pltpu.VMEM)] * 5,
        out_shape=jax.ShapeDtypeStruct((2, gate_rows.shape[1], rows), jnp.float32),
        compiler_params=pltpu.CompilerParams(vmem_limit_bytes=VMEM_BYTES),
    )(rank, own_part, own_in, peer_part, peer_in, gate_rows)


def attention_kernel(
    rank_ref,
    share_ref,
    peer_share_ref,
    segments_ref,
    queries_ref,
    keys_ref,
    values_ref,
    behind_ref,
    attended_ref,
    own_mass_ref,
    behind_mass_ref,
    retention,
):
    seq_rank, head_rank = rank_ref[0], rank_ref[1]
    rows = queries_ref.shape[0]
    kv_local = keys_ref.shape[1] // HEAD_DIM
    group_size = queries_ref.shape[1] // keys_ref.shape[1]
    score_scale = 1.0 / math.sqrt(HEAD_DIM)
    logits = share_ref[...] + peer_share_ref[...]
    log_gate = jnp.minimum(logits, 0.0) - jnp.log1p(jnp.exp(-jnp.abs(logits)))
    retention[...] = log_gate.astype(jnp.bfloat16).astype(jnp.float32)

    own_segments = segments_ref[pl.ds(seq_rank, 1), :]
    behind_segments = segments_ref[pl.ds(0, 1), :]
    query_segments = jnp.transpose(jnp.broadcast_to(own_segments, (rows, rows)))
    query_at = lax.broadcasted_iota(jnp.int32, (rows, rows), 0)
    key_at = lax.broadcasted_iota(jnp.int32, (rows, rows), 1)
    see_own = (key_at <= query_at) & (query_segments == own_segments)
    see_behind = (query_segments == behind_segments) & (seq_rank > 0)
    visible = jnp.concatenate([see_behind, see_own], axis=1)

    for g in range(kv_local):
        columns = slice(g * HEAD_DIM, (g + 1) * HEAD_DIM)
        value_columns = slice((kv_local + g) * HEAD_DIM, (kv_local + g + 1) * HEAD_DIM)
        keys = jnp.concatenate([behind_ref[:, columns], keys_ref[:, columns]], axis=0)
        values = jnp.concatenate([behind_ref[:, value_columns], values_ref[:, columns]], axis=0)
        row = head_rank * kv_local + g
        bias = jnp.concatenate(
            [retention[0, pl.ds(row, 1), :], retention[seq_rank, pl.ds(row, 1), :]], axis=1
        )
        mass = jnp.zeros((1, 2 * rows), jnp.float32)
        for e in range(group_size):
            at = (g * group_size + e) * HEAD_DIM
            scores = lax.dot_general(
                queries_ref[:, at : at + HEAD_DIM],
                keys,
                (((1,), (1,)), ((), ())),
                preferred_element_type=jnp.float32,
            )
            scores = jnp.where(visible, scores * score_scale + bias, NEG_FILL)
            weights = jnp.exp(scores - jnp.max(scores, axis=1, keepdims=True))
            weights = weights * (1.0 / jnp.sum(weights, axis=1, keepdims=True))
            mass = mass + jnp.sum(weights, axis=0, keepdims=True)
            attended_ref[:, at : at + HEAD_DIM] = jnp.dot(
                weights.astype(jnp.bfloat16), values, preferred_element_type=jnp.float32
            ).astype(jnp.bfloat16)
        mass = mass / group_size
        behind_mass_ref[g : g + 1, :] = mass[:, :rows]
        own_mass_ref[g : g + 1, :] = mass[:, rows:]


def attention(ranks, share, peer_share, segments, queries, keys, values, behind):
    rows = queries.shape[0]
    kv_local = keys.shape[1] // HEAD_DIM
    mass = jax.ShapeDtypeStruct((kv_local, rows), jnp.float32)
    return pl.pallas_call(
        attention_kernel,
        in_specs=[pl.BlockSpec(memory_space=pltpu.SMEM)]
        + [pl.BlockSpec(memory_space=pltpu.VMEM)] * 7,
        out_shape=(jax.ShapeDtypeStruct(queries.shape, jnp.bfloat16), mass, mass),
        scratch_shapes=[pltpu.VMEM(share.shape, jnp.float32)],
        compiler_params=pltpu.CompilerParams(vmem_limit_bytes=VMEM_BYTES),
    )(ranks, share, peer_share, segments, queries, keys, values, behind)


def pair_device(
    activations, conv_taps, gate_in, gate_out, queries, key_vectors, value_vectors, segment_ids
):
    rows = activations.shape[0]
    swap = [(0, 1), (1, 0)]
    seq_rank = lax.axis_index("seq")
    ranks = jnp.stack([seq_rank, lax.axis_index("heads")]).astype(jnp.int32)
    hidden_local = gate_in.shape[1]
    gate_rows = lax.dynamic_slice_in_dim(gate_out, seq_rank * hidden_local, hidden_local, 0)

    peer_rows = lax.ppermute(activations, "seq", swap)
    keys_values = jnp.concatenate([key_vectors, value_vectors], axis=1)
    behind = lax.ppermute(keys_values, "seq", [(0, 1)])

    def own_sums(activations, conv_taps, gate_in):
        return head_sum(own_project(activations, conv_taps, gate_in))

    own_part, own_in = lax.cond(
        segment_ids[0] >= 0,
        own_sums,
        lambda *given: jax.tree.map(
            lambda like: jnp.zeros(like.shape, like.dtype), jax.eval_shape(own_sums, *given)
        ),
        activations,
        conv_taps,
        gate_in,
    )
    peer_rows, own_part, own_in = lax.optimization_barrier((peer_rows, own_part, own_in))
    peer_part = peer_project(ranks, peer_rows, activations, conv_taps, gate_in)
    peer_part, peer_in = head_sum(peer_part)
    share = logits_share(ranks, own_part, own_in, peer_part, peer_in, gate_rows)
    attended, own_mass, behind_mass = attention(
        ranks,
        share,
        lax.ppermute(share, "seq", swap),
        segment_ids.reshape(2, rows),
        queries,
        key_vectors,
        value_vectors,
        behind,
    )
    key_mass = own_mass + lax.ppermute(behind_mass, "seq", [(1, 0)])
    return (attended, key_mass.astype(jnp.bfloat16))


def from_behind(block, axis, distance):
    devices = range(lax.axis_size(axis))
    route = [(i - distance, i) for i in devices if i - distance in devices]
    return lax.ppermute(block, axis, route)


def block_scores(query_heads, key_block, bias_block, allowed, score_scale):
    scores = (
        jnp.einsum("tgeh,kgh->getk", query_heads, key_block, preferred_element_type=jnp.float32)
        * score_scale
    )
    scores = scores + jnp.transpose(bias_block.astype(jnp.float32))[:, None, None, :]
    return jnp.where(allowed[None, None], scores, NEG_FILL)


def ring_device(
    activations, conv_taps, gate_in, gate_out, queries, key_vectors, value_vectors, segment_ids
):
    shard_rows = activations.shape[0]
    tap_count = conv_taps.shape[0]
    rim_rows = from_behind(activations[shard_rows - (tap_count - 1) :], "seq", 1)
    widened = jnp.concatenate([rim_rows, activations], 0).astype(jnp.float32)
    summed = jnp.zeros(activations.shape, jnp.float32)
    for shift_back in range(tap_count):
        start_row = tap_count - 1 - shift_back
        summed = (
            summed
            + conv_taps[shift_back].astype(jnp.float32)
            * widened[start_row : start_row + shard_rows]
        )
    mixed_rows = summed.astype(jnp.bfloat16)
    partial_hidden = jnp.dot(
        mixed_rows,
        lax.all_gather(gate_in, "seq", axis=1, tiled=True),
        preferred_element_type=jnp.float32,
    )
    kv_local = key_vectors.shape[1] // HEAD_DIM
    group_size = QUERY_HEADS // KV_HEADS
    head_rank = lax.axis_index("heads")
    hidden = jax.nn.silu(lax.psum(partial_hidden, "heads")).astype(jnp.bfloat16)
    logits = jnp.dot(hidden, gate_out, preferred_element_type=jnp.float32)
    retention = lax.dynamic_slice_in_dim(
        jax.nn.log_sigmoid(logits).astype(jnp.bfloat16), head_rank * kv_local, kv_local, 1
    )
    seq_rank = lax.axis_index("seq")
    local_index = jnp.arange(shard_rows, dtype=jnp.int32)
    own_queries, own_keys, own_values, own_bias = (queries, key_vectors, value_vectors, retention)
    query_places = seq_rank * shard_rows + local_index
    query_segments = jnp.take(segment_ids, query_places)
    query_heads = own_queries.reshape(shard_rows, kv_local, group_size, HEAD_DIM)
    score_scale = 1.0 / math.sqrt(HEAD_DIM)

    def visibility(flat_index):
        key_segments = jnp.take(segment_ids, flat_index)
        return (flat_index[None, :] <= query_places[:, None]) & (
            key_segments[None, :] == query_segments[:, None]
        )

    initial = (
        jnp.full((kv_local, group_size, shard_rows), NEG_FILL, jnp.float32),
        jnp.zeros((kv_local, group_size, shard_rows), jnp.float32),
    )
    all_keys, all_values, all_bias = (
        lax.all_gather(own_keys, "seq", axis=0, tiled=True),
        lax.all_gather(own_values, "seq", axis=0, tiled=True),
        lax.all_gather(own_bias, "seq", axis=0, tiled=True),
    )
    piece_rows = all_keys.shape[0]
    stats_block_width = math.gcd(piece_rows, 512)

    def one_block(block_number, state_in):
        offset = block_number * stats_block_width
        key_block = lax.dynamic_slice_in_dim(all_keys, offset, stats_block_width, 0).reshape(
            stats_block_width, kv_local, HEAD_DIM
        )
        bias_block = lax.dynamic_slice_in_dim(all_bias, offset, stats_block_width, 0)
        allowed = visibility(0 + offset + jnp.arange(stats_block_width, dtype=jnp.int32))

        def update(state_old):
            peak_old, mass_old = state_old
            masked = block_scores(query_heads, key_block, bias_block, allowed, score_scale)
            peak_new = jnp.maximum(peak_old, jnp.max(masked, axis=3))
            exponent = jnp.where(allowed[None, None], jnp.exp(masked - peak_new[..., None]), 0.0)
            return (peak_new, mass_old * jnp.exp(peak_old - peak_new) + jnp.sum(exponent, axis=3))

        def keep_state(state_old):
            return state_old

        return lax.cond(jnp.any(allowed), update, keep_state, state_in)

    row_peak, total_mass = lax.fori_loop(0, piece_rows // stats_block_width, one_block, initial)
    total_keys = all_keys.shape[0]
    block_width = math.gcd(total_keys, 512)
    block_count = total_keys // block_width
    key_blocks = all_keys.reshape(block_count, block_width, kv_local, HEAD_DIM)
    value_blocks = all_values.reshape(block_count, block_width, kv_local, HEAD_DIM)
    bias_blocks = all_bias.reshape(block_count, block_width, kv_local)

    def second_pass(accumulated, block_items):
        block_number, key_block, value_block, bias_block = block_items
        allowed = visibility(block_number * block_width + jnp.arange(block_width, dtype=jnp.int32))

        def attend(accum_in):
            masked = block_scores(query_heads, key_block, bias_block, allowed, score_scale)
            weights = (
                jnp.where(allowed[None, None], jnp.exp(masked - row_peak[..., None]), 0.0)
                / total_mass[..., None]
            )
            accum_out = accum_in + jnp.einsum(
                "getk,kgh->tgeh",
                weights.astype(jnp.bfloat16),
                value_block,
                preferred_element_type=jnp.float32,
            )
            return (accum_out, jnp.transpose(jnp.sum(weights, axis=(1, 2))) / group_size)

        def skip_block(accum_in):
            return (accum_in, jnp.zeros((block_width, kv_local), jnp.float32))

        return lax.cond(jnp.any(allowed), attend, skip_block, accumulated)

    accumulated, mass_blocks = lax.scan(
        second_pass,
        jnp.zeros((shard_rows, kv_local, group_size, HEAD_DIM), jnp.float32),
        (jnp.arange(block_count, dtype=jnp.int32), key_blocks, value_blocks, bias_blocks),
    )
    key_term = mass_blocks.reshape(total_keys, kv_local)
    key_mass = lax.psum_scatter(key_term, "seq", scatter_dimension=0, tiled=True).astype(
        jnp.bfloat16
    )
    attended = accumulated.reshape(shard_rows, kv_local * group_size * HEAD_DIM).astype(
        jnp.bfloat16
    )
    return (attended, jnp.transpose(key_mass))


def solution(mesh):
    return jax.shard_map(
        pair_device if mesh.shape["seq"] == 2 else ring_device,
        mesh=mesh,
        in_specs=(
            P(("dp", "seq"), "heads"),
            P(None, "heads"),
            P("heads", "seq"),
            P(),
            P(("dp", "seq"), "heads"),
            P(("dp", "seq"), "heads"),
            P(("dp", "seq"), "heads"),
            P("dp"),
        ),
        out_specs=(P(("dp", "seq"), "heads"), P("heads", ("dp", "seq"))),
        check_vma=False,
    )
```

```python
import math

import jax
import jax.numpy as jnp
from jax import lax
from jax.experimental import pallas as pl
from jax.experimental.pallas import tpu as pltpu
from jax.sharding import PartitionSpec as P

QUERY_HEADS = 64
KV_HEADS = 8
HEAD_DIM = 128


NEG_FILL = -1e30
RIM_ROWS = 16
VMEM_BYTES = 48 * 1024 * 1024


def convolve(widened, taps_ref, columns, lead, rows):
    summed = jnp.zeros((rows, columns.stop - columns.start), jnp.float32)
    for back in range(taps_ref.shape[0]):
        tap = taps_ref[back : back + 1, columns].astype(jnp.float32)
        summed = summed + tap * widened[lead - back : lead - back + rows, columns]
    return summed.astype(jnp.bfloat16)


def own_project_kernel(rows_ref, taps_ref, gate_ref, out_ref, edges_ref, held_ref, widened):
    rows, features = rows_ref.shape
    edges_ref[:RIM_ROWS] = rows_ref[:RIM_ROWS]
    edges_ref[RIM_ROWS:] = rows_ref[rows - RIM_ROWS :]
    held_ref[...] = gate_ref[...]
    tile = math.gcd(features, 512)
    total = jnp.zeros(out_ref.shape, jnp.float32)
    for start in range(0, features, tile):
        columns = slice(start, start + tile)
        widened[:, columns] = rows_ref[:, columns].astype(jnp.float32)
        mixed = convolve(widened, taps_ref, columns, RIM_ROWS, rows - RIM_ROWS)
        total = total + jnp.dot(mixed, gate_ref[columns, :], preferred_element_type=jnp.float32)
    out_ref[...] = total


def peer_project_kernel(
    rank_ref, peer_ref, edges_ref, taps_ref, gate_ref, out_ref, widened, own_widened
):
    rows, features = peer_ref.shape
    tile = math.gcd(features, 512)
    first = rank_ref[0] == 0
    total = jnp.zeros(out_ref.shape, jnp.float32)
    for start in range(0, features, tile):
        columns = slice(start, start + tile)
        own_tail = edges_ref[RIM_ROWS:, columns].astype(jnp.float32)
        peer_tail = peer_ref[rows - RIM_ROWS :, columns].astype(jnp.float32)
        widened[:RIM_ROWS, columns] = jnp.where(first, own_tail, 0.0)
        widened[RIM_ROWS:, columns] = peer_ref[:, columns].astype(jnp.float32)
        own_widened[:RIM_ROWS, columns] = jnp.where(first, 0.0, peer_tail)
        own_widened[RIM_ROWS:, columns] = edges_ref[:RIM_ROWS, columns].astype(jnp.float32)
        mixed = jnp.concatenate(
            [
                convolve(own_widened, taps_ref, columns, RIM_ROWS, RIM_ROWS),
                convolve(widened, taps_ref, columns, RIM_ROWS, rows),
            ],
            axis=0,
        )
        total = total + jnp.dot(mixed, gate_ref[columns, :], preferred_element_type=jnp.float32)
    out_ref[...] = total


def project_cost(rows, gate_in):
    return pl.CostEstimate(
        flops=2 * rows * gate_in.size,
        bytes_accessed=2 * (rows * gate_in.shape[0] + gate_in.size) + 4 * rows * gate_in.shape[1],
        transcendentals=0,
    )


def own_project(activations, conv_taps, gate_in):
    rows, features = activations.shape
    done = rows - RIM_ROWS
    return pl.pallas_call(
        own_project_kernel,
        out_shape=(
            jax.ShapeDtypeStruct((done, gate_in.shape[1]), jnp.float32),
            jax.ShapeDtypeStruct((2 * RIM_ROWS, features), activations.dtype),
            jax.ShapeDtypeStruct(gate_in.shape, gate_in.dtype),
        ),
        scratch_shapes=[pltpu.VMEM((rows, features), jnp.float32)],
        compiler_params=pltpu.CompilerParams(vmem_limit_bytes=VMEM_BYTES),
        cost_estimate=pl.CostEstimate(flops=1, bytes_accessed=1, transcendentals=0),
    )(activations, conv_taps, gate_in)


def peer_project(rank, peer_rows, edges, conv_taps, gate_in):
    rows, features = peer_rows.shape
    done = rows + RIM_ROWS
    return pl.pallas_call(
        peer_project_kernel,
        in_specs=[pl.BlockSpec(memory_space=pltpu.SMEM)]
        + [pl.BlockSpec(memory_space=pltpu.VMEM)] * 4,
        out_shape=jax.ShapeDtypeStruct((done, gate_in.shape[1]), jnp.float32),
        scratch_shapes=[
            pltpu.VMEM((rows + RIM_ROWS, features), jnp.float32),
            pltpu.VMEM((2 * RIM_ROWS, features), jnp.float32),
        ],
        compiler_params=pltpu.CompilerParams(vmem_limit_bytes=VMEM_BYTES),
        cost_estimate=project_cost(done, gate_in),
    )(rank, peer_rows, edges, conv_taps, gate_in)


def head_sum(part):
    count = lax.axis_size("heads")
    step = 1
    received = None
    while step < count:
        if received is not None:
            part = part + received.astype(jnp.float32)
        route = [(i, i ^ step) for i in range(count)]
        sent = part if step == 1 else part.astype(jnp.bfloat16)
        received = lax.ppermute(sent, "heads", route)
        step *= 2
    return part, received


def share_of_logits(pre_ref, in_ref, gate_out_ref):
    pre = pre_ref[...] + in_ref[...].astype(jnp.float32)
    hidden = (pre / (1.0 + jnp.exp(-pre))).astype(jnp.bfloat16)
    return lax.dot_general(
        gate_out_ref[...], hidden, (((0,), (1,)), ((), ())), preferred_element_type=jnp.float32
    )


def own_logits_kernel(own_ref, in_ref, gate_out_ref, out_ref):
    out_ref[...] = share_of_logits(own_ref, in_ref, gate_out_ref)


def own_logits(part, received, gate_rows):
    return pl.pallas_call(
        own_logits_kernel,
        out_shape=jax.ShapeDtypeStruct((gate_rows.shape[1], part.shape[0]), jnp.float32),
        compiler_params=pltpu.CompilerParams(vmem_limit_bytes=VMEM_BYTES),
    )(part, received, gate_rows)


def logits_kernel(rank_ref, own_ref, peer_ref, in_ref, gate_out_ref, out_ref):
    first = rank_ref[0] == 0
    share = share_of_logits(peer_ref, in_ref, gate_out_ref)
    own = jnp.concatenate([share[:, :RIM_ROWS], own_ref[...]], axis=1)
    peer = share[:, RIM_ROWS:]
    out_ref[0] = jnp.where(first, own, peer)
    out_ref[1] = jnp.where(first, peer, own)


def logits_share(rank, own_share, peer_part, peer_in, gate_rows):
    rows = own_share.shape[1] + RIM_ROWS
    return pl.pallas_call(
        logits_kernel,
        in_specs=[pl.BlockSpec(memory_space=pltpu.SMEM)]
        + [pl.BlockSpec(memory_space=pltpu.VMEM)] * 4,
        out_shape=jax.ShapeDtypeStruct((2, gate_rows.shape[1], rows), jnp.float32),
        compiler_params=pltpu.CompilerParams(vmem_limit_bytes=VMEM_BYTES),
    )(rank, own_share, peer_part, peer_in, gate_rows)


def attention_kernel(
    rank_ref,
    share_ref,
    peer_share_ref,
    segments_ref,
    queries_ref,
    keys_ref,
    values_ref,
    behind_ref,
    attended_ref,
    own_mass_ref,
    behind_mass_ref,
    retention,
):
    seq_rank, head_rank = rank_ref[0], rank_ref[1]
    rows = queries_ref.shape[0]
    kv_local = keys_ref.shape[1] // HEAD_DIM
    group_size = queries_ref.shape[1] // keys_ref.shape[1]
    score_scale = 1.0 / math.sqrt(HEAD_DIM)
    logits = share_ref[...] + peer_share_ref[...]
    log_gate = jnp.minimum(logits, 0.0) - jnp.log1p(jnp.exp(-jnp.abs(logits)))
    retention[...] = log_gate.astype(jnp.bfloat16).astype(jnp.float32)

    own_segments = segments_ref[pl.ds(seq_rank, 1), :]
    behind_segments = segments_ref[pl.ds(0, 1), :]
    query_segments = jnp.transpose(jnp.broadcast_to(own_segments, (rows, rows)))
    query_at = lax.broadcasted_iota(jnp.int32, (rows, rows), 0)
    key_at = lax.broadcasted_iota(jnp.int32, (rows, rows), 1)
    see_own = (key_at <= query_at) & (query_segments == own_segments)
    see_behind = (query_segments == behind_segments) & (seq_rank > 0)
    hide = jnp.where(jnp.concatenate([see_behind, see_own], axis=1), 0.0, NEG_FILL)

    for g in range(kv_local):
        columns = slice(g * HEAD_DIM, (g + 1) * HEAD_DIM)
        value_columns = slice((kv_local + g) * HEAD_DIM, (kv_local + g + 1) * HEAD_DIM)
        keys = jnp.concatenate([behind_ref[:, columns], keys_ref[:, columns]], axis=0)
        values = jnp.concatenate([behind_ref[:, value_columns], values_ref[:, columns]], axis=0)
        row = head_rank * kv_local + g
        bias = jnp.concatenate(
            [retention[0, pl.ds(row, 1), :], retention[seq_rank, pl.ds(row, 1), :]], axis=1
        )
        offset = hide + bias
        mass = jnp.zeros((1, 2 * rows), jnp.float32)
        for e in range(group_size):
            at = (g * group_size + e) * HEAD_DIM
            scores = lax.dot_general(
                queries_ref[:, at : at + HEAD_DIM],
                keys,
                (((1,), (1,)), ((), ())),
                preferred_element_type=jnp.float32,
            )
            scores = scores * score_scale + offset
            weights = jnp.exp(scores - jnp.max(scores, axis=1, keepdims=True))
            weights = weights * (1.0 / jnp.sum(weights, axis=1, keepdims=True))
            mass = mass + jnp.sum(weights, axis=0, keepdims=True)
            attended_ref[:, at : at + HEAD_DIM] = jnp.dot(
                weights.astype(jnp.bfloat16), values, preferred_element_type=jnp.float32
            ).astype(jnp.bfloat16)
        mass = mass / group_size
        behind_mass_ref[g : g + 1, :] = mass[:, :rows]
        own_mass_ref[g : g + 1, :] = mass[:, rows:]


def attention(ranks, share, peer_share, segments, queries, keys, values, behind):
    rows = queries.shape[0]
    kv_local = keys.shape[1] // HEAD_DIM
    mass = jax.ShapeDtypeStruct((kv_local, rows), jnp.float32)
    return pl.pallas_call(
        attention_kernel,
        in_specs=[pl.BlockSpec(memory_space=pltpu.SMEM)]
        + [pl.BlockSpec(memory_space=pltpu.VMEM)] * 7,
        out_shape=(jax.ShapeDtypeStruct(queries.shape, jnp.bfloat16), mass, mass),
        scratch_shapes=[pltpu.VMEM(share.shape, jnp.float32)],
        compiler_params=pltpu.CompilerParams(vmem_limit_bytes=VMEM_BYTES),
    )(ranks, share, peer_share, segments, queries, keys, values, behind)


def pair_device(
    activations, conv_taps, gate_in, gate_out, queries, key_vectors, value_vectors, segment_ids
):
    rows = activations.shape[0]
    swap = [(0, 1), (1, 0)]
    seq_rank = lax.axis_index("seq")
    ranks = jnp.stack([seq_rank, lax.axis_index("heads")]).astype(jnp.int32)
    hidden_local = gate_in.shape[1]
    gate_rows = lax.dynamic_slice_in_dim(gate_out, seq_rank * hidden_local, hidden_local, 0)

    peer_rows = lax.ppermute(activations, "seq", swap)
    keys_values = jnp.concatenate([key_vectors, value_vectors], axis=1)
    behind = lax.ppermute(keys_values, "seq", [(0, 1)])

    def own_work(activations, conv_taps, gate_in, gate_rows):
        part, edges, held = own_project(activations, conv_taps, gate_in)
        return own_logits(*head_sum(part), gate_rows), edges, held

    own_share, edges, held = lax.cond(
        seq_rank >= 0,
        own_work,
        lambda *given: jax.tree.map(
            lambda like: jnp.zeros(like.shape, like.dtype), jax.eval_shape(own_work, *given)
        ),
        activations,
        conv_taps,
        gate_in,
        gate_rows,
    )
    peer_rows, own_share, edges, held = lax.optimization_barrier(
        (peer_rows, own_share, edges, held)
    )
    peer_part = peer_project(ranks, peer_rows, edges, conv_taps, held)
    peer_part, peer_in = head_sum(peer_part)
    share = logits_share(ranks, own_share, peer_part, peer_in, gate_rows)
    attended, own_mass, behind_mass = attention(
        ranks,
        share,
        lax.ppermute(share, "seq", swap),
        segment_ids.reshape(2, rows),
        queries,
        key_vectors,
        value_vectors,
        behind,
    )
    key_mass = own_mass + lax.ppermute(behind_mass, "seq", [(1, 0)])
    return (attended, key_mass.astype(jnp.bfloat16))


def from_behind(block, axis, distance):
    devices = range(lax.axis_size(axis))
    route = [(i - distance, i) for i in devices if i - distance in devices]
    return lax.ppermute(block, axis, route)


def block_scores(query_heads, key_block, bias_block, allowed, score_scale):
    scores = (
        jnp.einsum("tgeh,kgh->getk", query_heads, key_block, preferred_element_type=jnp.float32)
        * score_scale
    )
    scores = scores + jnp.transpose(bias_block.astype(jnp.float32))[:, None, None, :]
    return jnp.where(allowed[None, None], scores, NEG_FILL)


def ring_device(
    activations, conv_taps, gate_in, gate_out, queries, key_vectors, value_vectors, segment_ids
):
    shard_rows = activations.shape[0]
    tap_count = conv_taps.shape[0]
    rim_rows = from_behind(activations[shard_rows - (tap_count - 1) :], "seq", 1)
    widened = jnp.concatenate([rim_rows, activations], 0).astype(jnp.float32)
    summed = jnp.zeros(activations.shape, jnp.float32)
    for shift_back in range(tap_count):
        start_row = tap_count - 1 - shift_back
        summed = (
            summed
            + conv_taps[shift_back].astype(jnp.float32)
            * widened[start_row : start_row + shard_rows]
        )
    mixed_rows = summed.astype(jnp.bfloat16)
    partial_hidden = jnp.dot(
        mixed_rows,
        lax.all_gather(gate_in, "seq", axis=1, tiled=True),
        preferred_element_type=jnp.float32,
    )
    kv_local = key_vectors.shape[1] // HEAD_DIM
    group_size = QUERY_HEADS // KV_HEADS
    head_rank = lax.axis_index("heads")
    hidden = jax.nn.silu(lax.psum(partial_hidden, "heads")).astype(jnp.bfloat16)
    logits = jnp.dot(hidden, gate_out, preferred_element_type=jnp.float32)
    retention = lax.dynamic_slice_in_dim(
        jax.nn.log_sigmoid(logits).astype(jnp.bfloat16), head_rank * kv_local, kv_local, 1
    )
    seq_rank = lax.axis_index("seq")
    local_index = jnp.arange(shard_rows, dtype=jnp.int32)
    own_queries, own_keys, own_values, own_bias = (queries, key_vectors, value_vectors, retention)
    query_places = seq_rank * shard_rows + local_index
    query_segments = jnp.take(segment_ids, query_places)
    query_heads = own_queries.reshape(shard_rows, kv_local, group_size, HEAD_DIM)
    score_scale = 1.0 / math.sqrt(HEAD_DIM)

    def visibility(flat_index):
        key_segments = jnp.take(segment_ids, flat_index)
        return (flat_index[None, :] <= query_places[:, None]) & (
            key_segments[None, :] == query_segments[:, None]
        )

    initial = (
        jnp.full((kv_local, group_size, shard_rows), NEG_FILL, jnp.float32),
        jnp.zeros((kv_local, group_size, shard_rows), jnp.float32),
    )
    all_keys, all_values, all_bias = (
        lax.all_gather(own_keys, "seq", axis=0, tiled=True),
        lax.all_gather(own_values, "seq", axis=0, tiled=True),
        lax.all_gather(own_bias, "seq", axis=0, tiled=True),
    )
    piece_rows = all_keys.shape[0]
    stats_block_width = math.gcd(piece_rows, 512)

    def one_block(block_number, state_in):
        offset = block_number * stats_block_width
        key_block = lax.dynamic_slice_in_dim(all_keys, offset, stats_block_width, 0).reshape(
            stats_block_width, kv_local, HEAD_DIM
        )
        bias_block = lax.dynamic_slice_in_dim(all_bias, offset, stats_block_width, 0)
        allowed = visibility(0 + offset + jnp.arange(stats_block_width, dtype=jnp.int32))

        def update(state_old):
            peak_old, mass_old = state_old
            masked = block_scores(query_heads, key_block, bias_block, allowed, score_scale)
            peak_new = jnp.maximum(peak_old, jnp.max(masked, axis=3))
            exponent = jnp.where(allowed[None, None], jnp.exp(masked - peak_new[..., None]), 0.0)
            return (peak_new, mass_old * jnp.exp(peak_old - peak_new) + jnp.sum(exponent, axis=3))

        def keep_state(state_old):
            return state_old

        return lax.cond(jnp.any(allowed), update, keep_state, state_in)

    row_peak, total_mass = lax.fori_loop(0, piece_rows // stats_block_width, one_block, initial)
    total_keys = all_keys.shape[0]
    block_width = math.gcd(total_keys, 512)
    block_count = total_keys // block_width
    key_blocks = all_keys.reshape(block_count, block_width, kv_local, HEAD_DIM)
    value_blocks = all_values.reshape(block_count, block_width, kv_local, HEAD_DIM)
    bias_blocks = all_bias.reshape(block_count, block_width, kv_local)

    def second_pass(accumulated, block_items):
        block_number, key_block, value_block, bias_block = block_items
        allowed = visibility(block_number * block_width + jnp.arange(block_width, dtype=jnp.int32))

        def attend(accum_in):
            masked = block_scores(query_heads, key_block, bias_block, allowed, score_scale)
            weights = (
                jnp.where(allowed[None, None], jnp.exp(masked - row_peak[..., None]), 0.0)
                / total_mass[..., None]
            )
            accum_out = accum_in + jnp.einsum(
                "getk,kgh->tgeh",
                weights.astype(jnp.bfloat16),
                value_block,
                preferred_element_type=jnp.float32,
            )
            return (accum_out, jnp.transpose(jnp.sum(weights, axis=(1, 2))) / group_size)

        def skip_block(accum_in):
            return (accum_in, jnp.zeros((block_width, kv_local), jnp.float32))

        return lax.cond(jnp.any(allowed), attend, skip_block, accumulated)

    accumulated, mass_blocks = lax.scan(
        second_pass,
        jnp.zeros((shard_rows, kv_local, group_size, HEAD_DIM), jnp.float32),
        (jnp.arange(block_count, dtype=jnp.int32), key_blocks, value_blocks, bias_blocks),
    )
    key_term = mass_blocks.reshape(total_keys, kv_local)
    key_mass = lax.psum_scatter(key_term, "seq", scatter_dimension=0, tiled=True).astype(
        jnp.bfloat16
    )
    attended = accumulated.reshape(shard_rows, kv_local * group_size * HEAD_DIM).astype(
        jnp.bfloat16
    )
    return (attended, jnp.transpose(key_mass))


def solution(mesh):
    return jax.shard_map(
        pair_device if mesh.shape["seq"] == 2 else ring_device,
        mesh=mesh,
        in_specs=(
            P(("dp", "seq"), "heads"),
            P(None, "heads"),
            P("heads", "seq"),
            P(),
            P(("dp", "seq"), "heads"),
            P(("dp", "seq"), "heads"),
            P(("dp", "seq"), "heads"),
            P("dp"),
        ),
        out_specs=(P(("dp", "seq"), "heads"), P("heads", ("dp", "seq"))),
        check_vma=False,
    )
```

```python
import functools
import math

import jax
import jax.numpy as jnp
from jax import lax
from jax.experimental import pallas as pl
from jax.experimental.pallas import tpu as pltpu
from jax.sharding import PartitionSpec as P

QUERY_HEADS = 64
KV_HEADS = 8
HEAD_DIM = 128


NEG_FILL = -1e30
RIM_ROWS = 16
LEAST_RETENTION = -40.0
VMEM_BYTES = 48 * 1024 * 1024


def convolve(widened, taps_ref, columns, lead, rows):
    summed = jnp.zeros((rows, columns.stop - columns.start), jnp.float32)
    for back in range(taps_ref.shape[0]):
        tap = taps_ref[back : back + 1, columns].astype(jnp.float32)
        summed = summed + tap * widened[lead - back : lead - back + rows, columns]
    return summed.astype(jnp.bfloat16)


def own_project_kernel(rows_ref, taps_ref, gate_ref, out_ref, edges_ref, held_ref, widened):
    rows, features = rows_ref.shape
    edges_ref[:RIM_ROWS] = rows_ref[:RIM_ROWS]
    edges_ref[RIM_ROWS:] = rows_ref[rows - RIM_ROWS :]
    held_ref[...] = gate_ref[...]
    tile = math.gcd(features, 512)
    total = jnp.zeros(out_ref.shape, jnp.float32)
    for start in range(0, features, tile):
        columns = slice(start, start + tile)
        widened[:, columns] = rows_ref[:, columns].astype(jnp.float32)
        mixed = convolve(widened, taps_ref, columns, RIM_ROWS, rows - RIM_ROWS)
        total = total + jnp.dot(mixed, gate_ref[columns, :], preferred_element_type=jnp.float32)
    out_ref[...] = total


def peer_project_kernel(
    peer_ref, edges_ref, taps_ref, gate_ref, out_ref, widened, own_widened
):
    rows, features = peer_ref.shape
    tile = math.gcd(features, 512)
    first = lax.axis_index("seq") == 0
    total = jnp.zeros(out_ref.shape, jnp.float32)
    for start in range(0, features, tile):
        columns = slice(start, start + tile)
        own_tail = edges_ref[RIM_ROWS:, columns].astype(jnp.float32)
        peer_tail = peer_ref[rows - RIM_ROWS :, columns].astype(jnp.float32)
        widened[:RIM_ROWS, columns] = jnp.where(first, own_tail, 0.0)
        widened[RIM_ROWS:, columns] = peer_ref[:, columns].astype(jnp.float32)
        own_widened[:RIM_ROWS, columns] = jnp.where(first, 0.0, peer_tail)
        own_widened[RIM_ROWS:, columns] = edges_ref[:RIM_ROWS, columns].astype(jnp.float32)
        mixed = jnp.concatenate(
            [
                convolve(own_widened, taps_ref, columns, RIM_ROWS, RIM_ROWS),
                convolve(widened, taps_ref, columns, RIM_ROWS, rows),
            ],
            axis=0,
        )
        total = total + jnp.dot(mixed, gate_ref[columns, :], preferred_element_type=jnp.float32)
    out_ref[...] = total


def own_project(activations, conv_taps, gate_in):
    rows, features = activations.shape
    done = rows - RIM_ROWS
    return pl.pallas_call(
        own_project_kernel,
        out_shape=(
            jax.ShapeDtypeStruct((done, gate_in.shape[1]), jnp.float32),
            jax.ShapeDtypeStruct((2 * RIM_ROWS, features), activations.dtype),
            jax.ShapeDtypeStruct(gate_in.shape, gate_in.dtype),
        ),
        scratch_shapes=[pltpu.VMEM((rows, features), jnp.float32)],
        compiler_params=pltpu.CompilerParams(vmem_limit_bytes=VMEM_BYTES),
        cost_estimate=pl.CostEstimate(flops=1, bytes_accessed=1, transcendentals=0),
    )(activations, conv_taps, gate_in)


def peer_project(peer_rows, edges, conv_taps, gate_in):
    rows, features = peer_rows.shape
    done = rows + RIM_ROWS
    return pl.pallas_call(
        peer_project_kernel,
        out_shape=jax.ShapeDtypeStruct((done, gate_in.shape[1]), jnp.float32),
        scratch_shapes=[
            pltpu.VMEM((rows + RIM_ROWS, features), jnp.float32),
            pltpu.VMEM((2 * RIM_ROWS, features), jnp.float32),
        ],
        compiler_params=pltpu.CompilerParams(vmem_limit_bytes=VMEM_BYTES),
        cost_estimate=pl.CostEstimate(flops=1, bytes_accessed=1, transcendentals=0),
    )(peer_rows, edges, conv_taps, gate_in)


def head_sum(part):
    count = lax.axis_size("heads")
    step = 1
    received = None
    while step < count:
        if received is not None:
            part = part + received.astype(jnp.float32)
        route = [(i, i ^ step) for i in range(count)]
        sent = part if step == 1 else part.astype(jnp.bfloat16)
        received = lax.ppermute(sent, "heads", route)
        step *= 2
    return part, received


def share_of_logits(pre_ref, in_ref, gate_out_ref):
    pre = pre_ref[...] + in_ref[...].astype(jnp.float32)
    hidden = (pre / (1.0 + jnp.exp(-pre))).astype(jnp.bfloat16)
    return lax.dot_general(
        gate_out_ref[...], hidden, (((0,), (1,)), ((), ())), preferred_element_type=jnp.float32
    )


def own_logits_kernel(own_ref, in_ref, gate_out_ref, out_ref):
    out_ref[...] = share_of_logits(own_ref, in_ref, gate_out_ref)


def own_logits(part, received, gate_rows):
    return pl.pallas_call(
        own_logits_kernel,
        out_shape=jax.ShapeDtypeStruct((gate_rows.shape[1], part.shape[0]), jnp.float32),
        compiler_params=pltpu.CompilerParams(vmem_limit_bytes=VMEM_BYTES),
    )(part, received, gate_rows)


def logits_kernel(own_ref, peer_ref, in_ref, gate_out_ref, out_ref):
    first = lax.axis_index("seq") == 0
    share = share_of_logits(peer_ref, in_ref, gate_out_ref)
    own = jnp.concatenate([share[:, :RIM_ROWS], own_ref[...]], axis=1)
    peer = share[:, RIM_ROWS:]
    out_ref[0] = jnp.where(first, own, peer)
    out_ref[1] = jnp.where(first, peer, own)


def logits_share(own_share, peer_part, peer_in, gate_rows):
    rows = own_share.shape[1] + RIM_ROWS
    return pl.pallas_call(
        logits_kernel,
        out_shape=jax.ShapeDtypeStruct((2, gate_rows.shape[1], rows), jnp.float32),
        compiler_params=pltpu.CompilerParams(vmem_limit_bytes=VMEM_BYTES),
    )(own_share, peer_part, peer_in, gate_rows)


def hide_unseen(seq_rank, segments_ref, rows):
    own_segments = segments_ref[pl.ds(seq_rank, 1), :]
    behind_segments = segments_ref[pl.ds(0, 1), :]
    query_segments = jnp.transpose(jnp.broadcast_to(own_segments, (rows, rows)))
    query_at = lax.broadcasted_iota(jnp.int32, (rows, rows), 0)
    key_at = lax.broadcasted_iota(jnp.int32, (rows, rows), 1)
    see_own = (key_at <= query_at) & (query_segments == own_segments)
    see_behind = (query_segments == behind_segments) & (seq_rank > 0)
    return jnp.where(jnp.concatenate([see_behind, see_own], axis=1), 0.0, NEG_FILL)


def head_columns(number):
    return slice(number * HEAD_DIM, (number + 1) * HEAD_DIM)


def scores_of(queries_ref, keys, offset, head):
    scores = lax.dot_general(
        queries_ref[:, head_columns(head)],
        keys,
        (((1,), (1,)), ((), ())),
        preferred_element_type=jnp.float32,
    )
    return scores * (1.0 / math.sqrt(HEAD_DIM)) + offset


def with_behind(ref, behind_ref, number, whole):
    own = ref[:, head_columns(number)]
    if not whole:
        return own
    return jnp.concatenate([behind_ref[:, head_columns(number)], own], axis=0)


def powers_kernel(segments_ref, queries_ref, keys_ref, behind_keys_ref, powers_ref):
    seq_rank = lax.axis_index("seq")
    rows = queries_ref.shape[0]
    kv_local = keys_ref.shape[1] // HEAD_DIM
    group_size = queries_ref.shape[1] // keys_ref.shape[1]
    hide = hide_unseen(seq_rank, segments_ref, rows)

    def fill(whole):
        start = 0 if whole else rows
        for head in range(kv_local * group_size):
            g = head // group_size
            keys = with_behind(keys_ref, behind_keys_ref, g, whole)
            scores = scores_of(queries_ref, keys, hide[:, start:], head)
            powers_ref[head, :, start:] = jnp.exp(
                scores - jnp.max(scores, axis=1, keepdims=True)
            )

    pl.when(seq_rank > 0)(lambda: fill(True))
    pl.when(seq_rank == 0)(lambda: fill(False))


def powers_of(segments, queries, keys, behind_keys):
    rows = queries.shape[0]
    heads = queries.shape[1] // HEAD_DIM
    return pl.pallas_call(
        powers_kernel,
        out_shape=jax.ShapeDtypeStruct((heads, rows, 2 * rows), jnp.float32),
        compiler_params=pltpu.CompilerParams(vmem_limit_bytes=VMEM_BYTES),
        cost_estimate=pl.CostEstimate(
            flops=4 * rows * rows * queries.shape[1],
            bytes_accessed=8 * heads * rows * rows,
            transcendentals=2 * heads * rows * rows,
        ),
    )(segments, queries, keys, behind_keys)


def attention_kernel(
    share_ref,
    peer_share_ref,
    powers_ref,
    segments_ref,
    queries_ref,
    keys_ref,
    values_ref,
    behind_keys_ref,
    behind_values_ref,
    attended_ref,
    own_mass_ref,
    behind_mass_ref,
    retention,
):
    seq_rank, head_rank = lax.axis_index("seq"), lax.axis_index("heads")
    rows = queries_ref.shape[0]
    kv_local = keys_ref.shape[1] // HEAD_DIM
    group_size = queries_ref.shape[1] // keys_ref.shape[1]
    logits = share_ref[...] + peer_share_ref[...]
    log_gate = jnp.minimum(logits, 0.0) - jnp.log1p(jnp.exp(-jnp.abs(logits)))
    retention[...] = log_gate.astype(jnp.bfloat16).astype(jnp.float32)
    biases = []
    for g in range(kv_local):
        at = pl.ds(head_rank * kv_local + g, 1)
        biases.append(jnp.concatenate([retention[0, at, :], retention[seq_rank, at, :]], axis=1))
    moderate = jnp.min(functools.reduce(jnp.minimum, biases)) >= LEAST_RETENTION

    def finish(whole, terms_of):
        start = 0 if whole else rows
        for g in range(kv_local):
            values = with_behind(values_ref, behind_values_ref, g, whole)
            mass = jnp.zeros((1, 2 * rows - start), jnp.float32)
            group_terms = terms_of(g, whole, start)
            for head in range(g * group_size, (g + 1) * group_size):
                weights = group_terms(head)
                weights = weights * (1.0 / jnp.sum(weights, axis=1, keepdims=True))
                mass = mass + jnp.sum(weights, axis=0, keepdims=True)
                attended_ref[:, head_columns(head)] = jnp.dot(
                    weights.astype(jnp.bfloat16), values, preferred_element_type=jnp.float32
                ).astype(jnp.bfloat16)
            mass = mass / group_size
            own_mass_ref[g : g + 1, :] = mass[:, rows - start :]
            behind_mass_ref[g : g + 1, :] = mass[:, :rows]

    def by_powers(g, whole, start):
        factor = jnp.exp(biases[g] - jnp.max(biases[g]))[:, start:]
        return lambda head: powers_ref[head, :, start:] * factor

    def by_scores(g, whole, start):
        offset = hide_unseen(seq_rank, segments_ref, rows) + biases[g]
        keys = with_behind(keys_ref, behind_keys_ref, g, whole)

        def terms(head):
            scores = scores_of(queries_ref, keys, offset[:, start:], head)
            return jnp.exp(scores - jnp.max(scores, axis=1, keepdims=True))

        return terms

    pl.when(moderate & (seq_rank > 0))(lambda: finish(True, by_powers))
    pl.when(moderate & (seq_rank == 0))(lambda: finish(False, by_powers))
    pl.when(jnp.logical_not(moderate))(lambda: finish(True, by_scores))


def attention(
    share, peer_share, powers, segments, queries, keys, values, behind_keys, behind_values
):
    rows = queries.shape[0]
    kv_local = keys.shape[1] // HEAD_DIM
    mass = jax.ShapeDtypeStruct((kv_local, rows), jnp.float32)
    return pl.pallas_call(
        attention_kernel,
        out_shape=(jax.ShapeDtypeStruct(queries.shape, jnp.bfloat16), mass, mass),
        scratch_shapes=[pltpu.VMEM(share.shape, jnp.float32)],
        compiler_params=pltpu.CompilerParams(vmem_limit_bytes=VMEM_BYTES),
    )(share, peer_share, powers, segments, queries, keys, values, behind_keys, behind_values)


def pair_device(
    activations, conv_taps, gate_in, gate_out, queries, key_vectors, value_vectors, segment_ids
):
    rows = activations.shape[0]
    swap = [(0, 1), (1, 0)]
    seq_rank = lax.axis_index("seq")
    segments = segment_ids.reshape(2, rows)
    hidden_local = gate_in.shape[1]
    gate_rows = lax.dynamic_slice_in_dim(gate_out, seq_rank * hidden_local, hidden_local, 0)

    peer_rows = lax.ppermute(activations, "seq", swap)
    behind_keys = lax.ppermute(key_vectors, "seq", [(0, 1)])
    behind_values = lax.ppermute(value_vectors, "seq", [(0, 1)])

    def own_work(activations, conv_taps, gate_in, gate_rows):
        part, edges, held = own_project(activations, conv_taps, gate_in)
        return own_logits(*head_sum(part), gate_rows), edges, held

    own_share, edges, held = lax.cond(
        seq_rank >= 0,
        own_work,
        lambda *given: jax.tree.map(
            lambda like: jnp.zeros(like.shape, like.dtype), jax.eval_shape(own_work, *given)
        ),
        activations,
        conv_taps,
        gate_in,
        gate_rows,
    )
    peer_rows, own_share, edges, held = lax.optimization_barrier(
        (peer_rows, own_share, edges, held)
    )
    peer_part = peer_project(peer_rows, edges, conv_taps, held)
    peer_part, behind_keys = lax.optimization_barrier((peer_part, behind_keys))
    peer_part, peer_in = head_sum(peer_part)
    powers = powers_of(segments, queries, key_vectors, behind_keys)
    share = logits_share(own_share, peer_part, peer_in, gate_rows)
    share, powers = lax.optimization_barrier((share, powers))
    attended, own_mass, behind_mass = attention(
        share,
        lax.ppermute(share, "seq", swap),
        powers,
        segments,
        queries,
        key_vectors,
        value_vectors,
        behind_keys,
        behind_values,
    )
    key_mass = own_mass + lax.ppermute(behind_mass, "seq", [(1, 0)])
    return (attended, key_mass.astype(jnp.bfloat16))


def from_behind(block, axis, distance):
    devices = range(lax.axis_size(axis))
    route = [(i - distance, i) for i in devices if i - distance in devices]
    return lax.ppermute(block, axis, route)


def block_scores(query_heads, key_block, bias_block, allowed, score_scale):
    scores = (
        jnp.einsum("tgeh,kgh->getk", query_heads, key_block, preferred_element_type=jnp.float32)
        * score_scale
    )
    scores = scores + jnp.transpose(bias_block.astype(jnp.float32))[:, None, None, :]
    return jnp.where(allowed[None, None], scores, NEG_FILL)


def ring_device(
    activations, conv_taps, gate_in, gate_out, queries, key_vectors, value_vectors, segment_ids
):
    shard_rows = activations.shape[0]
    tap_count = conv_taps.shape[0]
    rim_rows = from_behind(activations[shard_rows - (tap_count - 1) :], "seq", 1)
    widened = jnp.concatenate([rim_rows, activations], 0).astype(jnp.float32)
    summed = jnp.zeros(activations.shape, jnp.float32)
    for shift_back in range(tap_count):
        start_row = tap_count - 1 - shift_back
        summed = (
            summed
            + conv_taps[shift_back].astype(jnp.float32)
            * widened[start_row : start_row + shard_rows]
        )
    mixed_rows = summed.astype(jnp.bfloat16)
    partial_hidden = jnp.dot(
        mixed_rows,
        lax.all_gather(gate_in, "seq", axis=1, tiled=True),
        preferred_element_type=jnp.float32,
    )
    kv_local = key_vectors.shape[1] // HEAD_DIM
    group_size = QUERY_HEADS // KV_HEADS
    head_rank = lax.axis_index("heads")
    hidden = jax.nn.silu(lax.psum(partial_hidden, "heads")).astype(jnp.bfloat16)
    logits = jnp.dot(hidden, gate_out, preferred_element_type=jnp.float32)
    retention = lax.dynamic_slice_in_dim(
        jax.nn.log_sigmoid(logits).astype(jnp.bfloat16), head_rank * kv_local, kv_local, 1
    )
    seq_rank = lax.axis_index("seq")
    local_index = jnp.arange(shard_rows, dtype=jnp.int32)
    own_queries, own_keys, own_values, own_bias = (queries, key_vectors, value_vectors, retention)
    query_places = seq_rank * shard_rows + local_index
    query_segments = jnp.take(segment_ids, query_places)
    query_heads = own_queries.reshape(shard_rows, kv_local, group_size, HEAD_DIM)
    score_scale = 1.0 / math.sqrt(HEAD_DIM)

    def visibility(flat_index):
        key_segments = jnp.take(segment_ids, flat_index)
        return (flat_index[None, :] <= query_places[:, None]) & (
            key_segments[None, :] == query_segments[:, None]
        )

    initial = (
        jnp.full((kv_local, group_size, shard_rows), NEG_FILL, jnp.float32),
        jnp.zeros((kv_local, group_size, shard_rows), jnp.float32),
    )
    all_keys, all_values, all_bias = (
        lax.all_gather(own_keys, "seq", axis=0, tiled=True),
        lax.all_gather(own_values, "seq", axis=0, tiled=True),
        lax.all_gather(own_bias, "seq", axis=0, tiled=True),
    )
    piece_rows = all_keys.shape[0]
    stats_block_width = math.gcd(piece_rows, 512)

    def one_block(block_number, state_in):
        offset = block_number * stats_block_width
        key_block = lax.dynamic_slice_in_dim(all_keys, offset, stats_block_width, 0).reshape(
            stats_block_width, kv_local, HEAD_DIM
        )
        bias_block = lax.dynamic_slice_in_dim(all_bias, offset, stats_block_width, 0)
        allowed = visibility(0 + offset + jnp.arange(stats_block_width, dtype=jnp.int32))

        def update(state_old):
            peak_old, mass_old = state_old
            masked = block_scores(query_heads, key_block, bias_block, allowed, score_scale)
            peak_new = jnp.maximum(peak_old, jnp.max(masked, axis=3))
            exponent = jnp.where(allowed[None, None], jnp.exp(masked - peak_new[..., None]), 0.0)
            return (peak_new, mass_old * jnp.exp(peak_old - peak_new) + jnp.sum(exponent, axis=3))

        def keep_state(state_old):
            return state_old

        return lax.cond(jnp.any(allowed), update, keep_state, state_in)

    row_peak, total_mass = lax.fori_loop(0, piece_rows // stats_block_width, one_block, initial)
    total_keys = all_keys.shape[0]
    block_width = math.gcd(total_keys, 512)
    block_count = total_keys // block_width
    key_blocks = all_keys.reshape(block_count, block_width, kv_local, HEAD_DIM)
    value_blocks = all_values.reshape(block_count, block_width, kv_local, HEAD_DIM)
    bias_blocks = all_bias.reshape(block_count, block_width, kv_local)

    def second_pass(accumulated, block_items):
        block_number, key_block, value_block, bias_block = block_items
        allowed = visibility(block_number * block_width + jnp.arange(block_width, dtype=jnp.int32))

        def attend(accum_in):
            masked = block_scores(query_heads, key_block, bias_block, allowed, score_scale)
            weights = (
                jnp.where(allowed[None, None], jnp.exp(masked - row_peak[..., None]), 0.0)
                / total_mass[..., None]
            )
            accum_out = accum_in + jnp.einsum(
                "getk,kgh->tgeh",
                weights.astype(jnp.bfloat16),
                value_block,
                preferred_element_type=jnp.float32,
            )
            return (accum_out, jnp.transpose(jnp.sum(weights, axis=(1, 2))) / group_size)

        def skip_block(accum_in):
            return (accum_in, jnp.zeros((block_width, kv_local), jnp.float32))

        return lax.cond(jnp.any(allowed), attend, skip_block, accumulated)

    accumulated, mass_blocks = lax.scan(
        second_pass,
        jnp.zeros((shard_rows, kv_local, group_size, HEAD_DIM), jnp.float32),
        (jnp.arange(block_count, dtype=jnp.int32), key_blocks, value_blocks, bias_blocks),
    )
    key_term = mass_blocks.reshape(total_keys, kv_local)
    key_mass = lax.psum_scatter(key_term, "seq", scatter_dimension=0, tiled=True).astype(
        jnp.bfloat16
    )
    attended = accumulated.reshape(shard_rows, kv_local * group_size * HEAD_DIM).astype(
        jnp.bfloat16
    )
    return (attended, jnp.transpose(key_mass))


def solution(mesh):
    return jax.shard_map(
        pair_device if mesh.shape["seq"] == 2 else ring_device,
        mesh=mesh,
        in_specs=(
            P(("dp", "seq"), "heads"),
            P(None, "heads"),
            P("heads", "seq"),
            P(),
            P(("dp", "seq"), "heads"),
            P(("dp", "seq"), "heads"),
            P(("dp", "seq"), "heads"),
            P("dp"),
        ),
        out_specs=(P(("dp", "seq"), "heads"), P("heads", ("dp", "seq"))),
        check_vma=False,
    )
```

```python
import functools
import math

import jax
import jax.numpy as jnp
from jax import lax
from jax.experimental import pallas as pl
from jax.experimental.pallas import tpu as pltpu
from jax.sharding import PartitionSpec as P

QUERY_HEADS = 64
KV_HEADS = 8
HEAD_DIM = 128


NEG_FILL = -1e30
RIM_ROWS = 16
LEAST_RETENTION = -40.0
VMEM_BYTES = 48 * 1024 * 1024


def convolve(widened, taps_ref, columns, lead, rows):
    summed = jnp.zeros((rows, columns.stop - columns.start), jnp.float32)
    for back in range(taps_ref.shape[0]):
        tap = taps_ref[back : back + 1, columns].astype(jnp.float32)
        summed = summed + tap * widened[lead - back : lead - back + rows, columns]
    return summed.astype(jnp.bfloat16)


def own_project_kernel(rows_ref, taps_ref, gate_ref, out_ref, edges_ref, held_ref, widened):
    rows, features = rows_ref.shape
    edges_ref[:RIM_ROWS] = rows_ref[:RIM_ROWS]
    edges_ref[RIM_ROWS:] = rows_ref[rows - RIM_ROWS :]
    held_ref[...] = gate_ref[...]
    tile = math.gcd(features, 512)
    total = jnp.zeros(out_ref.shape, jnp.float32)
    for start in range(0, features, tile):
        columns = slice(start, start + tile)
        widened[:, columns] = rows_ref[:, columns].astype(jnp.float32)
        mixed = convolve(widened, taps_ref, columns, RIM_ROWS, rows - RIM_ROWS)
        total = total + jnp.dot(mixed, gate_ref[columns, :], preferred_element_type=jnp.float32)
    out_ref[...] = total


def peer_project_kernel(
    peer_ref, edges_ref, taps_ref, gate_ref, near_ref, far_ref, far_sent_ref, widened, own_widened
):
    rows, features = peer_ref.shape
    tile = math.gcd(features, 512)
    first = lax.axis_index("seq") == 0
    half = near_ref.shape[1]
    total = jnp.zeros((near_ref.shape[0], 2 * half), jnp.float32)
    for start in range(0, features, tile):
        columns = slice(start, start + tile)
        own_tail = edges_ref[RIM_ROWS:, columns].astype(jnp.float32)
        peer_tail = peer_ref[rows - RIM_ROWS :, columns].astype(jnp.float32)
        widened[:RIM_ROWS, columns] = jnp.where(first, own_tail, 0.0)
        widened[RIM_ROWS:, columns] = peer_ref[:, columns].astype(jnp.float32)
        own_widened[:RIM_ROWS, columns] = jnp.where(first, 0.0, peer_tail)
        own_widened[RIM_ROWS:, columns] = edges_ref[:RIM_ROWS, columns].astype(jnp.float32)
        mixed = jnp.concatenate(
            [
                convolve(own_widened, taps_ref, columns, RIM_ROWS, RIM_ROWS),
                convolve(widened, taps_ref, columns, RIM_ROWS, rows),
            ],
            axis=0,
        )
        total = total + jnp.dot(mixed, gate_ref[columns, :], preferred_element_type=jnp.float32)
    near_ref[...] = total[:, :half]
    far_ref[...] = total[:, half:]
    far_sent_ref[...] = total[:, half:].astype(jnp.bfloat16)


def own_project(activations, conv_taps, gate_in):
    rows, features = activations.shape
    done = rows - RIM_ROWS
    return pl.pallas_call(
        own_project_kernel,
        out_shape=(
            jax.ShapeDtypeStruct((done, gate_in.shape[1]), jnp.float32),
            jax.ShapeDtypeStruct((2 * RIM_ROWS, features), activations.dtype),
            jax.ShapeDtypeStruct(gate_in.shape, gate_in.dtype),
        ),
        scratch_shapes=[pltpu.VMEM((rows, features), jnp.float32)],
        compiler_params=pltpu.CompilerParams(vmem_limit_bytes=VMEM_BYTES),
        cost_estimate=pl.CostEstimate(flops=1, bytes_accessed=1, transcendentals=0),
    )(activations, conv_taps, gate_in)


def peer_project(peer_rows, edges, conv_taps, gate_in):
    rows, features = peer_rows.shape
    done = rows + RIM_ROWS
    half = gate_in.shape[1] // 2
    return pl.pallas_call(
        peer_project_kernel,
        out_shape=(
            jax.ShapeDtypeStruct((done, half), jnp.float32),
            jax.ShapeDtypeStruct((done, half), jnp.float32),
            jax.ShapeDtypeStruct((done, half), jnp.bfloat16),
        ),
        scratch_shapes=[
            pltpu.VMEM((rows + RIM_ROWS, features), jnp.float32),
            pltpu.VMEM((2 * RIM_ROWS, features), jnp.float32),
        ],
        compiler_params=pltpu.CompilerParams(vmem_limit_bytes=VMEM_BYTES),
        cost_estimate=pl.CostEstimate(flops=1, bytes_accessed=1, transcendentals=0),
    )(peer_rows, edges, conv_taps, gate_in)


def head_sum(part):
    count = lax.axis_size("heads")
    step = 1
    received = None
    while step < count:
        if received is not None:
            part = part + received.astype(jnp.float32)
        received = exchange_heads(part if step == 1 else part.astype(jnp.bfloat16), step)
        step *= 2
    return part, received


def exchange_heads(block, step):
    count = lax.axis_size("heads")
    return lax.ppermute(block, "heads", [(i, i ^ step) for i in range(count)])


def in_one_piece(work, *given):
    shapes = jax.eval_shape(work, *given)
    return lax.cond(
        lax.axis_index("seq") >= 0,
        work,
        lambda *given: jax.tree.map(lambda like: jnp.zeros(like.shape, like.dtype), shapes),
        *given,
    )


def far_sum(block, sent):
    step = lax.axis_size("heads") // 2
    received = exchange_heads(sent, step)

    def nearer(block, received):
        distance = step
        while distance > 1:
            distance //= 2
            block = block + received.astype(jnp.float32)
            received = exchange_heads(block, distance)
        return block, received

    return in_one_piece(nearer, block, received)


def share_of_logits(pre_ref, in_ref, gate_rows):
    pre = pre_ref[...] + in_ref[...].astype(jnp.float32)
    hidden = (pre / (1.0 + jnp.exp(-pre))).astype(jnp.bfloat16)
    return lax.dot_general(
        gate_rows, hidden, (((0,), (1,)), ((), ())), preferred_element_type=jnp.float32
    )


def own_logits_kernel(own_ref, in_ref, gate_out_ref, out_ref):
    out_ref[...] = share_of_logits(own_ref, in_ref, gate_out_ref[...])


def own_logits(part, received, gate_rows):
    return pl.pallas_call(
        own_logits_kernel,
        out_shape=jax.ShapeDtypeStruct((gate_rows.shape[1], part.shape[0]), jnp.float32),
        compiler_params=pltpu.CompilerParams(vmem_limit_bytes=VMEM_BYTES),
    )(part, received, gate_rows)


def logits_kernel(own_ref, near_ref, near_in_ref, far_ref, far_in_ref, gate_out_ref, out_ref):
    first = lax.axis_index("seq") == 0
    half = near_ref.shape[1]
    share = share_of_logits(near_ref, near_in_ref, gate_out_ref[:half])
    share = share + share_of_logits(far_ref, far_in_ref, gate_out_ref[half:])
    own = jnp.concatenate([share[:, :RIM_ROWS], own_ref[...]], axis=1)
    peer = share[:, RIM_ROWS:]
    out_ref[0] = jnp.where(first, own, peer)
    out_ref[1] = jnp.where(first, peer, own)


def logits_share(own_share, near, near_in, far, far_in, gate_rows):
    rows = own_share.shape[1] + RIM_ROWS
    return pl.pallas_call(
        logits_kernel,
        out_shape=jax.ShapeDtypeStruct((2, gate_rows.shape[1], rows), jnp.float32),
        compiler_params=pltpu.CompilerParams(vmem_limit_bytes=VMEM_BYTES),
    )(own_share, near, near_in, far, far_in, gate_rows)


def hide_unseen(seq_rank, segments_ref, rows):
    own_segments = segments_ref[pl.ds(seq_rank, 1), :]
    behind_segments = segments_ref[pl.ds(0, 1), :]
    query_segments = jnp.transpose(jnp.broadcast_to(own_segments, (rows, rows)))
    query_at = lax.broadcasted_iota(jnp.int32, (rows, rows), 0)
    key_at = lax.broadcasted_iota(jnp.int32, (rows, rows), 1)
    see_own = (key_at <= query_at) & (query_segments == own_segments)
    see_behind = (query_segments == behind_segments) & (seq_rank > 0)
    return jnp.where(jnp.concatenate([see_behind, see_own], axis=1), 0.0, NEG_FILL)


def head_columns(number):
    return slice(number * HEAD_DIM, (number + 1) * HEAD_DIM)


def scores_of(queries_ref, keys, offset, head):
    scores = lax.dot_general(
        queries_ref[:, head_columns(head)],
        keys,
        (((1,), (1,)), ((), ())),
        preferred_element_type=jnp.float32,
    )
    return scores * (1.0 / math.sqrt(HEAD_DIM)) + offset


def with_behind(ref, behind_ref, number, whole):
    own = ref[:, head_columns(number)]
    if not whole:
        return own
    return jnp.concatenate([behind_ref[:, head_columns(number)], own], axis=0)


def powers_kernel(segments_ref, queries_ref, keys_ref, behind_keys_ref, powers_ref):
    seq_rank = lax.axis_index("seq")
    rows = queries_ref.shape[0]
    kv_local = keys_ref.shape[1] // HEAD_DIM
    group_size = queries_ref.shape[1] // keys_ref.shape[1]
    hide = hide_unseen(seq_rank, segments_ref, rows)

    def fill(whole):
        start = 0 if whole else rows
        for head in range(kv_local * group_size):
            g = head // group_size
            keys = with_behind(keys_ref, behind_keys_ref, g, whole)
            scores = scores_of(queries_ref, keys, hide[:, start:], head)
            powers_ref[head, :, start:] = jnp.exp(
                scores - jnp.max(scores, axis=1, keepdims=True)
            )

    pl.when(seq_rank > 0)(lambda: fill(True))
    pl.when(seq_rank == 0)(lambda: fill(False))


def powers_of(segments, queries, keys, behind_keys):
    rows = queries.shape[0]
    heads = queries.shape[1] // HEAD_DIM
    return pl.pallas_call(
        powers_kernel,
        out_shape=jax.ShapeDtypeStruct((heads, rows, 2 * rows), jnp.float32),
        compiler_params=pltpu.CompilerParams(vmem_limit_bytes=VMEM_BYTES),
        cost_estimate=pl.CostEstimate(
            flops=4 * rows * rows * queries.shape[1],
            bytes_accessed=8 * heads * rows * rows,
            transcendentals=2 * heads * rows * rows,
        ),
    )(segments, queries, keys, behind_keys)


def attention_kernel(
    share_ref,
    peer_share_ref,
    powers_ref,
    segments_ref,
    queries_ref,
    keys_ref,
    values_ref,
    behind_keys_ref,
    behind_values_ref,
    attended_ref,
    own_mass_ref,
    behind_mass_ref,
    retention,
):
    seq_rank, head_rank = lax.axis_index("seq"), lax.axis_index("heads")
    rows = queries_ref.shape[0]
    kv_local = keys_ref.shape[1] // HEAD_DIM
    group_size = queries_ref.shape[1] // keys_ref.shape[1]
    logits = share_ref[...] + peer_share_ref[...]
    log_gate = jnp.minimum(logits, 0.0) - jnp.log1p(jnp.exp(-jnp.abs(logits)))
    retention[...] = log_gate.astype(jnp.bfloat16).astype(jnp.float32)
    biases = []
    for g in range(kv_local):
        at = pl.ds(head_rank * kv_local + g, 1)
        biases.append(jnp.concatenate([retention[0, at, :], retention[seq_rank, at, :]], axis=1))
    moderate = jnp.min(functools.reduce(jnp.minimum, biases)) >= LEAST_RETENTION

    def finish(whole, terms_of):
        start = 0 if whole else rows
        for g in range(kv_local):
            values = with_behind(values_ref, behind_values_ref, g, whole)
            mass = jnp.zeros((1, 2 * rows - start), jnp.float32)
            group_terms = terms_of(g, whole, start)
            for head in range(g * group_size, (g + 1) * group_size):
                weights = group_terms(head)
                weights = weights * (1.0 / jnp.sum(weights, axis=1, keepdims=True))
                mass = mass + jnp.sum(weights, axis=0, keepdims=True)
                attended_ref[:, head_columns(head)] = jnp.dot(
                    weights.astype(jnp.bfloat16), values, preferred_element_type=jnp.float32
                ).astype(jnp.bfloat16)
            mass = mass / group_size
            own_mass_ref[g : g + 1, :] = mass[:, rows - start :]
            behind_mass_ref[g : g + 1, :] = mass[:, :rows] if whole else jnp.zeros((1, rows))

    def by_powers(g, whole, start):
        factor = jnp.exp(biases[g] - jnp.max(biases[g]))[:, start:]
        return lambda head: powers_ref[head, :, start:] * factor

    def by_scores(g, whole, start):
        offset = hide_unseen(seq_rank, segments_ref, rows) + biases[g]
        keys = with_behind(keys_ref, behind_keys_ref, g, whole)

        def terms(head):
            scores = scores_of(queries_ref, keys, offset[:, start:], head)
            return jnp.exp(scores - jnp.max(scores, axis=1, keepdims=True))

        return terms

    pl.when(moderate & (seq_rank > 0))(lambda: finish(True, by_powers))
    pl.when(moderate & (seq_rank == 0))(lambda: finish(False, by_powers))
    pl.when(jnp.logical_not(moderate))(lambda: finish(True, by_scores))


def attention(
    share, peer_share, powers, segments, queries, keys, values, behind_keys, behind_values
):
    rows = queries.shape[0]
    kv_local = keys.shape[1] // HEAD_DIM
    mass = jax.ShapeDtypeStruct((kv_local, rows), jnp.float32)
    return pl.pallas_call(
        attention_kernel,
        out_shape=(jax.ShapeDtypeStruct(queries.shape, jnp.bfloat16), mass, mass),
        scratch_shapes=[pltpu.VMEM(share.shape, jnp.float32)],
        compiler_params=pltpu.CompilerParams(vmem_limit_bytes=VMEM_BYTES),
    )(share, peer_share, powers, segments, queries, keys, values, behind_keys, behind_values)


def pair_device(
    activations, conv_taps, gate_in, gate_out, queries, key_vectors, value_vectors, segment_ids
):
    rows = activations.shape[0]
    swap = [(0, 1), (1, 0)]
    seq_rank = lax.axis_index("seq")
    segments = segment_ids.reshape(2, rows)
    hidden_local = gate_in.shape[1]
    gate_rows = lax.dynamic_slice_in_dim(gate_out, seq_rank * hidden_local, hidden_local, 0)

    peer_rows = lax.ppermute(activations, "seq", swap)
    behind_keys = lax.ppermute(key_vectors, "seq", swap)
    behind_values = lax.ppermute(value_vectors, "seq", swap)

    def own_work(activations, conv_taps, gate_in, gate_rows):
        part, edges, held = own_project(activations, conv_taps, gate_in)
        return own_logits(*head_sum(part), gate_rows), edges, held

    own_share, edges, held = in_one_piece(own_work, activations, conv_taps, gate_in, gate_rows)
    peer_rows, own_share, edges, held = lax.optimization_barrier(
        (peer_rows, own_share, edges, held)
    )
    near, far, far_sent = peer_project(peer_rows, edges, conv_taps, held)
    near, far, far_sent, behind_keys = lax.optimization_barrier(
        (near, far, far_sent, behind_keys)
    )
    near, near_in = head_sum(near)
    far, far_in = far_sum(far, far_sent)
    share = logits_share(own_share, near, near_in, far, far_in, gate_rows)
    share, queries = lax.optimization_barrier((share, queries))
    powers = powers_of(segments, queries, key_vectors, behind_keys)
    attended, own_mass, behind_mass = attention(
        share,
        lax.ppermute(share, "seq", swap),
        powers,
        segments,
        queries,
        key_vectors,
        value_vectors,
        behind_keys,
        behind_values,
    )
    key_mass = own_mass + lax.ppermute(behind_mass, "seq", swap)
    return (attended, key_mass.astype(jnp.bfloat16))


def from_behind(block, axis, distance):
    devices = range(lax.axis_size(axis))
    route = [(i - distance, i) for i in devices if i - distance in devices]
    return lax.ppermute(block, axis, route)


def block_scores(query_heads, key_block, bias_block, allowed, score_scale):
    scores = (
        jnp.einsum("tgeh,kgh->getk", query_heads, key_block, preferred_element_type=jnp.float32)
        * score_scale
    )
    scores = scores + jnp.transpose(bias_block.astype(jnp.float32))[:, None, None, :]
    return jnp.where(allowed[None, None], scores, NEG_FILL)


def ring_device(
    activations, conv_taps, gate_in, gate_out, queries, key_vectors, value_vectors, segment_ids
):
    shard_rows = activations.shape[0]
    tap_count = conv_taps.shape[0]
    rim_rows = from_behind(activations[shard_rows - (tap_count - 1) :], "seq", 1)
    widened = jnp.concatenate([rim_rows, activations], 0).astype(jnp.float32)
    summed = jnp.zeros(activations.shape, jnp.float32)
    for shift_back in range(tap_count):
        start_row = tap_count - 1 - shift_back
        summed = (
            summed
            + conv_taps[shift_back].astype(jnp.float32)
            * widened[start_row : start_row + shard_rows]
        )
    mixed_rows = summed.astype(jnp.bfloat16)
    partial_hidden = jnp.dot(
        mixed_rows,
        lax.all_gather(gate_in, "seq", axis=1, tiled=True),
        preferred_element_type=jnp.float32,
    )
    kv_local = key_vectors.shape[1] // HEAD_DIM
    group_size = QUERY_HEADS // KV_HEADS
    head_rank = lax.axis_index("heads")
    hidden = jax.nn.silu(lax.psum(partial_hidden, "heads")).astype(jnp.bfloat16)
    logits = jnp.dot(hidden, gate_out, preferred_element_type=jnp.float32)
    retention = lax.dynamic_slice_in_dim(
        jax.nn.log_sigmoid(logits).astype(jnp.bfloat16), head_rank * kv_local, kv_local, 1
    )
    seq_rank = lax.axis_index("seq")
    local_index = jnp.arange(shard_rows, dtype=jnp.int32)
    own_queries, own_keys, own_values, own_bias = (queries, key_vectors, value_vectors, retention)
    query_places = seq_rank * shard_rows + local_index
    query_segments = jnp.take(segment_ids, query_places)
    query_heads = own_queries.reshape(shard_rows, kv_local, group_size, HEAD_DIM)
    score_scale = 1.0 / math.sqrt(HEAD_DIM)

    def visibility(flat_index):
        key_segments = jnp.take(segment_ids, flat_index)
        return (flat_index[None, :] <= query_places[:, None]) & (
            key_segments[None, :] == query_segments[:, None]
        )

    initial = (
        jnp.full((kv_local, group_size, shard_rows), NEG_FILL, jnp.float32),
        jnp.zeros((kv_local, group_size, shard_rows), jnp.float32),
    )
    all_keys, all_values, all_bias = (
        lax.all_gather(own_keys, "seq", axis=0, tiled=True),
        lax.all_gather(own_values, "seq", axis=0, tiled=True),
        lax.all_gather(own_bias, "seq", axis=0, tiled=True),
    )
    piece_rows = all_keys.shape[0]
    stats_block_width = math.gcd(piece_rows, 512)

    def one_block(block_number, state_in):
        offset = block_number * stats_block_width
        key_block = lax.dynamic_slice_in_dim(all_keys, offset, stats_block_width, 0).reshape(
            stats_block_width, kv_local, HEAD_DIM
        )
        bias_block = lax.dynamic_slice_in_dim(all_bias, offset, stats_block_width, 0)
        allowed = visibility(0 + offset + jnp.arange(stats_block_width, dtype=jnp.int32))

        def update(state_old):
            peak_old, mass_old = state_old
            masked = block_scores(query_heads, key_block, bias_block, allowed, score_scale)
            peak_new = jnp.maximum(peak_old, jnp.max(masked, axis=3))
            exponent = jnp.where(allowed[None, None], jnp.exp(masked - peak_new[..., None]), 0.0)
            return (peak_new, mass_old * jnp.exp(peak_old - peak_new) + jnp.sum(exponent, axis=3))

        def keep_state(state_old):
            return state_old

        return lax.cond(jnp.any(allowed), update, keep_state, state_in)

    row_peak, total_mass = lax.fori_loop(0, piece_rows // stats_block_width, one_block, initial)
    total_keys = all_keys.shape[0]
    block_width = math.gcd(total_keys, 512)
    block_count = total_keys // block_width
    key_blocks = all_keys.reshape(block_count, block_width, kv_local, HEAD_DIM)
    value_blocks = all_values.reshape(block_count, block_width, kv_local, HEAD_DIM)
    bias_blocks = all_bias.reshape(block_count, block_width, kv_local)

    def second_pass(accumulated, block_items):
        block_number, key_block, value_block, bias_block = block_items
        allowed = visibility(block_number * block_width + jnp.arange(block_width, dtype=jnp.int32))

        def attend(accum_in):
            masked = block_scores(query_heads, key_block, bias_block, allowed, score_scale)
            weights = (
                jnp.where(allowed[None, None], jnp.exp(masked - row_peak[..., None]), 0.0)
                / total_mass[..., None]
            )
            accum_out = accum_in + jnp.einsum(
                "getk,kgh->tgeh",
                weights.astype(jnp.bfloat16),
                value_block,
                preferred_element_type=jnp.float32,
            )
            return (accum_out, jnp.transpose(jnp.sum(weights, axis=(1, 2))) / group_size)

        def skip_block(accum_in):
            return (accum_in, jnp.zeros((block_width, kv_local), jnp.float32))

        return lax.cond(jnp.any(allowed), attend, skip_block, accumulated)

    accumulated, mass_blocks = lax.scan(
        second_pass,
        jnp.zeros((shard_rows, kv_local, group_size, HEAD_DIM), jnp.float32),
        (jnp.arange(block_count, dtype=jnp.int32), key_blocks, value_blocks, bias_blocks),
    )
    key_term = mass_blocks.reshape(total_keys, kv_local)
    key_mass = lax.psum_scatter(key_term, "seq", scatter_dimension=0, tiled=True).astype(
        jnp.bfloat16
    )
    attended = accumulated.reshape(shard_rows, kv_local * group_size * HEAD_DIM).astype(
        jnp.bfloat16
    )
    return (attended, jnp.transpose(key_mass))


def solution(mesh):
    return jax.shard_map(
        pair_device if mesh.shape["seq"] == 2 else ring_device,
        mesh=mesh,
        in_specs=(
            P(("dp", "seq"), "heads"),
            P(None, "heads"),
            P("heads", "seq"),
            P(),
            P(("dp", "seq"), "heads"),
            P(("dp", "seq"), "heads"),
            P(("dp", "seq"), "heads"),
            P("dp"),
        ),
        out_specs=(P(("dp", "seq"), "heads"), P("heads", ("dp", "seq"))),
        check_vma=False,
    )
```

```python
import functools
import math

import jax
import jax.numpy as jnp
from jax import lax
from jax.experimental import pallas as pl
from jax.experimental.pallas import tpu as pltpu
from jax.sharding import PartitionSpec as P

QUERY_HEADS = 64
KV_HEADS = 8
HEAD_DIM = 128


NEG_FILL = -1e30
RIM_ROWS = 16
LEAST_RETENTION = -40.0
VMEM_BYTES = 48 * 1024 * 1024


def convolve(widened, taps_ref, columns, lead, rows):
    summed = jnp.zeros((rows, columns.stop - columns.start), jnp.float32)
    for back in range(taps_ref.shape[0]):
        tap = taps_ref[back : back + 1, columns].astype(jnp.float32)
        summed = summed + tap * widened[lead - back : lead - back + rows, columns]
    return summed.astype(jnp.bfloat16)


def own_project_kernel(rows_ref, taps_ref, gate_ref, out_ref, edges_ref, held_ref, widened):
    rows, features = rows_ref.shape
    edges_ref[:RIM_ROWS] = rows_ref[:RIM_ROWS]
    edges_ref[RIM_ROWS:] = rows_ref[rows - RIM_ROWS :]
    held_ref[...] = gate_ref[...]
    tile = math.gcd(features, 512)
    total = jnp.zeros(out_ref.shape, jnp.float32)
    for start in range(0, features, tile):
        columns = slice(start, start + tile)
        widened[:, columns] = rows_ref[:, columns].astype(jnp.float32)
        mixed = convolve(widened, taps_ref, columns, RIM_ROWS, rows - RIM_ROWS)
        total = total + jnp.dot(mixed, gate_ref[columns, :], preferred_element_type=jnp.float32)
    out_ref[...] = total


def peer_project_kernel(
    peer_ref, edges_ref, taps_ref, gate_ref, near_ref, far_ref, far_sent_ref, widened, own_widened
):
    rows, features = peer_ref.shape
    tile = math.gcd(features, 512)
    first = lax.axis_index("seq") == 0
    half = near_ref.shape[1]
    total = jnp.zeros((near_ref.shape[0], 2 * half), jnp.float32)
    for start in range(0, features, tile):
        columns = slice(start, start + tile)
        own_tail = edges_ref[RIM_ROWS:, columns].astype(jnp.float32)
        peer_tail = peer_ref[rows - RIM_ROWS :, columns].astype(jnp.float32)
        widened[:RIM_ROWS, columns] = jnp.where(first, own_tail, 0.0)
        widened[RIM_ROWS:, columns] = peer_ref[:, columns].astype(jnp.float32)
        own_widened[:RIM_ROWS, columns] = jnp.where(first, 0.0, peer_tail)
        own_widened[RIM_ROWS:, columns] = edges_ref[:RIM_ROWS, columns].astype(jnp.float32)
        mixed = jnp.concatenate(
            [
                convolve(own_widened, taps_ref, columns, RIM_ROWS, RIM_ROWS),
                convolve(widened, taps_ref, columns, RIM_ROWS, rows),
            ],
            axis=0,
        )
        total = total + jnp.dot(mixed, gate_ref[columns, :], preferred_element_type=jnp.float32)
    near_ref[...] = total[:, :half]
    far_ref[...] = total[:, half:]
    far_sent_ref[...] = total[:, half:].astype(jnp.bfloat16)


def own_project(activations, conv_taps, gate_in):
    rows, features = activations.shape
    done = rows - RIM_ROWS
    return pl.pallas_call(
        own_project_kernel,
        out_shape=(
            jax.ShapeDtypeStruct((done, gate_in.shape[1]), jnp.float32),
            jax.ShapeDtypeStruct((2 * RIM_ROWS, features), activations.dtype),
            jax.ShapeDtypeStruct(gate_in.shape, gate_in.dtype),
        ),
        scratch_shapes=[pltpu.VMEM((rows, features), jnp.float32)],
        compiler_params=pltpu.CompilerParams(vmem_limit_bytes=VMEM_BYTES),
        cost_estimate=pl.CostEstimate(flops=1, bytes_accessed=1, transcendentals=0),
    )(activations, conv_taps, gate_in)


def peer_project(peer_rows, edges, conv_taps, gate_in):
    rows, features = peer_rows.shape
    done = rows + RIM_ROWS
    half = gate_in.shape[1] // 2
    return pl.pallas_call(
        peer_project_kernel,
        out_shape=(
            jax.ShapeDtypeStruct((done, half), jnp.float32),
            jax.ShapeDtypeStruct((done, half), jnp.float32),
            jax.ShapeDtypeStruct((done, half), jnp.bfloat16),
        ),
        scratch_shapes=[
            pltpu.VMEM((rows + RIM_ROWS, features), jnp.float32),
            pltpu.VMEM((2 * RIM_ROWS, features), jnp.float32),
        ],
        compiler_params=pltpu.CompilerParams(vmem_limit_bytes=VMEM_BYTES),
        cost_estimate=pl.CostEstimate(flops=1, bytes_accessed=1, transcendentals=0),
    )(peer_rows, edges, conv_taps, gate_in)


def head_sum(part):
    count = lax.axis_size("heads")
    step = 1
    received = None
    while step < count:
        if received is not None:
            part = part + received.astype(jnp.float32)
        received = exchange_heads(part if step == 1 else part.astype(jnp.bfloat16), step)
        step *= 2
    return part, received


def exchange_heads(block, step):
    count = lax.axis_size("heads")
    return lax.ppermute(block, "heads", [(i, i ^ step) for i in range(count)])


def in_one_piece(work, *given):
    shapes = jax.eval_shape(work, *given)
    return lax.cond(
        lax.axis_index("seq") >= 0,
        work,
        lambda *given: jax.tree.map(lambda like: jnp.zeros(like.shape, like.dtype), shapes),
        *given,
    )


def far_logits(block, sent, gate_rows):
    step = lax.axis_size("heads") // 2
    received = exchange_heads(sent, step)

    def nearer(block, received, gate_rows):
        distance = step
        while distance > 1:
            distance //= 2
            block = block + received.astype(jnp.float32)
            received = exchange_heads(block, distance)
        return partial_logits(block, received, gate_rows)

    return in_one_piece(nearer, block, received, gate_rows)


def share_of_logits(pre_ref, in_ref, gate_rows):
    pre = pre_ref[...] + in_ref[...].astype(jnp.float32)
    hidden = (pre / (1.0 + jnp.exp(-pre))).astype(jnp.bfloat16)
    return lax.dot_general(
        gate_rows, hidden, (((0,), (1,)), ((), ())), preferred_element_type=jnp.float32
    )


def partial_logits_kernel(own_ref, in_ref, gate_out_ref, out_ref):
    out_ref[...] = share_of_logits(own_ref, in_ref, gate_out_ref[...])


def partial_logits(part, received, gate_rows):
    return pl.pallas_call(
        partial_logits_kernel,
        out_shape=jax.ShapeDtypeStruct((gate_rows.shape[1], part.shape[0]), jnp.float32),
        compiler_params=pltpu.CompilerParams(vmem_limit_bytes=VMEM_BYTES),
    )(part, received, gate_rows)


def logits_kernel(own_ref, far_share_ref, near_ref, near_in_ref, gate_out_ref, out_ref):
    first = lax.axis_index("seq") == 0
    share = share_of_logits(near_ref, near_in_ref, gate_out_ref[...]) + far_share_ref[...]
    own = jnp.concatenate([share[:, :RIM_ROWS], own_ref[...]], axis=1)
    peer = share[:, RIM_ROWS:]
    out_ref[0] = jnp.where(first, own, peer)
    out_ref[1] = jnp.where(first, peer, own)


def logits_share(own_share, far_share, near, near_in, gate_rows):
    rows = own_share.shape[1] + RIM_ROWS
    return pl.pallas_call(
        logits_kernel,
        out_shape=jax.ShapeDtypeStruct((2, gate_rows.shape[1], rows), jnp.float32),
        compiler_params=pltpu.CompilerParams(vmem_limit_bytes=VMEM_BYTES),
    )(own_share, far_share, near, near_in, gate_rows)


def hide_unseen(seq_rank, segments_ref, rows):
    own_segments = segments_ref[pl.ds(seq_rank, 1), :]
    behind_segments = segments_ref[pl.ds(0, 1), :]
    query_segments = jnp.transpose(jnp.broadcast_to(own_segments, (rows, rows)))
    query_at = lax.broadcasted_iota(jnp.int32, (rows, rows), 0)
    key_at = lax.broadcasted_iota(jnp.int32, (rows, rows), 1)
    see_own = (key_at <= query_at) & (query_segments == own_segments)
    see_behind = (query_segments == behind_segments) & (seq_rank > 0)
    return jnp.where(jnp.concatenate([see_behind, see_own], axis=1), 0.0, NEG_FILL)


def head_columns(number):
    return slice(number * HEAD_DIM, (number + 1) * HEAD_DIM)


def scores_of(queries_ref, keys, offset, head):
    scores = lax.dot_general(
        queries_ref[:, head_columns(head)],
        keys,
        (((1,), (1,)), ((), ())),
        preferred_element_type=jnp.float32,
    )
    return scores * (1.0 / math.sqrt(HEAD_DIM)) + offset


def with_behind(ref, behind_ref, number, whole):
    own = ref[:, head_columns(number)]
    if not whole:
        return own
    return jnp.concatenate([behind_ref[:, head_columns(number)], own], axis=0)


def powers_kernel(segments_ref, queries_ref, keys_ref, behind_keys_ref, powers_ref):
    seq_rank = lax.axis_index("seq")
    rows = queries_ref.shape[0]
    kv_local = keys_ref.shape[1] // HEAD_DIM
    group_size = queries_ref.shape[1] // keys_ref.shape[1]
    hide = hide_unseen(seq_rank, segments_ref, rows)

    def fill(whole):
        start = 0 if whole else rows
        for head in range(kv_local * group_size):
            g = head // group_size
            keys = with_behind(keys_ref, behind_keys_ref, g, whole)
            scores = scores_of(queries_ref, keys, hide[:, start:], head)
            powers_ref[head, :, start:] = jnp.exp(
                scores - jnp.max(scores, axis=1, keepdims=True)
            )

    pl.when(seq_rank > 0)(lambda: fill(True))
    pl.when(seq_rank == 0)(lambda: fill(False))


def powers_of(segments, queries, keys, behind_keys):
    rows = queries.shape[0]
    heads = queries.shape[1] // HEAD_DIM
    return pl.pallas_call(
        powers_kernel,
        out_shape=jax.ShapeDtypeStruct((heads, rows, 2 * rows), jnp.float32),
        compiler_params=pltpu.CompilerParams(vmem_limit_bytes=VMEM_BYTES),
        cost_estimate=pl.CostEstimate(
            flops=4 * rows * rows * queries.shape[1],
            bytes_accessed=8 * heads * rows * rows,
            transcendentals=2 * heads * rows * rows,
        ),
    )(segments, queries, keys, behind_keys)


def weights_kernel(
    share_ref,
    peer_share_ref,
    powers_ref,
    segments_ref,
    queries_ref,
    keys_ref,
    behind_keys_ref,
    weights_ref,
    own_mass_ref,
    behind_mass_ref,
    retention,
):
    seq_rank, head_rank = lax.axis_index("seq"), lax.axis_index("heads")
    rows = queries_ref.shape[0]
    kv_local = keys_ref.shape[1] // HEAD_DIM
    group_size = queries_ref.shape[1] // keys_ref.shape[1]
    logits = share_ref[...] + peer_share_ref[...]
    log_gate = jnp.minimum(logits, 0.0) - jnp.log1p(jnp.exp(-jnp.abs(logits)))
    retention[...] = log_gate.astype(jnp.bfloat16).astype(jnp.float32)
    biases = []
    for g in range(kv_local):
        at = pl.ds(head_rank * kv_local + g, 1)
        biases.append(jnp.concatenate([retention[0, at, :], retention[seq_rank, at, :]], axis=1))
    moderate = jnp.min(functools.reduce(jnp.minimum, biases)) >= LEAST_RETENTION

    def finish(whole, terms_of):
        start = 0 if whole else rows
        for g in range(kv_local):
            mass = jnp.zeros((1, 2 * rows - start), jnp.float32)
            group_terms = terms_of(g, whole, start)
            for head in range(g * group_size, (g + 1) * group_size):
                weights = group_terms(head)
                weights = weights * (1.0 / jnp.sum(weights, axis=1, keepdims=True))
                mass = mass + jnp.sum(weights, axis=0, keepdims=True)
                weights_ref[head, :, start:] = weights.astype(jnp.bfloat16)
            mass = mass / group_size
            own_mass_ref[g : g + 1, :] = mass[:, rows - start :]
            behind_mass_ref[g : g + 1, :] = mass[:, :rows] if whole else jnp.zeros((1, rows))

    def by_powers(g, whole, start):
        factor = jnp.exp(biases[g] - jnp.max(biases[g]))[:, start:]
        return lambda head: powers_ref[head, :, start:] * factor

    def by_scores(g, whole, start):
        offset = hide_unseen(seq_rank, segments_ref, rows) + biases[g]
        keys = with_behind(keys_ref, behind_keys_ref, g, whole)

        def terms(head):
            scores = scores_of(queries_ref, keys, offset[:, start:], head)
            return jnp.exp(scores - jnp.max(scores, axis=1, keepdims=True))

        return terms

    pl.when(moderate & (seq_rank > 0))(lambda: finish(True, by_powers))
    pl.when(moderate & (seq_rank == 0))(lambda: finish(False, by_powers))
    pl.when(jnp.logical_not(moderate))(lambda: finish(True, by_scores))


def weights_of(share, peer_share, powers, segments, queries, keys, behind_keys):
    rows = queries.shape[0]
    mass = jax.ShapeDtypeStruct((keys.shape[1] // HEAD_DIM, rows), jnp.float32)
    return pl.pallas_call(
        weights_kernel,
        out_shape=(jax.ShapeDtypeStruct(powers.shape, jnp.bfloat16), mass, mass),
        scratch_shapes=[pltpu.VMEM(share.shape, jnp.float32)],
        compiler_params=pltpu.CompilerParams(vmem_limit_bytes=VMEM_BYTES),
    )(share, peer_share, powers, segments, queries, keys, behind_keys)


def attend_kernel(weights_ref, values_ref, behind_values_ref, attended_ref):
    seq_rank = lax.axis_index("seq")
    heads, rows = weights_ref.shape[:2]
    group_size = attended_ref.shape[1] // values_ref.shape[1]

    def fill(whole):
        start = 0 if whole else rows
        for head in range(heads):
            values = with_behind(values_ref, behind_values_ref, head // group_size, whole)
            attended_ref[:, head_columns(head)] = jnp.dot(
                weights_ref[head, :, start:], values, preferred_element_type=jnp.float32
            ).astype(jnp.bfloat16)

    pl.when(seq_rank > 0)(lambda: fill(True))
    pl.when(seq_rank == 0)(lambda: fill(False))


def attend(weights, values, behind_values):
    heads, rows = weights.shape[:2]
    return pl.pallas_call(
        attend_kernel,
        out_shape=jax.ShapeDtypeStruct((rows, heads * HEAD_DIM), jnp.bfloat16),
        compiler_params=pltpu.CompilerParams(vmem_limit_bytes=VMEM_BYTES),
        cost_estimate=pl.CostEstimate(
            flops=4 * rows * rows * heads * HEAD_DIM,
            bytes_accessed=2 * (weights.size + rows * heads * HEAD_DIM),
            transcendentals=0,
        ),
    )(weights, values, behind_values)


def pair_device(
    activations, conv_taps, gate_in, gate_out, queries, key_vectors, value_vectors, segment_ids
):
    rows = activations.shape[0]
    swap = [(0, 1), (1, 0)]
    seq_rank = lax.axis_index("seq")
    segments = segment_ids.reshape(2, rows)
    hidden_local = gate_in.shape[1]
    gate_rows = lax.dynamic_slice_in_dim(gate_out, seq_rank * hidden_local, hidden_local, 0)

    peer_rows = lax.ppermute(activations, "seq", swap)

    def own_work(activations, conv_taps, gate_in, gate_rows):
        part, edges, held = own_project(activations, conv_taps, gate_in)
        return partial_logits(*head_sum(part), gate_rows), edges, held

    own_share, edges, held = in_one_piece(own_work, activations, conv_taps, gate_in, gate_rows)
    peer_rows, own_share, edges, held = lax.optimization_barrier(
        (peer_rows, own_share, edges, held)
    )
    near, far, far_sent = peer_project(peer_rows, edges, conv_taps, held)
    behind_keys = lax.ppermute(key_vectors, "seq", swap)
    behind_values = lax.ppermute(value_vectors, "seq", swap)
    half = near.shape[1]
    near, near_in = head_sum(near)
    far_share = far_logits(far, far_sent, gate_rows[half:])
    share = logits_share(own_share, far_share, near, near_in, gate_rows[:half])
    share, queries = lax.optimization_barrier((share, queries))
    powers = powers_of(segments, queries, key_vectors, behind_keys)
    weights, own_mass, behind_mass = weights_of(
        share,
        lax.ppermute(share, "seq", swap),
        powers,
        segments,
        queries,
        key_vectors,
        behind_keys,
    )
    attended = attend(weights, value_vectors, behind_values)
    key_mass = own_mass + lax.ppermute(behind_mass, "seq", swap)
    return (attended, key_mass.astype(jnp.bfloat16))


def from_behind(block, axis, distance):
    devices = range(lax.axis_size(axis))
    route = [(i - distance, i) for i in devices if i - distance in devices]
    return lax.ppermute(block, axis, route)


def block_scores(query_heads, key_block, bias_block, allowed, score_scale):
    scores = (
        jnp.einsum("tgeh,kgh->getk", query_heads, key_block, preferred_element_type=jnp.float32)
        * score_scale
    )
    scores = scores + jnp.transpose(bias_block.astype(jnp.float32))[:, None, None, :]
    return jnp.where(allowed[None, None], scores, NEG_FILL)


def ring_device(
    activations, conv_taps, gate_in, gate_out, queries, key_vectors, value_vectors, segment_ids
):
    shard_rows = activations.shape[0]
    tap_count = conv_taps.shape[0]
    rim_rows = from_behind(activations[shard_rows - (tap_count - 1) :], "seq", 1)
    widened = jnp.concatenate([rim_rows, activations], 0).astype(jnp.float32)
    summed = jnp.zeros(activations.shape, jnp.float32)
    for shift_back in range(tap_count):
        start_row = tap_count - 1 - shift_back
        summed = (
            summed
            + conv_taps[shift_back].astype(jnp.float32)
            * widened[start_row : start_row + shard_rows]
        )
    mixed_rows = summed.astype(jnp.bfloat16)
    partial_hidden = jnp.dot(
        mixed_rows,
        lax.all_gather(gate_in, "seq", axis=1, tiled=True),
        preferred_element_type=jnp.float32,
    )
    kv_local = key_vectors.shape[1] // HEAD_DIM
    group_size = QUERY_HEADS // KV_HEADS
    head_rank = lax.axis_index("heads")
    hidden = jax.nn.silu(lax.psum(partial_hidden, "heads")).astype(jnp.bfloat16)
    logits = jnp.dot(hidden, gate_out, preferred_element_type=jnp.float32)
    retention = lax.dynamic_slice_in_dim(
        jax.nn.log_sigmoid(logits).astype(jnp.bfloat16), head_rank * kv_local, kv_local, 1
    )
    seq_rank = lax.axis_index("seq")
    local_index = jnp.arange(shard_rows, dtype=jnp.int32)
    own_queries, own_keys, own_values, own_bias = (queries, key_vectors, value_vectors, retention)
    query_places = seq_rank * shard_rows + local_index
    query_segments = jnp.take(segment_ids, query_places)
    query_heads = own_queries.reshape(shard_rows, kv_local, group_size, HEAD_DIM)
    score_scale = 1.0 / math.sqrt(HEAD_DIM)

    def visibility(flat_index):
        key_segments = jnp.take(segment_ids, flat_index)
        return (flat_index[None, :] <= query_places[:, None]) & (
            key_segments[None, :] == query_segments[:, None]
        )

    initial = (
        jnp.full((kv_local, group_size, shard_rows), NEG_FILL, jnp.float32),
        jnp.zeros((kv_local, group_size, shard_rows), jnp.float32),
    )
    all_keys, all_values, all_bias = (
        lax.all_gather(own_keys, "seq", axis=0, tiled=True),
        lax.all_gather(own_values, "seq", axis=0, tiled=True),
        lax.all_gather(own_bias, "seq", axis=0, tiled=True),
    )
    piece_rows = all_keys.shape[0]
    stats_block_width = math.gcd(piece_rows, 512)

    def one_block(block_number, state_in):
        offset = block_number * stats_block_width
        key_block = lax.dynamic_slice_in_dim(all_keys, offset, stats_block_width, 0).reshape(
            stats_block_width, kv_local, HEAD_DIM
        )
        bias_block = lax.dynamic_slice_in_dim(all_bias, offset, stats_block_width, 0)
        allowed = visibility(0 + offset + jnp.arange(stats_block_width, dtype=jnp.int32))

        def update(state_old):
            peak_old, mass_old = state_old
            masked = block_scores(query_heads, key_block, bias_block, allowed, score_scale)
            peak_new = jnp.maximum(peak_old, jnp.max(masked, axis=3))
            exponent = jnp.where(allowed[None, None], jnp.exp(masked - peak_new[..., None]), 0.0)
            return (peak_new, mass_old * jnp.exp(peak_old - peak_new) + jnp.sum(exponent, axis=3))

        def keep_state(state_old):
            return state_old

        return lax.cond(jnp.any(allowed), update, keep_state, state_in)

    row_peak, total_mass = lax.fori_loop(0, piece_rows // stats_block_width, one_block, initial)
    total_keys = all_keys.shape[0]
    block_width = math.gcd(total_keys, 512)
    block_count = total_keys // block_width
    key_blocks = all_keys.reshape(block_count, block_width, kv_local, HEAD_DIM)
    value_blocks = all_values.reshape(block_count, block_width, kv_local, HEAD_DIM)
    bias_blocks = all_bias.reshape(block_count, block_width, kv_local)

    def second_pass(accumulated, block_items):
        block_number, key_block, value_block, bias_block = block_items
        allowed = visibility(block_number * block_width + jnp.arange(block_width, dtype=jnp.int32))

        def attend(accum_in):
            masked = block_scores(query_heads, key_block, bias_block, allowed, score_scale)
            weights = (
                jnp.where(allowed[None, None], jnp.exp(masked - row_peak[..., None]), 0.0)
                / total_mass[..., None]
            )
            accum_out = accum_in + jnp.einsum(
                "getk,kgh->tgeh",
                weights.astype(jnp.bfloat16),
                value_block,
                preferred_element_type=jnp.float32,
            )
            return (accum_out, jnp.transpose(jnp.sum(weights, axis=(1, 2))) / group_size)

        def skip_block(accum_in):
            return (accum_in, jnp.zeros((block_width, kv_local), jnp.float32))

        return lax.cond(jnp.any(allowed), attend, skip_block, accumulated)

    accumulated, mass_blocks = lax.scan(
        second_pass,
        jnp.zeros((shard_rows, kv_local, group_size, HEAD_DIM), jnp.float32),
        (jnp.arange(block_count, dtype=jnp.int32), key_blocks, value_blocks, bias_blocks),
    )
    key_term = mass_blocks.reshape(total_keys, kv_local)
    key_mass = lax.psum_scatter(key_term, "seq", scatter_dimension=0, tiled=True).astype(
        jnp.bfloat16
    )
    attended = accumulated.reshape(shard_rows, kv_local * group_size * HEAD_DIM).astype(
        jnp.bfloat16
    )
    return (attended, jnp.transpose(key_mass))


def solution(mesh):
    return jax.shard_map(
        pair_device if mesh.shape["seq"] == 2 else ring_device,
        mesh=mesh,
        in_specs=(
            P(("dp", "seq"), "heads"),
            P(None, "heads"),
            P("heads", "seq"),
            P(),
            P(("dp", "seq"), "heads"),
            P(("dp", "seq"), "heads"),
            P(("dp", "seq"), "heads"),
            P("dp"),
        ),
        out_specs=(P(("dp", "seq"), "heads"), P("heads", ("dp", "seq"))),
        check_vma=False,
    )
```

```python
import functools
import math

import jax
import jax.numpy as jnp
from jax import lax
from jax.experimental import pallas as pl
from jax.experimental.pallas import tpu as pltpu
from jax.sharding import PartitionSpec as P

QUERY_HEADS = 64
KV_HEADS = 8
HEAD_DIM = 128


NEG_FILL = -1e30
RIM_ROWS = 16
LEAST_RETENTION = -40.0
VMEM_BYTES = 16 * 1024 * 1024


def convolve(widened, taps_ref, columns, lead, rows):
    summed = jnp.zeros((rows, columns.stop - columns.start), jnp.float32)
    for back in range(taps_ref.shape[0]):
        tap = taps_ref[back : back + 1, columns].astype(jnp.float32)
        summed = summed + tap * widened[lead - back : lead - back + rows, columns]
    return summed.astype(jnp.bfloat16)


def own_project_kernel(
    rows_ref, taps_ref, gate_ref, out_ref, edges_ref, held_taps_ref, held_ref, widened
):
    rows, features = rows_ref.shape
    edges_ref[:RIM_ROWS] = rows_ref[:RIM_ROWS]
    edges_ref[RIM_ROWS:] = rows_ref[rows - RIM_ROWS :]
    held_taps_ref[...] = taps_ref[...].astype(jnp.float32)
    held_ref[...] = gate_ref[...]
    tile = math.gcd(features, 512)
    total = jnp.zeros(out_ref.shape, jnp.float32)
    for start in range(0, features, tile):
        columns = slice(start, start + tile)
        widened[:, columns] = rows_ref[:, columns].astype(jnp.float32)
        mixed = convolve(widened, taps_ref, columns, RIM_ROWS, rows - RIM_ROWS)
        total = total + jnp.dot(mixed, gate_ref[columns, :], preferred_element_type=jnp.float32)
    out_ref[...] = total


def peer_project_kernel(
    peer_ref, edges_ref, taps_ref, gate_ref, near_ref, far_ref, far_sent_ref, widened, own_widened
):
    rows, features = peer_ref.shape
    tile = math.gcd(features, 512)
    first = lax.axis_index("seq") == 0
    half = near_ref.shape[1]
    total = jnp.zeros((near_ref.shape[0], 2 * half), jnp.float32)
    for start in range(0, features, tile):
        columns = slice(start, start + tile)
        own_tail = edges_ref[RIM_ROWS:, columns].astype(jnp.float32)
        peer_tail = peer_ref[rows - RIM_ROWS :, columns].astype(jnp.float32)
        widened[:RIM_ROWS, columns] = jnp.where(first, own_tail, 0.0)
        widened[RIM_ROWS:, columns] = peer_ref[:, columns].astype(jnp.float32)
        own_widened[:RIM_ROWS, columns] = jnp.where(first, 0.0, peer_tail)
        own_widened[RIM_ROWS:, columns] = edges_ref[:RIM_ROWS, columns].astype(jnp.float32)
        mixed = jnp.concatenate(
            [
                convolve(own_widened, taps_ref, columns, RIM_ROWS, RIM_ROWS),
                convolve(widened, taps_ref, columns, RIM_ROWS, rows),
            ],
            axis=0,
        )
        total = total + jnp.dot(mixed, gate_ref[columns, :], preferred_element_type=jnp.float32)
    near_ref[...] = total[:, :half]
    far_ref[...] = total[:, half:]
    far_sent_ref[...] = total[:, half:].astype(jnp.bfloat16)


def own_project(activations, conv_taps, gate_in):
    rows, features = activations.shape
    done = rows - RIM_ROWS
    return pl.pallas_call(
        own_project_kernel,
        out_shape=(
            jax.ShapeDtypeStruct((done, gate_in.shape[1]), jnp.float32),
            jax.ShapeDtypeStruct((2 * RIM_ROWS, features), activations.dtype),
            jax.ShapeDtypeStruct(conv_taps.shape, jnp.float32),
            jax.ShapeDtypeStruct(gate_in.shape, gate_in.dtype),
        ),
        scratch_shapes=[pltpu.VMEM((rows, features), jnp.float32)],
        compiler_params=pltpu.CompilerParams(vmem_limit_bytes=VMEM_BYTES),
        cost_estimate=pl.CostEstimate(flops=1, bytes_accessed=1, transcendentals=0),
    )(activations, conv_taps, gate_in)


def peer_project(peer_rows, edges, conv_taps, gate_in):
    rows, features = peer_rows.shape
    done = rows + RIM_ROWS
    half = gate_in.shape[1] // 2
    return pl.pallas_call(
        peer_project_kernel,
        out_shape=(
            jax.ShapeDtypeStruct((done, half), jnp.float32),
            jax.ShapeDtypeStruct((done, half), jnp.float32),
            jax.ShapeDtypeStruct((done, half), jnp.bfloat16),
        ),
        scratch_shapes=[
            pltpu.VMEM((rows + RIM_ROWS, features), jnp.float32),
            pltpu.VMEM((2 * RIM_ROWS, features), jnp.float32),
        ],
        compiler_params=pltpu.CompilerParams(vmem_limit_bytes=VMEM_BYTES),
        cost_estimate=pl.CostEstimate(flops=1, bytes_accessed=1, transcendentals=0),
    )(peer_rows, edges, conv_taps, gate_in)


def head_sum(part):
    count = lax.axis_size("heads")
    step = 1
    received = None
    while step < count:
        if received is not None:
            part = part + received.astype(jnp.float32)
        received = exchange_heads(part if step == 1 else part.astype(jnp.bfloat16), step)
        step *= 2
    return part, received


def exchange_heads(block, step):
    count = lax.axis_size("heads")
    return lax.ppermute(block, "heads", [(i, i ^ step) for i in range(count)])


def in_one_piece(work, *given):
    shapes = jax.eval_shape(work, *given)
    return lax.cond(
        lax.axis_index("seq") >= 0,
        work,
        lambda *given: jax.tree.map(lambda like: jnp.zeros(like.shape, like.dtype), shapes),
        *given,
    )


def far_logits(block, sent, gate_rows):
    step = lax.axis_size("heads") // 2
    received = exchange_heads(sent, step)

    def nearer(block, received, gate_rows):
        distance = step
        while distance > 1:
            distance //= 2
            block = block + received.astype(jnp.float32)
            received = exchange_heads(block, distance)
        return partial_logits(block, received, gate_rows)

    return in_one_piece(nearer, block, received, gate_rows)


def share_of_logits(pre_ref, in_ref, gate_rows):
    pre = pre_ref[...] + in_ref[...].astype(jnp.float32)
    hidden = (pre / (1.0 + jnp.exp(-pre))).astype(jnp.bfloat16)
    return lax.dot_general(
        gate_rows, hidden, (((0,), (1,)), ((), ())), preferred_element_type=jnp.float32
    )


def partial_logits_kernel(own_ref, in_ref, gate_out_ref, out_ref):
    out_ref[...] = share_of_logits(own_ref, in_ref, gate_out_ref[...])


def partial_logits(part, received, gate_rows):
    return pl.pallas_call(
        partial_logits_kernel,
        out_shape=jax.ShapeDtypeStruct((gate_rows.shape[1], part.shape[0]), jnp.float32),
        compiler_params=pltpu.CompilerParams(vmem_limit_bytes=VMEM_BYTES),
    )(part, received, gate_rows)


def logits_kernel(own_ref, far_share_ref, near_ref, near_in_ref, gate_out_ref, out_ref):
    first = lax.axis_index("seq") == 0
    share = share_of_logits(near_ref, near_in_ref, gate_out_ref[...]) + far_share_ref[...]
    own = jnp.concatenate([share[:, :RIM_ROWS], own_ref[...]], axis=1)
    peer = share[:, RIM_ROWS:]
    out_ref[0] = jnp.where(first, own, peer)
    out_ref[1] = jnp.where(first, peer, own)


def logits_share(own_share, far_share, near, near_in, gate_rows):
    rows = own_share.shape[1] + RIM_ROWS
    return pl.pallas_call(
        logits_kernel,
        out_shape=jax.ShapeDtypeStruct((2, gate_rows.shape[1], rows), jnp.float32),
        compiler_params=pltpu.CompilerParams(vmem_limit_bytes=VMEM_BYTES),
    )(own_share, far_share, near, near_in, gate_rows)


def hide_unseen(seq_rank, segments_ref, rows):
    own_segments = segments_ref[pl.ds(seq_rank, 1), :]
    behind_segments = segments_ref[pl.ds(0, 1), :]
    query_segments = jnp.transpose(jnp.broadcast_to(own_segments, (rows, rows)))
    query_at = lax.broadcasted_iota(jnp.int32, (rows, rows), 0)
    key_at = lax.broadcasted_iota(jnp.int32, (rows, rows), 1)
    see_own = (key_at <= query_at) & (query_segments == own_segments)
    see_behind = (query_segments == behind_segments) & (seq_rank > 0)
    return jnp.where(jnp.concatenate([see_behind, see_own], axis=1), 0.0, NEG_FILL)


def head_columns(number):
    return slice(number * HEAD_DIM, (number + 1) * HEAD_DIM)


def scores_of(queries_ref, keys, offset, head):
    scores = lax.dot_general(
        queries_ref[:, head_columns(head)],
        keys,
        (((1,), (1,)), ((), ())),
        preferred_element_type=jnp.float32,
    )
    return scores * (1.0 / math.sqrt(HEAD_DIM)) + offset


def with_behind(ref, behind_ref, number, whole):
    own = ref[:, head_columns(number)]
    if not whole:
        return own
    return jnp.concatenate([behind_ref[:, head_columns(number)], own], axis=0)


def powers_kernel(segments_ref, queries_ref, keys_ref, behind_keys_ref, powers_ref):
    seq_rank = lax.axis_index("seq")
    rows = queries_ref.shape[0]
    kv_local = keys_ref.shape[1] // HEAD_DIM
    group_size = queries_ref.shape[1] // keys_ref.shape[1]
    hide = hide_unseen(seq_rank, segments_ref, rows)

    def fill(whole):
        start = 0 if whole else rows
        for head in range(kv_local * group_size):
            g = head // group_size
            keys = with_behind(keys_ref, behind_keys_ref, g, whole)
            scores = scores_of(queries_ref, keys, hide[:, start:], head)
            powers_ref[head, :, start:] = jnp.exp(
                scores - jnp.max(scores, axis=1, keepdims=True)
            )

    pl.when(seq_rank > 0)(lambda: fill(True))
    pl.when(seq_rank == 0)(lambda: fill(False))


def powers_of(segments, queries, keys, behind_keys):
    rows = queries.shape[0]
    heads = queries.shape[1] // HEAD_DIM
    return pl.pallas_call(
        powers_kernel,
        out_shape=jax.ShapeDtypeStruct((heads, rows, 2 * rows), jnp.float32),
        compiler_params=pltpu.CompilerParams(vmem_limit_bytes=VMEM_BYTES),
        cost_estimate=pl.CostEstimate(
            flops=4 * rows * rows * queries.shape[1],
            bytes_accessed=8 * heads * rows * rows,
            transcendentals=2 * heads * rows * rows,
        ),
    )(segments, queries, keys, behind_keys)


def weights_kernel(
    share_ref,
    peer_share_ref,
    powers_ref,
    segments_ref,
    queries_ref,
    keys_ref,
    behind_keys_ref,
    weights_ref,
    own_mass_ref,
    behind_mass_ref,
    retention,
):
    seq_rank, head_rank = lax.axis_index("seq"), lax.axis_index("heads")
    rows = queries_ref.shape[0]
    kv_local = keys_ref.shape[1] // HEAD_DIM
    group_size = queries_ref.shape[1] // keys_ref.shape[1]
    logits = share_ref[...] + peer_share_ref[...]
    log_gate = jnp.minimum(logits, 0.0) - jnp.log1p(jnp.exp(-jnp.abs(logits)))
    retention[...] = log_gate.astype(jnp.bfloat16).astype(jnp.float32)
    biases = []
    for g in range(kv_local):
        at = pl.ds(head_rank * kv_local + g, 1)
        biases.append(jnp.concatenate([retention[0, at, :], retention[seq_rank, at, :]], axis=1))
    moderate = jnp.min(functools.reduce(jnp.minimum, biases)) >= LEAST_RETENTION

    def finish(whole, terms_of):
        start = 0 if whole else rows
        for g in range(kv_local):
            mass = jnp.zeros((1, 2 * rows - start), jnp.float32)
            group_terms = terms_of(g, whole, start)
            for head in range(g * group_size, (g + 1) * group_size):
                weights = group_terms(head)
                weights = weights * (1.0 / jnp.sum(weights, axis=1, keepdims=True))
                mass = mass + jnp.sum(weights, axis=0, keepdims=True)
                weights_ref[head, :, start:] = weights.astype(jnp.bfloat16)
            mass = mass / group_size
            own_mass_ref[g : g + 1, :] = mass[:, rows - start :]
            behind_mass_ref[g : g + 1, :] = mass[:, :rows] if whole else jnp.zeros((1, rows))

    def by_powers(g, whole, start):
        factor = jnp.exp(biases[g] - jnp.max(biases[g]))[:, start:]
        return lambda head: powers_ref[head, :, start:] * factor

    def by_scores(g, whole, start):
        offset = hide_unseen(seq_rank, segments_ref, rows) + biases[g]
        keys = with_behind(keys_ref, behind_keys_ref, g, whole)

        def terms(head):
            scores = scores_of(queries_ref, keys, offset[:, start:], head)
            return jnp.exp(scores - jnp.max(scores, axis=1, keepdims=True))

        return terms

    pl.when(moderate & (seq_rank > 0))(lambda: finish(True, by_powers))
    pl.when(moderate & (seq_rank == 0))(lambda: finish(False, by_powers))
    pl.when(jnp.logical_not(moderate))(lambda: finish(True, by_scores))


def weights_of(share, peer_share, powers, segments, queries, keys, behind_keys):
    rows = queries.shape[0]
    mass = jax.ShapeDtypeStruct((keys.shape[1] // HEAD_DIM, rows), jnp.float32)
    return pl.pallas_call(
        weights_kernel,
        out_shape=(jax.ShapeDtypeStruct(powers.shape, jnp.bfloat16), mass, mass),
        scratch_shapes=[pltpu.VMEM(share.shape, jnp.float32)],
        compiler_params=pltpu.CompilerParams(vmem_limit_bytes=VMEM_BYTES),
    )(share, peer_share, powers, segments, queries, keys, behind_keys)


def attend_kernel(weights_ref, values_ref, behind_values_ref, attended_ref):
    seq_rank = lax.axis_index("seq")
    heads, rows = weights_ref.shape[:2]
    group_size = attended_ref.shape[1] // values_ref.shape[1]

    def fill(whole):
        start = 0 if whole else rows
        for head in range(heads):
            values = with_behind(values_ref, behind_values_ref, head // group_size, whole)
            attended_ref[:, head_columns(head)] = jnp.dot(
                weights_ref[head, :, start:], values, preferred_element_type=jnp.float32
            ).astype(jnp.bfloat16)

    pl.when(seq_rank > 0)(lambda: fill(True))
    pl.when(seq_rank == 0)(lambda: fill(False))


def attend(weights, values, behind_values):
    heads, rows = weights.shape[:2]
    return pl.pallas_call(
        attend_kernel,
        out_shape=jax.ShapeDtypeStruct((rows, heads * HEAD_DIM), jnp.bfloat16),
        compiler_params=pltpu.CompilerParams(vmem_limit_bytes=VMEM_BYTES),
        cost_estimate=pl.CostEstimate(
            flops=4 * rows * rows * heads * HEAD_DIM,
            bytes_accessed=2 * (weights.size + rows * heads * HEAD_DIM),
            transcendentals=0,
        ),
    )(weights, values, behind_values)


def pair_device(
    activations, conv_taps, gate_in, gate_out, queries, key_vectors, value_vectors, segment_ids
):
    rows = activations.shape[0]
    swap = [(0, 1), (1, 0)]
    seq_rank = lax.axis_index("seq")
    segments = segment_ids.reshape(2, rows)
    hidden_local = gate_in.shape[1]
    gate_rows = lax.dynamic_slice_in_dim(gate_out, seq_rank * hidden_local, hidden_local, 0)

    peer_rows = lax.ppermute(activations, "seq", swap)

    def own_work(activations, conv_taps, gate_in, gate_rows):
        part, *held = own_project(activations, conv_taps, gate_in)
        return partial_logits(*head_sum(part), gate_rows), held

    own_share, held = in_one_piece(own_work, activations, conv_taps, gate_in, gate_rows)
    peer_rows, own_share, held = lax.optimization_barrier((peer_rows, own_share, held))
    near, far, far_sent = peer_project(peer_rows, *held)
    behind_keys = lax.ppermute(key_vectors, "seq", swap)
    behind_values = lax.ppermute(value_vectors, "seq", swap)
    half = near.shape[1]
    near, near_in = head_sum(near)
    far_share = far_logits(far, far_sent, gate_rows[half:])
    share = logits_share(own_share, far_share, near, near_in, gate_rows[:half])
    share, queries = lax.optimization_barrier((share, queries))
    powers = powers_of(segments, queries, key_vectors, behind_keys)
    weights, own_mass, behind_mass = weights_of(
        share,
        lax.ppermute(share, "seq", swap),
        powers,
        segments,
        queries,
        key_vectors,
        behind_keys,
    )
    attended = attend(weights, value_vectors, behind_values)
    key_mass = own_mass + lax.ppermute(behind_mass, "seq", swap)
    return (attended, key_mass.astype(jnp.bfloat16))


def from_behind(block, axis, distance):
    devices = range(lax.axis_size(axis))
    route = [(i - distance, i) for i in devices if i - distance in devices]
    return lax.ppermute(block, axis, route)


def block_scores(query_heads, key_block, bias_block, allowed, score_scale):
    scores = (
        jnp.einsum("tgeh,kgh->getk", query_heads, key_block, preferred_element_type=jnp.float32)
        * score_scale
    )
    scores = scores + jnp.transpose(bias_block.astype(jnp.float32))[:, None, None, :]
    return jnp.where(allowed[None, None], scores, NEG_FILL)


def ring_device(
    activations, conv_taps, gate_in, gate_out, queries, key_vectors, value_vectors, segment_ids
):
    shard_rows = activations.shape[0]
    tap_count = conv_taps.shape[0]
    rim_rows = from_behind(activations[shard_rows - (tap_count - 1) :], "seq", 1)
    widened = jnp.concatenate([rim_rows, activations], 0).astype(jnp.float32)
    summed = jnp.zeros(activations.shape, jnp.float32)
    for shift_back in range(tap_count):
        start_row = tap_count - 1 - shift_back
        summed = (
            summed
            + conv_taps[shift_back].astype(jnp.float32)
            * widened[start_row : start_row + shard_rows]
        )
    mixed_rows = summed.astype(jnp.bfloat16)
    partial_hidden = jnp.dot(
        mixed_rows,
        lax.all_gather(gate_in, "seq", axis=1, tiled=True),
        preferred_element_type=jnp.float32,
    )
    kv_local = key_vectors.shape[1] // HEAD_DIM
    group_size = QUERY_HEADS // KV_HEADS
    head_rank = lax.axis_index("heads")
    hidden = jax.nn.silu(lax.psum(partial_hidden, "heads")).astype(jnp.bfloat16)
    logits = jnp.dot(hidden, gate_out, preferred_element_type=jnp.float32)
    retention = lax.dynamic_slice_in_dim(
        jax.nn.log_sigmoid(logits).astype(jnp.bfloat16), head_rank * kv_local, kv_local, 1
    )
    seq_rank = lax.axis_index("seq")
    local_index = jnp.arange(shard_rows, dtype=jnp.int32)
    own_queries, own_keys, own_values, own_bias = (queries, key_vectors, value_vectors, retention)
    query_places = seq_rank * shard_rows + local_index
    query_segments = jnp.take(segment_ids, query_places)
    query_heads = own_queries.reshape(shard_rows, kv_local, group_size, HEAD_DIM)
    score_scale = 1.0 / math.sqrt(HEAD_DIM)

    def visibility(flat_index):
        key_segments = jnp.take(segment_ids, flat_index)
        return (flat_index[None, :] <= query_places[:, None]) & (
            key_segments[None, :] == query_segments[:, None]
        )

    initial = (
        jnp.full((kv_local, group_size, shard_rows), NEG_FILL, jnp.float32),
        jnp.zeros((kv_local, group_size, shard_rows), jnp.float32),
    )
    all_keys, all_values, all_bias = (
        lax.all_gather(own_keys, "seq", axis=0, tiled=True),
        lax.all_gather(own_values, "seq", axis=0, tiled=True),
        lax.all_gather(own_bias, "seq", axis=0, tiled=True),
    )
    piece_rows = all_keys.shape[0]
    stats_block_width = math.gcd(piece_rows, 512)

    def one_block(block_number, state_in):
        offset = block_number * stats_block_width
        key_block = lax.dynamic_slice_in_dim(all_keys, offset, stats_block_width, 0).reshape(
            stats_block_width, kv_local, HEAD_DIM
        )
        bias_block = lax.dynamic_slice_in_dim(all_bias, offset, stats_block_width, 0)
        allowed = visibility(0 + offset + jnp.arange(stats_block_width, dtype=jnp.int32))

        def update(state_old):
            peak_old, mass_old = state_old
            masked = block_scores(query_heads, key_block, bias_block, allowed, score_scale)
            peak_new = jnp.maximum(peak_old, jnp.max(masked, axis=3))
            exponent = jnp.where(allowed[None, None], jnp.exp(masked - peak_new[..., None]), 0.0)
            return (peak_new, mass_old * jnp.exp(peak_old - peak_new) + jnp.sum(exponent, axis=3))

        def keep_state(state_old):
            return state_old

        return lax.cond(jnp.any(allowed), update, keep_state, state_in)

    row_peak, total_mass = lax.fori_loop(0, piece_rows // stats_block_width, one_block, initial)
    total_keys = all_keys.shape[0]
    block_width = math.gcd(total_keys, 512)
    block_count = total_keys // block_width
    key_blocks = all_keys.reshape(block_count, block_width, kv_local, HEAD_DIM)
    value_blocks = all_values.reshape(block_count, block_width, kv_local, HEAD_DIM)
    bias_blocks = all_bias.reshape(block_count, block_width, kv_local)

    def second_pass(accumulated, block_items):
        block_number, key_block, value_block, bias_block = block_items
        allowed = visibility(block_number * block_width + jnp.arange(block_width, dtype=jnp.int32))

        def attend(accum_in):
            masked = block_scores(query_heads, key_block, bias_block, allowed, score_scale)
            weights = (
                jnp.where(allowed[None, None], jnp.exp(masked - row_peak[..., None]), 0.0)
                / total_mass[..., None]
            )
            accum_out = accum_in + jnp.einsum(
                "getk,kgh->tgeh",
                weights.astype(jnp.bfloat16),
                value_block,
                preferred_element_type=jnp.float32,
            )
            return (accum_out, jnp.transpose(jnp.sum(weights, axis=(1, 2))) / group_size)

        def skip_block(accum_in):
            return (accum_in, jnp.zeros((block_width, kv_local), jnp.float32))

        return lax.cond(jnp.any(allowed), attend, skip_block, accumulated)

    accumulated, mass_blocks = lax.scan(
        second_pass,
        jnp.zeros((shard_rows, kv_local, group_size, HEAD_DIM), jnp.float32),
        (jnp.arange(block_count, dtype=jnp.int32), key_blocks, value_blocks, bias_blocks),
    )
    key_term = mass_blocks.reshape(total_keys, kv_local)
    key_mass = lax.psum_scatter(key_term, "seq", scatter_dimension=0, tiled=True).astype(
        jnp.bfloat16
    )
    attended = accumulated.reshape(shard_rows, kv_local * group_size * HEAD_DIM).astype(
        jnp.bfloat16
    )
    return (attended, jnp.transpose(key_mass))


def solution(mesh):
    return jax.shard_map(
        pair_device if mesh.shape["seq"] == 2 else ring_device,
        mesh=mesh,
        in_specs=(
            P(("dp", "seq"), "heads"),
            P(None, "heads"),
            P("heads", "seq"),
            P(),
            P(("dp", "seq"), "heads"),
            P(("dp", "seq"), "heads"),
            P(("dp", "seq"), "heads"),
            P("dp"),
        ),
        out_specs=(P(("dp", "seq"), "heads"), P("heads", ("dp", "seq"))),
        check_vma=False,
    )
```

```python
import functools
import math

import jax
import jax.numpy as jnp
from jax import lax
from jax.experimental import pallas as pl
from jax.experimental.pallas import tpu as pltpu
from jax.sharding import PartitionSpec as P

QUERY_HEADS = 64
KV_HEADS = 8
HEAD_DIM = 128


NEG_FILL = -1e30
RIM_ROWS = 16
TILE = 512
LEAST_RETENTION = -40.0
VMEM_BYTES = 16 * 1024 * 1024


def convolve(widened, taps, lead, rows):
    summed = jnp.zeros((rows, widened.shape[1]), jnp.float32)
    for back in range(taps.shape[0]):
        summed = summed + taps[back : back + 1] * widened[lead - back : lead - back + rows]
    return summed.astype(jnp.bfloat16)


def own_project_kernel(
    rows_ref, taps_ref, gate_ref, out_ref, edges_ref, held_taps_ref, held_ref, widened
):
    rows, features = rows_ref.shape
    edges_ref[:RIM_ROWS] = rows_ref[:RIM_ROWS]
    edges_ref[RIM_ROWS:] = rows_ref[rows - RIM_ROWS :]
    held_taps_ref[...] = taps_ref[...].astype(jnp.float32)
    held_ref[...] = gate_ref[...]
    tile = widened.shape[2]
    total = jnp.zeros(out_ref.shape, jnp.float32)
    for step in range(features // tile):
        columns = slice(step * tile, (step + 1) * tile)
        wide = widened.at[step % 2]
        wide[...] = rows_ref[:, columns].astype(jnp.float32)
        taps = taps_ref[:, columns].astype(jnp.float32)
        mixed = convolve(wide, taps, RIM_ROWS, rows - RIM_ROWS)
        total = total + jnp.dot(mixed, gate_ref[columns, :], preferred_element_type=jnp.float32)
    out_ref[...] = total


def peer_project_kernel(
    peer_ref, edges_ref, taps_ref, gate_ref, near_ref, far_ref, far_sent_ref, widened, own_widened
):
    rows, features = peer_ref.shape
    tile = widened.shape[2]
    first = lax.axis_index("seq") == 0
    half = near_ref.shape[1]
    total = jnp.zeros((near_ref.shape[0], 2 * half), jnp.float32)
    for step in range(features // tile):
        columns = slice(step * tile, (step + 1) * tile)
        wide, own_wide = widened.at[step % 2], own_widened.at[step % 2]
        own_tail = edges_ref[RIM_ROWS:, columns].astype(jnp.float32)
        peer_tail = peer_ref[rows - RIM_ROWS :, columns].astype(jnp.float32)
        wide[:RIM_ROWS] = jnp.where(first, own_tail, 0.0)
        wide[RIM_ROWS:] = peer_ref[:, columns].astype(jnp.float32)
        own_wide[:RIM_ROWS] = jnp.where(first, 0.0, peer_tail)
        own_wide[RIM_ROWS:] = edges_ref[:RIM_ROWS, columns].astype(jnp.float32)
        taps = taps_ref[:, columns].astype(jnp.float32)
        mixed = jnp.concatenate(
            [
                convolve(own_wide, taps, RIM_ROWS, RIM_ROWS),
                convolve(wide, taps, RIM_ROWS, rows),
            ],
            axis=0,
        )
        total = total + jnp.dot(mixed, gate_ref[columns, :], preferred_element_type=jnp.float32)
    near_ref[...] = total[:, :half]
    far_ref[...] = total[:, half:]
    far_sent_ref[...] = total[:, half:].astype(jnp.bfloat16)


def own_project(activations, conv_taps, gate_in):
    rows, features = activations.shape
    done = rows - RIM_ROWS
    return pl.pallas_call(
        own_project_kernel,
        out_shape=(
            jax.ShapeDtypeStruct((done, gate_in.shape[1]), jnp.float32),
            jax.ShapeDtypeStruct((2 * RIM_ROWS, features), activations.dtype),
            jax.ShapeDtypeStruct(conv_taps.shape, jnp.float32),
            jax.ShapeDtypeStruct(gate_in.shape, gate_in.dtype),
        ),
        scratch_shapes=[pltpu.VMEM((2, rows, math.gcd(features, TILE)), jnp.float32)],
        compiler_params=pltpu.CompilerParams(vmem_limit_bytes=VMEM_BYTES),
        cost_estimate=pl.CostEstimate(flops=1, bytes_accessed=1, transcendentals=0),
    )(activations, conv_taps, gate_in)


def peer_project(peer_rows, edges, conv_taps, gate_in):
    rows, features = peer_rows.shape
    done = rows + RIM_ROWS
    half = gate_in.shape[1] // 2
    return pl.pallas_call(
        peer_project_kernel,
        out_shape=(
            jax.ShapeDtypeStruct((done, half), jnp.float32),
            jax.ShapeDtypeStruct((done, half), jnp.float32),
            jax.ShapeDtypeStruct((done, half), jnp.bfloat16),
        ),
        scratch_shapes=[
            pltpu.VMEM((2, rows + RIM_ROWS, math.gcd(features, TILE)), jnp.float32),
            pltpu.VMEM((2, 2 * RIM_ROWS, math.gcd(features, TILE)), jnp.float32),
        ],
        compiler_params=pltpu.CompilerParams(vmem_limit_bytes=VMEM_BYTES),
        cost_estimate=pl.CostEstimate(flops=1, bytes_accessed=1, transcendentals=0),
    )(peer_rows, edges, conv_taps, gate_in)


def head_sum(part):
    count = lax.axis_size("heads")
    step = 1
    received = None
    while step < count:
        if received is not None:
            part = part + received.astype(jnp.float32)
        received = exchange_heads(part if step == 1 else part.astype(jnp.bfloat16), step)
        step *= 2
    return part, received


def exchange_heads(block, step):
    count = lax.axis_size("heads")
    return lax.ppermute(block, "heads", [(i, i ^ step) for i in range(count)])


def in_one_piece(work, *given):
    shapes = jax.eval_shape(work, *given)
    return lax.cond(
        lax.axis_index("seq") >= 0,
        work,
        lambda *given: jax.tree.map(lambda like: jnp.zeros(like.shape, like.dtype), shapes),
        *given,
    )


def far_logits(block, sent, gate_rows):
    step = lax.axis_size("heads") // 2
    received = exchange_heads(sent, step)

    def nearer(block, received, gate_rows):
        distance = step
        while distance > 1:
            distance //= 2
            block = block + received.astype(jnp.float32)
            received = exchange_heads(block, distance)
        return partial_logits(block, received, gate_rows)

    return in_one_piece(nearer, block, received, gate_rows)


def share_of_logits(pre_ref, in_ref, gate_rows):
    pre = pre_ref[...] + in_ref[...].astype(jnp.float32)
    hidden = (pre / (1.0 + jnp.exp(-pre))).astype(jnp.bfloat16)
    return lax.dot_general(
        gate_rows, hidden, (((0,), (1,)), ((), ())), preferred_element_type=jnp.float32
    )


def partial_logits_kernel(own_ref, in_ref, gate_out_ref, out_ref):
    out_ref[...] = share_of_logits(own_ref, in_ref, gate_out_ref[...])


def partial_logits(part, received, gate_rows):
    return pl.pallas_call(
        partial_logits_kernel,
        out_shape=jax.ShapeDtypeStruct((gate_rows.shape[1], part.shape[0]), jnp.float32),
        compiler_params=pltpu.CompilerParams(vmem_limit_bytes=VMEM_BYTES),
    )(part, received, gate_rows)


def logits_kernel(own_ref, far_share_ref, near_ref, near_in_ref, gate_out_ref, out_ref):
    first = lax.axis_index("seq") == 0
    share = share_of_logits(near_ref, near_in_ref, gate_out_ref[...]) + far_share_ref[...]
    own = jnp.concatenate([share[:, :RIM_ROWS], own_ref[...]], axis=1)
    peer = share[:, RIM_ROWS:]
    out_ref[0] = jnp.where(first, own, peer)
    out_ref[1] = jnp.where(first, peer, own)


def logits_share(own_share, far_share, near, near_in, gate_rows):
    rows = own_share.shape[1] + RIM_ROWS
    return pl.pallas_call(
        logits_kernel,
        out_shape=jax.ShapeDtypeStruct((2, gate_rows.shape[1], rows), jnp.float32),
        compiler_params=pltpu.CompilerParams(vmem_limit_bytes=VMEM_BYTES),
    )(own_share, far_share, near, near_in, gate_rows)


def hide_unseen(seq_rank, segments_ref, rows):
    own_segments = segments_ref[pl.ds(seq_rank, 1), :]
    behind_segments = segments_ref[pl.ds(0, 1), :]
    query_segments = jnp.transpose(jnp.broadcast_to(own_segments, (rows, rows)))
    query_at = lax.broadcasted_iota(jnp.int32, (rows, rows), 0)
    key_at = lax.broadcasted_iota(jnp.int32, (rows, rows), 1)
    see_own = (key_at <= query_at) & (query_segments == own_segments)
    see_behind = (query_segments == behind_segments) & (seq_rank > 0)
    return jnp.where(jnp.concatenate([see_behind, see_own], axis=1), 0.0, NEG_FILL)


def head_columns(number):
    return slice(number * HEAD_DIM, (number + 1) * HEAD_DIM)


def scores_of(queries_ref, keys, offset, head):
    scores = lax.dot_general(
        queries_ref[:, head_columns(head)],
        keys,
        (((1,), (1,)), ((), ())),
        preferred_element_type=jnp.float32,
    )
    return scores * (1.0 / math.sqrt(HEAD_DIM)) + offset


def with_behind(ref, behind_ref, number, whole):
    own = ref[:, head_columns(number)]
    if not whole:
        return own
    return jnp.concatenate([behind_ref[:, head_columns(number)], own], axis=0)


def powers_kernel(segments_ref, queries_ref, keys_ref, behind_keys_ref, powers_ref):
    seq_rank = lax.axis_index("seq")
    rows = queries_ref.shape[0]
    kv_local = keys_ref.shape[1] // HEAD_DIM
    group_size = queries_ref.shape[1] // keys_ref.shape[1]
    hide = hide_unseen(seq_rank, segments_ref, rows)

    def fill(whole):
        start = 0 if whole else rows
        for head in range(kv_local * group_size):
            g = head // group_size
            keys = with_behind(keys_ref, behind_keys_ref, g, whole)
            scores = scores_of(queries_ref, keys, hide[:, start:], head)
            powers_ref[head, :, start:] = jnp.exp(
                scores - jnp.max(scores, axis=1, keepdims=True)
            )

    pl.when(seq_rank > 0)(lambda: fill(True))
    pl.when(seq_rank == 0)(lambda: fill(False))


def powers_of(segments, queries, keys, behind_keys):
    rows = queries.shape[0]
    heads = queries.shape[1] // HEAD_DIM
    return pl.pallas_call(
        powers_kernel,
        out_shape=jax.ShapeDtypeStruct((heads, rows, 2 * rows), jnp.float32),
        compiler_params=pltpu.CompilerParams(vmem_limit_bytes=VMEM_BYTES),
        cost_estimate=pl.CostEstimate(
            flops=4 * rows * rows * queries.shape[1],
            bytes_accessed=8 * heads * rows * rows,
            transcendentals=2 * heads * rows * rows,
        ),
    )(segments, queries, keys, behind_keys)


def weights_kernel(
    share_ref,
    peer_share_ref,
    powers_ref,
    segments_ref,
    queries_ref,
    keys_ref,
    behind_keys_ref,
    weights_ref,
    own_mass_ref,
    behind_mass_ref,
    retention,
):
    seq_rank, head_rank = lax.axis_index("seq"), lax.axis_index("heads")
    rows = queries_ref.shape[0]
    kv_local = keys_ref.shape[1] // HEAD_DIM
    group_size = queries_ref.shape[1] // keys_ref.shape[1]
    logits = share_ref[...] + peer_share_ref[...]
    log_gate = jnp.minimum(logits, 0.0) - jnp.log1p(jnp.exp(-jnp.abs(logits)))
    retention[...] = log_gate.astype(jnp.bfloat16).astype(jnp.float32)
    biases = []
    for g in range(kv_local):
        at = pl.ds(head_rank * kv_local + g, 1)
        biases.append(jnp.concatenate([retention[0, at, :], retention[seq_rank, at, :]], axis=1))
    moderate = jnp.min(functools.reduce(jnp.minimum, biases)) >= LEAST_RETENTION

    def finish(whole, terms_of):
        start = 0 if whole else rows
        for g in range(kv_local):
            mass = jnp.zeros((1, 2 * rows - start), jnp.float32)
            group_terms = terms_of(g, whole, start)
            for head in range(g * group_size, (g + 1) * group_size):
                weights = group_terms(head)
                weights = weights * (1.0 / jnp.sum(weights, axis=1, keepdims=True))
                mass = mass + jnp.sum(weights, axis=0, keepdims=True)
                weights_ref[head, :, start:] = weights.astype(jnp.bfloat16)
            mass = mass / group_size
            own_mass_ref[g : g + 1, :] = mass[:, rows - start :]
            behind_mass_ref[g : g + 1, :] = mass[:, :rows] if whole else jnp.zeros((1, rows))

    def by_powers(g, whole, start):
        factor = jnp.exp(biases[g] - jnp.max(biases[g]))[:, start:]
        return lambda head: powers_ref[head, :, start:] * factor

    def by_scores(g, whole, start):
        offset = hide_unseen(seq_rank, segments_ref, rows) + biases[g]
        keys = with_behind(keys_ref, behind_keys_ref, g, whole)

        def terms(head):
            scores = scores_of(queries_ref, keys, offset[:, start:], head)
            return jnp.exp(scores - jnp.max(scores, axis=1, keepdims=True))

        return terms

    pl.when(moderate & (seq_rank > 0))(lambda: finish(True, by_powers))
    pl.when(moderate & (seq_rank == 0))(lambda: finish(False, by_powers))
    pl.when(jnp.logical_not(moderate))(lambda: finish(True, by_scores))


def weights_of(share, peer_share, powers, segments, queries, keys, behind_keys):
    rows = queries.shape[0]
    mass = jax.ShapeDtypeStruct((keys.shape[1] // HEAD_DIM, rows), jnp.float32)
    return pl.pallas_call(
        weights_kernel,
        out_shape=(jax.ShapeDtypeStruct(powers.shape, jnp.bfloat16), mass, mass),
        scratch_shapes=[pltpu.VMEM(share.shape, jnp.float32)],
        compiler_params=pltpu.CompilerParams(vmem_limit_bytes=VMEM_BYTES),
    )(share, peer_share, powers, segments, queries, keys, behind_keys)


def attend_kernel(weights_ref, values_ref, behind_values_ref, attended_ref):
    seq_rank = lax.axis_index("seq")
    heads, rows = weights_ref.shape[:2]
    group_size = attended_ref.shape[1] // values_ref.shape[1]

    def fill(whole):
        start = 0 if whole else rows
        for head in range(heads):
            values = with_behind(values_ref, behind_values_ref, head // group_size, whole)
            attended_ref[:, head_columns(head)] = jnp.dot(
                weights_ref[head, :, start:], values, preferred_element_type=jnp.float32
            ).astype(jnp.bfloat16)

    pl.when(seq_rank > 0)(lambda: fill(True))
    pl.when(seq_rank == 0)(lambda: fill(False))


def attend(weights, values, behind_values):
    heads, rows = weights.shape[:2]
    return pl.pallas_call(
        attend_kernel,
        out_shape=jax.ShapeDtypeStruct((rows, heads * HEAD_DIM), jnp.bfloat16),
        compiler_params=pltpu.CompilerParams(vmem_limit_bytes=VMEM_BYTES),
        cost_estimate=pl.CostEstimate(
            flops=4 * rows * rows * heads * HEAD_DIM,
            bytes_accessed=2 * (weights.size + rows * heads * HEAD_DIM),
            transcendentals=0,
        ),
    )(weights, values, behind_values)


def pair_device(
    activations, conv_taps, gate_in, gate_out, queries, key_vectors, value_vectors, segment_ids
):
    rows = activations.shape[0]
    swap = [(0, 1), (1, 0)]
    seq_rank = lax.axis_index("seq")
    segments = segment_ids.reshape(2, rows)
    hidden_local = gate_in.shape[1]
    gate_rows = lax.dynamic_slice_in_dim(gate_out, seq_rank * hidden_local, hidden_local, 0)

    peer_rows = lax.ppermute(activations, "seq", swap)

    def own_work(activations, conv_taps, gate_in, gate_rows):
        part, *held = own_project(activations, conv_taps, gate_in)
        return partial_logits(*head_sum(part), gate_rows), held

    own_share, held = in_one_piece(own_work, activations, conv_taps, gate_in, gate_rows)
    peer_rows, own_share, held = lax.optimization_barrier((peer_rows, own_share, held))
    near, far, far_sent = peer_project(peer_rows, *held)
    behind_keys = lax.ppermute(key_vectors, "seq", swap)
    behind_values = lax.ppermute(value_vectors, "seq", swap)
    half = near.shape[1]
    near, near_in = head_sum(near)
    far_share = far_logits(far, far_sent, gate_rows[half:])
    share = logits_share(own_share, far_share, near, near_in, gate_rows[:half])
    share, queries = lax.optimization_barrier((share, queries))
    powers = powers_of(segments, queries, key_vectors, behind_keys)
    weights, own_mass, behind_mass = weights_of(
        share,
        lax.ppermute(share, "seq", swap),
        powers,
        segments,
        queries,
        key_vectors,
        behind_keys,
    )
    attended = attend(weights, value_vectors, behind_values)
    key_mass = own_mass + lax.ppermute(behind_mass, "seq", swap)
    return (attended, key_mass.astype(jnp.bfloat16))


def from_behind(block, axis, distance):
    devices = range(lax.axis_size(axis))
    route = [(i - distance, i) for i in devices if i - distance in devices]
    return lax.ppermute(block, axis, route)


def block_scores(query_heads, key_block, bias_block, allowed, score_scale):
    scores = (
        jnp.einsum("tgeh,kgh->getk", query_heads, key_block, preferred_element_type=jnp.float32)
        * score_scale
    )
    scores = scores + jnp.transpose(bias_block.astype(jnp.float32))[:, None, None, :]
    return jnp.where(allowed[None, None], scores, NEG_FILL)


def ring_device(
    activations, conv_taps, gate_in, gate_out, queries, key_vectors, value_vectors, segment_ids
):
    shard_rows = activations.shape[0]
    tap_count = conv_taps.shape[0]
    rim_rows = from_behind(activations[shard_rows - (tap_count - 1) :], "seq", 1)
    widened = jnp.concatenate([rim_rows, activations], 0).astype(jnp.float32)
    summed = jnp.zeros(activations.shape, jnp.float32)
    for shift_back in range(tap_count):
        start_row = tap_count - 1 - shift_back
        summed = (
            summed
            + conv_taps[shift_back].astype(jnp.float32)
            * widened[start_row : start_row + shard_rows]
        )
    mixed_rows = summed.astype(jnp.bfloat16)
    partial_hidden = jnp.dot(
        mixed_rows,
        lax.all_gather(gate_in, "seq", axis=1, tiled=True),
        preferred_element_type=jnp.float32,
    )
    kv_local = key_vectors.shape[1] // HEAD_DIM
    group_size = QUERY_HEADS // KV_HEADS
    head_rank = lax.axis_index("heads")
    hidden = jax.nn.silu(lax.psum(partial_hidden, "heads")).astype(jnp.bfloat16)
    logits = jnp.dot(hidden, gate_out, preferred_element_type=jnp.float32)
    retention = lax.dynamic_slice_in_dim(
        jax.nn.log_sigmoid(logits).astype(jnp.bfloat16), head_rank * kv_local, kv_local, 1
    )
    seq_rank = lax.axis_index("seq")
    local_index = jnp.arange(shard_rows, dtype=jnp.int32)
    own_queries, own_keys, own_values, own_bias = (queries, key_vectors, value_vectors, retention)
    query_places = seq_rank * shard_rows + local_index
    query_segments = jnp.take(segment_ids, query_places)
    query_heads = own_queries.reshape(shard_rows, kv_local, group_size, HEAD_DIM)
    score_scale = 1.0 / math.sqrt(HEAD_DIM)

    def visibility(flat_index):
        key_segments = jnp.take(segment_ids, flat_index)
        return (flat_index[None, :] <= query_places[:, None]) & (
            key_segments[None, :] == query_segments[:, None]
        )

    initial = (
        jnp.full((kv_local, group_size, shard_rows), NEG_FILL, jnp.float32),
        jnp.zeros((kv_local, group_size, shard_rows), jnp.float32),
    )
    all_keys, all_values, all_bias = (
        lax.all_gather(own_keys, "seq", axis=0, tiled=True),
        lax.all_gather(own_values, "seq", axis=0, tiled=True),
        lax.all_gather(own_bias, "seq", axis=0, tiled=True),
    )
    piece_rows = all_keys.shape[0]
    stats_block_width = math.gcd(piece_rows, 512)

    def one_block(block_number, state_in):
        offset = block_number * stats_block_width
        key_block = lax.dynamic_slice_in_dim(all_keys, offset, stats_block_width, 0).reshape(
            stats_block_width, kv_local, HEAD_DIM
        )
        bias_block = lax.dynamic_slice_in_dim(all_bias, offset, stats_block_width, 0)
        allowed = visibility(0 + offset + jnp.arange(stats_block_width, dtype=jnp.int32))

        def update(state_old):
            peak_old, mass_old = state_old
            masked = block_scores(query_heads, key_block, bias_block, allowed, score_scale)
            peak_new = jnp.maximum(peak_old, jnp.max(masked, axis=3))
            exponent = jnp.where(allowed[None, None], jnp.exp(masked - peak_new[..., None]), 0.0)
            return (peak_new, mass_old * jnp.exp(peak_old - peak_new) + jnp.sum(exponent, axis=3))

        def keep_state(state_old):
            return state_old

        return lax.cond(jnp.any(allowed), update, keep_state, state_in)

    row_peak, total_mass = lax.fori_loop(0, piece_rows // stats_block_width, one_block, initial)
    total_keys = all_keys.shape[0]
    block_width = math.gcd(total_keys, 512)
    block_count = total_keys // block_width
    key_blocks = all_keys.reshape(block_count, block_width, kv_local, HEAD_DIM)
    value_blocks = all_values.reshape(block_count, block_width, kv_local, HEAD_DIM)
    bias_blocks = all_bias.reshape(block_count, block_width, kv_local)

    def second_pass(accumulated, block_items):
        block_number, key_block, value_block, bias_block = block_items
        allowed = visibility(block_number * block_width + jnp.arange(block_width, dtype=jnp.int32))

        def attend(accum_in):
            masked = block_scores(query_heads, key_block, bias_block, allowed, score_scale)
            weights = (
                jnp.where(allowed[None, None], jnp.exp(masked - row_peak[..., None]), 0.0)
                / total_mass[..., None]
            )
            accum_out = accum_in + jnp.einsum(
                "getk,kgh->tgeh",
                weights.astype(jnp.bfloat16),
                value_block,
                preferred_element_type=jnp.float32,
            )
            return (accum_out, jnp.transpose(jnp.sum(weights, axis=(1, 2))) / group_size)

        def skip_block(accum_in):
            return (accum_in, jnp.zeros((block_width, kv_local), jnp.float32))

        return lax.cond(jnp.any(allowed), attend, skip_block, accumulated)

    accumulated, mass_blocks = lax.scan(
        second_pass,
        jnp.zeros((shard_rows, kv_local, group_size, HEAD_DIM), jnp.float32),
        (jnp.arange(block_count, dtype=jnp.int32), key_blocks, value_blocks, bias_blocks),
    )
    key_term = mass_blocks.reshape(total_keys, kv_local)
    key_mass = lax.psum_scatter(key_term, "seq", scatter_dimension=0, tiled=True).astype(
        jnp.bfloat16
    )
    attended = accumulated.reshape(shard_rows, kv_local * group_size * HEAD_DIM).astype(
        jnp.bfloat16
    )
    return (attended, jnp.transpose(key_mass))


def solution(mesh):
    return jax.shard_map(
        pair_device if mesh.shape["seq"] == 2 else ring_device,
        mesh=mesh,
        in_specs=(
            P(("dp", "seq"), "heads"),
            P(None, "heads"),
            P("heads", "seq"),
            P(),
            P(("dp", "seq"), "heads"),
            P(("dp", "seq"), "heads"),
            P(("dp", "seq"), "heads"),
            P("dp"),
        ),
        out_specs=(P(("dp", "seq"), "heads"), P("heads", ("dp", "seq"))),
        check_vma=False,
    )
```

```python
import functools
import math

import jax
import jax.numpy as jnp
from jax import lax
from jax.experimental import pallas as pl
from jax.experimental.pallas import tpu as pltpu
from jax.sharding import PartitionSpec as P

QUERY_HEADS = 64
KV_HEADS = 8
HEAD_DIM = 128


NEG_FILL = -1e30
RIM_ROWS = 16
LEAST_RETENTION = -40.0
VMEM_BYTES = 16 * 1024 * 1024


def convolve(widened, taps, lead, rows):
    summed = jnp.zeros((rows, widened.shape[1]), jnp.float32)
    for back in range(taps.shape[0]):
        summed = summed + taps[back : back + 1] * widened[lead - back : lead - back + rows]
    return summed.astype(jnp.bfloat16)


def own_project_kernel(rows_ref, taps_ref, gate_ref, out_ref, held_taps_ref, held_ref, widened):
    rows, features = rows_ref.shape
    held_taps_ref[...] = taps_ref[...].astype(jnp.float32)
    held_ref[:features] = gate_ref[...]
    tile = widened.shape[2]
    total = jnp.zeros(out_ref.shape, jnp.float32)
    for step in range(features // tile):
        columns = slice(step * tile, (step + 1) * tile)
        edges = features + step * 2 * RIM_ROWS
        held_ref[edges : edges + RIM_ROWS, :tile] = rows_ref[:RIM_ROWS, columns]
        held_ref[edges + RIM_ROWS : edges + 2 * RIM_ROWS, :tile] = rows_ref[
            rows - RIM_ROWS :, columns
        ]
        wide = widened.at[step % 2]
        wide[...] = rows_ref[:, columns].astype(jnp.float32)
        taps = taps_ref[:, columns].astype(jnp.float32)
        mixed = convolve(wide, taps, RIM_ROWS, rows - RIM_ROWS)
        total = total + jnp.dot(mixed, gate_ref[columns, :], preferred_element_type=jnp.float32)
    out_ref[...] = total


def peer_project_kernel(
    peer_ref, taps_ref, held_ref, near_ref, far_ref, widened, own_widened
):
    rows, features = peer_ref.shape
    tile = widened.shape[2]
    first = lax.axis_index("seq") == 0
    half = near_ref.shape[1]
    total = jnp.zeros((near_ref.shape[0], 2 * half), jnp.float32)
    for step in range(features // tile):
        columns = slice(step * tile, (step + 1) * tile)
        wide, own_wide = widened.at[step % 2], own_widened.at[step % 2]
        edges = held_ref.at[
            features + step * 2 * RIM_ROWS : features + (step + 1) * 2 * RIM_ROWS, :tile
        ]
        own_tail = edges[RIM_ROWS:].astype(jnp.float32)
        peer_tail = peer_ref[rows - RIM_ROWS :, columns].astype(jnp.float32)
        wide[:RIM_ROWS] = jnp.where(first, own_tail, 0.0)
        wide[RIM_ROWS:] = peer_ref[:, columns].astype(jnp.float32)
        own_wide[:RIM_ROWS] = jnp.where(first, 0.0, peer_tail)
        own_wide[RIM_ROWS:] = edges[:RIM_ROWS].astype(jnp.float32)
        taps = taps_ref[:, columns].astype(jnp.float32)
        mixed = jnp.concatenate(
            [
                convolve(own_wide, taps, RIM_ROWS, RIM_ROWS),
                convolve(wide, taps, RIM_ROWS, rows),
            ],
            axis=0,
        )
        total = total + jnp.dot(mixed, held_ref[columns, :], preferred_element_type=jnp.float32)
    near_ref[...] = total[:, :half]
    far_ref[...] = total[:, half:].astype(jnp.bfloat16)


def own_project(activations, conv_taps, gate_in):
    rows, features = activations.shape
    done = rows - RIM_ROWS
    tile = math.gcd(features, gate_in.shape[1])
    return pl.pallas_call(
        own_project_kernel,
        out_shape=(
            jax.ShapeDtypeStruct((done, gate_in.shape[1]), jnp.float32),
            jax.ShapeDtypeStruct(conv_taps.shape, jnp.float32),
            jax.ShapeDtypeStruct(
                (features + features // tile * 2 * RIM_ROWS, gate_in.shape[1]), gate_in.dtype
            ),
        ),
        scratch_shapes=[pltpu.VMEM((2, rows, tile), jnp.float32)],
        compiler_params=pltpu.CompilerParams(vmem_limit_bytes=VMEM_BYTES),
        cost_estimate=pl.CostEstimate(flops=1, bytes_accessed=1, transcendentals=0),
    )(activations, conv_taps, gate_in)


def peer_project(peer_rows, taps, held):
    rows, features = peer_rows.shape
    done = rows + RIM_ROWS
    tile = math.gcd(features, held.shape[1])
    half = held.shape[1] // 2
    return pl.pallas_call(
        peer_project_kernel,
        out_shape=(
            jax.ShapeDtypeStruct((done, half), jnp.float32),
            jax.ShapeDtypeStruct((done, half), jnp.bfloat16),
        ),
        scratch_shapes=[
            pltpu.VMEM((2, rows + RIM_ROWS, tile), jnp.float32),
            pltpu.VMEM((2, 2 * RIM_ROWS, tile), jnp.float32),
        ],
        compiler_params=pltpu.CompilerParams(vmem_limit_bytes=VMEM_BYTES),
        cost_estimate=pl.CostEstimate(flops=1, bytes_accessed=1, transcendentals=0),
    )(peer_rows, taps, held)


def head_sum(part):
    count = lax.axis_size("heads")
    step = 1
    received = None
    while step < count:
        if received is not None:
            part = part + received.astype(jnp.float32)
        received = exchange_heads(part if step == 1 else part.astype(jnp.bfloat16), step)
        step *= 2
    return part, received


def exchange_heads(block, step):
    count = lax.axis_size("heads")
    return lax.ppermute(block, "heads", [(i, i ^ step) for i in range(count)])


def in_one_piece(work, *given):
    shapes = jax.eval_shape(work, *given)
    return lax.cond(
        lax.axis_index("seq") >= 0,
        work,
        lambda *given: jax.tree.map(lambda like: jnp.zeros(like.shape, like.dtype), shapes),
        *given,
    )


def far_logits(block, gate_rows):
    step = lax.axis_size("heads") // 2
    received = exchange_heads(block, step)

    def nearer(block, received, gate_rows):
        distance = step
        while distance > 1:
            distance //= 2
            block = block.astype(jnp.float32) + received.astype(jnp.float32)
            received = exchange_heads(block, distance)
        return partial_logits(block, received, gate_rows)

    return in_one_piece(nearer, block, received, gate_rows)


def share_of_logits(pre_ref, in_ref, gate_rows):
    pre = pre_ref[...] + in_ref[...].astype(jnp.float32)
    hidden = (pre / (1.0 + jnp.exp(-pre))).astype(jnp.bfloat16)
    return lax.dot_general(
        gate_rows, hidden, (((0,), (1,)), ((), ())), preferred_element_type=jnp.float32
    )


def partial_logits_kernel(own_ref, in_ref, gate_out_ref, out_ref):
    out_ref[...] = share_of_logits(own_ref, in_ref, gate_out_ref[...])


def partial_logits(part, received, gate_rows):
    return pl.pallas_call(
        partial_logits_kernel,
        out_shape=jax.ShapeDtypeStruct((gate_rows.shape[1], part.shape[0]), jnp.float32),
        compiler_params=pltpu.CompilerParams(vmem_limit_bytes=VMEM_BYTES),
    )(part, received, gate_rows)


def logits_kernel(own_ref, far_share_ref, near_ref, near_in_ref, gate_out_ref, out_ref):
    first = lax.axis_index("seq") == 0
    share = share_of_logits(near_ref, near_in_ref, gate_out_ref[...]) + far_share_ref[...]
    own = jnp.concatenate([share[:, :RIM_ROWS], own_ref[...]], axis=1)
    peer = share[:, RIM_ROWS:]
    out_ref[0] = jnp.where(first, own, peer)
    out_ref[1] = jnp.where(first, peer, own)


def logits_share(own_share, far_share, near, near_in, gate_rows):
    rows = own_share.shape[1] + RIM_ROWS
    return pl.pallas_call(
        logits_kernel,
        out_shape=jax.ShapeDtypeStruct((2, gate_rows.shape[1], rows), jnp.float32),
        compiler_params=pltpu.CompilerParams(vmem_limit_bytes=VMEM_BYTES),
    )(own_share, far_share, near, near_in, gate_rows)


def hide_unseen(seq_rank, segments_ref, rows):
    own_segments = segments_ref[pl.ds(seq_rank, 1), :]
    behind_segments = segments_ref[pl.ds(0, 1), :]
    query_segments = jnp.transpose(jnp.broadcast_to(own_segments, (rows, rows)))
    query_at = lax.broadcasted_iota(jnp.int32, (rows, rows), 0)
    key_at = lax.broadcasted_iota(jnp.int32, (rows, rows), 1)
    see_own = (key_at <= query_at) & (query_segments == own_segments)
    see_behind = (query_segments == behind_segments) & (seq_rank > 0)
    return jnp.where(jnp.concatenate([see_behind, see_own], axis=1), 0.0, NEG_FILL)


def head_columns(number):
    return slice(number * HEAD_DIM, (number + 1) * HEAD_DIM)


def scores_of(queries_ref, keys, offset, head):
    scores = lax.dot_general(
        queries_ref[:, head_columns(head)],
        keys,
        (((1,), (1,)), ((), ())),
        preferred_element_type=jnp.float32,
    )
    return scores * (1.0 / math.sqrt(HEAD_DIM)) + offset


def with_behind(ref, behind_ref, number, whole):
    own = ref[:, head_columns(number)]
    if not whole:
        return own
    return jnp.concatenate([behind_ref[:, head_columns(number)], own], axis=0)


def powers_kernel(segments_ref, queries_ref, keys_ref, behind_keys_ref, powers_ref):
    seq_rank = lax.axis_index("seq")
    rows = queries_ref.shape[0]
    kv_local = keys_ref.shape[1] // HEAD_DIM
    group_size = queries_ref.shape[1] // keys_ref.shape[1]
    hide = hide_unseen(seq_rank, segments_ref, rows)

    def fill(whole):
        start = 0 if whole else rows
        for head in range(kv_local * group_size):
            g = head // group_size
            keys = with_behind(keys_ref, behind_keys_ref, g, whole)
            scores = scores_of(queries_ref, keys, hide[:, start:], head)
            powers_ref[head, :, start:] = jnp.exp(
                scores - jnp.max(scores, axis=1, keepdims=True)
            )

    pl.when(seq_rank > 0)(lambda: fill(True))
    pl.when(seq_rank == 0)(lambda: fill(False))


def powers_of(segments, queries, keys, behind_keys):
    rows = queries.shape[0]
    heads = queries.shape[1] // HEAD_DIM
    return pl.pallas_call(
        powers_kernel,
        out_shape=jax.ShapeDtypeStruct((heads, rows, 2 * rows), jnp.float32),
        compiler_params=pltpu.CompilerParams(vmem_limit_bytes=VMEM_BYTES),
        cost_estimate=pl.CostEstimate(
            flops=4 * rows * rows * queries.shape[1],
            bytes_accessed=8 * heads * rows * rows,
            transcendentals=2 * heads * rows * rows,
        ),
    )(segments, queries, keys, behind_keys)


def weights_kernel(
    share_ref,
    peer_share_ref,
    powers_ref,
    segments_ref,
    queries_ref,
    keys_ref,
    behind_keys_ref,
    weights_ref,
    own_mass_ref,
    behind_mass_ref,
    retention,
):
    seq_rank, head_rank = lax.axis_index("seq"), lax.axis_index("heads")
    rows = queries_ref.shape[0]
    kv_local = keys_ref.shape[1] // HEAD_DIM
    group_size = queries_ref.shape[1] // keys_ref.shape[1]
    logits = share_ref[...] + peer_share_ref[...]
    log_gate = jnp.minimum(logits, 0.0) - jnp.log1p(jnp.exp(-jnp.abs(logits)))
    retention[...] = log_gate.astype(jnp.bfloat16).astype(jnp.float32)
    biases = []
    for g in range(kv_local):
        at = pl.ds(head_rank * kv_local + g, 1)
        biases.append(jnp.concatenate([retention[0, at, :], retention[seq_rank, at, :]], axis=1))
    moderate = jnp.min(functools.reduce(jnp.minimum, biases)) >= LEAST_RETENTION

    def finish(whole, terms_of):
        start = 0 if whole else rows
        for g in range(kv_local):
            mass = jnp.zeros((1, 2 * rows - start), jnp.float32)
            group_terms = terms_of(g, whole, start)
            for head in range(g * group_size, (g + 1) * group_size):
                weights = group_terms(head)
                weights = weights * (1.0 / jnp.sum(weights, axis=1, keepdims=True))
                mass = mass + jnp.sum(weights, axis=0, keepdims=True)
                weights_ref[head, :, start:] = weights.astype(jnp.bfloat16)
            mass = mass / group_size
            own_mass_ref[g : g + 1, :] = mass[:, rows - start :]
            behind_mass_ref[g : g + 1, :] = mass[:, :rows] if whole else jnp.zeros((1, rows))

    def by_powers(g, whole, start):
        factor = jnp.exp(biases[g] - jnp.max(biases[g]))[:, start:]
        return lambda head: powers_ref[head, :, start:] * factor

    def by_scores(g, whole, start):
        offset = hide_unseen(seq_rank, segments_ref, rows) + biases[g]
        keys = with_behind(keys_ref, behind_keys_ref, g, whole)

        def terms(head):
            scores = scores_of(queries_ref, keys, offset[:, start:], head)
            return jnp.exp(scores - jnp.max(scores, axis=1, keepdims=True))

        return terms

    pl.when(moderate & (seq_rank > 0))(lambda: finish(True, by_powers))
    pl.when(moderate & (seq_rank == 0))(lambda: finish(False, by_powers))
    pl.when(jnp.logical_not(moderate))(lambda: finish(True, by_scores))


def weights_of(share, peer_share, powers, segments, queries, keys, behind_keys):
    rows = queries.shape[0]
    mass = jax.ShapeDtypeStruct((keys.shape[1] // HEAD_DIM, rows), jnp.float32)
    return pl.pallas_call(
        weights_kernel,
        out_shape=(jax.ShapeDtypeStruct(powers.shape, jnp.bfloat16), mass, mass),
        scratch_shapes=[pltpu.VMEM(share.shape, jnp.float32)],
        compiler_params=pltpu.CompilerParams(vmem_limit_bytes=VMEM_BYTES),
    )(share, peer_share, powers, segments, queries, keys, behind_keys)


def attend_kernel(weights_ref, values_ref, behind_values_ref, attended_ref):
    seq_rank = lax.axis_index("seq")
    heads, rows = weights_ref.shape[:2]
    group_size = attended_ref.shape[1] // values_ref.shape[1]

    def fill(whole):
        start = 0 if whole else rows
        for head in range(heads):
            values = with_behind(values_ref, behind_values_ref, head // group_size, whole)
            attended_ref[:, head_columns(head)] = jnp.dot(
                weights_ref[head, :, start:], values, preferred_element_type=jnp.float32
            ).astype(jnp.bfloat16)

    pl.when(seq_rank > 0)(lambda: fill(True))
    pl.when(seq_rank == 0)(lambda: fill(False))


def attend(weights, values, behind_values):
    heads, rows = weights.shape[:2]
    return pl.pallas_call(
        attend_kernel,
        out_shape=jax.ShapeDtypeStruct((rows, heads * HEAD_DIM), jnp.bfloat16),
        compiler_params=pltpu.CompilerParams(vmem_limit_bytes=VMEM_BYTES),
        cost_estimate=pl.CostEstimate(
            flops=4 * rows * rows * heads * HEAD_DIM,
            bytes_accessed=2 * (weights.size + rows * heads * HEAD_DIM),
            transcendentals=0,
        ),
    )(weights, values, behind_values)


def pair_device(
    activations, conv_taps, gate_in, gate_out, queries, key_vectors, value_vectors, segment_ids
):
    rows = activations.shape[0]
    swap = [(0, 1), (1, 0)]
    seq_rank = lax.axis_index("seq")
    segments = segment_ids.reshape(2, rows)
    hidden_local = gate_in.shape[1]
    gate_rows = lax.dynamic_slice_in_dim(gate_out, seq_rank * hidden_local, hidden_local, 0)

    peer_rows = lax.ppermute(activations, "seq", swap)

    def own_work(activations, conv_taps, gate_in, gate_rows):
        part, *held = own_project(activations, conv_taps, gate_in)
        return partial_logits(*head_sum(part), gate_rows), held

    own_share, held = in_one_piece(own_work, activations, conv_taps, gate_in, gate_rows)
    peer_rows, own_share, held = lax.optimization_barrier((peer_rows, own_share, held))
    near, far = peer_project(peer_rows, *held)
    behind_keys = lax.ppermute(key_vectors, "seq", swap)
    behind_values = lax.ppermute(value_vectors, "seq", swap)
    half = near.shape[1]
    near, near_in = head_sum(near)
    far_share = far_logits(far, gate_rows[half:])
    share = logits_share(own_share, far_share, near, near_in, gate_rows[:half])
    share, queries = lax.optimization_barrier((share, queries))
    powers = powers_of(segments, queries, key_vectors, behind_keys)
    weights, own_mass, behind_mass = weights_of(
        share,
        lax.ppermute(share, "seq", swap),
        powers,
        segments,
        queries,
        key_vectors,
        behind_keys,
    )
    attended = attend(weights, value_vectors, behind_values)
    key_mass = own_mass + lax.ppermute(behind_mass, "seq", swap)
    return (attended, key_mass.astype(jnp.bfloat16))


def from_behind(block, axis, distance):
    devices = range(lax.axis_size(axis))
    route = [(i - distance, i) for i in devices if i - distance in devices]
    return lax.ppermute(block, axis, route)


def block_scores(query_heads, key_block, bias_block, allowed, score_scale):
    scores = (
        jnp.einsum("tgeh,kgh->getk", query_heads, key_block, preferred_element_type=jnp.float32)
        * score_scale
    )
    scores = scores + jnp.transpose(bias_block.astype(jnp.float32))[:, None, None, :]
    return jnp.where(allowed[None, None], scores, NEG_FILL)


def ring_device(
    activations, conv_taps, gate_in, gate_out, queries, key_vectors, value_vectors, segment_ids
):
    shard_rows = activations.shape[0]
    tap_count = conv_taps.shape[0]
    rim_rows = from_behind(activations[shard_rows - (tap_count - 1) :], "seq", 1)
    widened = jnp.concatenate([rim_rows, activations], 0).astype(jnp.float32)
    summed = jnp.zeros(activations.shape, jnp.float32)
    for shift_back in range(tap_count):
        start_row = tap_count - 1 - shift_back
        summed = (
            summed
            + conv_taps[shift_back].astype(jnp.float32)
            * widened[start_row : start_row + shard_rows]
        )
    mixed_rows = summed.astype(jnp.bfloat16)
    partial_hidden = jnp.dot(
        mixed_rows,
        lax.all_gather(gate_in, "seq", axis=1, tiled=True),
        preferred_element_type=jnp.float32,
    )
    kv_local = key_vectors.shape[1] // HEAD_DIM
    group_size = QUERY_HEADS // KV_HEADS
    head_rank = lax.axis_index("heads")
    hidden = jax.nn.silu(lax.psum(partial_hidden, "heads")).astype(jnp.bfloat16)
    logits = jnp.dot(hidden, gate_out, preferred_element_type=jnp.float32)
    retention = lax.dynamic_slice_in_dim(
        jax.nn.log_sigmoid(logits).astype(jnp.bfloat16), head_rank * kv_local, kv_local, 1
    )
    seq_rank = lax.axis_index("seq")
    local_index = jnp.arange(shard_rows, dtype=jnp.int32)
    own_queries, own_keys, own_values, own_bias = (queries, key_vectors, value_vectors, retention)
    query_places = seq_rank * shard_rows + local_index
    query_segments = jnp.take(segment_ids, query_places)
    query_heads = own_queries.reshape(shard_rows, kv_local, group_size, HEAD_DIM)
    score_scale = 1.0 / math.sqrt(HEAD_DIM)

    def visibility(flat_index):
        key_segments = jnp.take(segment_ids, flat_index)
        return (flat_index[None, :] <= query_places[:, None]) & (
            key_segments[None, :] == query_segments[:, None]
        )

    initial = (
        jnp.full((kv_local, group_size, shard_rows), NEG_FILL, jnp.float32),
        jnp.zeros((kv_local, group_size, shard_rows), jnp.float32),
    )
    all_keys, all_values, all_bias = (
        lax.all_gather(own_keys, "seq", axis=0, tiled=True),
        lax.all_gather(own_values, "seq", axis=0, tiled=True),
        lax.all_gather(own_bias, "seq", axis=0, tiled=True),
    )
    piece_rows = all_keys.shape[0]
    stats_block_width = math.gcd(piece_rows, 512)

    def one_block(block_number, state_in):
        offset = block_number * stats_block_width
        key_block = lax.dynamic_slice_in_dim(all_keys, offset, stats_block_width, 0).reshape(
            stats_block_width, kv_local, HEAD_DIM
        )
        bias_block = lax.dynamic_slice_in_dim(all_bias, offset, stats_block_width, 0)
        allowed = visibility(0 + offset + jnp.arange(stats_block_width, dtype=jnp.int32))

        def update(state_old):
            peak_old, mass_old = state_old
            masked = block_scores(query_heads, key_block, bias_block, allowed, score_scale)
            peak_new = jnp.maximum(peak_old, jnp.max(masked, axis=3))
            exponent = jnp.where(allowed[None, None], jnp.exp(masked - peak_new[..., None]), 0.0)
            return (peak_new, mass_old * jnp.exp(peak_old - peak_new) + jnp.sum(exponent, axis=3))

        def keep_state(state_old):
            return state_old

        return lax.cond(jnp.any(allowed), update, keep_state, state_in)

    row_peak, total_mass = lax.fori_loop(0, piece_rows // stats_block_width, one_block, initial)
    total_keys = all_keys.shape[0]
    block_width = math.gcd(total_keys, 512)
    block_count = total_keys // block_width
    key_blocks = all_keys.reshape(block_count, block_width, kv_local, HEAD_DIM)
    value_blocks = all_values.reshape(block_count, block_width, kv_local, HEAD_DIM)
    bias_blocks = all_bias.reshape(block_count, block_width, kv_local)

    def second_pass(accumulated, block_items):
        block_number, key_block, value_block, bias_block = block_items
        allowed = visibility(block_number * block_width + jnp.arange(block_width, dtype=jnp.int32))

        def attend(accum_in):
            masked = block_scores(query_heads, key_block, bias_block, allowed, score_scale)
            weights = (
                jnp.where(allowed[None, None], jnp.exp(masked - row_peak[..., None]), 0.0)
                / total_mass[..., None]
            )
            accum_out = accum_in + jnp.einsum(
                "getk,kgh->tgeh",
                weights.astype(jnp.bfloat16),
                value_block,
                preferred_element_type=jnp.float32,
            )
            return (accum_out, jnp.transpose(jnp.sum(weights, axis=(1, 2))) / group_size)

        def skip_block(accum_in):
            return (accum_in, jnp.zeros((block_width, kv_local), jnp.float32))

        return lax.cond(jnp.any(allowed), attend, skip_block, accumulated)

    accumulated, mass_blocks = lax.scan(
        second_pass,
        jnp.zeros((shard_rows, kv_local, group_size, HEAD_DIM), jnp.float32),
        (jnp.arange(block_count, dtype=jnp.int32), key_blocks, value_blocks, bias_blocks),
    )
    key_term = mass_blocks.reshape(total_keys, kv_local)
    key_mass = lax.psum_scatter(key_term, "seq", scatter_dimension=0, tiled=True).astype(
        jnp.bfloat16
    )
    attended = accumulated.reshape(shard_rows, kv_local * group_size * HEAD_DIM).astype(
        jnp.bfloat16
    )
    return (attended, jnp.transpose(key_mass))


def solution(mesh):
    return jax.shard_map(
        pair_device if mesh.shape["seq"] == 2 else ring_device,
        mesh=mesh,
        in_specs=(
            P(("dp", "seq"), "heads"),
            P(None, "heads"),
            P("heads", "seq"),
            P(),
            P(("dp", "seq"), "heads"),
            P(("dp", "seq"), "heads"),
            P(("dp", "seq"), "heads"),
            P("dp"),
        ),
        out_specs=(P(("dp", "seq"), "heads"), P("heads", ("dp", "seq"))),
        check_vma=False,
    )
```

```python
import functools
import math

import jax
import jax.numpy as jnp
from jax import lax
from jax.experimental import pallas as pl
from jax.experimental.pallas import tpu as pltpu
from jax.sharding import PartitionSpec as P

QUERY_HEADS = 64
KV_HEADS = 8
HEAD_DIM = 128


NEG_FILL = -1e30
RIM_ROWS = 16
LEAST_RETENTION = -40.0
VMEM_BYTES = 16 * 1024 * 1024


def convolve(widened, taps, lead, rows):
    summed = jnp.zeros((rows, widened.shape[1]), jnp.float32)
    for back in range(taps.shape[0]):
        summed = summed + taps[back : back + 1] * widened[lead - back : lead - back + rows]
    return summed.astype(jnp.bfloat16)


def own_project_kernel(rows_ref, taps_ref, gate_ref, out_ref, held_taps_ref, held_ref, widened):
    rows, features = rows_ref.shape
    held_taps_ref[...] = taps_ref[...].astype(jnp.float32)
    held_ref[:features] = gate_ref[...]
    tile = widened.shape[2]
    total = jnp.zeros(out_ref.shape, jnp.float32)
    for step in range(features // tile):
        columns = slice(step * tile, (step + 1) * tile)
        edges = features + step * 2 * RIM_ROWS
        held_ref[edges : edges + RIM_ROWS, :tile] = rows_ref[:RIM_ROWS, columns]
        held_ref[edges + RIM_ROWS : edges + 2 * RIM_ROWS, :tile] = rows_ref[
            rows - RIM_ROWS :, columns
        ]
        wide = widened.at[step % 2]
        wide[...] = rows_ref[:, columns].astype(jnp.float32)
        taps = taps_ref[:, columns].astype(jnp.float32)
        mixed = convolve(wide, taps, RIM_ROWS, rows - RIM_ROWS)
        total = total + jnp.dot(mixed, gate_ref[columns, :], preferred_element_type=jnp.float32)
    out_ref[...] = total


def peer_project_kernel(
    upper_ref, lower_ref, taps_ref, held_ref, near_ref, far_ref, widened, own_widened
):
    middle, features = upper_ref.shape
    rows = middle + lower_ref.shape[0]
    tile = widened.shape[2]
    first = lax.axis_index("seq") == 0
    half = near_ref.shape[1]
    total = jnp.zeros((near_ref.shape[0], 2 * half), jnp.float32)
    for step in range(features // tile):
        columns = slice(step * tile, (step + 1) * tile)
        wide, own_wide = widened.at[step % 2], own_widened.at[step % 2]
        edges = held_ref.at[
            features + step * 2 * RIM_ROWS : features + (step + 1) * 2 * RIM_ROWS, :tile
        ]
        own_tail = edges[RIM_ROWS:].astype(jnp.float32)
        peer_tail = lower_ref[rows - middle - RIM_ROWS :, columns].astype(jnp.float32)
        wide[:RIM_ROWS] = jnp.where(first, own_tail, 0.0)
        wide[RIM_ROWS : RIM_ROWS + middle] = upper_ref[:, columns].astype(jnp.float32)
        wide[RIM_ROWS + middle :] = lower_ref[:, columns].astype(jnp.float32)
        own_wide[:RIM_ROWS] = jnp.where(first, 0.0, peer_tail)
        own_wide[RIM_ROWS:] = edges[:RIM_ROWS].astype(jnp.float32)
        taps = taps_ref[:, columns].astype(jnp.float32)
        mixed = jnp.concatenate(
            [
                convolve(own_wide, taps, RIM_ROWS, RIM_ROWS),
                convolve(wide, taps, RIM_ROWS, rows),
            ],
            axis=0,
        )
        total = total + jnp.dot(mixed, held_ref[columns, :], preferred_element_type=jnp.float32)
    near_ref[...] = total[:, :half]
    far_ref[...] = total[:, half:].astype(jnp.bfloat16)


def own_project(activations, conv_taps, gate_in):
    rows, features = activations.shape
    done = rows - RIM_ROWS
    tile = math.gcd(features, gate_in.shape[1])
    return pl.pallas_call(
        own_project_kernel,
        out_shape=(
            jax.ShapeDtypeStruct((done, gate_in.shape[1]), jnp.float32),
            jax.ShapeDtypeStruct(conv_taps.shape, jnp.float32),
            jax.ShapeDtypeStruct(
                (features + features // tile * 2 * RIM_ROWS, gate_in.shape[1]), gate_in.dtype
            ),
        ),
        scratch_shapes=[pltpu.VMEM((2, rows, tile), jnp.float32)],
        compiler_params=pltpu.CompilerParams(vmem_limit_bytes=VMEM_BYTES),
        cost_estimate=pl.CostEstimate(flops=1, bytes_accessed=1, transcendentals=0),
    )(activations, conv_taps, gate_in)


def peer_project(upper, lower, taps, held):
    rows, features = upper.shape[0] + lower.shape[0], upper.shape[1]
    done = rows + RIM_ROWS
    tile = math.gcd(features, held.shape[1])
    half = held.shape[1] // 2
    return pl.pallas_call(
        peer_project_kernel,
        out_shape=(
            jax.ShapeDtypeStruct((done, half), jnp.float32),
            jax.ShapeDtypeStruct((done, half), jnp.bfloat16),
        ),
        scratch_shapes=[
            pltpu.VMEM((2, rows + RIM_ROWS, tile), jnp.float32),
            pltpu.VMEM((2, 2 * RIM_ROWS, tile), jnp.float32),
        ],
        compiler_params=pltpu.CompilerParams(vmem_limit_bytes=VMEM_BYTES),
        cost_estimate=pl.CostEstimate(flops=1, bytes_accessed=1, transcendentals=0),
    )(upper, lower, taps, held)


def head_sum(part):
    count = lax.axis_size("heads")
    step = 1
    received = None
    while step < count:
        if received is not None:
            part = part + received.astype(jnp.float32)
        received = exchange_heads(part if step == 1 else part.astype(jnp.bfloat16), step)
        step *= 2
    return part, received


def exchange_heads(block, step):
    count = lax.axis_size("heads")
    return lax.ppermute(block, "heads", [(i, i ^ step) for i in range(count)])


def in_one_piece(work, *given):
    shapes = jax.eval_shape(work, *given)
    return lax.cond(
        lax.axis_index("seq") >= 0,
        work,
        lambda *given: jax.tree.map(lambda like: jnp.zeros(like.shape, like.dtype), shapes),
        *given,
    )


def far_logits(block, gate_out):
    step = lax.axis_size("heads") // 2
    received = exchange_heads(block, step)

    def nearer(block, received, gate_out):
        distance = step
        while distance > 1:
            distance //= 2
            block = block.astype(jnp.float32) + received.astype(jnp.float32)
            received = exchange_heads(block, distance)
        return partial_logits(block, received, gate_out, block.shape[1])

    return in_one_piece(nearer, block, received, gate_out)


def share_of_logits(pre_ref, in_ref, gate_out_ref, offset):
    pre = pre_ref[...] + in_ref[...].astype(jnp.float32)
    hidden = (pre / (1.0 + jnp.exp(-pre))).astype(jnp.bfloat16)
    share = gate_out_ref.shape[1] // lax.axis_size("seq")
    start = pl.multiple_of(lax.axis_index("seq") * share + offset, HEAD_DIM)
    gate_columns = gate_out_ref[:, pl.ds(start, pre.shape[1])]
    return lax.dot_general(
        gate_columns, hidden, (((1,), (1,)), ((), ())), preferred_element_type=jnp.float32
    )


def partial_logits_kernel(offset, own_ref, in_ref, gate_out_ref, out_ref):
    out_ref[...] = share_of_logits(own_ref, in_ref, gate_out_ref, offset)


def partial_logits(part, received, gate_out, offset):
    return pl.pallas_call(
        functools.partial(partial_logits_kernel, offset),
        out_shape=jax.ShapeDtypeStruct((gate_out.shape[0], part.shape[0]), jnp.float32),
        compiler_params=pltpu.CompilerParams(vmem_limit_bytes=VMEM_BYTES),
    )(part, received, gate_out)


def logits_kernel(own_ref, far_share_ref, near_ref, near_in_ref, gate_out_ref, out_ref):
    first = lax.axis_index("seq") == 0
    share = share_of_logits(near_ref, near_in_ref, gate_out_ref, 0) + far_share_ref[...]
    own = jnp.concatenate([share[:, :RIM_ROWS], own_ref[...]], axis=1)
    peer = share[:, RIM_ROWS:]
    out_ref[0] = jnp.where(first, own, peer)
    out_ref[1] = jnp.where(first, peer, own)


def logits_share(own_share, far_share, near, near_in, gate_out):
    rows = own_share.shape[1] + RIM_ROWS
    return pl.pallas_call(
        logits_kernel,
        out_shape=jax.ShapeDtypeStruct((2, gate_out.shape[0], rows), jnp.float32),
        compiler_params=pltpu.CompilerParams(vmem_limit_bytes=VMEM_BYTES),
    )(own_share, far_share, near, near_in, gate_out)


def hide_unseen(seq_rank, segments_ref, rows):
    own_segments = segments_ref[pl.ds(seq_rank, 1), :]
    behind_segments = segments_ref[pl.ds(0, 1), :]
    query_segments = jnp.transpose(jnp.broadcast_to(own_segments, (rows, rows)))
    query_at = lax.broadcasted_iota(jnp.int32, (rows, rows), 0)
    key_at = lax.broadcasted_iota(jnp.int32, (rows, rows), 1)
    see_own = (key_at <= query_at) & (query_segments == own_segments)
    see_behind = (query_segments == behind_segments) & (seq_rank > 0)
    return jnp.where(jnp.concatenate([see_behind, see_own], axis=1), 0.0, NEG_FILL)


def head_columns(number):
    return slice(number * HEAD_DIM, (number + 1) * HEAD_DIM)


def scores_of(queries_ref, keys, offset, head):
    scores = lax.dot_general(
        queries_ref[:, head_columns(head)],
        keys,
        (((1,), (1,)), ((), ())),
        preferred_element_type=jnp.float32,
    )
    return scores * (1.0 / math.sqrt(HEAD_DIM)) + offset


def with_behind(ref, behind_ref, number, whole):
    own = ref[:, head_columns(number)]
    if not whole:
        return own
    return jnp.concatenate([behind_ref[:, head_columns(number)], own], axis=0)


def powers_kernel(segments_ref, queries_ref, keys_ref, behind_keys_ref, powers_ref):
    seq_rank = lax.axis_index("seq")
    rows = queries_ref.shape[0]
    kv_local = keys_ref.shape[1] // HEAD_DIM
    group_size = queries_ref.shape[1] // keys_ref.shape[1]
    hide = hide_unseen(seq_rank, segments_ref, rows)

    def fill(whole):
        start = 0 if whole else rows
        for head in range(kv_local * group_size):
            g = head // group_size
            keys = with_behind(keys_ref, behind_keys_ref, g, whole)
            scores = scores_of(queries_ref, keys, hide[:, start:], head)
            powers_ref[head, :, start:] = jnp.exp(
                scores - jnp.max(scores, axis=1, keepdims=True)
            )

    pl.when(seq_rank > 0)(lambda: fill(True))
    pl.when(seq_rank == 0)(lambda: fill(False))


def powers_of(segments, queries, keys, behind_keys):
    rows = queries.shape[0]
    heads = queries.shape[1] // HEAD_DIM
    return pl.pallas_call(
        powers_kernel,
        out_shape=jax.ShapeDtypeStruct((heads, rows, 2 * rows), jnp.float32),
        compiler_params=pltpu.CompilerParams(vmem_limit_bytes=VMEM_BYTES),
        cost_estimate=pl.CostEstimate(
            flops=4 * rows * rows * queries.shape[1],
            bytes_accessed=8 * heads * rows * rows,
            transcendentals=2 * heads * rows * rows,
        ),
    )(segments, queries, keys, behind_keys)


def weights_kernel(
    share_ref,
    peer_share_ref,
    powers_ref,
    segments_ref,
    queries_ref,
    keys_ref,
    behind_keys_ref,
    weights_ref,
    own_mass_ref,
    behind_mass_ref,
    retention,
):
    seq_rank, head_rank = lax.axis_index("seq"), lax.axis_index("heads")
    rows = queries_ref.shape[0]
    kv_local = keys_ref.shape[1] // HEAD_DIM
    group_size = queries_ref.shape[1] // keys_ref.shape[1]
    logits = share_ref[...] + peer_share_ref[...]
    log_gate = jnp.minimum(logits, 0.0) - jnp.log1p(jnp.exp(-jnp.abs(logits)))
    retention[...] = log_gate.astype(jnp.bfloat16).astype(jnp.float32)
    biases = []
    for g in range(kv_local):
        at = pl.ds(head_rank * kv_local + g, 1)
        biases.append(jnp.concatenate([retention[0, at, :], retention[seq_rank, at, :]], axis=1))
    moderate = jnp.min(functools.reduce(jnp.minimum, biases)) >= LEAST_RETENTION

    def finish(whole, terms_of):
        start = 0 if whole else rows
        for g in range(kv_local):
            mass = jnp.zeros((1, 2 * rows - start), jnp.float32)
            group_terms = terms_of(g, whole, start)
            for head in range(g * group_size, (g + 1) * group_size):
                weights = group_terms(head)
                weights = weights * (1.0 / jnp.sum(weights, axis=1, keepdims=True))
                mass = mass + jnp.sum(weights, axis=0, keepdims=True)
                weights_ref[head, :, start:] = weights.astype(jnp.bfloat16)
            mass = mass / group_size
            own_mass_ref[g : g + 1, :] = mass[:, rows - start :]
            behind_mass_ref[g : g + 1, :] = mass[:, :rows] if whole else jnp.zeros((1, rows))

    def by_powers(g, whole, start):
        factor = jnp.exp(biases[g] - jnp.max(biases[g]))[:, start:]
        return lambda head: powers_ref[head, :, start:] * factor

    def by_scores(g, whole, start):
        offset = hide_unseen(seq_rank, segments_ref, rows) + biases[g]
        keys = with_behind(keys_ref, behind_keys_ref, g, whole)

        def terms(head):
            scores = scores_of(queries_ref, keys, offset[:, start:], head)
            return jnp.exp(scores - jnp.max(scores, axis=1, keepdims=True))

        return terms

    pl.when(moderate & (seq_rank > 0))(lambda: finish(True, by_powers))
    pl.when(moderate & (seq_rank == 0))(lambda: finish(False, by_powers))
    pl.when(jnp.logical_not(moderate))(lambda: finish(True, by_scores))


def weights_of(share, peer_share, powers, segments, queries, keys, behind_keys):
    rows = queries.shape[0]
    mass = jax.ShapeDtypeStruct((keys.shape[1] // HEAD_DIM, rows), jnp.float32)
    return pl.pallas_call(
        weights_kernel,
        out_shape=(jax.ShapeDtypeStruct(powers.shape, jnp.bfloat16), mass, mass),
        scratch_shapes=[pltpu.VMEM(share.shape, jnp.float32)],
        compiler_params=pltpu.CompilerParams(vmem_limit_bytes=VMEM_BYTES),
    )(share, peer_share, powers, segments, queries, keys, behind_keys)


def attend_kernel(weights_ref, values_ref, behind_values_ref, attended_ref):
    seq_rank = lax.axis_index("seq")
    heads, rows = weights_ref.shape[:2]
    group_size = attended_ref.shape[1] // values_ref.shape[1]

    def fill(whole):
        start = 0 if whole else rows
        for head in range(heads):
            values = with_behind(values_ref, behind_values_ref, head // group_size, whole)
            attended_ref[:, head_columns(head)] = jnp.dot(
                weights_ref[head, :, start:], values, preferred_element_type=jnp.float32
            ).astype(jnp.bfloat16)

    pl.when(seq_rank > 0)(lambda: fill(True))
    pl.when(seq_rank == 0)(lambda: fill(False))


def attend(weights, values, behind_values):
    heads, rows = weights.shape[:2]
    return pl.pallas_call(
        attend_kernel,
        out_shape=jax.ShapeDtypeStruct((rows, heads * HEAD_DIM), jnp.bfloat16),
        compiler_params=pltpu.CompilerParams(vmem_limit_bytes=VMEM_BYTES),
        cost_estimate=pl.CostEstimate(
            flops=4 * rows * rows * heads * HEAD_DIM,
            bytes_accessed=2 * (weights.size + rows * heads * HEAD_DIM),
            transcendentals=0,
        ),
    )(weights, values, behind_values)


def pair_device(
    activations, conv_taps, gate_in, gate_out, queries, key_vectors, value_vectors, segment_ids
):
    rows = activations.shape[0]
    swap = [(0, 1), (1, 0)]
    segments = segment_ids.reshape(2, rows)
    gate_out = jnp.transpose(gate_out)

    middle = rows // 2
    peer_rows = [
        lax.ppermute(block, "seq", swap) for block in (activations[:middle], activations[middle:])
    ]

    def own_work(activations, conv_taps, gate_in, gate_out):
        part, *held = own_project(activations, conv_taps, gate_in)
        return partial_logits(*head_sum(part), gate_out, 0), held

    own_share, held = in_one_piece(own_work, activations, conv_taps, gate_in, gate_out)
    peer_rows, own_share, held = lax.optimization_barrier((peer_rows, own_share, held))
    near, far = peer_project(*peer_rows, *held)
    behind_keys = lax.ppermute(key_vectors, "seq", swap)
    behind_values = lax.ppermute(value_vectors, "seq", swap)
    near, near_in = head_sum(near)
    far_share = far_logits(far, gate_out)
    share = logits_share(own_share, far_share, near, near_in, gate_out)
    share, queries = lax.optimization_barrier((share, queries))
    powers = powers_of(segments, queries, key_vectors, behind_keys)
    weights, own_mass, behind_mass = weights_of(
        share,
        lax.ppermute(share, "seq", swap),
        powers,
        segments,
        queries,
        key_vectors,
        behind_keys,
    )
    attended = attend(weights, value_vectors, behind_values)
    key_mass = own_mass + lax.ppermute(behind_mass, "seq", swap)
    return (attended, key_mass.astype(jnp.bfloat16))


def from_behind(block, axis, distance):
    devices = range(lax.axis_size(axis))
    route = [(i - distance, i) for i in devices if i - distance in devices]
    return lax.ppermute(block, axis, route)


def block_scores(query_heads, key_block, bias_block, allowed, score_scale):
    scores = (
        jnp.einsum("tgeh,kgh->getk", query_heads, key_block, preferred_element_type=jnp.float32)
        * score_scale
    )
    scores = scores + jnp.transpose(bias_block.astype(jnp.float32))[:, None, None, :]
    return jnp.where(allowed[None, None], scores, NEG_FILL)


def ring_device(
    activations, conv_taps, gate_in, gate_out, queries, key_vectors, value_vectors, segment_ids
):
    shard_rows = activations.shape[0]
    tap_count = conv_taps.shape[0]
    rim_rows = from_behind(activations[shard_rows - (tap_count - 1) :], "seq", 1)
    widened = jnp.concatenate([rim_rows, activations], 0).astype(jnp.float32)
    summed = jnp.zeros(activations.shape, jnp.float32)
    for shift_back in range(tap_count):
        start_row = tap_count - 1 - shift_back
        summed = (
            summed
            + conv_taps[shift_back].astype(jnp.float32)
            * widened[start_row : start_row + shard_rows]
        )
    mixed_rows = summed.astype(jnp.bfloat16)
    partial_hidden = jnp.dot(
        mixed_rows,
        lax.all_gather(gate_in, "seq", axis=1, tiled=True),
        preferred_element_type=jnp.float32,
    )
    kv_local = key_vectors.shape[1] // HEAD_DIM
    group_size = QUERY_HEADS // KV_HEADS
    head_rank = lax.axis_index("heads")
    hidden = jax.nn.silu(lax.psum(partial_hidden, "heads")).astype(jnp.bfloat16)
    logits = jnp.dot(hidden, gate_out, preferred_element_type=jnp.float32)
    retention = lax.dynamic_slice_in_dim(
        jax.nn.log_sigmoid(logits).astype(jnp.bfloat16), head_rank * kv_local, kv_local, 1
    )
    seq_rank = lax.axis_index("seq")
    local_index = jnp.arange(shard_rows, dtype=jnp.int32)
    own_queries, own_keys, own_values, own_bias = (queries, key_vectors, value_vectors, retention)
    query_places = seq_rank * shard_rows + local_index
    query_segments = jnp.take(segment_ids, query_places)
    query_heads = own_queries.reshape(shard_rows, kv_local, group_size, HEAD_DIM)
    score_scale = 1.0 / math.sqrt(HEAD_DIM)

    def visibility(flat_index):
        key_segments = jnp.take(segment_ids, flat_index)
        return (flat_index[None, :] <= query_places[:, None]) & (
            key_segments[None, :] == query_segments[:, None]
        )

    initial = (
        jnp.full((kv_local, group_size, shard_rows), NEG_FILL, jnp.float32),
        jnp.zeros((kv_local, group_size, shard_rows), jnp.float32),
    )
    all_keys, all_values, all_bias = (
        lax.all_gather(own_keys, "seq", axis=0, tiled=True),
        lax.all_gather(own_values, "seq", axis=0, tiled=True),
        lax.all_gather(own_bias, "seq", axis=0, tiled=True),
    )
    piece_rows = all_keys.shape[0]
    stats_block_width = math.gcd(piece_rows, 512)

    def one_block(block_number, state_in):
        offset = block_number * stats_block_width
        key_block = lax.dynamic_slice_in_dim(all_keys, offset, stats_block_width, 0).reshape(
            stats_block_width, kv_local, HEAD_DIM
        )
        bias_block = lax.dynamic_slice_in_dim(all_bias, offset, stats_block_width, 0)
        allowed = visibility(0 + offset + jnp.arange(stats_block_width, dtype=jnp.int32))

        def update(state_old):
            peak_old, mass_old = state_old
            masked = block_scores(query_heads, key_block, bias_block, allowed, score_scale)
            peak_new = jnp.maximum(peak_old, jnp.max(masked, axis=3))
            exponent = jnp.where(allowed[None, None], jnp.exp(masked - peak_new[..., None]), 0.0)
            return (peak_new, mass_old * jnp.exp(peak_old - peak_new) + jnp.sum(exponent, axis=3))

        def keep_state(state_old):
            return state_old

        return lax.cond(jnp.any(allowed), update, keep_state, state_in)

    row_peak, total_mass = lax.fori_loop(0, piece_rows // stats_block_width, one_block, initial)
    total_keys = all_keys.shape[0]
    block_width = math.gcd(total_keys, 512)
    block_count = total_keys // block_width
    key_blocks = all_keys.reshape(block_count, block_width, kv_local, HEAD_DIM)
    value_blocks = all_values.reshape(block_count, block_width, kv_local, HEAD_DIM)
    bias_blocks = all_bias.reshape(block_count, block_width, kv_local)

    def second_pass(accumulated, block_items):
        block_number, key_block, value_block, bias_block = block_items
        allowed = visibility(block_number * block_width + jnp.arange(block_width, dtype=jnp.int32))

        def attend(accum_in):
            masked = block_scores(query_heads, key_block, bias_block, allowed, score_scale)
            weights = (
                jnp.where(allowed[None, None], jnp.exp(masked - row_peak[..., None]), 0.0)
                / total_mass[..., None]
            )
            accum_out = accum_in + jnp.einsum(
                "getk,kgh->tgeh",
                weights.astype(jnp.bfloat16),
                value_block,
                preferred_element_type=jnp.float32,
            )
            return (accum_out, jnp.transpose(jnp.sum(weights, axis=(1, 2))) / group_size)

        def skip_block(accum_in):
            return (accum_in, jnp.zeros((block_width, kv_local), jnp.float32))

        return lax.cond(jnp.any(allowed), attend, skip_block, accumulated)

    accumulated, mass_blocks = lax.scan(
        second_pass,
        jnp.zeros((shard_rows, kv_local, group_size, HEAD_DIM), jnp.float32),
        (jnp.arange(block_count, dtype=jnp.int32), key_blocks, value_blocks, bias_blocks),
    )
    key_term = mass_blocks.reshape(total_keys, kv_local)
    key_mass = lax.psum_scatter(key_term, "seq", scatter_dimension=0, tiled=True).astype(
        jnp.bfloat16
    )
    attended = accumulated.reshape(shard_rows, kv_local * group_size * HEAD_DIM).astype(
        jnp.bfloat16
    )
    return (attended, jnp.transpose(key_mass))


def solution(mesh):
    return jax.shard_map(
        pair_device if mesh.shape["seq"] == 2 else ring_device,
        mesh=mesh,
        in_specs=(
            P(("dp", "seq"), "heads"),
            P(None, "heads"),
            P("heads", "seq"),
            P(),
            P(("dp", "seq"), "heads"),
            P(("dp", "seq"), "heads"),
            P(("dp", "seq"), "heads"),
            P("dp"),
        ),
        out_specs=(P(("dp", "seq"), "heads"), P("heads", ("dp", "seq"))),
        check_vma=False,
    )
```

```python
import functools
import math

import jax
import jax.numpy as jnp
from jax import lax
from jax.experimental import pallas as pl
from jax.experimental.pallas import tpu as pltpu
from jax.sharding import PartitionSpec as P

QUERY_HEADS = 64
KV_HEADS = 8
HEAD_DIM = 128


NEG_FILL = -1e30
RIM_ROWS = 16
LEAST_RETENTION = -40.0
VMEM_BYTES = 16 * 1024 * 1024


def convolve(widened, taps, lead, rows):
    summed = jnp.zeros((rows, widened.shape[1]), jnp.float32)
    for back in range(taps.shape[0]):
        summed = summed + taps[back : back + 1] * widened[lead - back : lead - back + rows]
    return summed.astype(jnp.bfloat16)


def own_project_kernel(rows_ref, taps_ref, gate_ref, out_ref, held_taps_ref, held_ref, widened):
    rows, features = rows_ref.shape
    held_taps_ref[...] = taps_ref[...].astype(jnp.float32)
    held_ref[:features] = gate_ref[...]
    tile = widened.shape[2]
    total = jnp.zeros(out_ref.shape, jnp.float32)
    for step in range(features // tile):
        columns = slice(step * tile, (step + 1) * tile)
        edges = features + step * 2 * RIM_ROWS
        held_ref[edges : edges + RIM_ROWS, :tile] = rows_ref[:RIM_ROWS, columns]
        held_ref[edges + RIM_ROWS : edges + 2 * RIM_ROWS, :tile] = rows_ref[
            rows - RIM_ROWS :, columns
        ]
        wide = widened.at[step % 2]
        wide[...] = rows_ref[:, columns].astype(jnp.float32)
        taps = taps_ref[:, columns].astype(jnp.float32)
        mixed = convolve(wide, taps, RIM_ROWS, rows - RIM_ROWS)
        total = total + jnp.dot(mixed, gate_ref[columns, :], preferred_element_type=jnp.float32)
    out_ref[...] = total


def peer_project_kernel(
    peer_ref, taps_ref, held_ref, near_ref, far_ref, widened, own_widened
):
    rows, features = peer_ref.shape
    tile = widened.shape[2]
    first = lax.axis_index("seq") == 0
    half = near_ref.shape[1]
    total = jnp.zeros((near_ref.shape[0], 2 * half), jnp.float32)
    for step in range(features // tile):
        columns = slice(step * tile, (step + 1) * tile)
        wide, own_wide = widened.at[step % 2], own_widened.at[step % 2]
        edges = held_ref.at[
            features + step * 2 * RIM_ROWS : features + (step + 1) * 2 * RIM_ROWS, :tile
        ]
        own_tail = edges[RIM_ROWS:].astype(jnp.float32)
        peer_tail = peer_ref[rows - RIM_ROWS :, columns].astype(jnp.float32)
        wide[:RIM_ROWS] = jnp.where(first, own_tail, 0.0)
        wide[RIM_ROWS:] = peer_ref[:, columns].astype(jnp.float32)
        own_wide[:RIM_ROWS] = jnp.where(first, 0.0, peer_tail)
        own_wide[RIM_ROWS:] = edges[:RIM_ROWS].astype(jnp.float32)
        taps = taps_ref[:, columns].astype(jnp.float32)
        mixed = jnp.concatenate(
            [
                convolve(own_wide, taps, RIM_ROWS, RIM_ROWS),
                convolve(wide, taps, RIM_ROWS, rows),
            ],
            axis=0,
        )
        total = total + jnp.dot(mixed, held_ref[columns, :], preferred_element_type=jnp.float32)
    near_ref[...] = total[:, :half]
    far_ref[...] = total[:, half:].astype(jnp.bfloat16)


def own_project(activations, conv_taps, gate_in):
    rows, features = activations.shape
    done = rows - RIM_ROWS
    tile = math.gcd(features, gate_in.shape[1])
    return pl.pallas_call(
        own_project_kernel,
        out_shape=(
            jax.ShapeDtypeStruct((done, gate_in.shape[1]), jnp.float32),
            jax.ShapeDtypeStruct(conv_taps.shape, jnp.float32),
            jax.ShapeDtypeStruct(
                (features + features // tile * 2 * RIM_ROWS, gate_in.shape[1]), gate_in.dtype
            ),
        ),
        scratch_shapes=[pltpu.VMEM((2, rows, tile), jnp.float32)],
        compiler_params=pltpu.CompilerParams(vmem_limit_bytes=VMEM_BYTES),
        cost_estimate=pl.CostEstimate(flops=1, bytes_accessed=1, transcendentals=0),
    )(activations, conv_taps, gate_in)


def peer_project(peer_rows, taps, held):
    rows, features = peer_rows.shape
    done = rows + RIM_ROWS
    tile = math.gcd(features, held.shape[1])
    half = held.shape[1] // 2
    return pl.pallas_call(
        peer_project_kernel,
        out_shape=(
            jax.ShapeDtypeStruct((done, half), jnp.float32),
            jax.ShapeDtypeStruct((done, half), jnp.bfloat16),
        ),
        scratch_shapes=[
            pltpu.VMEM((2, rows + RIM_ROWS, tile), jnp.float32),
            pltpu.VMEM((2, 2 * RIM_ROWS, tile), jnp.float32),
        ],
        compiler_params=pltpu.CompilerParams(vmem_limit_bytes=VMEM_BYTES),
        cost_estimate=pl.CostEstimate(flops=1, bytes_accessed=1, transcendentals=0),
    )(peer_rows, taps, held)


def head_sum(part):
    count = lax.axis_size("heads")
    step = 1
    received = None
    while step < count:
        if received is not None:
            part = part + received.astype(jnp.float32)
        received = exchange_heads(part if step == 1 else part.astype(jnp.bfloat16), step)
        step *= 2
    return part, received


def exchange_heads(block, step):
    count = lax.axis_size("heads")
    return lax.ppermute(block, "heads", [(i, i ^ step) for i in range(count)])


def in_one_piece(work, *given):
    shapes = jax.eval_shape(work, *given)
    return lax.cond(
        lax.axis_index("seq") >= 0,
        work,
        lambda *given: jax.tree.map(lambda like: jnp.zeros(like.shape, like.dtype), shapes),
        *given,
    )


def far_logits(block, gate_out):
    step = lax.axis_size("heads") // 2
    received = exchange_heads(block, step)

    def nearer(block, received, gate_out):
        distance = step
        while distance > 1:
            distance //= 2
            block = block.astype(jnp.float32) + received.astype(jnp.float32)
            received = exchange_heads(block, distance)
        return partial_logits(block, received, gate_out, block.shape[1])

    return in_one_piece(nearer, block, received, gate_out)


def share_of_logits(pre_ref, in_ref, gate_out_ref, offset):
    pre = pre_ref[...] + in_ref[...].astype(jnp.float32)
    hidden = (pre / (1.0 + jnp.exp(-pre))).astype(jnp.bfloat16)
    share = gate_out_ref.shape[1] // lax.axis_size("seq")
    start = pl.multiple_of(lax.axis_index("seq") * share + offset, HEAD_DIM)
    gate_columns = gate_out_ref[:, pl.ds(start, pre.shape[1])]
    return lax.dot_general(
        gate_columns, hidden, (((1,), (1,)), ((), ())), preferred_element_type=jnp.float32
    )


def partial_logits_kernel(offset, own_ref, in_ref, gate_out_ref, out_ref):
    out_ref[...] = share_of_logits(own_ref, in_ref, gate_out_ref, offset)


def partial_logits(part, received, gate_out, offset):
    return pl.pallas_call(
        functools.partial(partial_logits_kernel, offset),
        out_shape=jax.ShapeDtypeStruct((gate_out.shape[0], part.shape[0]), jnp.float32),
        compiler_params=pltpu.CompilerParams(vmem_limit_bytes=VMEM_BYTES),
    )(part, received, gate_out)


def logits_kernel(own_ref, far_share_ref, near_ref, near_in_ref, gate_out_ref, out_ref):
    first = lax.axis_index("seq") == 0
    share = share_of_logits(near_ref, near_in_ref, gate_out_ref, 0) + far_share_ref[...]
    own = jnp.concatenate([share[:, :RIM_ROWS], own_ref[...]], axis=1)
    peer = share[:, RIM_ROWS:]
    out_ref[0] = jnp.where(first, own, peer)
    out_ref[1] = jnp.where(first, peer, own)


def logits_share(own_share, far_share, near, near_in, gate_out):
    rows = own_share.shape[1] + RIM_ROWS
    return pl.pallas_call(
        logits_kernel,
        out_shape=jax.ShapeDtypeStruct((2, gate_out.shape[0], rows), jnp.float32),
        compiler_params=pltpu.CompilerParams(vmem_limit_bytes=VMEM_BYTES),
    )(own_share, far_share, near, near_in, gate_out)


def hide_unseen(seq_rank, segments_ref, rows):
    own_segments = segments_ref[pl.ds(seq_rank, 1), :]
    behind_segments = segments_ref[pl.ds(0, 1), :]
    query_segments = jnp.transpose(jnp.broadcast_to(own_segments, (rows, rows)))
    query_at = lax.broadcasted_iota(jnp.int32, (rows, rows), 0)
    key_at = lax.broadcasted_iota(jnp.int32, (rows, rows), 1)
    see_own = (key_at <= query_at) & (query_segments == own_segments)
    see_behind = (query_segments == behind_segments) & (seq_rank > 0)
    return jnp.where(jnp.concatenate([see_behind, see_own], axis=1), 0.0, NEG_FILL)


def head_columns(number):
    return slice(number * HEAD_DIM, (number + 1) * HEAD_DIM)


def scores_of(queries_ref, keys, offset, head):
    scores = lax.dot_general(
        queries_ref[:, head_columns(head)],
        keys,
        (((1,), (1,)), ((), ())),
        preferred_element_type=jnp.float32,
    )
    return scores * (1.0 / math.sqrt(HEAD_DIM)) + offset


def with_behind(ref, behind_ref, number, whole):
    own = ref[:, head_columns(number)]
    if not whole:
        return own
    return jnp.concatenate([behind_ref[:, head_columns(number)], own], axis=0)


def powers_kernel(segments_ref, queries_ref, keys_ref, behind_keys_ref, powers_ref):
    seq_rank = lax.axis_index("seq")
    rows = queries_ref.shape[0]
    kv_local = keys_ref.shape[1] // HEAD_DIM
    group_size = queries_ref.shape[1] // keys_ref.shape[1]
    hide = hide_unseen(seq_rank, segments_ref, rows)

    def fill(whole):
        start = 0 if whole else rows
        for head in range(kv_local * group_size):
            g = head // group_size
            keys = with_behind(keys_ref, behind_keys_ref, g, whole)
            scores = scores_of(queries_ref, keys, hide[:, start:], head)
            powers_ref[head, :, start:] = jnp.exp(
                scores - jnp.max(scores, axis=1, keepdims=True)
            )

    pl.when(seq_rank > 0)(lambda: fill(True))
    pl.when(seq_rank == 0)(lambda: fill(False))


def powers_of(segments, queries, keys, behind_keys):
    rows = queries.shape[0]
    heads = queries.shape[1] // HEAD_DIM
    return pl.pallas_call(
        powers_kernel,
        out_shape=jax.ShapeDtypeStruct((heads, rows, 2 * rows), jnp.float32),
        compiler_params=pltpu.CompilerParams(vmem_limit_bytes=VMEM_BYTES),
        cost_estimate=pl.CostEstimate(
            flops=4 * rows * rows * queries.shape[1],
            bytes_accessed=8 * heads * rows * rows,
            transcendentals=2 * heads * rows * rows,
        ),
    )(segments, queries, keys, behind_keys)


def weights_kernel(
    share_ref,
    peer_share_ref,
    powers_ref,
    segments_ref,
    queries_ref,
    keys_ref,
    behind_keys_ref,
    weights_ref,
    own_mass_ref,
    behind_mass_ref,
    retention,
):
    seq_rank, head_rank = lax.axis_index("seq"), lax.axis_index("heads")
    rows = queries_ref.shape[0]
    kv_local = keys_ref.shape[1] // HEAD_DIM
    group_size = queries_ref.shape[1] // keys_ref.shape[1]
    logits = share_ref[...] + peer_share_ref[...]
    log_gate = jnp.minimum(logits, 0.0) - jnp.log1p(jnp.exp(-jnp.abs(logits)))
    retention[...] = log_gate.astype(jnp.bfloat16).astype(jnp.float32)
    biases = []
    for g in range(kv_local):
        at = pl.ds(head_rank * kv_local + g, 1)
        biases.append(jnp.concatenate([retention[0, at, :], retention[seq_rank, at, :]], axis=1))
    moderate = jnp.min(functools.reduce(jnp.minimum, biases)) >= LEAST_RETENTION

    def finish(whole, terms_of):
        start = 0 if whole else rows
        for g in range(kv_local):
            mass = jnp.zeros((1, 2 * rows - start), jnp.float32)
            group_terms = terms_of(g, whole, start)
            for head in range(g * group_size, (g + 1) * group_size):
                weights = group_terms(head)
                weights = weights * (1.0 / jnp.sum(weights, axis=1, keepdims=True))
                mass = mass + jnp.sum(weights, axis=0, keepdims=True)
                weights_ref[head, :, start:] = weights.astype(jnp.bfloat16)
            mass = mass / group_size
            own_mass_ref[g : g + 1, :] = mass[:, rows - start :]
            behind_mass_ref[g : g + 1, :] = mass[:, :rows] if whole else jnp.zeros((1, rows))

    def by_powers(g, whole, start):
        factor = jnp.exp(biases[g] - jnp.max(biases[g]))[:, start:]
        return lambda head: powers_ref[head, :, start:] * factor

    def by_scores(g, whole, start):
        offset = hide_unseen(seq_rank, segments_ref, rows) + biases[g]
        keys = with_behind(keys_ref, behind_keys_ref, g, whole)

        def terms(head):
            scores = scores_of(queries_ref, keys, offset[:, start:], head)
            return jnp.exp(scores - jnp.max(scores, axis=1, keepdims=True))

        return terms

    pl.when(moderate & (seq_rank > 0))(lambda: finish(True, by_powers))
    pl.when(moderate & (seq_rank == 0))(lambda: finish(False, by_powers))
    pl.when(jnp.logical_not(moderate))(lambda: finish(True, by_scores))


def weights_of(share, peer_share, powers, segments, queries, keys, behind_keys):
    rows = queries.shape[0]
    mass = jax.ShapeDtypeStruct((keys.shape[1] // HEAD_DIM, rows), jnp.float32)
    return pl.pallas_call(
        weights_kernel,
        out_shape=(jax.ShapeDtypeStruct(powers.shape, jnp.bfloat16), mass, mass),
        scratch_shapes=[pltpu.VMEM(share.shape, jnp.float32)],
        compiler_params=pltpu.CompilerParams(vmem_limit_bytes=VMEM_BYTES),
    )(share, peer_share, powers, segments, queries, keys, behind_keys)


def attend_kernel(weights_ref, values_ref, behind_values_ref, attended_ref):
    seq_rank = lax.axis_index("seq")
    heads, rows = weights_ref.shape[:2]
    group_size = attended_ref.shape[1] // values_ref.shape[1]

    def fill(whole):
        start = 0 if whole else rows
        for head in range(heads):
            values = with_behind(values_ref, behind_values_ref, head // group_size, whole)
            attended_ref[:, head_columns(head)] = jnp.dot(
                weights_ref[head, :, start:], values, preferred_element_type=jnp.float32
            ).astype(jnp.bfloat16)

    pl.when(seq_rank > 0)(lambda: fill(True))
    pl.when(seq_rank == 0)(lambda: fill(False))


def attend(weights, values, behind_values):
    heads, rows = weights.shape[:2]
    return pl.pallas_call(
        attend_kernel,
        out_shape=jax.ShapeDtypeStruct((rows, heads * HEAD_DIM), jnp.bfloat16),
        compiler_params=pltpu.CompilerParams(vmem_limit_bytes=VMEM_BYTES),
        cost_estimate=pl.CostEstimate(
            flops=4 * rows * rows * heads * HEAD_DIM,
            bytes_accessed=2 * (weights.size + rows * heads * HEAD_DIM),
            transcendentals=0,
        ),
    )(weights, values, behind_values)


def pair_device(
    activations, conv_taps, gate_in, gate_out, queries, key_vectors, value_vectors, segment_ids
):
    rows = activations.shape[0]
    swap = [(0, 1), (1, 0)]
    segments = segment_ids.reshape(2, rows)
    gate_out = jnp.transpose(gate_out)

    peer_rows = lax.ppermute(activations, "seq", swap)

    def own_work(activations, conv_taps, gate_in, gate_out):
        part, *held = own_project(activations, conv_taps, gate_in)
        return partial_logits(*head_sum(part), gate_out, 0), held

    own_share, held = in_one_piece(own_work, activations, conv_taps, gate_in, gate_out)
    own_share, held, key_vectors = lax.optimization_barrier((own_share, held, key_vectors))
    behind_keys = lax.ppermute(key_vectors, "seq", swap)
    peer_rows, own_share, held = lax.optimization_barrier((peer_rows, own_share, held))
    near, far = peer_project(peer_rows, *held)
    near, far, behind_keys = lax.optimization_barrier((near, far, behind_keys))
    behind_values = lax.ppermute(value_vectors, "seq", swap)
    near, near_in = head_sum(near)
    far_share = far_logits(far, gate_out)
    share = logits_share(own_share, far_share, near, near_in, gate_out)
    share, queries = lax.optimization_barrier((share, queries))
    powers = powers_of(segments, queries, key_vectors, behind_keys)
    weights, own_mass, behind_mass = weights_of(
        share,
        lax.ppermute(share, "seq", swap),
        powers,
        segments,
        queries,
        key_vectors,
        behind_keys,
    )
    attended = attend(weights, value_vectors, behind_values)
    key_mass = own_mass + lax.ppermute(behind_mass, "seq", swap)
    return (attended, key_mass.astype(jnp.bfloat16))


def from_behind(block, axis, distance):
    devices = range(lax.axis_size(axis))
    route = [(i - distance, i) for i in devices if i - distance in devices]
    return lax.ppermute(block, axis, route)


def block_scores(query_heads, key_block, bias_block, allowed, score_scale):
    scores = (
        jnp.einsum("tgeh,kgh->getk", query_heads, key_block, preferred_element_type=jnp.float32)
        * score_scale
    )
    scores = scores + jnp.transpose(bias_block.astype(jnp.float32))[:, None, None, :]
    return jnp.where(allowed[None, None], scores, NEG_FILL)


def ring_device(
    activations, conv_taps, gate_in, gate_out, queries, key_vectors, value_vectors, segment_ids
):
    shard_rows = activations.shape[0]
    tap_count = conv_taps.shape[0]
    rim_rows = from_behind(activations[shard_rows - (tap_count - 1) :], "seq", 1)
    widened = jnp.concatenate([rim_rows, activations], 0).astype(jnp.float32)
    summed = jnp.zeros(activations.shape, jnp.float32)
    for shift_back in range(tap_count):
        start_row = tap_count - 1 - shift_back
        summed = (
            summed
            + conv_taps[shift_back].astype(jnp.float32)
            * widened[start_row : start_row + shard_rows]
        )
    mixed_rows = summed.astype(jnp.bfloat16)
    partial_hidden = jnp.dot(
        mixed_rows,
        lax.all_gather(gate_in, "seq", axis=1, tiled=True),
        preferred_element_type=jnp.float32,
    )
    kv_local = key_vectors.shape[1] // HEAD_DIM
    group_size = QUERY_HEADS // KV_HEADS
    head_rank = lax.axis_index("heads")
    hidden = jax.nn.silu(lax.psum(partial_hidden, "heads")).astype(jnp.bfloat16)
    logits = jnp.dot(hidden, gate_out, preferred_element_type=jnp.float32)
    retention = lax.dynamic_slice_in_dim(
        jax.nn.log_sigmoid(logits).astype(jnp.bfloat16), head_rank * kv_local, kv_local, 1
    )
    seq_rank = lax.axis_index("seq")
    local_index = jnp.arange(shard_rows, dtype=jnp.int32)
    own_queries, own_keys, own_values, own_bias = (queries, key_vectors, value_vectors, retention)
    query_places = seq_rank * shard_rows + local_index
    query_segments = jnp.take(segment_ids, query_places)
    query_heads = own_queries.reshape(shard_rows, kv_local, group_size, HEAD_DIM)
    score_scale = 1.0 / math.sqrt(HEAD_DIM)

    def visibility(flat_index):
        key_segments = jnp.take(segment_ids, flat_index)
        return (flat_index[None, :] <= query_places[:, None]) & (
            key_segments[None, :] == query_segments[:, None]
        )

    initial = (
        jnp.full((kv_local, group_size, shard_rows), NEG_FILL, jnp.float32),
        jnp.zeros((kv_local, group_size, shard_rows), jnp.float32),
    )
    all_keys, all_values, all_bias = (
        lax.all_gather(own_keys, "seq", axis=0, tiled=True),
        lax.all_gather(own_values, "seq", axis=0, tiled=True),
        lax.all_gather(own_bias, "seq", axis=0, tiled=True),
    )
    piece_rows = all_keys.shape[0]
    stats_block_width = math.gcd(piece_rows, 512)

    def one_block(block_number, state_in):
        offset = block_number * stats_block_width
        key_block = lax.dynamic_slice_in_dim(all_keys, offset, stats_block_width, 0).reshape(
            stats_block_width, kv_local, HEAD_DIM
        )
        bias_block = lax.dynamic_slice_in_dim(all_bias, offset, stats_block_width, 0)
        allowed = visibility(0 + offset + jnp.arange(stats_block_width, dtype=jnp.int32))

        def update(state_old):
            peak_old, mass_old = state_old
            masked = block_scores(query_heads, key_block, bias_block, allowed, score_scale)
            peak_new = jnp.maximum(peak_old, jnp.max(masked, axis=3))
            exponent = jnp.where(allowed[None, None], jnp.exp(masked - peak_new[..., None]), 0.0)
            return (peak_new, mass_old * jnp.exp(peak_old - peak_new) + jnp.sum(exponent, axis=3))

        def keep_state(state_old):
            return state_old

        return lax.cond(jnp.any(allowed), update, keep_state, state_in)

    row_peak, total_mass = lax.fori_loop(0, piece_rows // stats_block_width, one_block, initial)
    total_keys = all_keys.shape[0]
    block_width = math.gcd(total_keys, 512)
    block_count = total_keys // block_width
    key_blocks = all_keys.reshape(block_count, block_width, kv_local, HEAD_DIM)
    value_blocks = all_values.reshape(block_count, block_width, kv_local, HEAD_DIM)
    bias_blocks = all_bias.reshape(block_count, block_width, kv_local)

    def second_pass(accumulated, block_items):
        block_number, key_block, value_block, bias_block = block_items
        allowed = visibility(block_number * block_width + jnp.arange(block_width, dtype=jnp.int32))

        def attend(accum_in):
            masked = block_scores(query_heads, key_block, bias_block, allowed, score_scale)
            weights = (
                jnp.where(allowed[None, None], jnp.exp(masked - row_peak[..., None]), 0.0)
                / total_mass[..., None]
            )
            accum_out = accum_in + jnp.einsum(
                "getk,kgh->tgeh",
                weights.astype(jnp.bfloat16),
                value_block,
                preferred_element_type=jnp.float32,
            )
            return (accum_out, jnp.transpose(jnp.sum(weights, axis=(1, 2))) / group_size)

        def skip_block(accum_in):
            return (accum_in, jnp.zeros((block_width, kv_local), jnp.float32))

        return lax.cond(jnp.any(allowed), attend, skip_block, accumulated)

    accumulated, mass_blocks = lax.scan(
        second_pass,
        jnp.zeros((shard_rows, kv_local, group_size, HEAD_DIM), jnp.float32),
        (jnp.arange(block_count, dtype=jnp.int32), key_blocks, value_blocks, bias_blocks),
    )
    key_term = mass_blocks.reshape(total_keys, kv_local)
    key_mass = lax.psum_scatter(key_term, "seq", scatter_dimension=0, tiled=True).astype(
        jnp.bfloat16
    )
    attended = accumulated.reshape(shard_rows, kv_local * group_size * HEAD_DIM).astype(
        jnp.bfloat16
    )
    return (attended, jnp.transpose(key_mass))


def solution(mesh):
    return jax.shard_map(
        pair_device if mesh.shape["seq"] == 2 else ring_device,
        mesh=mesh,
        in_specs=(
            P(("dp", "seq"), "heads"),
            P(None, "heads"),
            P("heads", "seq"),
            P(),
            P(("dp", "seq"), "heads"),
            P(("dp", "seq"), "heads"),
            P(("dp", "seq"), "heads"),
            P("dp"),
        ),
        out_specs=(P(("dp", "seq"), "heads"), P("heads", ("dp", "seq"))),
        check_vma=False,
    )
```

```python
import functools
import math

import jax
import jax.numpy as jnp
from jax import lax
from jax.experimental import pallas as pl
from jax.experimental.pallas import tpu as pltpu
from jax.sharding import PartitionSpec as P

QUERY_HEADS = 64
KV_HEADS = 8
HEAD_DIM = 128


NEG_FILL = -1e30
RIM_ROWS = 16
LEAST_RETENTION = -40.0
VMEM_BYTES = 16 * 1024 * 1024


def convolve(widened, taps, lead, rows):
    summed = jnp.zeros((rows, widened.shape[1]), jnp.float32)
    for back in range(taps.shape[0]):
        summed = summed + taps[back : back + 1] * widened[lead - back : lead - back + rows]
    return summed.astype(jnp.bfloat16)


def own_project_kernel(rows_ref, taps_ref, gate_ref, out_ref, held_taps_ref, held_ref, widened):
    rows, features = rows_ref.shape
    held_taps_ref[...] = taps_ref[...].astype(jnp.float32)
    held_ref[:features] = gate_ref[...]
    tile = widened.shape[2]
    total = jnp.zeros(out_ref.shape, jnp.float32)
    for step in range(features // tile):
        columns = slice(step * tile, (step + 1) * tile)
        edges = features + step * 2 * RIM_ROWS
        held_ref[edges : edges + RIM_ROWS, :tile] = rows_ref[:RIM_ROWS, columns]
        held_ref[edges + RIM_ROWS : edges + 2 * RIM_ROWS, :tile] = rows_ref[
            rows - RIM_ROWS :, columns
        ]
        wide = widened.at[step % 2]
        wide[...] = rows_ref[:, columns].astype(jnp.float32)
        taps = taps_ref[:, columns].astype(jnp.float32)
        mixed = convolve(wide, taps, RIM_ROWS, rows - RIM_ROWS)
        total = total + jnp.dot(mixed, gate_ref[columns, :], preferred_element_type=jnp.float32)
    out_ref[...] = total


def peer_project_kernel(
    peer_ref, taps_ref, held_ref, near_ref, far_ref, widened, own_widened
):
    rows, features = peer_ref.shape
    tile = widened.shape[2]
    first = lax.axis_index("seq") == 0
    half = near_ref.shape[1]
    total = jnp.zeros((near_ref.shape[0], 2 * half), jnp.float32)
    for step in range(features // tile):
        columns = slice(step * tile, (step + 1) * tile)
        wide, own_wide = widened.at[step % 2], own_widened.at[step % 2]
        edges = held_ref.at[
            features + step * 2 * RIM_ROWS : features + (step + 1) * 2 * RIM_ROWS, :tile
        ]
        own_tail = edges[RIM_ROWS:].astype(jnp.float32)
        peer_tail = peer_ref[rows - RIM_ROWS :, columns].astype(jnp.float32)
        wide[:RIM_ROWS] = jnp.where(first, own_tail, 0.0)
        wide[RIM_ROWS:] = peer_ref[:, columns].astype(jnp.float32)
        own_wide[:RIM_ROWS] = jnp.where(first, 0.0, peer_tail)
        own_wide[RIM_ROWS:] = edges[:RIM_ROWS].astype(jnp.float32)
        taps = taps_ref[:, columns].astype(jnp.float32)
        mixed = jnp.concatenate(
            [
                convolve(own_wide, taps, RIM_ROWS, RIM_ROWS),
                convolve(wide, taps, RIM_ROWS, rows),
            ],
            axis=0,
        )
        total = total + jnp.dot(mixed, held_ref[columns, :], preferred_element_type=jnp.float32)
    near_ref[...] = total[:, :half]
    far_ref[...] = total[:, half:].astype(jnp.bfloat16)


def own_project(activations, conv_taps, gate_in):
    rows, features = activations.shape
    done = rows - RIM_ROWS
    tile = math.gcd(features, gate_in.shape[1])
    return pl.pallas_call(
        own_project_kernel,
        out_shape=(
            jax.ShapeDtypeStruct((done, gate_in.shape[1]), jnp.float32),
            jax.ShapeDtypeStruct(conv_taps.shape, jnp.float32),
            jax.ShapeDtypeStruct(
                (features + features // tile * 2 * RIM_ROWS, gate_in.shape[1]), gate_in.dtype
            ),
        ),
        scratch_shapes=[pltpu.VMEM((2, rows, tile), jnp.float32)],
        compiler_params=pltpu.CompilerParams(vmem_limit_bytes=VMEM_BYTES),
        cost_estimate=pl.CostEstimate(flops=1, bytes_accessed=1, transcendentals=0),
    )(activations, conv_taps, gate_in)


def peer_project(peer_rows, taps, held):
    rows, features = peer_rows.shape
    done = rows + RIM_ROWS
    tile = math.gcd(features, held.shape[1])
    half = held.shape[1] // 2
    return pl.pallas_call(
        peer_project_kernel,
        out_shape=(
            jax.ShapeDtypeStruct((done, half), jnp.float32),
            jax.ShapeDtypeStruct((done, half), jnp.bfloat16),
        ),
        scratch_shapes=[
            pltpu.VMEM((2, rows + RIM_ROWS, tile), jnp.float32),
            pltpu.VMEM((2, 2 * RIM_ROWS, tile), jnp.float32),
        ],
        compiler_params=pltpu.CompilerParams(vmem_limit_bytes=VMEM_BYTES),
        cost_estimate=pl.CostEstimate(flops=1, bytes_accessed=1, transcendentals=0),
    )(peer_rows, taps, held)


def head_sum(part):
    count = lax.axis_size("heads")
    step = 1
    received = None
    while step < count:
        if received is not None:
            part = part + received.astype(jnp.float32)
        received = exchange_heads(part if step == 1 else part.astype(jnp.bfloat16), step)
        step *= 2
    return part, received


def exchange_heads(block, step):
    count = lax.axis_size("heads")
    return lax.ppermute(block, "heads", [(i, i ^ step) for i in range(count)])


def in_one_piece(work, *given):
    shapes = jax.eval_shape(work, *given)
    return lax.cond(
        lax.axis_index("seq") >= 0,
        work,
        lambda *given: jax.tree.map(lambda like: jnp.zeros(like.shape, like.dtype), shapes),
        *given,
    )


def far_logits(block, gate_out):
    step = lax.axis_size("heads") // 2
    received = exchange_heads(block, step)

    def nearer(block, received, gate_out):
        distance = step
        while distance > 1:
            distance //= 2
            block = block.astype(jnp.float32) + received.astype(jnp.float32)
            received = exchange_heads(block, distance)
        return partial_logits(block, received, gate_out, block.shape[1])

    return in_one_piece(nearer, block, received, gate_out)


def share_of_logits(pre_ref, in_ref, gate_out_ref, offset):
    pre = pre_ref[...] + in_ref[...].astype(jnp.float32)
    hidden = (pre / (1.0 + jnp.exp(-pre))).astype(jnp.bfloat16)
    share = gate_out_ref.shape[1] // lax.axis_size("seq")
    start = pl.multiple_of(lax.axis_index("seq") * share + offset, HEAD_DIM)
    gate_columns = gate_out_ref[:, pl.ds(start, pre.shape[1])]
    return lax.dot_general(
        gate_columns, hidden, (((1,), (1,)), ((), ())), preferred_element_type=jnp.float32
    )


def partial_logits_kernel(offset, own_ref, in_ref, gate_out_ref, out_ref):
    out_ref[...] = share_of_logits(own_ref, in_ref, gate_out_ref, offset)


def partial_logits(part, received, gate_out, offset):
    return pl.pallas_call(
        functools.partial(partial_logits_kernel, offset),
        out_shape=jax.ShapeDtypeStruct((gate_out.shape[0], part.shape[0]), jnp.float32),
        compiler_params=pltpu.CompilerParams(vmem_limit_bytes=VMEM_BYTES),
    )(part, received, gate_out)


def logits_kernel(own_ref, far_share_ref, near_ref, near_in_ref, gate_out_ref, out_ref):
    first = lax.axis_index("seq") == 0
    share = share_of_logits(near_ref, near_in_ref, gate_out_ref, 0) + far_share_ref[...]
    own = jnp.concatenate([share[:, :RIM_ROWS], own_ref[...]], axis=1)
    peer = share[:, RIM_ROWS:]
    out_ref[0] = jnp.where(first, own, peer)
    out_ref[1] = jnp.where(first, peer, own)


def logits_share(own_share, far_share, near, near_in, gate_out):
    rows = own_share.shape[1] + RIM_ROWS
    return pl.pallas_call(
        logits_kernel,
        out_shape=jax.ShapeDtypeStruct((2, gate_out.shape[0], rows), jnp.float32),
        compiler_params=pltpu.CompilerParams(vmem_limit_bytes=VMEM_BYTES),
    )(own_share, far_share, near, near_in, gate_out)


def hide_unseen(seq_rank, segments_ref, rows):
    own_segments = segments_ref[pl.ds(seq_rank, 1), :]
    behind_segments = segments_ref[pl.ds(0, 1), :]
    query_segments = jnp.transpose(jnp.broadcast_to(own_segments, (rows, rows)))
    query_at = lax.broadcasted_iota(jnp.int32, (rows, rows), 0)
    key_at = lax.broadcasted_iota(jnp.int32, (rows, rows), 1)
    see_own = (key_at <= query_at) & (query_segments == own_segments)
    see_behind = (query_segments == behind_segments) & (seq_rank > 0)
    return jnp.where(jnp.concatenate([see_behind, see_own], axis=1), 0.0, NEG_FILL)


def head_columns(number):
    return slice(number * HEAD_DIM, (number + 1) * HEAD_DIM)


def scores_of(queries_ref, keys, offset, head):
    scores = lax.dot_general(
        queries_ref[:, head_columns(head)],
        keys,
        (((1,), (1,)), ((), ())),
        preferred_element_type=jnp.float32,
    )
    return scores * (1.0 / math.sqrt(HEAD_DIM)) + offset


def with_behind(ref, behind_ref, number, whole):
    own = ref[:, head_columns(number)]
    if not whole:
        return own
    return jnp.concatenate([behind_ref[:, head_columns(number)], own], axis=0)


def powers_kernel(segments_ref, queries_ref, keys_ref, behind_keys_ref, powers_ref):
    seq_rank = lax.axis_index("seq")
    rows = queries_ref.shape[0]
    kv_local = keys_ref.shape[1] // HEAD_DIM
    group_size = queries_ref.shape[1] // keys_ref.shape[1]
    hide = hide_unseen(seq_rank, segments_ref, rows)

    def fill(whole):
        start = 0 if whole else rows
        for head in range(kv_local * group_size):
            g = head // group_size
            keys = with_behind(keys_ref, behind_keys_ref, g, whole)
            scores = scores_of(queries_ref, keys, hide[:, start:], head)
            powers_ref[head, :, start:] = jnp.exp(
                scores - jnp.max(scores, axis=1, keepdims=True)
            )

    pl.when(seq_rank > 0)(lambda: fill(True))
    pl.when(seq_rank == 0)(lambda: fill(False))


def powers_of(segments, queries, keys, behind_keys):
    rows = queries.shape[0]
    heads = queries.shape[1] // HEAD_DIM
    return pl.pallas_call(
        powers_kernel,
        out_shape=jax.ShapeDtypeStruct((heads, rows, 2 * rows), jnp.float32),
        compiler_params=pltpu.CompilerParams(vmem_limit_bytes=VMEM_BYTES),
        cost_estimate=pl.CostEstimate(
            flops=4 * rows * rows * queries.shape[1],
            bytes_accessed=8 * heads * rows * rows,
            transcendentals=2 * heads * rows * rows,
        ),
    )(segments, queries, keys, behind_keys)


def weights_kernel(
    share_ref,
    peer_share_ref,
    powers_ref,
    segments_ref,
    queries_ref,
    keys_ref,
    behind_keys_ref,
    weights_ref,
    own_mass_ref,
    behind_mass_ref,
    retention,
):
    seq_rank, head_rank = lax.axis_index("seq"), lax.axis_index("heads")
    rows = queries_ref.shape[0]
    kv_local = keys_ref.shape[1] // HEAD_DIM
    group_size = queries_ref.shape[1] // keys_ref.shape[1]
    logits = share_ref[...] + peer_share_ref[...]
    log_gate = jnp.minimum(logits, 0.0) - jnp.log1p(jnp.exp(-jnp.abs(logits)))
    retention[...] = log_gate.astype(jnp.bfloat16).astype(jnp.float32)
    biases = []
    for g in range(kv_local):
        at = pl.ds(head_rank * kv_local + g, 1)
        biases.append(jnp.concatenate([retention[0, at, :], retention[seq_rank, at, :]], axis=1))
    moderate = jnp.min(functools.reduce(jnp.minimum, biases)) >= LEAST_RETENTION

    def finish(whole, terms_of):
        start = 0 if whole else rows
        for g in range(kv_local):
            mass = jnp.zeros((1, 2 * rows - start), jnp.float32)
            group_terms = terms_of(g, whole, start)
            for head in range(g * group_size, (g + 1) * group_size):
                weights = group_terms(head)
                weights = weights * (1.0 / jnp.sum(weights, axis=1, keepdims=True))
                mass = mass + jnp.sum(weights, axis=0, keepdims=True)
                weights_ref[head, :, start:] = weights.astype(jnp.bfloat16)
            mass = mass / group_size
            own_mass_ref[g : g + 1, :] = mass[:, rows - start :]
            behind_mass_ref[g : g + 1, :] = mass[:, :rows] if whole else jnp.zeros((1, rows))

    def by_powers(g, whole, start):
        factor = jnp.exp(biases[g] - jnp.max(biases[g]))[:, start:]
        return lambda head: powers_ref[head, :, start:] * factor

    def by_scores(g, whole, start):
        offset = hide_unseen(seq_rank, segments_ref, rows) + biases[g]
        keys = with_behind(keys_ref, behind_keys_ref, g, whole)

        def terms(head):
            scores = scores_of(queries_ref, keys, offset[:, start:], head)
            return jnp.exp(scores - jnp.max(scores, axis=1, keepdims=True))

        return terms

    pl.when(moderate & (seq_rank > 0))(lambda: finish(True, by_powers))
    pl.when(moderate & (seq_rank == 0))(lambda: finish(False, by_powers))
    pl.when(jnp.logical_not(moderate))(lambda: finish(True, by_scores))


def weights_of(share, peer_share, powers, segments, queries, keys, behind_keys):
    rows = queries.shape[0]
    mass = jax.ShapeDtypeStruct((keys.shape[1] // HEAD_DIM, rows), jnp.float32)
    return pl.pallas_call(
        weights_kernel,
        out_shape=(jax.ShapeDtypeStruct(powers.shape, jnp.bfloat16), mass, mass),
        scratch_shapes=[pltpu.VMEM(share.shape, jnp.float32)],
        compiler_params=pltpu.CompilerParams(vmem_limit_bytes=VMEM_BYTES),
    )(share, peer_share, powers, segments, queries, keys, behind_keys)


def attend_kernel(weights_ref, values_ref, behind_values_ref, attended_ref):
    seq_rank = lax.axis_index("seq")
    heads, rows = weights_ref.shape[:2]
    group_size = attended_ref.shape[1] // values_ref.shape[1]

    def fill(whole):
        start = 0 if whole else rows
        for head in range(heads):
            values = with_behind(values_ref, behind_values_ref, head // group_size, whole)
            attended_ref[:, head_columns(head)] = jnp.dot(
                weights_ref[head, :, start:], values, preferred_element_type=jnp.float32
            ).astype(jnp.bfloat16)

    pl.when(seq_rank > 0)(lambda: fill(True))
    pl.when(seq_rank == 0)(lambda: fill(False))


def attend(weights, values, behind_values):
    heads, rows = weights.shape[:2]
    return pl.pallas_call(
        attend_kernel,
        out_shape=jax.ShapeDtypeStruct((rows, heads * HEAD_DIM), jnp.bfloat16),
        compiler_params=pltpu.CompilerParams(vmem_limit_bytes=VMEM_BYTES),
        cost_estimate=pl.CostEstimate(
            flops=4 * rows * rows * heads * HEAD_DIM,
            bytes_accessed=2 * (weights.size + rows * heads * HEAD_DIM),
            transcendentals=0,
        ),
    )(weights, values, behind_values)


def pair_device(
    activations, conv_taps, gate_in, gate_out, queries, key_vectors, value_vectors, segment_ids
):
    rows = activations.shape[0]
    swap = [(0, 1), (1, 0)]
    segments = segment_ids.reshape(2, rows)
    gate_out = jnp.transpose(gate_out)

    peer_rows = lax.ppermute(activations, "seq", swap)

    def own_work(activations, conv_taps, gate_in, gate_out):
        part, *held = own_project(activations, conv_taps, gate_in)
        return partial_logits(*head_sum(part), gate_out, 0), held

    own_share, held = in_one_piece(own_work, activations, conv_taps, gate_in, gate_out)
    peer_rows, own_share, held = lax.optimization_barrier((peer_rows, own_share, held))
    near, far = peer_project(peer_rows, *held)
    behind_keys = lax.ppermute(key_vectors, "seq", swap)
    behind_values = lax.ppermute(value_vectors, "seq", swap)
    near, near_in = head_sum(near)
    far_share = far_logits(far, gate_out)
    share = logits_share(own_share, far_share, near, near_in, gate_out)
    share, queries = lax.optimization_barrier((share, queries))
    powers = powers_of(segments, queries, key_vectors, behind_keys)
    weights, own_mass, behind_mass = weights_of(
        share,
        lax.ppermute(share, "seq", swap),
        powers,
        segments,
        queries,
        key_vectors,
        behind_keys,
    )
    attended = attend(weights, value_vectors, behind_values)
    key_mass = own_mass + lax.ppermute(behind_mass, "seq", swap)
    return (attended, key_mass.astype(jnp.bfloat16))


def from_behind(block, axis, distance):
    devices = range(lax.axis_size(axis))
    route = [(i - distance, i) for i in devices if i - distance in devices]
    return lax.ppermute(block, axis, route)


def block_scores(query_heads, key_block, bias_block, allowed, score_scale):
    scores = (
        jnp.einsum("tgeh,kgh->getk", query_heads, key_block, preferred_element_type=jnp.float32)
        * score_scale
    )
    scores = scores + jnp.transpose(bias_block.astype(jnp.float32))[:, None, None, :]
    return jnp.where(allowed[None, None], scores, NEG_FILL)


def ring_device(
    activations, conv_taps, gate_in, gate_out, queries, key_vectors, value_vectors, segment_ids
):
    shard_rows = activations.shape[0]
    tap_count = conv_taps.shape[0]
    rim_rows = from_behind(activations[shard_rows - (tap_count - 1) :], "seq", 1)
    widened = jnp.concatenate([rim_rows, activations], 0).astype(jnp.float32)
    summed = jnp.zeros(activations.shape, jnp.float32)
    for shift_back in range(tap_count):
        start_row = tap_count - 1 - shift_back
        summed = (
            summed
            + conv_taps[shift_back].astype(jnp.float32)
            * widened[start_row : start_row + shard_rows]
        )
    mixed_rows = summed.astype(jnp.bfloat16)
    partial_hidden = jnp.dot(
        mixed_rows,
        lax.all_gather(gate_in, "seq", axis=1, tiled=True),
        preferred_element_type=jnp.float32,
    )
    kv_local = key_vectors.shape[1] // HEAD_DIM
    group_size = QUERY_HEADS // KV_HEADS
    head_rank = lax.axis_index("heads")
    hidden = jax.nn.silu(lax.psum(partial_hidden, "heads")).astype(jnp.bfloat16)
    logits = jnp.dot(hidden, gate_out, preferred_element_type=jnp.float32)
    retention = lax.dynamic_slice_in_dim(
        jax.nn.log_sigmoid(logits).astype(jnp.bfloat16), head_rank * kv_local, kv_local, 1
    )
    seq_rank = lax.axis_index("seq")
    local_index = jnp.arange(shard_rows, dtype=jnp.int32)
    own_queries, own_keys, own_values, own_bias = (queries, key_vectors, value_vectors, retention)
    query_places = seq_rank * shard_rows + local_index
    query_segments = jnp.take(segment_ids, query_places)
    query_heads = own_queries.reshape(shard_rows, kv_local, group_size, HEAD_DIM)
    score_scale = 1.0 / math.sqrt(HEAD_DIM)

    def visibility(flat_index):
        key_segments = jnp.take(segment_ids, flat_index)
        return (flat_index[None, :] <= query_places[:, None]) & (
            key_segments[None, :] == query_segments[:, None]
        )

    initial = (
        jnp.full((kv_local, group_size, shard_rows), NEG_FILL, jnp.float32),
        jnp.zeros((kv_local, group_size, shard_rows), jnp.float32),
    )
    all_keys, all_values, all_bias = (
        lax.all_gather(own_keys, "seq", axis=0, tiled=True),
        lax.all_gather(own_values, "seq", axis=0, tiled=True),
        lax.all_gather(own_bias, "seq", axis=0, tiled=True),
    )
    piece_rows = all_keys.shape[0]
    stats_block_width = math.gcd(piece_rows, 512)

    def one_block(block_number, state_in):
        offset = block_number * stats_block_width
        key_block = lax.dynamic_slice_in_dim(all_keys, offset, stats_block_width, 0).reshape(
            stats_block_width, kv_local, HEAD_DIM
        )
        bias_block = lax.dynamic_slice_in_dim(all_bias, offset, stats_block_width, 0)
        allowed = visibility(0 + offset + jnp.arange(stats_block_width, dtype=jnp.int32))

        def update(state_old):
            peak_old, mass_old = state_old
            masked = block_scores(query_heads, key_block, bias_block, allowed, score_scale)
            peak_new = jnp.maximum(peak_old, jnp.max(masked, axis=3))
            exponent = jnp.where(allowed[None, None], jnp.exp(masked - peak_new[..., None]), 0.0)
            return (peak_new, mass_old * jnp.exp(peak_old - peak_new) + jnp.sum(exponent, axis=3))

        def keep_state(state_old):
            return state_old

        return lax.cond(jnp.any(allowed), update, keep_state, state_in)

    row_peak, total_mass = lax.fori_loop(0, piece_rows // stats_block_width, one_block, initial)
    total_keys = all_keys.shape[0]
    block_width = math.gcd(total_keys, 512)
    block_count = total_keys // block_width
    key_blocks = all_keys.reshape(block_count, block_width, kv_local, HEAD_DIM)
    value_blocks = all_values.reshape(block_count, block_width, kv_local, HEAD_DIM)
    bias_blocks = all_bias.reshape(block_count, block_width, kv_local)

    def second_pass(accumulated, block_items):
        block_number, key_block, value_block, bias_block = block_items
        allowed = visibility(block_number * block_width + jnp.arange(block_width, dtype=jnp.int32))

        def attend(accum_in):
            masked = block_scores(query_heads, key_block, bias_block, allowed, score_scale)
            weights = (
                jnp.where(allowed[None, None], jnp.exp(masked - row_peak[..., None]), 0.0)
                / total_mass[..., None]
            )
            accum_out = accum_in + jnp.einsum(
                "getk,kgh->tgeh",
                weights.astype(jnp.bfloat16),
                value_block,
                preferred_element_type=jnp.float32,
            )
            return (accum_out, jnp.transpose(jnp.sum(weights, axis=(1, 2))) / group_size)

        def skip_block(accum_in):
            return (accum_in, jnp.zeros((block_width, kv_local), jnp.float32))

        return lax.cond(jnp.any(allowed), attend, skip_block, accumulated)

    accumulated, mass_blocks = lax.scan(
        second_pass,
        jnp.zeros((shard_rows, kv_local, group_size, HEAD_DIM), jnp.float32),
        (jnp.arange(block_count, dtype=jnp.int32), key_blocks, value_blocks, bias_blocks),
    )
    key_term = mass_blocks.reshape(total_keys, kv_local)
    key_mass = lax.psum_scatter(key_term, "seq", scatter_dimension=0, tiled=True).astype(
        jnp.bfloat16
    )
    attended = accumulated.reshape(shard_rows, kv_local * group_size * HEAD_DIM).astype(
        jnp.bfloat16
    )
    return (attended, jnp.transpose(key_mass))


def solution(mesh):
    return jax.shard_map(
        pair_device if mesh.shape["seq"] == 2 else ring_device,
        mesh=mesh,
        in_specs=(
            P(("dp", "seq"), "heads"),
            P(None, "heads"),
            P("heads", "seq"),
            P(),
            P(("dp", "seq"), "heads"),
            P(("dp", "seq"), "heads"),
            P(("dp", "seq"), "heads"),
            P("dp"),
        ),
        out_specs=(P(("dp", "seq"), "heads"), P("heads", ("dp", "seq"))),
        check_vma=False,
    )
```

```python
import functools
import math

import jax
import jax.numpy as jnp
from jax import lax
from jax.experimental import pallas as pl
from jax.experimental.pallas import tpu as pltpu
from jax.sharding import PartitionSpec as P

QUERY_HEADS = 64
KV_HEADS = 8
HEAD_DIM = 128


NEG_FILL = -1e30
RIM_ROWS = 16
LEAST_RETENTION = -40.0
VMEM_BYTES = 16 * 1024 * 1024


def convolve(widened, taps, lead, rows):
    summed = jnp.zeros((rows, widened.shape[1]), jnp.float32)
    for back in range(taps.shape[0]):
        summed = summed + taps[back : back + 1] * widened[lead - back : lead - back + rows]
    return summed.astype(jnp.bfloat16)


def split_by_core(total, kept_ref, given_ref):
    half = kept_ref.shape[1]
    low, high = total[:, :half], total[:, half:]
    even = lax.rem(lax.axis_index("heads"), 2) == 0
    kept_ref[...] = jnp.where(even, low, high)
    given_ref[...] = jnp.where(even, high, low)


def own_project_kernel(
    rows_ref, taps_ref, gate_ref, kept_ref, given_ref, held_taps_ref, held_ref, widened
):
    rows, features = rows_ref.shape
    held_taps_ref[...] = taps_ref[...].astype(jnp.float32)
    held_ref[:features] = gate_ref[...]
    tile = widened.shape[2]
    total = jnp.zeros((rows - RIM_ROWS, gate_ref.shape[1]), jnp.float32)
    for step in range(features // tile):
        columns = slice(step * tile, (step + 1) * tile)
        edges = features + step * 2 * RIM_ROWS
        held_ref[edges : edges + RIM_ROWS, :tile] = rows_ref[:RIM_ROWS, columns]
        held_ref[edges + RIM_ROWS : edges + 2 * RIM_ROWS, :tile] = rows_ref[
            rows - RIM_ROWS :, columns
        ]
        wide = widened.at[step % 2]
        wide[...] = rows_ref[:, columns].astype(jnp.float32)
        taps = taps_ref[:, columns].astype(jnp.float32)
        mixed = convolve(wide, taps, RIM_ROWS, rows - RIM_ROWS)
        total = total + jnp.dot(mixed, gate_ref[columns, :], preferred_element_type=jnp.float32)
    split_by_core(total, kept_ref, given_ref)


def peer_project_kernel(
    peer_ref, taps_ref, held_ref, kept_ref, given_ref, widened, own_widened
):
    rows, features = peer_ref.shape
    tile = widened.shape[2]
    first = lax.axis_index("seq") == 0
    total = jnp.zeros((kept_ref.shape[0], held_ref.shape[1]), jnp.float32)
    for step in range(features // tile):
        columns = slice(step * tile, (step + 1) * tile)
        wide, own_wide = widened.at[step % 2], own_widened.at[step % 2]
        edges = held_ref.at[
            features + step * 2 * RIM_ROWS : features + (step + 1) * 2 * RIM_ROWS, :tile
        ]
        own_tail = edges[RIM_ROWS:].astype(jnp.float32)
        peer_tail = peer_ref[rows - RIM_ROWS :, columns].astype(jnp.float32)
        wide[:RIM_ROWS] = jnp.where(first, own_tail, 0.0)
        wide[RIM_ROWS:] = peer_ref[:, columns].astype(jnp.float32)
        own_wide[:RIM_ROWS] = jnp.where(first, 0.0, peer_tail)
        own_wide[RIM_ROWS:] = edges[:RIM_ROWS].astype(jnp.float32)
        taps = taps_ref[:, columns].astype(jnp.float32)
        mixed = jnp.concatenate(
            [
                convolve(own_wide, taps, RIM_ROWS, RIM_ROWS),
                convolve(wide, taps, RIM_ROWS, rows),
            ],
            axis=0,
        )
        total = total + jnp.dot(mixed, held_ref[columns, :], preferred_element_type=jnp.float32)
    split_by_core(total, kept_ref, given_ref)


def own_project(activations, conv_taps, gate_in):
    rows, features = activations.shape
    done = rows - RIM_ROWS
    tile = math.gcd(features, gate_in.shape[1])
    return pl.pallas_call(
        own_project_kernel,
        out_shape=(
            jax.ShapeDtypeStruct((done, gate_in.shape[1] // 2), jnp.float32),
            jax.ShapeDtypeStruct((done, gate_in.shape[1] // 2), jnp.float32),
            jax.ShapeDtypeStruct(conv_taps.shape, jnp.float32),
            jax.ShapeDtypeStruct(
                (features + features // tile * 2 * RIM_ROWS, gate_in.shape[1]), gate_in.dtype
            ),
        ),
        scratch_shapes=[pltpu.VMEM((2, rows, tile), jnp.float32)],
        compiler_params=pltpu.CompilerParams(vmem_limit_bytes=VMEM_BYTES),
        cost_estimate=pl.CostEstimate(flops=1, bytes_accessed=1, transcendentals=0),
    )(activations, conv_taps, gate_in)


def peer_project(peer_rows, taps, held):
    rows, features = peer_rows.shape
    done = rows + RIM_ROWS
    tile = math.gcd(features, held.shape[1])
    half = held.shape[1] // 2
    return pl.pallas_call(
        peer_project_kernel,
        out_shape=(
            jax.ShapeDtypeStruct((done, half), jnp.float32),
            jax.ShapeDtypeStruct((done, half), jnp.float32),
        ),
        scratch_shapes=[
            pltpu.VMEM((2, rows + RIM_ROWS, tile), jnp.float32),
            pltpu.VMEM((2, 2 * RIM_ROWS, tile), jnp.float32),
        ],
        compiler_params=pltpu.CompilerParams(vmem_limit_bytes=VMEM_BYTES),
        cost_estimate=pl.CostEstimate(flops=1, bytes_accessed=1, transcendentals=0),
    )(peer_rows, taps, held)


def exchange_heads(block, step):
    count = lax.axis_size("heads")
    return lax.ppermute(block, "heads", [(i, i ^ step) for i in range(count)])


def head_sum(kept, given):
    received = exchange_heads(given, 1)
    step = 2
    while step < lax.axis_size("heads"):
        kept = kept + received.astype(jnp.float32)
        received = exchange_heads(kept.astype(jnp.bfloat16), step)
        step *= 2
    return kept, received


def in_one_piece(work, *given):
    shapes = jax.eval_shape(work, *given)
    return lax.cond(
        lax.axis_index("seq") >= 0,
        work,
        lambda *given: jax.tree.map(lambda like: jnp.zeros(like.shape, like.dtype), shapes),
        *given,
    )


def share_of_logits(kept_ref, in_ref, gate_out_ref):
    pre = kept_ref[...] + in_ref[...].astype(jnp.float32)
    hidden = (pre / (1.0 + jnp.exp(-pre))).astype(jnp.bfloat16)
    half = pre.shape[1]
    part = 2 * lax.axis_index("seq") + lax.rem(lax.axis_index("heads"), 2)
    gate_columns = gate_out_ref[:, pl.ds(pl.multiple_of(part * half, HEAD_DIM), half)]
    return lax.dot_general(
        gate_columns, hidden, (((1,), (1,)), ((), ())), preferred_element_type=jnp.float32
    )


def partial_logits_kernel(kept_ref, in_ref, gate_out_ref, out_ref):
    out_ref[...] = share_of_logits(kept_ref, in_ref, gate_out_ref)


def partial_logits(kept, received, gate_out):
    return pl.pallas_call(
        partial_logits_kernel,
        out_shape=jax.ShapeDtypeStruct((gate_out.shape[0], kept.shape[0]), jnp.float32),
        compiler_params=pltpu.CompilerParams(vmem_limit_bytes=VMEM_BYTES),
    )(kept, received, gate_out)


def logits_kernel(own_ref, kept_ref, in_ref, gate_out_ref, out_ref):
    first = lax.axis_index("seq") == 0
    share = share_of_logits(kept_ref, in_ref, gate_out_ref)
    own = jnp.concatenate([share[:, :RIM_ROWS], own_ref[...]], axis=1)
    peer = share[:, RIM_ROWS:]
    out_ref[0] = jnp.where(first, own, peer)
    out_ref[1] = jnp.where(first, peer, own)


def logits_share(own_share, kept, received, gate_out):
    rows = own_share.shape[1] + RIM_ROWS
    return pl.pallas_call(
        logits_kernel,
        out_shape=jax.ShapeDtypeStruct((2, gate_out.shape[0], rows), jnp.float32),
        compiler_params=pltpu.CompilerParams(vmem_limit_bytes=VMEM_BYTES),
    )(own_share, kept, received, gate_out)


def hide_unseen(seq_rank, segments_ref, rows):
    own_segments = segments_ref[pl.ds(seq_rank, 1), :]
    behind_segments = segments_ref[pl.ds(0, 1), :]
    query_segments = jnp.transpose(jnp.broadcast_to(own_segments, (rows, rows)))
    query_at = lax.broadcasted_iota(jnp.int32, (rows, rows), 0)
    key_at = lax.broadcasted_iota(jnp.int32, (rows, rows), 1)
    see_own = (key_at <= query_at) & (query_segments == own_segments)
    see_behind = (query_segments == behind_segments) & (seq_rank > 0)
    return jnp.where(jnp.concatenate([see_behind, see_own], axis=1), 0.0, NEG_FILL)


def head_columns(number):
    return slice(number * HEAD_DIM, (number + 1) * HEAD_DIM)


def scores_of(queries_ref, keys, offset, head):
    scores = lax.dot_general(
        queries_ref[:, head_columns(head)],
        keys,
        (((1,), (1,)), ((), ())),
        preferred_element_type=jnp.float32,
    )
    return scores * (1.0 / math.sqrt(HEAD_DIM)) + offset


def with_behind(ref, behind_ref, number, whole):
    own = ref[:, head_columns(number)]
    if not whole:
        return own
    return jnp.concatenate([behind_ref[:, head_columns(number)], own], axis=0)


def powers_kernel(segments_ref, queries_ref, keys_ref, behind_keys_ref, powers_ref):
    seq_rank = lax.axis_index("seq")
    rows = queries_ref.shape[0]
    kv_local = keys_ref.shape[1] // HEAD_DIM
    group_size = queries_ref.shape[1] // keys_ref.shape[1]
    hide = hide_unseen(seq_rank, segments_ref, rows)

    def fill(whole):
        start = 0 if whole else rows
        for head in range(kv_local * group_size):
            g = head // group_size
            keys = with_behind(keys_ref, behind_keys_ref, g, whole)
            scores = scores_of(queries_ref, keys, hide[:, start:], head)
            powers_ref[head, :, start:] = jnp.exp(
                scores - jnp.max(scores, axis=1, keepdims=True)
            )

    pl.when(seq_rank > 0)(lambda: fill(True))
    pl.when(seq_rank == 0)(lambda: fill(False))


def powers_of(segments, queries, keys, behind_keys):
    rows = queries.shape[0]
    heads = queries.shape[1] // HEAD_DIM
    return pl.pallas_call(
        powers_kernel,
        out_shape=jax.ShapeDtypeStruct((heads, rows, 2 * rows), jnp.float32),
        compiler_params=pltpu.CompilerParams(vmem_limit_bytes=VMEM_BYTES),
        cost_estimate=pl.CostEstimate(
            flops=4 * rows * rows * queries.shape[1],
            bytes_accessed=8 * heads * rows * rows,
            transcendentals=2 * heads * rows * rows,
        ),
    )(segments, queries, keys, behind_keys)


def weights_kernel(
    share_ref,
    core_share_ref,
    peer_share_ref,
    peer_core_share_ref,
    powers_ref,
    segments_ref,
    queries_ref,
    keys_ref,
    behind_keys_ref,
    weights_ref,
    own_mass_ref,
    behind_mass_ref,
    retention,
):
    seq_rank, head_rank = lax.axis_index("seq"), lax.axis_index("heads")
    rows = queries_ref.shape[0]
    kv_local = keys_ref.shape[1] // HEAD_DIM
    group_size = queries_ref.shape[1] // keys_ref.shape[1]
    logits = share_ref[...] + core_share_ref[...]
    logits = logits + (peer_share_ref[...] + peer_core_share_ref[...])
    log_gate = jnp.minimum(logits, 0.0) - jnp.log1p(jnp.exp(-jnp.abs(logits)))
    retention[...] = log_gate.astype(jnp.bfloat16).astype(jnp.float32)
    biases = []
    for g in range(kv_local):
        at = pl.ds(head_rank * kv_local + g, 1)
        biases.append(jnp.concatenate([retention[0, at, :], retention[seq_rank, at, :]], axis=1))
    moderate = jnp.min(functools.reduce(jnp.minimum, biases)) >= LEAST_RETENTION

    def finish(whole, terms_of):
        start = 0 if whole else rows
        for g in range(kv_local):
            mass = jnp.zeros((1, 2 * rows - start), jnp.float32)
            group_terms = terms_of(g, whole, start)
            for head in range(g * group_size, (g + 1) * group_size):
                weights = group_terms(head)
                weights = weights * (1.0 / jnp.sum(weights, axis=1, keepdims=True))
                mass = mass + jnp.sum(weights, axis=0, keepdims=True)
                weights_ref[head, :, start:] = weights.astype(jnp.bfloat16)
            mass = mass / group_size
            own_mass_ref[g : g + 1, :] = mass[:, rows - start :]
            behind_mass_ref[g : g + 1, :] = mass[:, :rows] if whole else jnp.zeros((1, rows))

    def by_powers(g, whole, start):
        factor = jnp.exp(biases[g] - jnp.max(biases[g]))[:, start:]
        return lambda head: powers_ref[head, :, start:] * factor

    def by_scores(g, whole, start):
        offset = hide_unseen(seq_rank, segments_ref, rows) + biases[g]
        keys = with_behind(keys_ref, behind_keys_ref, g, whole)

        def terms(head):
            scores = scores_of(queries_ref, keys, offset[:, start:], head)
            return jnp.exp(scores - jnp.max(scores, axis=1, keepdims=True))

        return terms

    pl.when(moderate & (seq_rank > 0))(lambda: finish(True, by_powers))
    pl.when(moderate & (seq_rank == 0))(lambda: finish(False, by_powers))
    pl.when(jnp.logical_not(moderate))(lambda: finish(True, by_scores))


def weights_of(shares, powers, segments, queries, keys, behind_keys):
    rows = queries.shape[0]
    mass = jax.ShapeDtypeStruct((keys.shape[1] // HEAD_DIM, rows), jnp.float32)
    return pl.pallas_call(
        weights_kernel,
        out_shape=(jax.ShapeDtypeStruct(powers.shape, jnp.bfloat16), mass, mass),
        scratch_shapes=[pltpu.VMEM(shares[0].shape, jnp.float32)],
        compiler_params=pltpu.CompilerParams(vmem_limit_bytes=VMEM_BYTES),
    )(*shares, powers, segments, queries, keys, behind_keys)


def attend_kernel(weights_ref, values_ref, behind_values_ref, attended_ref):
    seq_rank = lax.axis_index("seq")
    heads, rows = weights_ref.shape[:2]
    group_size = attended_ref.shape[1] // values_ref.shape[1]

    def fill(whole):
        start = 0 if whole else rows
        for head in range(heads):
            values = with_behind(values_ref, behind_values_ref, head // group_size, whole)
            attended_ref[:, head_columns(head)] = jnp.dot(
                weights_ref[head, :, start:], values, preferred_element_type=jnp.float32
            ).astype(jnp.bfloat16)

    pl.when(seq_rank > 0)(lambda: fill(True))
    pl.when(seq_rank == 0)(lambda: fill(False))


def attend(weights, values, behind_values):
    heads, rows = weights.shape[:2]
    return pl.pallas_call(
        attend_kernel,
        out_shape=jax.ShapeDtypeStruct((rows, heads * HEAD_DIM), jnp.bfloat16),
        compiler_params=pltpu.CompilerParams(vmem_limit_bytes=VMEM_BYTES),
        cost_estimate=pl.CostEstimate(
            flops=4 * rows * rows * heads * HEAD_DIM,
            bytes_accessed=2 * (weights.size + rows * heads * HEAD_DIM),
            transcendentals=0,
        ),
    )(weights, values, behind_values)


def pair_device(
    activations, conv_taps, gate_in, gate_out, queries, key_vectors, value_vectors, segment_ids
):
    rows = activations.shape[0]
    swap = [(0, 1), (1, 0)]
    segments = segment_ids.reshape(2, rows)
    gate_out = jnp.transpose(gate_out)

    peer_rows = lax.ppermute(activations, "seq", swap)

    def own_work(activations, conv_taps, gate_in, gate_out):
        kept, given, *held = own_project(activations, conv_taps, gate_in)
        return partial_logits(*head_sum(kept, given), gate_out), held

    own_share, held = in_one_piece(own_work, activations, conv_taps, gate_in, gate_out)
    peer_rows, own_share, held = lax.optimization_barrier((peer_rows, own_share, held))
    kept, given = peer_project(peer_rows, *held)
    behind_keys = lax.ppermute(key_vectors, "seq", swap)
    behind_values = lax.ppermute(value_vectors, "seq", swap)
    share = logits_share(own_share, *head_sum(kept, given), gate_out)
    share, queries = lax.optimization_barrier((share, queries))
    powers = powers_of(segments, queries, key_vectors, behind_keys)
    count = lax.axis_size("heads")
    both = [
        (seq * count + head, (1 - seq) * count + (head ^ 1))
        for seq in range(2)
        for head in range(count)
    ]
    shares = (
        share,
        exchange_heads(share, 1),
        lax.ppermute(share, "seq", swap),
        lax.ppermute(share, ("seq", "heads"), both),
    )
    weights, own_mass, behind_mass = weights_of(
        shares,
        powers,
        segments,
        queries,
        key_vectors,
        behind_keys,
    )
    attended = attend(weights, value_vectors, behind_values)
    key_mass = own_mass + lax.ppermute(behind_mass, "seq", swap)
    return (attended, key_mass.astype(jnp.bfloat16))


def from_behind(block, axis, distance):
    devices = range(lax.axis_size(axis))
    route = [(i - distance, i) for i in devices if i - distance in devices]
    return lax.ppermute(block, axis, route)


def block_scores(query_heads, key_block, bias_block, allowed, score_scale):
    scores = (
        jnp.einsum("tgeh,kgh->getk", query_heads, key_block, preferred_element_type=jnp.float32)
        * score_scale
    )
    scores = scores + jnp.transpose(bias_block.astype(jnp.float32))[:, None, None, :]
    return jnp.where(allowed[None, None], scores, NEG_FILL)


def ring_device(
    activations, conv_taps, gate_in, gate_out, queries, key_vectors, value_vectors, segment_ids
):
    shard_rows = activations.shape[0]
    tap_count = conv_taps.shape[0]
    rim_rows = from_behind(activations[shard_rows - (tap_count - 1) :], "seq", 1)
    widened = jnp.concatenate([rim_rows, activations], 0).astype(jnp.float32)
    summed = jnp.zeros(activations.shape, jnp.float32)
    for shift_back in range(tap_count):
        start_row = tap_count - 1 - shift_back
        summed = (
            summed
            + conv_taps[shift_back].astype(jnp.float32)
            * widened[start_row : start_row + shard_rows]
        )
    mixed_rows = summed.astype(jnp.bfloat16)
    partial_hidden = jnp.dot(
        mixed_rows,
        lax.all_gather(gate_in, "seq", axis=1, tiled=True),
        preferred_element_type=jnp.float32,
    )
    kv_local = key_vectors.shape[1] // HEAD_DIM
    group_size = QUERY_HEADS // KV_HEADS
    head_rank = lax.axis_index("heads")
    hidden = jax.nn.silu(lax.psum(partial_hidden, "heads")).astype(jnp.bfloat16)
    logits = jnp.dot(hidden, gate_out, preferred_element_type=jnp.float32)
    retention = lax.dynamic_slice_in_dim(
        jax.nn.log_sigmoid(logits).astype(jnp.bfloat16), head_rank * kv_local, kv_local, 1
    )
    seq_rank = lax.axis_index("seq")
    local_index = jnp.arange(shard_rows, dtype=jnp.int32)
    own_queries, own_keys, own_values, own_bias = (queries, key_vectors, value_vectors, retention)
    query_places = seq_rank * shard_rows + local_index
    query_segments = jnp.take(segment_ids, query_places)
    query_heads = own_queries.reshape(shard_rows, kv_local, group_size, HEAD_DIM)
    score_scale = 1.0 / math.sqrt(HEAD_DIM)

    def visibility(flat_index):
        key_segments = jnp.take(segment_ids, flat_index)
        return (flat_index[None, :] <= query_places[:, None]) & (
            key_segments[None, :] == query_segments[:, None]
        )

    initial = (
        jnp.full((kv_local, group_size, shard_rows), NEG_FILL, jnp.float32),
        jnp.zeros((kv_local, group_size, shard_rows), jnp.float32),
    )
    all_keys, all_values, all_bias = (
        lax.all_gather(own_keys, "seq", axis=0, tiled=True),
        lax.all_gather(own_values, "seq", axis=0, tiled=True),
        lax.all_gather(own_bias, "seq", axis=0, tiled=True),
    )
    piece_rows = all_keys.shape[0]
    stats_block_width = math.gcd(piece_rows, 512)

    def one_block(block_number, state_in):
        offset = block_number * stats_block_width
        key_block = lax.dynamic_slice_in_dim(all_keys, offset, stats_block_width, 0).reshape(
            stats_block_width, kv_local, HEAD_DIM
        )
        bias_block = lax.dynamic_slice_in_dim(all_bias, offset, stats_block_width, 0)
        allowed = visibility(0 + offset + jnp.arange(stats_block_width, dtype=jnp.int32))

        def update(state_old):
            peak_old, mass_old = state_old
            masked = block_scores(query_heads, key_block, bias_block, allowed, score_scale)
            peak_new = jnp.maximum(peak_old, jnp.max(masked, axis=3))
            exponent = jnp.where(allowed[None, None], jnp.exp(masked - peak_new[..., None]), 0.0)
            return (peak_new, mass_old * jnp.exp(peak_old - peak_new) + jnp.sum(exponent, axis=3))

        def keep_state(state_old):
            return state_old

        return lax.cond(jnp.any(allowed), update, keep_state, state_in)

    row_peak, total_mass = lax.fori_loop(0, piece_rows // stats_block_width, one_block, initial)
    total_keys = all_keys.shape[0]
    block_width = math.gcd(total_keys, 512)
    block_count = total_keys // block_width
    key_blocks = all_keys.reshape(block_count, block_width, kv_local, HEAD_DIM)
    value_blocks = all_values.reshape(block_count, block_width, kv_local, HEAD_DIM)
    bias_blocks = all_bias.reshape(block_count, block_width, kv_local)

    def second_pass(accumulated, block_items):
        block_number, key_block, value_block, bias_block = block_items
        allowed = visibility(block_number * block_width + jnp.arange(block_width, dtype=jnp.int32))

        def attend(accum_in):
            masked = block_scores(query_heads, key_block, bias_block, allowed, score_scale)
            weights = (
                jnp.where(allowed[None, None], jnp.exp(masked - row_peak[..., None]), 0.0)
                / total_mass[..., None]
            )
            accum_out = accum_in + jnp.einsum(
                "getk,kgh->tgeh",
                weights.astype(jnp.bfloat16),
                value_block,
                preferred_element_type=jnp.float32,
            )
            return (accum_out, jnp.transpose(jnp.sum(weights, axis=(1, 2))) / group_size)

        def skip_block(accum_in):
            return (accum_in, jnp.zeros((block_width, kv_local), jnp.float32))

        return lax.cond(jnp.any(allowed), attend, skip_block, accumulated)

    accumulated, mass_blocks = lax.scan(
        second_pass,
        jnp.zeros((shard_rows, kv_local, group_size, HEAD_DIM), jnp.float32),
        (jnp.arange(block_count, dtype=jnp.int32), key_blocks, value_blocks, bias_blocks),
    )
    key_term = mass_blocks.reshape(total_keys, kv_local)
    key_mass = lax.psum_scatter(key_term, "seq", scatter_dimension=0, tiled=True).astype(
        jnp.bfloat16
    )
    attended = accumulated.reshape(shard_rows, kv_local * group_size * HEAD_DIM).astype(
        jnp.bfloat16
    )
    return (attended, jnp.transpose(key_mass))


def solution(mesh):
    return jax.shard_map(
        pair_device if mesh.shape["seq"] == 2 else ring_device,
        mesh=mesh,
        in_specs=(
            P(("dp", "seq"), "heads"),
            P(None, "heads"),
            P("heads", "seq"),
            P(),
            P(("dp", "seq"), "heads"),
            P(("dp", "seq"), "heads"),
            P(("dp", "seq"), "heads"),
            P("dp"),
        ),
        out_specs=(P(("dp", "seq"), "heads"), P("heads", ("dp", "seq"))),
        check_vma=False,
    )
```

```python
import functools
import math

import jax
import jax.numpy as jnp
from jax import lax
from jax.experimental import pallas as pl
from jax.experimental.pallas import tpu as pltpu
from jax.sharding import PartitionSpec as P

QUERY_HEADS = 64
KV_HEADS = 8
HEAD_DIM = 128


NEG_FILL = -1e30
RIM_ROWS = 16
LEAST_RETENTION = -40.0
VMEM_BYTES = 16 * 1024 * 1024


def convolve(widened, taps, lead, rows):
    summed = jnp.zeros((rows, widened.shape[1]), jnp.float32)
    for back in range(taps.shape[0]):
        summed = summed + taps[back : back + 1] * widened[lead - back : lead - back + rows]
    return summed.astype(jnp.bfloat16)


def split_by_core(total, kept_ref, given_ref):
    half = kept_ref.shape[1]
    low, high = total[:, :half], total[:, half:]
    even = lax.rem(lax.axis_index("heads"), 2) == 0
    kept_ref[...] = jnp.where(even, low, high)
    given_ref[...] = jnp.where(even, high, low)


def own_project_kernel(
    rows_ref, taps_ref, gate_ref, kept_ref, given_ref, held_taps_ref, held_ref, widened
):
    rows, features = rows_ref.shape
    held_taps_ref[...] = taps_ref[...].astype(jnp.float32)
    held_ref[:features] = gate_ref[...]
    tile = widened.shape[2]
    total = jnp.zeros((rows - RIM_ROWS, gate_ref.shape[1]), jnp.float32)
    for step in range(features // tile):
        columns = slice(step * tile, (step + 1) * tile)
        edges = features + step * 2 * RIM_ROWS
        held_ref[edges : edges + RIM_ROWS, :tile] = rows_ref[:RIM_ROWS, columns]
        held_ref[edges + RIM_ROWS : edges + 2 * RIM_ROWS, :tile] = rows_ref[
            rows - RIM_ROWS :, columns
        ]
        wide = widened.at[step % 2]
        wide[...] = rows_ref[:, columns].astype(jnp.float32)
        taps = taps_ref[:, columns].astype(jnp.float32)
        mixed = convolve(wide, taps, RIM_ROWS, rows - RIM_ROWS)
        total = total + jnp.dot(mixed, gate_ref[columns, :], preferred_element_type=jnp.float32)
    split_by_core(total, kept_ref, given_ref)


def peer_project_kernel(
    peer_ref, taps_ref, held_ref, kept_ref, given_ref, widened, own_widened
):
    rows, features = peer_ref.shape
    tile = widened.shape[2]
    first = lax.axis_index("seq") == 0
    total = jnp.zeros((kept_ref.shape[0], held_ref.shape[1]), jnp.float32)
    for step in range(features // tile):
        columns = slice(step * tile, (step + 1) * tile)
        wide, own_wide = widened.at[step % 2], own_widened.at[step % 2]
        edges = held_ref.at[
            features + step * 2 * RIM_ROWS : features + (step + 1) * 2 * RIM_ROWS, :tile
        ]
        own_tail = edges[RIM_ROWS:].astype(jnp.float32)
        peer_tail = peer_ref[rows - RIM_ROWS :, columns].astype(jnp.float32)
        wide[:RIM_ROWS] = jnp.where(first, own_tail, 0.0)
        wide[RIM_ROWS:] = peer_ref[:, columns].astype(jnp.float32)
        own_wide[:RIM_ROWS] = jnp.where(first, 0.0, peer_tail)
        own_wide[RIM_ROWS:] = edges[:RIM_ROWS].astype(jnp.float32)
        taps = taps_ref[:, columns].astype(jnp.float32)
        mixed = jnp.concatenate(
            [
                convolve(own_wide, taps, RIM_ROWS, RIM_ROWS),
                convolve(wide, taps, RIM_ROWS, rows),
            ],
            axis=0,
        )
        total = total + jnp.dot(mixed, held_ref[columns, :], preferred_element_type=jnp.float32)
    split_by_core(total, kept_ref, given_ref)


def own_project(activations, conv_taps, gate_in):
    rows, features = activations.shape
    done = rows - RIM_ROWS
    tile = math.gcd(features, gate_in.shape[1])
    return pl.pallas_call(
        own_project_kernel,
        out_shape=(
            jax.ShapeDtypeStruct((done, gate_in.shape[1] // 2), jnp.float32),
            jax.ShapeDtypeStruct((done, gate_in.shape[1] // 2), jnp.float32),
            jax.ShapeDtypeStruct(conv_taps.shape, jnp.float32),
            jax.ShapeDtypeStruct(
                (features + features // tile * 2 * RIM_ROWS, gate_in.shape[1]), gate_in.dtype
            ),
        ),
        scratch_shapes=[pltpu.VMEM((2, rows, tile), jnp.float32)],
        compiler_params=pltpu.CompilerParams(vmem_limit_bytes=VMEM_BYTES),
        cost_estimate=pl.CostEstimate(flops=1, bytes_accessed=1, transcendentals=0),
    )(activations, conv_taps, gate_in)


def peer_project(peer_rows, taps, held):
    rows, features = peer_rows.shape
    done = rows + RIM_ROWS
    tile = math.gcd(features, held.shape[1])
    half = held.shape[1] // 2
    return pl.pallas_call(
        peer_project_kernel,
        out_shape=(
            jax.ShapeDtypeStruct((done, half), jnp.float32),
            jax.ShapeDtypeStruct((done, half), jnp.float32),
        ),
        scratch_shapes=[
            pltpu.VMEM((2, rows + RIM_ROWS, tile), jnp.float32),
            pltpu.VMEM((2, 2 * RIM_ROWS, tile), jnp.float32),
        ],
        compiler_params=pltpu.CompilerParams(vmem_limit_bytes=VMEM_BYTES),
        cost_estimate=pl.CostEstimate(flops=1, bytes_accessed=1, transcendentals=0),
    )(peer_rows, taps, held)


def exchange_heads(block, step):
    count = lax.axis_size("heads")
    return lax.ppermute(block, "heads", [(i, i ^ step) for i in range(count)])


def head_sum(kept, given):
    received = exchange_heads(given, 1)
    step = 2
    while step < lax.axis_size("heads"):
        kept = kept + received.astype(jnp.float32)
        received = exchange_heads(kept.astype(jnp.bfloat16), step)
        step *= 2
    return kept, received


def in_one_piece(work, *given):
    shapes = jax.eval_shape(work, *given)
    return lax.cond(
        lax.axis_index("seq") >= 0,
        work,
        lambda *given: jax.tree.map(lambda like: jnp.zeros(like.shape, like.dtype), shapes),
        *given,
    )


def share_of_logits(kept_ref, in_ref, gate_out_ref):
    pre = kept_ref[...] + in_ref[...].astype(jnp.float32)
    hidden = (pre / (1.0 + jnp.exp(-pre))).astype(jnp.bfloat16)
    half = pre.shape[1]
    part = 2 * lax.axis_index("seq") + lax.rem(lax.axis_index("heads"), 2)
    gate_columns = gate_out_ref[:, pl.ds(pl.multiple_of(part * half, HEAD_DIM), half)]
    return lax.dot_general(
        gate_columns, hidden, (((1,), (1,)), ((), ())), preferred_element_type=jnp.float32
    )


def partial_logits_kernel(kept_ref, in_ref, gate_out_ref, out_ref):
    out_ref[...] = share_of_logits(kept_ref, in_ref, gate_out_ref)


def partial_logits(kept, received, gate_out):
    return pl.pallas_call(
        partial_logits_kernel,
        out_shape=jax.ShapeDtypeStruct((gate_out.shape[0], kept.shape[0]), jnp.float32),
        compiler_params=pltpu.CompilerParams(vmem_limit_bytes=VMEM_BYTES),
    )(kept, received, gate_out)


def logits_kernel(own_ref, kept_ref, in_ref, gate_out_ref, out_ref):
    first = lax.axis_index("seq") == 0
    share = share_of_logits(kept_ref, in_ref, gate_out_ref)
    own = jnp.concatenate([share[:, :RIM_ROWS], own_ref[...]], axis=1)
    peer = share[:, RIM_ROWS:]
    out_ref[0] = jnp.where(first, own, peer)
    out_ref[1] = jnp.where(first, peer, own)


def logits_share(own_share, kept, received, gate_out):
    rows = own_share.shape[1] + RIM_ROWS
    return pl.pallas_call(
        logits_kernel,
        out_shape=jax.ShapeDtypeStruct((2, gate_out.shape[0], rows), jnp.float32),
        compiler_params=pltpu.CompilerParams(vmem_limit_bytes=VMEM_BYTES),
    )(own_share, kept, received, gate_out)


def hide_unseen(seq_rank, segments_ref, rows):
    own_segments = segments_ref[pl.ds(seq_rank, 1), :]
    behind_segments = segments_ref[pl.ds(0, 1), :]
    query_segments = jnp.transpose(jnp.broadcast_to(own_segments, (rows, rows)))
    query_at = lax.broadcasted_iota(jnp.int32, (rows, rows), 0)
    key_at = lax.broadcasted_iota(jnp.int32, (rows, rows), 1)
    see_own = (key_at <= query_at) & (query_segments == own_segments)
    see_behind = (query_segments == behind_segments) & (seq_rank > 0)
    return jnp.where(jnp.concatenate([see_behind, see_own], axis=1), 0.0, NEG_FILL)


def head_columns(number):
    return slice(number * HEAD_DIM, (number + 1) * HEAD_DIM)


def scores_of(queries_ref, keys, offset, head):
    scores = lax.dot_general(
        queries_ref[:, head_columns(head)],
        keys,
        (((1,), (1,)), ((), ())),
        preferred_element_type=jnp.float32,
    )
    return scores * (1.0 / math.sqrt(HEAD_DIM)) + offset


def with_behind(ref, behind_ref, number, whole):
    own = ref[:, head_columns(number)]
    if not whole:
        return own
    return jnp.concatenate([behind_ref[:, head_columns(number)], own], axis=0)


def powers_kernel(segments_ref, queries_ref, keys_ref, behind_keys_ref, powers_ref):
    seq_rank = lax.axis_index("seq")
    rows = queries_ref.shape[0]
    kv_local = keys_ref.shape[1] // HEAD_DIM
    group_size = queries_ref.shape[1] // keys_ref.shape[1]
    hide = hide_unseen(seq_rank, segments_ref, rows)

    def fill(whole):
        start = 0 if whole else rows
        for head in range(kv_local * group_size):
            g = head // group_size
            keys = with_behind(keys_ref, behind_keys_ref, g, whole)
            scores = scores_of(queries_ref, keys, hide[:, start:], head)
            powers_ref[head, :, start:] = jnp.exp(
                scores - jnp.max(scores, axis=1, keepdims=True)
            )

    pl.when(seq_rank > 0)(lambda: fill(True))
    pl.when(seq_rank == 0)(lambda: fill(False))


def powers_of(segments, queries, keys, behind_keys):
    rows = queries.shape[0]
    heads = queries.shape[1] // HEAD_DIM
    return pl.pallas_call(
        powers_kernel,
        out_shape=jax.ShapeDtypeStruct((heads, rows, 2 * rows), jnp.float32),
        compiler_params=pltpu.CompilerParams(vmem_limit_bytes=VMEM_BYTES),
        cost_estimate=pl.CostEstimate(
            flops=4 * rows * rows * queries.shape[1],
            bytes_accessed=8 * heads * rows * rows,
            transcendentals=2 * heads * rows * rows,
        ),
    )(segments, queries, keys, behind_keys)


def read_retention(share_refs, retention):
    seq_rank, head_rank = lax.axis_index("seq"), lax.axis_index("heads")
    logits = share_refs[0][...] + share_refs[1][...]
    logits = logits + (share_refs[2][...] + share_refs[3][...])
    log_gate = jnp.minimum(logits, 0.0) - jnp.log1p(jnp.exp(-jnp.abs(logits)))
    retention[...] = log_gate.astype(jnp.bfloat16).astype(jnp.float32)
    kv_local = retention.shape[1] // lax.axis_size("heads")
    biases = []
    for g in range(kv_local):
        at = pl.ds(head_rank * kv_local + g, 1)
        biases.append(jnp.concatenate([retention[0, at, :], retention[seq_rank, at, :]], axis=1))
    return biases


def weigh(whole, biases, powers_ref, segments_ref, queries_ref, keys_ref, behind_keys_ref, use):
    seq_rank = lax.axis_index("seq")
    rows = queries_ref.shape[0]
    group_size = queries_ref.shape[1] // keys_ref.shape[1]
    start = 0 if whole else rows
    moderate = jnp.min(functools.reduce(jnp.minimum, biases)) >= LEAST_RETENTION

    def finish(terms_of, store_mass):
        for g in range(len(biases)):
            mass = jnp.zeros((1, 2 * rows - start), jnp.float32)
            group_terms = terms_of(g)
            for head in range(g * group_size, (g + 1) * group_size):
                weights = group_terms(head)
                weights = weights * (1.0 / jnp.sum(weights, axis=1, keepdims=True))
                mass = mass + jnp.sum(weights, axis=0, keepdims=True)
                use(head, weights.astype(jnp.bfloat16))
            store_mass(g, mass / group_size)

    def by_powers(g):
        factor = jnp.exp(biases[g] - jnp.max(biases[g]))[:, start:]
        return lambda head: powers_ref[head, :, start:] * factor

    def by_scores(g):
        offset = (hide_unseen(seq_rank, segments_ref, rows) + biases[g])[:, start:]
        keys = with_behind(keys_ref, behind_keys_ref, g, whole)

        def terms(head):
            scores = scores_of(queries_ref, keys, offset, head)
            return jnp.exp(scores - jnp.max(scores, axis=1, keepdims=True))

        return terms

    def run(store_mass):
        pl.when(moderate)(lambda: finish(by_powers, store_mass))
        pl.when(jnp.logical_not(moderate))(lambda: finish(by_scores, store_mass))

    return run


def weights_kernel(*refs):
    *share_refs, powers_ref, segments_ref, queries_ref, keys_ref, behind_keys_ref = refs[:9]
    weights_ref, own_mass_ref, behind_mass_ref, retention = refs[9:]
    rows = queries_ref.shape[0]

    def whole():
        def use(head, weights):
            weights_ref[head] = weights

        def store_mass(g, mass):
            behind_mass_ref[g : g + 1, :] = mass[:, :rows]
            own_mass_ref[g : g + 1, :] = mass[:, rows:]

        biases = read_retention(share_refs, retention)
        weigh(
            True, biases, powers_ref, segments_ref, queries_ref, keys_ref, behind_keys_ref, use
        )(store_mass)

    def nothing():
        behind_mass_ref[...] = jnp.zeros(behind_mass_ref.shape, jnp.float32)

    pl.when(lax.axis_index("seq") > 0)(whole)
    pl.when(lax.axis_index("seq") == 0)(nothing)


def weights_of(shares, powers, segments, queries, keys, behind_keys):
    rows = queries.shape[0]
    mass = jax.ShapeDtypeStruct((keys.shape[1] // HEAD_DIM, rows), jnp.float32)
    return pl.pallas_call(
        weights_kernel,
        out_shape=(jax.ShapeDtypeStruct(powers.shape, jnp.bfloat16), mass, mass),
        scratch_shapes=[pltpu.VMEM(shares[0].shape, jnp.float32)],
        compiler_params=pltpu.CompilerParams(vmem_limit_bytes=VMEM_BYTES),
    )(*shares, powers, segments, queries, keys, behind_keys)


def attend_kernel(*refs):
    *share_refs, powers_ref, segments_ref, queries_ref, keys_ref, behind_keys_ref = refs[:9]
    weights_ref, mass_ref, values_ref, behind_values_ref = refs[9:13]
    attended_ref, own_mass_ref, retention = refs[13:]
    group_size = attended_ref.shape[1] // values_ref.shape[1]

    def attend_head(head, weights, whole):
        values = with_behind(values_ref, behind_values_ref, head // group_size, whole)
        attended_ref[:, head_columns(head)] = jnp.dot(
            weights, values, preferred_element_type=jnp.float32
        ).astype(jnp.bfloat16)

    def whole():
        own_mass_ref[...] = mass_ref[...]
        for head in range(weights_ref.shape[0]):
            attend_head(head, weights_ref[head], True)

    def alone():
        def use(head, weights):
            attend_head(head, weights, False)

        def store_mass(g, mass):
            own_mass_ref[g : g + 1, :] = mass

        biases = read_retention(share_refs, retention)
        weigh(
            False, biases, powers_ref, segments_ref, queries_ref, keys_ref, behind_keys_ref, use
        )(store_mass)

    pl.when(lax.axis_index("seq") > 0)(whole)
    pl.when(lax.axis_index("seq") == 0)(alone)


def attend(shares, powers, segments, queries, keys, behind_keys, weights, mass, values, behind):
    rows = queries.shape[0]
    return pl.pallas_call(
        attend_kernel,
        out_shape=(
            jax.ShapeDtypeStruct(queries.shape, jnp.bfloat16),
            jax.ShapeDtypeStruct(mass.shape, jnp.float32),
        ),
        scratch_shapes=[pltpu.VMEM(shares[0].shape, jnp.float32)],
        compiler_params=pltpu.CompilerParams(vmem_limit_bytes=VMEM_BYTES),
        cost_estimate=pl.CostEstimate(
            flops=4 * rows * rows * queries.shape[1],
            bytes_accessed=2 * (weights.size + queries.size),
            transcendentals=0,
        ),
    )(*shares, powers, segments, queries, keys, behind_keys, weights, mass, values, behind)


def pair_device(
    activations, conv_taps, gate_in, gate_out, queries, key_vectors, value_vectors, segment_ids
):
    rows = activations.shape[0]
    swap = [(0, 1), (1, 0)]
    segments = segment_ids.reshape(2, rows)
    gate_out = jnp.transpose(gate_out)

    peer_rows = lax.ppermute(activations, "seq", swap)

    def own_work(activations, conv_taps, gate_in, gate_out):
        kept, given, *held = own_project(activations, conv_taps, gate_in)
        return partial_logits(*head_sum(kept, given), gate_out), held

    own_share, held = in_one_piece(own_work, activations, conv_taps, gate_in, gate_out)
    peer_rows, own_share, held = lax.optimization_barrier((peer_rows, own_share, held))
    kept, given = peer_project(peer_rows, *held)
    behind_keys = lax.ppermute(key_vectors, "seq", swap)
    behind_values = lax.ppermute(value_vectors, "seq", swap)
    share = logits_share(own_share, *head_sum(kept, given), gate_out)
    share, queries = lax.optimization_barrier((share, queries))
    powers = powers_of(segments, queries, key_vectors, behind_keys)
    count = lax.axis_size("heads")
    both = [
        (seq * count + head, (1 - seq) * count + (head ^ 1))
        for seq in range(2)
        for head in range(count)
    ]
    shares = (
        share,
        exchange_heads(share, 1),
        lax.ppermute(share, "seq", swap),
        lax.ppermute(share, ("seq", "heads"), both),
    )
    given = (shares, powers, segments, queries, key_vectors, behind_keys)
    weights, own_mass, behind_mass = weights_of(*given)
    attended, own_mass = attend(*given, weights, own_mass, value_vectors, behind_values)
    key_mass = own_mass + lax.ppermute(behind_mass, "seq", swap)
    return (attended, key_mass.astype(jnp.bfloat16))


def from_behind(block, axis, distance):
    devices = range(lax.axis_size(axis))
    route = [(i - distance, i) for i in devices if i - distance in devices]
    return lax.ppermute(block, axis, route)


def block_scores(query_heads, key_block, bias_block, allowed, score_scale):
    scores = (
        jnp.einsum("tgeh,kgh->getk", query_heads, key_block, preferred_element_type=jnp.float32)
        * score_scale
    )
    scores = scores + jnp.transpose(bias_block.astype(jnp.float32))[:, None, None, :]
    return jnp.where(allowed[None, None], scores, NEG_FILL)


def ring_device(
    activations, conv_taps, gate_in, gate_out, queries, key_vectors, value_vectors, segment_ids
):
    shard_rows = activations.shape[0]
    tap_count = conv_taps.shape[0]
    rim_rows = from_behind(activations[shard_rows - (tap_count - 1) :], "seq", 1)
    widened = jnp.concatenate([rim_rows, activations], 0).astype(jnp.float32)
    summed = jnp.zeros(activations.shape, jnp.float32)
    for shift_back in range(tap_count):
        start_row = tap_count - 1 - shift_back
        summed = (
            summed
            + conv_taps[shift_back].astype(jnp.float32)
            * widened[start_row : start_row + shard_rows]
        )
    mixed_rows = summed.astype(jnp.bfloat16)
    partial_hidden = jnp.dot(
        mixed_rows,
        lax.all_gather(gate_in, "seq", axis=1, tiled=True),
        preferred_element_type=jnp.float32,
    )
    kv_local = key_vectors.shape[1] // HEAD_DIM
    group_size = QUERY_HEADS // KV_HEADS
    head_rank = lax.axis_index("heads")
    hidden = jax.nn.silu(lax.psum(partial_hidden, "heads")).astype(jnp.bfloat16)
    logits = jnp.dot(hidden, gate_out, preferred_element_type=jnp.float32)
    retention = lax.dynamic_slice_in_dim(
        jax.nn.log_sigmoid(logits).astype(jnp.bfloat16), head_rank * kv_local, kv_local, 1
    )
    seq_rank = lax.axis_index("seq")
    local_index = jnp.arange(shard_rows, dtype=jnp.int32)
    own_queries, own_keys, own_values, own_bias = (queries, key_vectors, value_vectors, retention)
    query_places = seq_rank * shard_rows + local_index
    query_segments = jnp.take(segment_ids, query_places)
    query_heads = own_queries.reshape(shard_rows, kv_local, group_size, HEAD_DIM)
    score_scale = 1.0 / math.sqrt(HEAD_DIM)

    def visibility(flat_index):
        key_segments = jnp.take(segment_ids, flat_index)
        return (flat_index[None, :] <= query_places[:, None]) & (
            key_segments[None, :] == query_segments[:, None]
        )

    initial = (
        jnp.full((kv_local, group_size, shard_rows), NEG_FILL, jnp.float32),
        jnp.zeros((kv_local, group_size, shard_rows), jnp.float32),
    )
    all_keys, all_values, all_bias = (
        lax.all_gather(own_keys, "seq", axis=0, tiled=True),
        lax.all_gather(own_values, "seq", axis=0, tiled=True),
        lax.all_gather(own_bias, "seq", axis=0, tiled=True),
    )
    piece_rows = all_keys.shape[0]
    stats_block_width = math.gcd(piece_rows, 512)

    def one_block(block_number, state_in):
        offset = block_number * stats_block_width
        key_block = lax.dynamic_slice_in_dim(all_keys, offset, stats_block_width, 0).reshape(
            stats_block_width, kv_local, HEAD_DIM
        )
        bias_block = lax.dynamic_slice_in_dim(all_bias, offset, stats_block_width, 0)
        allowed = visibility(0 + offset + jnp.arange(stats_block_width, dtype=jnp.int32))

        def update(state_old):
            peak_old, mass_old = state_old
            masked = block_scores(query_heads, key_block, bias_block, allowed, score_scale)
            peak_new = jnp.maximum(peak_old, jnp.max(masked, axis=3))
            exponent = jnp.where(allowed[None, None], jnp.exp(masked - peak_new[..., None]), 0.0)
            return (peak_new, mass_old * jnp.exp(peak_old - peak_new) + jnp.sum(exponent, axis=3))

        def keep_state(state_old):
            return state_old

        return lax.cond(jnp.any(allowed), update, keep_state, state_in)

    row_peak, total_mass = lax.fori_loop(0, piece_rows // stats_block_width, one_block, initial)
    total_keys = all_keys.shape[0]
    block_width = math.gcd(total_keys, 512)
    block_count = total_keys // block_width
    key_blocks = all_keys.reshape(block_count, block_width, kv_local, HEAD_DIM)
    value_blocks = all_values.reshape(block_count, block_width, kv_local, HEAD_DIM)
    bias_blocks = all_bias.reshape(block_count, block_width, kv_local)

    def second_pass(accumulated, block_items):
        block_number, key_block, value_block, bias_block = block_items
        allowed = visibility(block_number * block_width + jnp.arange(block_width, dtype=jnp.int32))

        def attend(accum_in):
            masked = block_scores(query_heads, key_block, bias_block, allowed, score_scale)
            weights = (
                jnp.where(allowed[None, None], jnp.exp(masked - row_peak[..., None]), 0.0)
                / total_mass[..., None]
            )
            accum_out = accum_in + jnp.einsum(
                "getk,kgh->tgeh",
                weights.astype(jnp.bfloat16),
                value_block,
                preferred_element_type=jnp.float32,
            )
            return (accum_out, jnp.transpose(jnp.sum(weights, axis=(1, 2))) / group_size)

        def skip_block(accum_in):
            return (accum_in, jnp.zeros((block_width, kv_local), jnp.float32))

        return lax.cond(jnp.any(allowed), attend, skip_block, accumulated)

    accumulated, mass_blocks = lax.scan(
        second_pass,
        jnp.zeros((shard_rows, kv_local, group_size, HEAD_DIM), jnp.float32),
        (jnp.arange(block_count, dtype=jnp.int32), key_blocks, value_blocks, bias_blocks),
    )
    key_term = mass_blocks.reshape(total_keys, kv_local)
    key_mass = lax.psum_scatter(key_term, "seq", scatter_dimension=0, tiled=True).astype(
        jnp.bfloat16
    )
    attended = accumulated.reshape(shard_rows, kv_local * group_size * HEAD_DIM).astype(
        jnp.bfloat16
    )
    return (attended, jnp.transpose(key_mass))


def solution(mesh):
    return jax.shard_map(
        pair_device if mesh.shape["seq"] == 2 else ring_device,
        mesh=mesh,
        in_specs=(
            P(("dp", "seq"), "heads"),
            P(None, "heads"),
            P("heads", "seq"),
            P(),
            P(("dp", "seq"), "heads"),
            P(("dp", "seq"), "heads"),
            P(("dp", "seq"), "heads"),
            P("dp"),
        ),
        out_specs=(P(("dp", "seq"), "heads"), P("heads", ("dp", "seq"))),
        check_vma=False,
    )
```

```python
import functools
import math

import jax
import jax.numpy as jnp
from jax import lax
from jax.experimental import pallas as pl
from jax.experimental.pallas import tpu as pltpu
from jax.sharding import PartitionSpec as P

QUERY_HEADS = 64
KV_HEADS = 8
HEAD_DIM = 128


NEG_FILL = -1e30
RIM_ROWS = 16
LEAST_RETENTION = -40.0
VMEM_BYTES = 16 * 1024 * 1024


def convolve(widened, taps, lead, rows):
    summed = jnp.zeros((rows, widened.shape[1]), jnp.float32)
    for back in range(taps.shape[0]):
        summed = summed + taps[back : back + 1] * widened[lead - back : lead - back + rows]
    return summed.astype(jnp.bfloat16)


def own_project_kernel(rows_ref, taps_ref, gate_ref, out_ref, held_taps_ref, held_ref, widened):
    rows, features = rows_ref.shape
    held_taps_ref[...] = taps_ref[...].astype(jnp.float32)
    held_ref[:features] = gate_ref[...]
    tile = widened.shape[2]
    total = jnp.zeros(out_ref.shape, jnp.float32)
    for step in range(features // tile):
        columns = slice(step * tile, (step + 1) * tile)
        edges = features + step * 2 * RIM_ROWS
        held_ref[edges : edges + RIM_ROWS, :tile] = rows_ref[:RIM_ROWS, columns]
        held_ref[edges + RIM_ROWS : edges + 2 * RIM_ROWS, :tile] = rows_ref[
            rows - RIM_ROWS :, columns
        ]
        wide = widened.at[step % 2]
        wide[...] = rows_ref[:, columns].astype(jnp.float32)
        taps = taps_ref[:, columns].astype(jnp.float32)
        mixed = convolve(wide, taps, RIM_ROWS, rows - RIM_ROWS)
        total = total + jnp.dot(mixed, gate_ref[columns, :], preferred_element_type=jnp.float32)
    out_ref[...] = total


def peer_project_kernel(
    peer_ref, taps_ref, held_ref, near_ref, far_ref, widened, own_widened
):
    rows, features = peer_ref.shape
    tile = widened.shape[2]
    first = lax.axis_index("seq") == 0
    half = near_ref.shape[1]
    total = jnp.zeros((near_ref.shape[0], 2 * half), jnp.float32)
    for step in range(features // tile):
        columns = slice(step * tile, (step + 1) * tile)
        wide, own_wide = widened.at[step % 2], own_widened.at[step % 2]
        edges = held_ref.at[
            features + step * 2 * RIM_ROWS : features + (step + 1) * 2 * RIM_ROWS, :tile
        ]
        own_tail = edges[RIM_ROWS:].astype(jnp.float32)
        peer_tail = peer_ref[rows - RIM_ROWS :, columns].astype(jnp.float32)
        wide[:RIM_ROWS] = jnp.where(first, own_tail, 0.0)
        wide[RIM_ROWS:] = peer_ref[:, columns].astype(jnp.float32)
        own_wide[:RIM_ROWS] = jnp.where(first, 0.0, peer_tail)
        own_wide[RIM_ROWS:] = edges[:RIM_ROWS].astype(jnp.float32)
        taps = taps_ref[:, columns].astype(jnp.float32)
        mixed = jnp.concatenate(
            [
                convolve(own_wide, taps, RIM_ROWS, RIM_ROWS),
                convolve(wide, taps, RIM_ROWS, rows),
            ],
            axis=0,
        )
        total = total + jnp.dot(mixed, held_ref[columns, :], preferred_element_type=jnp.float32)
    near_ref[...] = total[:, :half]
    far_ref[...] = total[:, half:].astype(jnp.bfloat16)


def own_project(activations, conv_taps, gate_in):
    rows, features = activations.shape
    done = rows - RIM_ROWS
    tile = math.gcd(features, gate_in.shape[1])
    return pl.pallas_call(
        own_project_kernel,
        out_shape=(
            jax.ShapeDtypeStruct((done, gate_in.shape[1]), jnp.float32),
            jax.ShapeDtypeStruct(conv_taps.shape, jnp.float32),
            jax.ShapeDtypeStruct(
                (features + features // tile * 2 * RIM_ROWS, gate_in.shape[1]), gate_in.dtype
            ),
        ),
        scratch_shapes=[pltpu.VMEM((2, rows, tile), jnp.float32)],
        compiler_params=pltpu.CompilerParams(vmem_limit_bytes=VMEM_BYTES),
        cost_estimate=pl.CostEstimate(flops=1, bytes_accessed=1, transcendentals=0),
    )(activations, conv_taps, gate_in)


def peer_project(peer_rows, taps, held):
    rows, features = peer_rows.shape
    done = rows + RIM_ROWS
    tile = math.gcd(features, held.shape[1])
    half = held.shape[1] // 2
    return pl.pallas_call(
        peer_project_kernel,
        out_shape=(
            jax.ShapeDtypeStruct((done, half), jnp.float32),
            jax.ShapeDtypeStruct((done, half), jnp.bfloat16),
        ),
        scratch_shapes=[
            pltpu.VMEM((2, rows + RIM_ROWS, tile), jnp.float32),
            pltpu.VMEM((2, 2 * RIM_ROWS, tile), jnp.float32),
        ],
        compiler_params=pltpu.CompilerParams(vmem_limit_bytes=VMEM_BYTES),
        cost_estimate=pl.CostEstimate(flops=1, bytes_accessed=1, transcendentals=0),
    )(peer_rows, taps, held)


def head_sum(part):
    count = lax.axis_size("heads")
    step = 1
    received = None
    while step < count:
        if received is not None:
            part = part + received.astype(jnp.float32)
        received = exchange_heads(part if step == 1 else part.astype(jnp.bfloat16), step)
        step *= 2
    return part, received


def exchange_heads(block, step):
    count = lax.axis_size("heads")
    return lax.ppermute(block, "heads", [(i, i ^ step) for i in range(count)])


def in_one_piece(work, *given):
    shapes = jax.eval_shape(work, *given)
    return lax.cond(
        lax.axis_index("seq") >= 0,
        work,
        lambda *given: jax.tree.map(lambda like: jnp.zeros(like.shape, like.dtype), shapes),
        *given,
    )


def far_logits(block, gate_out):
    step = lax.axis_size("heads") // 2
    received = exchange_heads(block, step)

    def nearer(block, received, gate_out):
        distance = step
        while distance > 1:
            distance //= 2
            block = block.astype(jnp.float32) + received.astype(jnp.float32)
            received = exchange_heads(block, distance)
        return partial_logits(block, received, gate_out, block.shape[1])

    return in_one_piece(nearer, block, received, gate_out)


def share_of_logits(pre_ref, in_ref, gate_out_ref, offset):
    pre = pre_ref[...] + in_ref[...].astype(jnp.float32)
    hidden = (pre / (1.0 + jnp.exp(-pre))).astype(jnp.bfloat16)
    share = gate_out_ref.shape[1] // lax.axis_size("seq")
    start = pl.multiple_of(lax.axis_index("seq") * share + offset, HEAD_DIM)
    gate_columns = gate_out_ref[:, pl.ds(start, pre.shape[1])]
    return lax.dot_general(
        gate_columns, hidden, (((1,), (1,)), ((), ())), preferred_element_type=jnp.float32
    )


def partial_logits_kernel(offset, own_ref, in_ref, gate_out_ref, out_ref):
    out_ref[...] = share_of_logits(own_ref, in_ref, gate_out_ref, offset)


def partial_logits(part, received, gate_out, offset):
    return pl.pallas_call(
        functools.partial(partial_logits_kernel, offset),
        out_shape=jax.ShapeDtypeStruct((gate_out.shape[0], part.shape[0]), jnp.float32),
        compiler_params=pltpu.CompilerParams(vmem_limit_bytes=VMEM_BYTES),
    )(part, received, gate_out)


def logits_kernel(own_ref, far_share_ref, near_ref, near_in_ref, gate_out_ref, out_ref):
    first = lax.axis_index("seq") == 0
    share = share_of_logits(near_ref, near_in_ref, gate_out_ref, 0) + far_share_ref[...]
    own = jnp.concatenate([share[:, :RIM_ROWS], own_ref[...]], axis=1)
    peer = share[:, RIM_ROWS:]
    out_ref[0] = jnp.where(first, own, peer)
    out_ref[1] = jnp.where(first, peer, own)


def logits_share(own_share, far_share, near, near_in, gate_out):
    rows = own_share.shape[1] + RIM_ROWS
    return pl.pallas_call(
        logits_kernel,
        out_shape=jax.ShapeDtypeStruct((2, gate_out.shape[0], rows), jnp.float32),
        compiler_params=pltpu.CompilerParams(vmem_limit_bytes=VMEM_BYTES),
    )(own_share, far_share, near, near_in, gate_out)


def hide_unseen(seq_rank, segments_ref, rows):
    own_segments = segments_ref[pl.ds(seq_rank, 1), :]
    behind_segments = segments_ref[pl.ds(0, 1), :]
    query_segments = jnp.transpose(jnp.broadcast_to(own_segments, (rows, rows)))
    query_at = lax.broadcasted_iota(jnp.int32, (rows, rows), 0)
    key_at = lax.broadcasted_iota(jnp.int32, (rows, rows), 1)
    see_own = (key_at <= query_at) & (query_segments == own_segments)
    see_behind = (query_segments == behind_segments) & (seq_rank > 0)
    return jnp.where(jnp.concatenate([see_behind, see_own], axis=1), 0.0, NEG_FILL)


def head_columns(number):
    return slice(number * HEAD_DIM, (number + 1) * HEAD_DIM)


def scores_of(queries_ref, keys, offset, head):
    scores = lax.dot_general(
        queries_ref[:, head_columns(head)],
        keys,
        (((1,), (1,)), ((), ())),
        preferred_element_type=jnp.float32,
    )
    return scores * (1.0 / math.sqrt(HEAD_DIM)) + offset


def with_behind(ref, behind_ref, number, whole):
    own = ref[:, head_columns(number)]
    if not whole:
        return own
    return jnp.concatenate([behind_ref[:, head_columns(number)], own], axis=0)


def powers_kernel(segments_ref, queries_ref, keys_ref, behind_keys_ref, powers_ref):
    seq_rank = lax.axis_index("seq")
    rows = queries_ref.shape[0]
    kv_local = keys_ref.shape[1] // HEAD_DIM
    group_size = queries_ref.shape[1] // keys_ref.shape[1]
    hide = hide_unseen(seq_rank, segments_ref, rows)

    def fill(whole):
        start = 0 if whole else rows
        for head in range(kv_local * group_size):
            g = head // group_size
            keys = with_behind(keys_ref, behind_keys_ref, g, whole)
            scores = scores_of(queries_ref, keys, hide[:, start:], head)
            powers_ref[head, :, start:] = jnp.exp(
                scores - jnp.max(scores, axis=1, keepdims=True)
            )

    pl.when(seq_rank > 0)(lambda: fill(True))
    pl.when(seq_rank == 0)(lambda: fill(False))


def powers_of(segments, queries, keys, behind_keys):
    rows = queries.shape[0]
    heads = queries.shape[1] // HEAD_DIM
    return pl.pallas_call(
        powers_kernel,
        out_shape=jax.ShapeDtypeStruct((heads, rows, 2 * rows), jnp.float32),
        compiler_params=pltpu.CompilerParams(vmem_limit_bytes=VMEM_BYTES),
        cost_estimate=pl.CostEstimate(
            flops=4 * rows * rows * queries.shape[1],
            bytes_accessed=8 * heads * rows * rows,
            transcendentals=2 * heads * rows * rows,
        ),
    )(segments, queries, keys, behind_keys)


def read_retention(share_refs, retention):
    seq_rank, head_rank = lax.axis_index("seq"), lax.axis_index("heads")
    logits = share_refs[0][...] + share_refs[1][...]
    log_gate = jnp.minimum(logits, 0.0) - jnp.log1p(jnp.exp(-jnp.abs(logits)))
    retention[...] = log_gate.astype(jnp.bfloat16).astype(jnp.float32)
    kv_local = retention.shape[1] // lax.axis_size("heads")
    biases = []
    for g in range(kv_local):
        at = pl.ds(head_rank * kv_local + g, 1)
        biases.append(jnp.concatenate([retention[0, at, :], retention[seq_rank, at, :]], axis=1))
    return biases


def weigh(whole, biases, powers_ref, segments_ref, queries_ref, keys_ref, behind_keys_ref, use):
    seq_rank = lax.axis_index("seq")
    rows = queries_ref.shape[0]
    group_size = queries_ref.shape[1] // keys_ref.shape[1]
    start = 0 if whole else rows
    moderate = jnp.min(functools.reduce(jnp.minimum, biases)) >= LEAST_RETENTION

    def finish(terms_of, store_mass):
        for g in range(len(biases)):
            mass = jnp.zeros((1, 2 * rows - start), jnp.float32)
            group_terms = terms_of(g)
            for head in range(g * group_size, (g + 1) * group_size):
                weights = group_terms(head)
                weights = weights * (1.0 / jnp.sum(weights, axis=1, keepdims=True))
                mass = mass + jnp.sum(weights, axis=0, keepdims=True)
                use(head, weights.astype(jnp.bfloat16))
            store_mass(g, mass / group_size)

    def by_powers(g):
        factor = jnp.exp(biases[g] - jnp.max(biases[g]))[:, start:]
        return lambda head: powers_ref[head, :, start:] * factor

    def by_scores(g):
        offset = (hide_unseen(seq_rank, segments_ref, rows) + biases[g])[:, start:]
        keys = with_behind(keys_ref, behind_keys_ref, g, whole)

        def terms(head):
            scores = scores_of(queries_ref, keys, offset, head)
            return jnp.exp(scores - jnp.max(scores, axis=1, keepdims=True))

        return terms

    def run(store_mass):
        pl.when(moderate)(lambda: finish(by_powers, store_mass))
        pl.when(jnp.logical_not(moderate))(lambda: finish(by_scores, store_mass))

    return run


def weights_kernel(*refs):
    *share_refs, powers_ref, segments_ref, queries_ref, keys_ref, behind_keys_ref = refs[:7]
    weights_ref, own_mass_ref, behind_mass_ref, retention = refs[7:]
    rows = queries_ref.shape[0]

    def whole():
        def use(head, weights):
            weights_ref[head] = weights

        def store_mass(g, mass):
            behind_mass_ref[g : g + 1, :] = mass[:, :rows]
            own_mass_ref[g : g + 1, :] = mass[:, rows:]

        biases = read_retention(share_refs, retention)
        weigh(
            True, biases, powers_ref, segments_ref, queries_ref, keys_ref, behind_keys_ref, use
        )(store_mass)

    def nothing():
        behind_mass_ref[...] = jnp.zeros(behind_mass_ref.shape, jnp.float32)

    pl.when(lax.axis_index("seq") > 0)(whole)
    pl.when(lax.axis_index("seq") == 0)(nothing)


def weights_of(shares, powers, segments, queries, keys, behind_keys):
    rows = queries.shape[0]
    mass = jax.ShapeDtypeStruct((keys.shape[1] // HEAD_DIM, rows), jnp.float32)
    return pl.pallas_call(
        weights_kernel,
        out_shape=(jax.ShapeDtypeStruct(powers.shape, jnp.bfloat16), mass, mass),
        scratch_shapes=[pltpu.VMEM(shares[0].shape, jnp.float32)],
        compiler_params=pltpu.CompilerParams(vmem_limit_bytes=VMEM_BYTES),
    )(*shares, powers, segments, queries, keys, behind_keys)


def attend_kernel(*refs):
    *share_refs, powers_ref, segments_ref, queries_ref, keys_ref, behind_keys_ref = refs[:7]
    weights_ref, mass_ref, values_ref, behind_values_ref = refs[7:11]
    attended_ref, own_mass_ref, retention = refs[11:]
    group_size = attended_ref.shape[1] // values_ref.shape[1]

    def attend_head(head, weights, whole):
        values = with_behind(values_ref, behind_values_ref, head // group_size, whole)
        attended_ref[:, head_columns(head)] = jnp.dot(
            weights, values, preferred_element_type=jnp.float32
        ).astype(jnp.bfloat16)

    def whole():
        own_mass_ref[...] = mass_ref[...]
        for head in range(weights_ref.shape[0]):
            attend_head(head, weights_ref[head], True)

    def alone():
        def use(head, weights):
            attend_head(head, weights, False)

        def store_mass(g, mass):
            own_mass_ref[g : g + 1, :] = mass

        biases = read_retention(share_refs, retention)
        weigh(
            False, biases, powers_ref, segments_ref, queries_ref, keys_ref, behind_keys_ref, use
        )(store_mass)

    pl.when(lax.axis_index("seq") > 0)(whole)
    pl.when(lax.axis_index("seq") == 0)(alone)


def attend(shares, powers, segments, queries, keys, behind_keys, weights, mass, values, behind):
    rows = queries.shape[0]
    return pl.pallas_call(
        attend_kernel,
        out_shape=(
            jax.ShapeDtypeStruct(queries.shape, jnp.bfloat16),
            jax.ShapeDtypeStruct(mass.shape, jnp.float32),
        ),
        scratch_shapes=[pltpu.VMEM(shares[0].shape, jnp.float32)],
        compiler_params=pltpu.CompilerParams(vmem_limit_bytes=VMEM_BYTES),
        cost_estimate=pl.CostEstimate(
            flops=4 * rows * rows * queries.shape[1],
            bytes_accessed=2 * (weights.size + queries.size),
            transcendentals=0,
        ),
    )(*shares, powers, segments, queries, keys, behind_keys, weights, mass, values, behind)


def pair_device(
    activations, conv_taps, gate_in, gate_out, queries, key_vectors, value_vectors, segment_ids
):
    rows = activations.shape[0]
    swap = [(0, 1), (1, 0)]
    segments = segment_ids.reshape(2, rows)
    gate_out = jnp.transpose(gate_out)

    peer_rows = lax.ppermute(activations, "seq", swap)

    def own_work(activations, conv_taps, gate_in, gate_out):
        part, *held = own_project(activations, conv_taps, gate_in)
        return partial_logits(*head_sum(part), gate_out, 0), held

    own_share, held = in_one_piece(own_work, activations, conv_taps, gate_in, gate_out)
    peer_rows, own_share, held = lax.optimization_barrier((peer_rows, own_share, held))
    near, far = peer_project(peer_rows, *held)
    behind_keys = lax.ppermute(key_vectors, "seq", swap)
    behind_values = lax.ppermute(value_vectors, "seq", swap)
    near, near_in = head_sum(near)
    far_share = far_logits(far, gate_out)
    share = logits_share(own_share, far_share, near, near_in, gate_out)
    share, queries = lax.optimization_barrier((share, queries))
    powers = powers_of(segments, queries, key_vectors, behind_keys)
    count = lax.axis_size("heads")
    across = [
        (seq * count + head, (1 - seq) * count + (head ^ 1))
        for seq in range(2)
        for head in range(count)
    ]
    shares = (share, lax.ppermute(share, ("seq", "heads"), across))
    given = (shares, powers, segments, queries, key_vectors, behind_keys)
    weights, own_mass, behind_mass = weights_of(*given)
    attended, own_mass = attend(*given, weights, own_mass, value_vectors, behind_values)
    key_mass = own_mass + lax.ppermute(behind_mass, "seq", swap)
    return (attended, key_mass.astype(jnp.bfloat16))


def from_behind(block, axis, distance):
    devices = range(lax.axis_size(axis))
    route = [(i - distance, i) for i in devices if i - distance in devices]
    return lax.ppermute(block, axis, route)


def block_scores(query_heads, key_block, bias_block, allowed, score_scale):
    scores = (
        jnp.einsum("tgeh,kgh->getk", query_heads, key_block, preferred_element_type=jnp.float32)
        * score_scale
    )
    scores = scores + jnp.transpose(bias_block.astype(jnp.float32))[:, None, None, :]
    return jnp.where(allowed[None, None], scores, NEG_FILL)


def ring_device(
    activations, conv_taps, gate_in, gate_out, queries, key_vectors, value_vectors, segment_ids
):
    shard_rows = activations.shape[0]
    tap_count = conv_taps.shape[0]
    rim_rows = from_behind(activations[shard_rows - (tap_count - 1) :], "seq", 1)
    widened = jnp.concatenate([rim_rows, activations], 0).astype(jnp.float32)
    summed = jnp.zeros(activations.shape, jnp.float32)
    for shift_back in range(tap_count):
        start_row = tap_count - 1 - shift_back
        summed = (
            summed
            + conv_taps[shift_back].astype(jnp.float32)
            * widened[start_row : start_row + shard_rows]
        )
    mixed_rows = summed.astype(jnp.bfloat16)
    partial_hidden = jnp.dot(
        mixed_rows,
        lax.all_gather(gate_in, "seq", axis=1, tiled=True),
        preferred_element_type=jnp.float32,
    )
    kv_local = key_vectors.shape[1] // HEAD_DIM
    group_size = QUERY_HEADS // KV_HEADS
    head_rank = lax.axis_index("heads")
    hidden = jax.nn.silu(lax.psum(partial_hidden, "heads")).astype(jnp.bfloat16)
    logits = jnp.dot(hidden, gate_out, preferred_element_type=jnp.float32)
    retention = lax.dynamic_slice_in_dim(
        jax.nn.log_sigmoid(logits).astype(jnp.bfloat16), head_rank * kv_local, kv_local, 1
    )
    seq_rank = lax.axis_index("seq")
    local_index = jnp.arange(shard_rows, dtype=jnp.int32)
    own_queries, own_keys, own_values, own_bias = (queries, key_vectors, value_vectors, retention)
    query_places = seq_rank * shard_rows + local_index
    query_segments = jnp.take(segment_ids, query_places)
    query_heads = own_queries.reshape(shard_rows, kv_local, group_size, HEAD_DIM)
    score_scale = 1.0 / math.sqrt(HEAD_DIM)

    def visibility(flat_index):
        key_segments = jnp.take(segment_ids, flat_index)
        return (flat_index[None, :] <= query_places[:, None]) & (
            key_segments[None, :] == query_segments[:, None]
        )

    initial = (
        jnp.full((kv_local, group_size, shard_rows), NEG_FILL, jnp.float32),
        jnp.zeros((kv_local, group_size, shard_rows), jnp.float32),
    )
    all_keys, all_values, all_bias = (
        lax.all_gather(own_keys, "seq", axis=0, tiled=True),
        lax.all_gather(own_values, "seq", axis=0, tiled=True),
        lax.all_gather(own_bias, "seq", axis=0, tiled=True),
    )
    piece_rows = all_keys.shape[0]
    stats_block_width = math.gcd(piece_rows, 512)

    def one_block(block_number, state_in):
        offset = block_number * stats_block_width
        key_block = lax.dynamic_slice_in_dim(all_keys, offset, stats_block_width, 0).reshape(
            stats_block_width, kv_local, HEAD_DIM
        )
        bias_block = lax.dynamic_slice_in_dim(all_bias, offset, stats_block_width, 0)
        allowed = visibility(0 + offset + jnp.arange(stats_block_width, dtype=jnp.int32))

        def update(state_old):
            peak_old, mass_old = state_old
            masked = block_scores(query_heads, key_block, bias_block, allowed, score_scale)
            peak_new = jnp.maximum(peak_old, jnp.max(masked, axis=3))
            exponent = jnp.where(allowed[None, None], jnp.exp(masked - peak_new[..., None]), 0.0)
            return (peak_new, mass_old * jnp.exp(peak_old - peak_new) + jnp.sum(exponent, axis=3))

        def keep_state(state_old):
            return state_old

        return lax.cond(jnp.any(allowed), update, keep_state, state_in)

    row_peak, total_mass = lax.fori_loop(0, piece_rows // stats_block_width, one_block, initial)
    total_keys = all_keys.shape[0]
    block_width = math.gcd(total_keys, 512)
    block_count = total_keys // block_width
    key_blocks = all_keys.reshape(block_count, block_width, kv_local, HEAD_DIM)
    value_blocks = all_values.reshape(block_count, block_width, kv_local, HEAD_DIM)
    bias_blocks = all_bias.reshape(block_count, block_width, kv_local)

    def second_pass(accumulated, block_items):
        block_number, key_block, value_block, bias_block = block_items
        allowed = visibility(block_number * block_width + jnp.arange(block_width, dtype=jnp.int32))

        def attend(accum_in):
            masked = block_scores(query_heads, key_block, bias_block, allowed, score_scale)
            weights = (
                jnp.where(allowed[None, None], jnp.exp(masked - row_peak[..., None]), 0.0)
                / total_mass[..., None]
            )
            accum_out = accum_in + jnp.einsum(
                "getk,kgh->tgeh",
                weights.astype(jnp.bfloat16),
                value_block,
                preferred_element_type=jnp.float32,
            )
            return (accum_out, jnp.transpose(jnp.sum(weights, axis=(1, 2))) / group_size)

        def skip_block(accum_in):
            return (accum_in, jnp.zeros((block_width, kv_local), jnp.float32))

        return lax.cond(jnp.any(allowed), attend, skip_block, accumulated)

    accumulated, mass_blocks = lax.scan(
        second_pass,
        jnp.zeros((shard_rows, kv_local, group_size, HEAD_DIM), jnp.float32),
        (jnp.arange(block_count, dtype=jnp.int32), key_blocks, value_blocks, bias_blocks),
    )
    key_term = mass_blocks.reshape(total_keys, kv_local)
    key_mass = lax.psum_scatter(key_term, "seq", scatter_dimension=0, tiled=True).astype(
        jnp.bfloat16
    )
    attended = accumulated.reshape(shard_rows, kv_local * group_size * HEAD_DIM).astype(
        jnp.bfloat16
    )
    return (attended, jnp.transpose(key_mass))


def solution(mesh):
    return jax.shard_map(
        pair_device if mesh.shape["seq"] == 2 else ring_device,
        mesh=mesh,
        in_specs=(
            P(("dp", "seq"), "heads"),
            P(None, "heads"),
            P("heads", "seq"),
            P(),
            P(("dp", "seq"), "heads"),
            P(("dp", "seq"), "heads"),
            P(("dp", "seq"), "heads"),
            P("dp"),
        ),
        out_specs=(P(("dp", "seq"), "heads"), P("heads", ("dp", "seq"))),
        check_vma=False,
    )
```

```python
import functools
import math

import jax
import jax.numpy as jnp
from jax import lax
from jax.experimental import pallas as pl
from jax.experimental.pallas import tpu as pltpu
from jax.sharding import PartitionSpec as P

QUERY_HEADS = 64
KV_HEADS = 8
HEAD_DIM = 128


NEG_FILL = -1e30
RIM_ROWS = 16
LEAST_RETENTION = -40.0
VMEM_BYTES = 16 * 1024 * 1024


def convolve(widened, taps, lead, rows):
    summed = jnp.zeros((rows, widened.shape[1]), jnp.float32)
    for back in range(taps.shape[0]):
        summed = summed + taps[back : back + 1] * widened[lead - back : lead - back + rows]
    return summed.astype(jnp.bfloat16)


def own_project_kernel(rows_ref, taps_ref, gate_ref, out_ref, held_taps_ref, held_ref, widened):
    rows, features = rows_ref.shape
    held_taps_ref[...] = taps_ref[...].astype(jnp.float32)
    held_ref[:features] = gate_ref[...]
    tile = widened.shape[2]
    total = jnp.zeros(out_ref.shape, jnp.float32)
    for step in range(features // tile):
        columns = slice(step * tile, (step + 1) * tile)
        edges = features + step * 2 * RIM_ROWS
        held_ref[edges : edges + RIM_ROWS, :tile] = rows_ref[:RIM_ROWS, columns]
        held_ref[edges + RIM_ROWS : edges + 2 * RIM_ROWS, :tile] = rows_ref[
            rows - RIM_ROWS :, columns
        ]
        wide = widened.at[step % 2]
        wide[...] = rows_ref[:, columns].astype(jnp.float32)
        taps = taps_ref[:, columns].astype(jnp.float32)
        mixed = convolve(wide, taps, RIM_ROWS, rows - RIM_ROWS)
        total = total + jnp.dot(mixed, gate_ref[columns, :], preferred_element_type=jnp.float32)
    out_ref[...] = total


def peer_project_kernel(
    peer_ref, taps_ref, held_ref, near_ref, far_ref, widened, own_widened
):
    rows, features = peer_ref.shape
    tile = widened.shape[2]
    first = lax.axis_index("seq") == 0
    half = near_ref.shape[1]
    total = jnp.zeros((near_ref.shape[0], 2 * half), jnp.float32)
    for step in range(features // tile):
        columns = slice(step * tile, (step + 1) * tile)
        wide, own_wide = widened.at[step % 2], own_widened.at[step % 2]
        edges = held_ref.at[
            features + step * 2 * RIM_ROWS : features + (step + 1) * 2 * RIM_ROWS, :tile
        ]
        own_tail = edges[RIM_ROWS:].astype(jnp.float32)
        peer_tail = peer_ref[rows - RIM_ROWS :, columns].astype(jnp.float32)
        wide[:RIM_ROWS] = jnp.where(first, own_tail, 0.0)
        wide[RIM_ROWS:] = peer_ref[:, columns].astype(jnp.float32)
        own_wide[:RIM_ROWS] = jnp.where(first, 0.0, peer_tail)
        own_wide[RIM_ROWS:] = edges[:RIM_ROWS].astype(jnp.float32)
        taps = taps_ref[:, columns].astype(jnp.float32)
        mixed = jnp.concatenate(
            [
                convolve(own_wide, taps, RIM_ROWS, RIM_ROWS),
                convolve(wide, taps, RIM_ROWS, rows),
            ],
            axis=0,
        )
        total = total + jnp.dot(mixed, held_ref[columns, :], preferred_element_type=jnp.float32)
    near_ref[...] = total[:, :half]
    far_ref[...] = total[:, half:].astype(jnp.bfloat16)


def own_project(activations, conv_taps, gate_in):
    rows, features = activations.shape
    done = rows - RIM_ROWS
    tile = math.gcd(features, gate_in.shape[1])
    return pl.pallas_call(
        own_project_kernel,
        out_shape=(
            jax.ShapeDtypeStruct((done, gate_in.shape[1]), jnp.float32),
            jax.ShapeDtypeStruct(conv_taps.shape, jnp.float32),
            jax.ShapeDtypeStruct(
                (features + features // tile * 2 * RIM_ROWS, gate_in.shape[1]), gate_in.dtype
            ),
        ),
        scratch_shapes=[pltpu.VMEM((2, rows, tile), jnp.float32)],
        compiler_params=pltpu.CompilerParams(vmem_limit_bytes=VMEM_BYTES),
        cost_estimate=pl.CostEstimate(flops=1, bytes_accessed=1, transcendentals=0),
    )(activations, conv_taps, gate_in)


def peer_project(peer_rows, taps, held):
    rows, features = peer_rows.shape
    done = rows + RIM_ROWS
    tile = math.gcd(features, held.shape[1])
    half = held.shape[1] // 2
    return pl.pallas_call(
        peer_project_kernel,
        out_shape=(
            jax.ShapeDtypeStruct((done, half), jnp.float32),
            jax.ShapeDtypeStruct((done, half), jnp.bfloat16),
        ),
        scratch_shapes=[
            pltpu.VMEM((2, rows + RIM_ROWS, tile), jnp.float32),
            pltpu.VMEM((2, 2 * RIM_ROWS, tile), jnp.float32),
        ],
        compiler_params=pltpu.CompilerParams(vmem_limit_bytes=VMEM_BYTES),
        cost_estimate=pl.CostEstimate(flops=1, bytes_accessed=1, transcendentals=0),
    )(peer_rows, taps, held)


def head_sum(part):
    count = lax.axis_size("heads")
    step = 1
    received = None
    while step < count:
        if received is not None:
            part = part + received.astype(jnp.float32)
        received = exchange_heads(part if step == 1 else part.astype(jnp.bfloat16), step)
        step *= 2
    return part, received


def exchange_heads(block, step):
    count = lax.axis_size("heads")
    return lax.ppermute(block, "heads", [(i, i ^ step) for i in range(count)])


def in_one_piece(work, *given):
    shapes = jax.eval_shape(work, *given)
    return lax.cond(
        lax.axis_index("seq") >= 0,
        work,
        lambda *given: jax.tree.map(lambda like: jnp.zeros(like.shape, like.dtype), shapes),
        *given,
    )


def far_logits(block, gate_out):
    step = lax.axis_size("heads") // 2
    received = exchange_heads(block, step)

    def nearer(block, received, gate_out):
        distance = step
        while distance > 1:
            distance //= 2
            block = block.astype(jnp.float32) + received.astype(jnp.float32)
            received = exchange_heads(block, distance)
        return partial_logits(block, received, gate_out, block.shape[1])

    return in_one_piece(nearer, block, received, gate_out)


def share_of_logits(pre_ref, in_ref, gate_out_ref, offset):
    pre = pre_ref[...] + in_ref[...].astype(jnp.float32)
    hidden = (pre / (1.0 + jnp.exp(-pre))).astype(jnp.bfloat16)
    share = gate_out_ref.shape[1] // lax.axis_size("seq")
    start = pl.multiple_of(lax.axis_index("seq") * share + offset, HEAD_DIM)
    gate_columns = gate_out_ref[:, pl.ds(start, pre.shape[1])]
    return lax.dot_general(
        gate_columns, hidden, (((1,), (1,)), ((), ())), preferred_element_type=jnp.float32
    )


def partial_logits_kernel(offset, own_ref, in_ref, gate_out_ref, out_ref):
    out_ref[...] = share_of_logits(own_ref, in_ref, gate_out_ref, offset)


def partial_logits(part, received, gate_out, offset):
    return pl.pallas_call(
        functools.partial(partial_logits_kernel, offset),
        out_shape=jax.ShapeDtypeStruct((gate_out.shape[0], part.shape[0]), jnp.float32),
        compiler_params=pltpu.CompilerParams(vmem_limit_bytes=VMEM_BYTES),
    )(part, received, gate_out)


def logits_kernel(own_ref, far_share_ref, near_ref, near_in_ref, gate_out_ref, out_ref):
    first = lax.axis_index("seq") == 0
    share = share_of_logits(near_ref, near_in_ref, gate_out_ref, 0) + far_share_ref[...]
    own = jnp.concatenate([share[:, :RIM_ROWS], own_ref[...]], axis=1)
    peer = share[:, RIM_ROWS:]
    out_ref[0] = jnp.where(first, own, peer)
    out_ref[1] = jnp.where(first, peer, own)


def logits_share(own_share, far_share, near, near_in, gate_out):
    rows = own_share.shape[1] + RIM_ROWS
    return pl.pallas_call(
        logits_kernel,
        out_shape=jax.ShapeDtypeStruct((2, gate_out.shape[0], rows), jnp.float32),
        compiler_params=pltpu.CompilerParams(vmem_limit_bytes=VMEM_BYTES),
    )(own_share, far_share, near, near_in, gate_out)


def hide_unseen(seq_rank, segments_ref, rows):
    own_segments = segments_ref[pl.ds(seq_rank, 1), :]
    behind_segments = segments_ref[pl.ds(0, 1), :]
    query_segments = jnp.transpose(jnp.broadcast_to(own_segments, (rows, rows)))
    query_at = lax.broadcasted_iota(jnp.int32, (rows, rows), 0)
    key_at = lax.broadcasted_iota(jnp.int32, (rows, rows), 1)
    see_own = (key_at <= query_at) & (query_segments == own_segments)
    see_behind = (query_segments == behind_segments) & (seq_rank > 0)
    return jnp.where(jnp.concatenate([see_behind, see_own], axis=1), 0.0, NEG_FILL)


def head_columns(number):
    return slice(number * HEAD_DIM, (number + 1) * HEAD_DIM)


def scores_of(queries_ref, keys, offset, head):
    scores = lax.dot_general(
        queries_ref[:, head_columns(head)],
        keys,
        (((1,), (1,)), ((), ())),
        preferred_element_type=jnp.float32,
    )
    return scores * (1.0 / math.sqrt(HEAD_DIM)) + offset


def with_behind(ref, behind_ref, number, whole):
    own = ref[:, head_columns(number)]
    if not whole:
        return own
    return jnp.concatenate([behind_ref[:, head_columns(number)], own], axis=0)


def powers_kernel(segments_ref, queries_ref, keys_ref, behind_keys_ref, powers_ref):
    seq_rank = lax.axis_index("seq")
    rows = queries_ref.shape[0]
    kv_local = keys_ref.shape[1] // HEAD_DIM
    group_size = queries_ref.shape[1] // keys_ref.shape[1]
    hide = hide_unseen(seq_rank, segments_ref, rows)

    def fill(whole):
        start = 0 if whole else rows
        for head in range(kv_local * group_size):
            g = head // group_size
            keys = with_behind(keys_ref, behind_keys_ref, g, whole)
            scores = scores_of(queries_ref, keys, hide[:, start:], head)
            powers_ref[head, :, start:] = jnp.exp(
                scores - jnp.max(scores, axis=1, keepdims=True)
            )

    pl.when(seq_rank > 0)(lambda: fill(True))
    pl.when(seq_rank == 0)(lambda: fill(False))


def powers_of(segments, queries, keys, behind_keys):
    rows = queries.shape[0]
    heads = queries.shape[1] // HEAD_DIM
    return pl.pallas_call(
        powers_kernel,
        out_shape=jax.ShapeDtypeStruct((heads, rows, 2 * rows), jnp.float32),
        compiler_params=pltpu.CompilerParams(vmem_limit_bytes=VMEM_BYTES),
        cost_estimate=pl.CostEstimate(
            flops=4 * rows * rows * queries.shape[1],
            bytes_accessed=8 * heads * rows * rows,
            transcendentals=2 * heads * rows * rows,
        ),
    )(segments, queries, keys, behind_keys)


def read_retention(share_refs, retention):
    seq_rank, head_rank = lax.axis_index("seq"), lax.axis_index("heads")
    logits = share_refs[0][...] + share_refs[1][...]
    log_gate = jnp.minimum(logits, 0.0) - jnp.log1p(jnp.exp(-jnp.abs(logits)))
    retention[...] = log_gate.astype(jnp.bfloat16).astype(jnp.float32)
    kv_local = retention.shape[1] // lax.axis_size("heads")
    biases = []
    for g in range(kv_local):
        at = pl.ds(head_rank * kv_local + g, 1)
        biases.append(jnp.concatenate([retention[0, at, :], retention[seq_rank, at, :]], axis=1))
    return biases


def by_group(
    whole, biases, powers_ref, segments_ref, queries_ref, keys_ref, behind_keys_ref, group
):
    rows = queries_ref.shape[0]
    start = 0 if whole else rows
    moderate = jnp.min(functools.reduce(jnp.minimum, biases)) >= LEAST_RETENTION

    def by_powers(g):
        factor = jnp.exp(biases[g] - jnp.max(biases[g]))[:, start:]
        return lambda head: powers_ref[head, :, start:] * factor

    def by_scores(g):
        hide = hide_unseen(lax.axis_index("seq"), segments_ref, rows)
        offset = (hide + biases[g])[:, start:]
        keys = with_behind(keys_ref, behind_keys_ref, g, whole)

        def terms(head):
            scores = scores_of(queries_ref, keys, offset, head)
            return jnp.exp(scores - jnp.max(scores, axis=1, keepdims=True))

        return terms

    def run(terms_of):
        for g in range(len(biases)):
            group(g, terms_of(g))

    pl.when(moderate)(lambda: run(by_powers))
    pl.when(jnp.logical_not(moderate))(lambda: run(by_scores))


def behind_mass_kernel(*refs):
    *share_refs, powers_ref, segments_ref, queries_ref, keys_ref, behind_keys_ref = refs[:7]
    mass_ref, retention = refs[7:]
    rows = queries_ref.shape[0]
    group_size = queries_ref.shape[1] // keys_ref.shape[1]

    def group(g, terms_of):
        mass = jnp.zeros((1, rows), jnp.float32)
        for head in range(g * group_size, (g + 1) * group_size):
            terms = terms_of(head)
            weights = terms[:, :rows] * (1.0 / jnp.sum(terms, axis=1, keepdims=True))
            mass = mass + jnp.sum(weights, axis=0, keepdims=True)
        mass_ref[g : g + 1, :] = mass / group_size

    def fill():
        biases = read_retention(share_refs, retention)
        by_group(
            True, biases, powers_ref, segments_ref, queries_ref, keys_ref, behind_keys_ref, group
        )

    def clear():
        mass_ref[...] = jnp.zeros(mass_ref.shape, jnp.float32)

    pl.when(lax.axis_index("seq") > 0)(fill)
    pl.when(lax.axis_index("seq") == 0)(clear)


def behind_mass_of(shares, powers, segments, queries, keys, behind_keys):
    return pl.pallas_call(
        behind_mass_kernel,
        out_shape=jax.ShapeDtypeStruct(
            (keys.shape[1] // HEAD_DIM, queries.shape[0]), jnp.float32
        ),
        scratch_shapes=[pltpu.VMEM(shares[0].shape, jnp.float32)],
        compiler_params=pltpu.CompilerParams(vmem_limit_bytes=VMEM_BYTES),
    )(*shares, powers, segments, queries, keys, behind_keys)


def attend_kernel(*refs):
    *share_refs, powers_ref, segments_ref, queries_ref, keys_ref, behind_keys_ref = refs[:7]
    values_ref, behind_values_ref, attended_ref, mass_ref, retention = refs[7:]
    rows = queries_ref.shape[0]
    group_size = queries_ref.shape[1] // keys_ref.shape[1]

    def fill(whole):
        def group(g, terms_of):
            values = with_behind(values_ref, behind_values_ref, g, whole)
            own = values.shape[0] - rows
            mass = jnp.zeros((1, rows), jnp.float32)
            for head in range(g * group_size, (g + 1) * group_size):
                terms = terms_of(head)
                weights = terms * (1.0 / jnp.sum(terms, axis=1, keepdims=True))
                mass = mass + jnp.sum(weights[:, own:], axis=0, keepdims=True)
                attended_ref[:, head_columns(head)] = jnp.dot(
                    weights.astype(jnp.bfloat16), values, preferred_element_type=jnp.float32
                ).astype(jnp.bfloat16)
            mass_ref[g : g + 1, :] = mass / group_size

        biases = read_retention(share_refs, retention)
        by_group(
            whole, biases, powers_ref, segments_ref, queries_ref, keys_ref, behind_keys_ref, group
        )

    pl.when(lax.axis_index("seq") > 0)(lambda: fill(True))
    pl.when(lax.axis_index("seq") == 0)(lambda: fill(False))


def attend(shares, powers, segments, queries, keys, behind_keys, values, behind_values, sent):
    rows = queries.shape[0]
    shares, powers, sent = lax.optimization_barrier((shares, powers, sent))
    attended, mass = pl.pallas_call(
        attend_kernel,
        out_shape=(
            jax.ShapeDtypeStruct(queries.shape, jnp.bfloat16),
            jax.ShapeDtypeStruct((keys.shape[1] // HEAD_DIM, rows), jnp.float32),
        ),
        scratch_shapes=[pltpu.VMEM(shares[0].shape, jnp.float32)],
        compiler_params=pltpu.CompilerParams(vmem_limit_bytes=VMEM_BYTES),
        cost_estimate=pl.CostEstimate(
            flops=4 * rows * rows * queries.shape[1],
            bytes_accessed=4 * queries.size,
            transcendentals=0,
        ),
    )(*shares, powers, segments, queries, keys, behind_keys, values, behind_values)
    return attended, mass, sent


def pair_device(
    activations, conv_taps, gate_in, gate_out, queries, key_vectors, value_vectors, segment_ids
):
    rows = activations.shape[0]
    swap = [(0, 1), (1, 0)]
    segments = segment_ids.reshape(2, rows)
    gate_out = jnp.transpose(gate_out)

    peer_rows = lax.ppermute(activations, "seq", swap)

    def own_work(activations, conv_taps, gate_in, gate_out):
        part, *held = own_project(activations, conv_taps, gate_in)
        return partial_logits(*head_sum(part), gate_out, 0), held

    own_share, held = in_one_piece(own_work, activations, conv_taps, gate_in, gate_out)
    peer_rows, own_share, held = lax.optimization_barrier((peer_rows, own_share, held))
    near, far = peer_project(peer_rows, *held)
    behind_keys = lax.ppermute(key_vectors, "seq", swap)
    behind_values = lax.ppermute(value_vectors, "seq", swap)
    near, near_in = head_sum(near)
    far_share = far_logits(far, gate_out)
    share = logits_share(own_share, far_share, near, near_in, gate_out)
    share, queries = lax.optimization_barrier((share, queries))
    powers = powers_of(segments, queries, key_vectors, behind_keys)
    count = lax.axis_size("heads")
    across = [
        (seq * count + head, (1 - seq) * count + (head ^ 1))
        for seq in range(2)
        for head in range(count)
    ]
    shares = (share, lax.ppermute(share, ("seq", "heads"), across))
    given = (shares, powers, segments, queries, key_vectors, behind_keys)
    sent = behind_mass_of(*given)
    attended, own_mass, sent = attend(*given, value_vectors, behind_values, sent)
    key_mass = own_mass + lax.ppermute(sent, "seq", swap)
    return (attended, key_mass.astype(jnp.bfloat16))


def from_behind(block, axis, distance):
    devices = range(lax.axis_size(axis))
    route = [(i - distance, i) for i in devices if i - distance in devices]
    return lax.ppermute(block, axis, route)


def block_scores(query_heads, key_block, bias_block, allowed, score_scale):
    scores = (
        jnp.einsum("tgeh,kgh->getk", query_heads, key_block, preferred_element_type=jnp.float32)
        * score_scale
    )
    scores = scores + jnp.transpose(bias_block.astype(jnp.float32))[:, None, None, :]
    return jnp.where(allowed[None, None], scores, NEG_FILL)


def ring_device(
    activations, conv_taps, gate_in, gate_out, queries, key_vectors, value_vectors, segment_ids
):
    shard_rows = activations.shape[0]
    tap_count = conv_taps.shape[0]
    rim_rows = from_behind(activations[shard_rows - (tap_count - 1) :], "seq", 1)
    widened = jnp.concatenate([rim_rows, activations], 0).astype(jnp.float32)
    summed = jnp.zeros(activations.shape, jnp.float32)
    for shift_back in range(tap_count):
        start_row = tap_count - 1 - shift_back
        summed = (
            summed
            + conv_taps[shift_back].astype(jnp.float32)
            * widened[start_row : start_row + shard_rows]
        )
    mixed_rows = summed.astype(jnp.bfloat16)
    partial_hidden = jnp.dot(
        mixed_rows,
        lax.all_gather(gate_in, "seq", axis=1, tiled=True),
        preferred_element_type=jnp.float32,
    )
    kv_local = key_vectors.shape[1] // HEAD_DIM
    group_size = QUERY_HEADS // KV_HEADS
    head_rank = lax.axis_index("heads")
    hidden = jax.nn.silu(lax.psum(partial_hidden, "heads")).astype(jnp.bfloat16)
    logits = jnp.dot(hidden, gate_out, preferred_element_type=jnp.float32)
    retention = lax.dynamic_slice_in_dim(
        jax.nn.log_sigmoid(logits).astype(jnp.bfloat16), head_rank * kv_local, kv_local, 1
    )
    seq_rank = lax.axis_index("seq")
    local_index = jnp.arange(shard_rows, dtype=jnp.int32)
    own_queries, own_keys, own_values, own_bias = (queries, key_vectors, value_vectors, retention)
    query_places = seq_rank * shard_rows + local_index
    query_segments = jnp.take(segment_ids, query_places)
    query_heads = own_queries.reshape(shard_rows, kv_local, group_size, HEAD_DIM)
    score_scale = 1.0 / math.sqrt(HEAD_DIM)

    def visibility(flat_index):
        key_segments = jnp.take(segment_ids, flat_index)
        return (flat_index[None, :] <= query_places[:, None]) & (
            key_segments[None, :] == query_segments[:, None]
        )

    initial = (
        jnp.full((kv_local, group_size, shard_rows), NEG_FILL, jnp.float32),
        jnp.zeros((kv_local, group_size, shard_rows), jnp.float32),
    )
    all_keys, all_values, all_bias = (
        lax.all_gather(own_keys, "seq", axis=0, tiled=True),
        lax.all_gather(own_values, "seq", axis=0, tiled=True),
        lax.all_gather(own_bias, "seq", axis=0, tiled=True),
    )
    piece_rows = all_keys.shape[0]
    stats_block_width = math.gcd(piece_rows, 512)

    def one_block(block_number, state_in):
        offset = block_number * stats_block_width
        key_block = lax.dynamic_slice_in_dim(all_keys, offset, stats_block_width, 0).reshape(
            stats_block_width, kv_local, HEAD_DIM
        )
        bias_block = lax.dynamic_slice_in_dim(all_bias, offset, stats_block_width, 0)
        allowed = visibility(0 + offset + jnp.arange(stats_block_width, dtype=jnp.int32))

        def update(state_old):
            peak_old, mass_old = state_old
            masked = block_scores(query_heads, key_block, bias_block, allowed, score_scale)
            peak_new = jnp.maximum(peak_old, jnp.max(masked, axis=3))
            exponent = jnp.where(allowed[None, None], jnp.exp(masked - peak_new[..., None]), 0.0)
            return (peak_new, mass_old * jnp.exp(peak_old - peak_new) + jnp.sum(exponent, axis=3))

        def keep_state(state_old):
            return state_old

        return lax.cond(jnp.any(allowed), update, keep_state, state_in)

    row_peak, total_mass = lax.fori_loop(0, piece_rows // stats_block_width, one_block, initial)
    total_keys = all_keys.shape[0]
    block_width = math.gcd(total_keys, 512)
    block_count = total_keys // block_width
    key_blocks = all_keys.reshape(block_count, block_width, kv_local, HEAD_DIM)
    value_blocks = all_values.reshape(block_count, block_width, kv_local, HEAD_DIM)
    bias_blocks = all_bias.reshape(block_count, block_width, kv_local)

    def second_pass(accumulated, block_items):
        block_number, key_block, value_block, bias_block = block_items
        allowed = visibility(block_number * block_width + jnp.arange(block_width, dtype=jnp.int32))

        def attend(accum_in):
            masked = block_scores(query_heads, key_block, bias_block, allowed, score_scale)
            weights = (
                jnp.where(allowed[None, None], jnp.exp(masked - row_peak[..., None]), 0.0)
                / total_mass[..., None]
            )
            accum_out = accum_in + jnp.einsum(
                "getk,kgh->tgeh",
                weights.astype(jnp.bfloat16),
                value_block,
                preferred_element_type=jnp.float32,
            )
            return (accum_out, jnp.transpose(jnp.sum(weights, axis=(1, 2))) / group_size)

        def skip_block(accum_in):
            return (accum_in, jnp.zeros((block_width, kv_local), jnp.float32))

        return lax.cond(jnp.any(allowed), attend, skip_block, accumulated)

    accumulated, mass_blocks = lax.scan(
        second_pass,
        jnp.zeros((shard_rows, kv_local, group_size, HEAD_DIM), jnp.float32),
        (jnp.arange(block_count, dtype=jnp.int32), key_blocks, value_blocks, bias_blocks),
    )
    key_term = mass_blocks.reshape(total_keys, kv_local)
    key_mass = lax.psum_scatter(key_term, "seq", scatter_dimension=0, tiled=True).astype(
        jnp.bfloat16
    )
    attended = accumulated.reshape(shard_rows, kv_local * group_size * HEAD_DIM).astype(
        jnp.bfloat16
    )
    return (attended, jnp.transpose(key_mass))


def solution(mesh):
    return jax.shard_map(
        pair_device if mesh.shape["seq"] == 2 else ring_device,
        mesh=mesh,
        in_specs=(
            P(("dp", "seq"), "heads"),
            P(None, "heads"),
            P("heads", "seq"),
            P(),
            P(("dp", "seq"), "heads"),
            P(("dp", "seq"), "heads"),
            P(("dp", "seq"), "heads"),
            P("dp"),
        ),
        out_specs=(P(("dp", "seq"), "heads"), P("heads", ("dp", "seq"))),
        check_vma=False,
    )
```

```python
import functools
import math

import jax
import jax.numpy as jnp
from jax import lax
from jax.experimental import pallas as pl
from jax.experimental.pallas import tpu as pltpu
from jax.sharding import PartitionSpec as P

QUERY_HEADS = 64
KV_HEADS = 8
HEAD_DIM = 128


NEG_FILL = -1e30
RIM_ROWS = 16
PIECE_HEADS = 4
LEAST_RETENTION = -40.0
VMEM_BYTES = 16 * 1024 * 1024


def convolve(widened, taps, lead, rows):
    summed = jnp.zeros((rows, widened.shape[1]), jnp.float32)
    for back in range(taps.shape[0]):
        summed = summed + taps[back : back + 1] * widened[lead - back : lead - back + rows]
    return summed.astype(jnp.bfloat16)


def own_project_kernel(rows_ref, taps_ref, gate_ref, out_ref, held_taps_ref, held_ref, widened):
    rows, features = rows_ref.shape
    held_taps_ref[...] = taps_ref[...].astype(jnp.float32)
    held_ref[:features] = gate_ref[...]
    tile = widened.shape[2]
    total = jnp.zeros(out_ref.shape, jnp.float32)
    for step in range(features // tile):
        columns = slice(step * tile, (step + 1) * tile)
        edges = features + step * 2 * RIM_ROWS
        held_ref[edges : edges + RIM_ROWS, :tile] = rows_ref[:RIM_ROWS, columns]
        held_ref[edges + RIM_ROWS : edges + 2 * RIM_ROWS, :tile] = rows_ref[
            rows - RIM_ROWS :, columns
        ]
        wide = widened.at[step % 2]
        wide[...] = rows_ref[:, columns].astype(jnp.float32)
        taps = taps_ref[:, columns].astype(jnp.float32)
        mixed = convolve(wide, taps, RIM_ROWS, rows - RIM_ROWS)
        total = total + jnp.dot(mixed, gate_ref[columns, :], preferred_element_type=jnp.float32)
    out_ref[...] = total


def peer_project_kernel(
    peer_ref, taps_ref, held_ref, near_ref, far_ref, widened, own_widened
):
    rows, features = peer_ref.shape
    tile = widened.shape[2]
    first = lax.axis_index("seq") == 0
    half = near_ref.shape[1]
    total = jnp.zeros((near_ref.shape[0], 2 * half), jnp.float32)
    for step in range(features // tile):
        columns = slice(step * tile, (step + 1) * tile)
        wide, own_wide = widened.at[step % 2], own_widened.at[step % 2]
        edges = held_ref.at[
            features + step * 2 * RIM_ROWS : features + (step + 1) * 2 * RIM_ROWS, :tile
        ]
        own_tail = edges[RIM_ROWS:].astype(jnp.float32)
        peer_tail = peer_ref[rows - RIM_ROWS :, columns].astype(jnp.float32)
        wide[:RIM_ROWS] = jnp.where(first, own_tail, 0.0)
        wide[RIM_ROWS:] = peer_ref[:, columns].astype(jnp.float32)
        own_wide[:RIM_ROWS] = jnp.where(first, 0.0, peer_tail)
        own_wide[RIM_ROWS:] = edges[:RIM_ROWS].astype(jnp.float32)
        taps = taps_ref[:, columns].astype(jnp.float32)
        mixed = jnp.concatenate(
            [
                convolve(own_wide, taps, RIM_ROWS, RIM_ROWS),
                convolve(wide, taps, RIM_ROWS, rows),
            ],
            axis=0,
        )
        total = total + jnp.dot(mixed, held_ref[columns, :], preferred_element_type=jnp.float32)
    near_ref[...] = total[:, :half]
    far_ref[...] = total[:, half:].astype(jnp.bfloat16)


def own_project(activations, conv_taps, gate_in):
    rows, features = activations.shape
    done = rows - RIM_ROWS
    tile = math.gcd(features, gate_in.shape[1])
    return pl.pallas_call(
        own_project_kernel,
        out_shape=(
            jax.ShapeDtypeStruct((done, gate_in.shape[1]), jnp.float32),
            jax.ShapeDtypeStruct(conv_taps.shape, jnp.float32),
            jax.ShapeDtypeStruct(
                (features + features // tile * 2 * RIM_ROWS, gate_in.shape[1]), gate_in.dtype
            ),
        ),
        scratch_shapes=[pltpu.VMEM((2, rows, tile), jnp.float32)],
        compiler_params=pltpu.CompilerParams(vmem_limit_bytes=VMEM_BYTES),
        cost_estimate=pl.CostEstimate(flops=1, bytes_accessed=1, transcendentals=0),
    )(activations, conv_taps, gate_in)


def peer_project(peer_rows, taps, held):
    rows, features = peer_rows.shape
    done = rows + RIM_ROWS
    tile = math.gcd(features, held.shape[1])
    half = held.shape[1] // 2
    return pl.pallas_call(
        peer_project_kernel,
        out_shape=(
            jax.ShapeDtypeStruct((done, half), jnp.float32),
            jax.ShapeDtypeStruct((done, half), jnp.bfloat16),
        ),
        scratch_shapes=[
            pltpu.VMEM((2, rows + RIM_ROWS, tile), jnp.float32),
            pltpu.VMEM((2, 2 * RIM_ROWS, tile), jnp.float32),
        ],
        compiler_params=pltpu.CompilerParams(vmem_limit_bytes=VMEM_BYTES),
        cost_estimate=pl.CostEstimate(flops=1, bytes_accessed=1, transcendentals=0),
    )(peer_rows, taps, held)


def head_sum(part):
    count = lax.axis_size("heads")
    step = 1
    received = None
    while step < count:
        if received is not None:
            part = part + received.astype(jnp.float32)
        received = exchange_heads(part if step == 1 else part.astype(jnp.bfloat16), step)
        step *= 2
    return part, received


def exchange_heads(block, step):
    count = lax.axis_size("heads")
    return lax.ppermute(block, "heads", [(i, i ^ step) for i in range(count)])


def in_one_piece(work, *given):
    shapes = jax.eval_shape(work, *given)
    return lax.cond(
        lax.axis_index("seq") >= 0,
        work,
        lambda *given: jax.tree.map(lambda like: jnp.zeros(like.shape, like.dtype), shapes),
        *given,
    )


def far_logits(block, gate_out):
    step = lax.axis_size("heads") // 2
    received = exchange_heads(block, step)

    def nearer(block, received, gate_out):
        distance = step
        while distance > 1:
            distance //= 2
            block = block.astype(jnp.float32) + received.astype(jnp.float32)
            received = exchange_heads(block.astype(jnp.bfloat16), distance)
        return partial_logits(block, received, gate_out, block.shape[1])

    return in_one_piece(nearer, block, received, gate_out)


def share_of_logits(pre_ref, in_ref, gate_out_ref, offset):
    pre = pre_ref[...] + in_ref[...].astype(jnp.float32)
    hidden = (pre / (1.0 + jnp.exp(-pre))).astype(jnp.bfloat16)
    share = gate_out_ref.shape[1] // lax.axis_size("seq")
    start = pl.multiple_of(lax.axis_index("seq") * share + offset, HEAD_DIM)
    gate_columns = gate_out_ref[:, pl.ds(start, pre.shape[1])]
    return lax.dot_general(
        gate_columns, hidden, (((1,), (1,)), ((), ())), preferred_element_type=jnp.float32
    )


def partial_logits_kernel(offset, own_ref, in_ref, gate_out_ref, out_ref):
    out_ref[...] = share_of_logits(own_ref, in_ref, gate_out_ref, offset)


def partial_logits(part, received, gate_out, offset):
    return pl.pallas_call(
        functools.partial(partial_logits_kernel, offset),
        out_shape=jax.ShapeDtypeStruct((gate_out.shape[0], part.shape[0]), jnp.float32),
        compiler_params=pltpu.CompilerParams(vmem_limit_bytes=VMEM_BYTES),
    )(part, received, gate_out)


def logits_kernel(own_ref, far_share_ref, near_ref, near_in_ref, gate_out_ref, out_ref):
    first = lax.axis_index("seq") == 0
    share = share_of_logits(near_ref, near_in_ref, gate_out_ref, 0) + far_share_ref[...]
    own = jnp.concatenate([share[:, :RIM_ROWS], own_ref[...]], axis=1)
    peer = share[:, RIM_ROWS:]
    out_ref[0] = jnp.where(first, own, peer)
    out_ref[1] = jnp.where(first, peer, own)


def logits_share(own_share, far_share, near, near_in, gate_out):
    rows = own_share.shape[1] + RIM_ROWS
    return pl.pallas_call(
        logits_kernel,
        out_shape=jax.ShapeDtypeStruct((2, gate_out.shape[0], rows), jnp.float32),
        compiler_params=pltpu.CompilerParams(vmem_limit_bytes=VMEM_BYTES),
    )(own_share, far_share, near, near_in, gate_out)


def hide_unseen(seq_rank, segments_ref, rows):
    own_segments = segments_ref[pl.ds(seq_rank, 1), :]
    behind_segments = segments_ref[pl.ds(0, 1), :]
    query_segments = jnp.transpose(jnp.broadcast_to(own_segments, (rows, rows)))
    query_at = lax.broadcasted_iota(jnp.int32, (rows, rows), 0)
    key_at = lax.broadcasted_iota(jnp.int32, (rows, rows), 1)
    see_own = (key_at <= query_at) & (query_segments == own_segments)
    see_behind = (query_segments == behind_segments) & (seq_rank > 0)
    return jnp.where(jnp.concatenate([see_behind, see_own], axis=1), 0.0, NEG_FILL)


def head_columns(number):
    return slice(number * HEAD_DIM, (number + 1) * HEAD_DIM)


def scores_of(queries_ref, keys, offset, head):
    scores = lax.dot_general(
        queries_ref[:, head_columns(head)],
        keys,
        (((1,), (1,)), ((), ())),
        preferred_element_type=jnp.float32,
    )
    return scores * (1.0 / math.sqrt(HEAD_DIM)) + offset


def with_behind(ref, behind_ref, number, whole):
    own = ref[:, head_columns(number)]
    if not whole:
        return own
    return jnp.concatenate([behind_ref[:, head_columns(number)], own], axis=0)


def powers_kernel(segments_ref, queries_ref, keys_ref, behind_keys_ref, powers_ref):
    seq_rank = lax.axis_index("seq")
    rows = queries_ref.shape[0]
    kv_local = keys_ref.shape[1] // HEAD_DIM
    group_size = queries_ref.shape[1] // keys_ref.shape[1]
    hide = hide_unseen(seq_rank, segments_ref, rows)

    def fill(whole):
        start = 0 if whole else rows
        for head in range(kv_local * group_size):
            g = head // group_size
            keys = with_behind(keys_ref, behind_keys_ref, g, whole)
            scores = scores_of(queries_ref, keys, hide[:, start:], head)
            powers_ref[head, :, start:] = jnp.exp(
                scores - jnp.max(scores, axis=1, keepdims=True)
            )

    pl.when(seq_rank > 0)(lambda: fill(True))
    pl.when(seq_rank == 0)(lambda: fill(False))


def powers_of(segments, queries, keys, behind_keys):
    rows = queries.shape[0]
    heads = queries.shape[1] // HEAD_DIM
    return pl.pallas_call(
        powers_kernel,
        out_shape=jax.ShapeDtypeStruct((heads, rows, 2 * rows), jnp.float32),
        compiler_params=pltpu.CompilerParams(vmem_limit_bytes=VMEM_BYTES),
        cost_estimate=pl.CostEstimate(
            flops=4 * rows * rows * queries.shape[1],
            bytes_accessed=8 * heads * rows * rows,
            transcendentals=2 * heads * rows * rows,
        ),
    )(segments, queries, keys, behind_keys)


def read_retention(share_refs, retention):
    seq_rank, head_rank = lax.axis_index("seq"), lax.axis_index("heads")
    logits = share_refs[0][...] + share_refs[1][...]
    log_gate = jnp.minimum(logits, 0.0) - jnp.log1p(jnp.exp(-jnp.abs(logits)))
    retention[...] = log_gate.astype(jnp.bfloat16).astype(jnp.float32)
    kv_local = retention.shape[1] // lax.axis_size("heads")
    biases = []
    for g in range(kv_local):
        at = pl.ds(head_rank * kv_local + g, 1)
        biases.append(jnp.concatenate([retention[0, at, :], retention[seq_rank, at, :]], axis=1))
    return biases


def by_group(
    whole,
    biases,
    powers_ref,
    segments_ref,
    queries_ref,
    keys_ref,
    behind_keys_ref,
    group,
    finish=None,
):
    rows = queries_ref.shape[0]
    start = 0 if whole else rows
    moderate = jnp.min(functools.reduce(jnp.minimum, biases)) >= LEAST_RETENTION

    def by_powers(g):
        factor = jnp.exp(biases[g] - jnp.max(biases[g]))[:, start:]
        return lambda head: powers_ref[head, :, start:] * factor

    def by_scores(g):
        hide = hide_unseen(lax.axis_index("seq"), segments_ref, rows)
        offset = (hide + biases[g])[:, start:]
        keys = with_behind(keys_ref, behind_keys_ref, g, whole)

        def terms(head):
            scores = scores_of(queries_ref, keys, offset, head)
            return jnp.exp(scores - jnp.max(scores, axis=1, keepdims=True))

        return terms

    def run(terms_of):
        for g in range(len(biases)):
            group(g, terms_of(g))

        if finish is not None:
            finish()

    pl.when(moderate)(lambda: run(by_powers))
    pl.when(jnp.logical_not(moderate))(lambda: run(by_scores))


def behind_mass_kernel(*refs):
    *share_refs, powers_ref, segments_ref, queries_ref, keys_ref, behind_keys_ref = refs[:7]
    mass_ref, retention = refs[7:]
    rows = queries_ref.shape[0]
    group_size = queries_ref.shape[1] // keys_ref.shape[1]

    def group(g, terms_of):
        mass = jnp.zeros((1, rows), jnp.float32)
        for head in range(g * group_size, (g + 1) * group_size):
            terms = terms_of(head)
            weights = terms[:, :rows] * (1.0 / jnp.sum(terms, axis=1, keepdims=True))
            mass = mass + jnp.sum(weights, axis=0, keepdims=True)
        mass_ref[g : g + 1, :] = mass / group_size

    def fill():
        biases = read_retention(share_refs, retention)
        by_group(
            True, biases, powers_ref, segments_ref, queries_ref, keys_ref, behind_keys_ref, group
        )

    def clear():
        mass_ref[...] = jnp.zeros(mass_ref.shape, jnp.float32)

    pl.when(lax.axis_index("seq") > 0)(fill)
    pl.when(lax.axis_index("seq") == 0)(clear)


def behind_mass_of(shares, powers, segments, queries, keys, behind_keys):
    return pl.pallas_call(
        behind_mass_kernel,
        out_shape=jax.ShapeDtypeStruct(
            (keys.shape[1] // HEAD_DIM, queries.shape[0]), jnp.float32
        ),
        scratch_shapes=[pltpu.VMEM(shares[0].shape, jnp.float32)],
        compiler_params=pltpu.CompilerParams(vmem_limit_bytes=VMEM_BYTES),
    )(*shares, powers, segments, queries, keys, behind_keys)


def attend_kernel(*refs):
    *share_refs, powers_ref, segments_ref, queries_ref, keys_ref, behind_keys_ref = refs[:7]
    values_ref, behind_values_ref, attended_hbm, mass_ref, retention, attended_ref, done = refs[7:]
    rows = queries_ref.shape[0]
    group_size = queries_ref.shape[1] // keys_ref.shape[1]

    def copy_out(piece):
        columns = slice(piece * PIECE_HEADS * HEAD_DIM, (piece + 1) * PIECE_HEADS * HEAD_DIM)
        return pltpu.make_async_copy(
            attended_ref.at[:, columns], attended_hbm.at[:, columns], done.at[piece]
        )

    def finish():
        for piece in range(done.shape[0]):
            copy_out(piece).wait()

    def fill(whole):
        def group(g, terms_of):
            values = with_behind(values_ref, behind_values_ref, g, whole)
            own = values.shape[0] - rows
            mass = jnp.zeros((1, rows), jnp.float32)
            for head in range(g * group_size, (g + 1) * group_size):
                terms = terms_of(head)
                weights = terms * (1.0 / jnp.sum(terms, axis=1, keepdims=True))
                mass = mass + jnp.sum(weights[:, own:], axis=0, keepdims=True)
                attended_ref[:, head_columns(head)] = jnp.dot(
                    weights.astype(jnp.bfloat16), values, preferred_element_type=jnp.float32
                ).astype(jnp.bfloat16)
                if (head + 1) % PIECE_HEADS == 0:
                    copy_out(head // PIECE_HEADS).start()
            mass_ref[g : g + 1, :] = mass / group_size

        biases = read_retention(share_refs, retention)
        by_group(
            whole,
            biases,
            powers_ref,
            segments_ref,
            queries_ref,
            keys_ref,
            behind_keys_ref,
            group,
            finish,
        )

    pl.when(lax.axis_index("seq") > 0)(lambda: fill(True))
    pl.when(lax.axis_index("seq") == 0)(lambda: fill(False))


def attend(shares, powers, segments, queries, keys, behind_keys, values, behind_values, sent):
    rows = queries.shape[0]
    shares, powers, sent = lax.optimization_barrier((shares, powers, sent))
    attended, mass = pl.pallas_call(
        attend_kernel,
        out_specs=(
            pl.BlockSpec(memory_space=pl.ANY),
            pl.BlockSpec(memory_space=pltpu.VMEM),
        ),
        out_shape=(
            jax.ShapeDtypeStruct(queries.shape, jnp.bfloat16),
            jax.ShapeDtypeStruct((keys.shape[1] // HEAD_DIM, rows), jnp.float32),
        ),
        scratch_shapes=[
            pltpu.VMEM(shares[0].shape, jnp.float32),
            pltpu.VMEM(queries.shape, jnp.bfloat16),
            pltpu.SemaphoreType.DMA((queries.shape[1] // HEAD_DIM // PIECE_HEADS,)),
        ],
        compiler_params=pltpu.CompilerParams(vmem_limit_bytes=VMEM_BYTES),
        cost_estimate=pl.CostEstimate(
            flops=4 * rows * rows * queries.shape[1],
            bytes_accessed=4 * queries.size,
            transcendentals=0,
        ),
    )(*shares, powers, segments, queries, keys, behind_keys, values, behind_values)
    return attended, mass, sent


def pair_device(
    activations, conv_taps, gate_in, gate_out, queries, key_vectors, value_vectors, segment_ids
):
    rows = activations.shape[0]
    swap = [(0, 1), (1, 0)]
    segments = segment_ids.reshape(2, rows)
    gate_out = jnp.transpose(gate_out)

    peer_rows = lax.ppermute(activations, "seq", swap)

    def own_work(activations, conv_taps, gate_in, gate_out):
        part, *held = own_project(activations, conv_taps, gate_in)
        return partial_logits(*head_sum(part), gate_out, 0), held

    own_share, held = in_one_piece(own_work, activations, conv_taps, gate_in, gate_out)
    peer_rows, own_share, held = lax.optimization_barrier((peer_rows, own_share, held))
    near, far = peer_project(peer_rows, *held)
    behind_keys = lax.ppermute(key_vectors, "seq", swap)
    behind_values = lax.ppermute(value_vectors, "seq", swap)
    near, near_in = head_sum(near)
    far_share = far_logits(far, gate_out)
    share = logits_share(own_share, far_share, near, near_in, gate_out)
    share, queries = lax.optimization_barrier((share, queries))
    powers = powers_of(segments, queries, key_vectors, behind_keys)
    count = lax.axis_size("heads")
    across = [
        (seq * count + head, (1 - seq) * count + (head ^ 1))
        for seq in range(2)
        for head in range(count)
    ]
    shares = (share, lax.ppermute(share, ("seq", "heads"), across))
    given = (shares, powers, segments, queries, key_vectors, behind_keys)
    sent = behind_mass_of(*given)
    attended, own_mass, sent = attend(*given, value_vectors, behind_values, sent)
    key_mass = own_mass + lax.ppermute(sent, "seq", swap)
    return (attended, key_mass.astype(jnp.bfloat16))


def from_behind(block, axis, distance):
    devices = range(lax.axis_size(axis))
    route = [(i - distance, i) for i in devices if i - distance in devices]
    return lax.ppermute(block, axis, route)


def block_scores(query_heads, key_block, bias_block, allowed, score_scale):
    scores = (
        jnp.einsum("tgeh,kgh->getk", query_heads, key_block, preferred_element_type=jnp.float32)
        * score_scale
    )
    scores = scores + jnp.transpose(bias_block.astype(jnp.float32))[:, None, None, :]
    return jnp.where(allowed[None, None], scores, NEG_FILL)


def ring_device(
    activations, conv_taps, gate_in, gate_out, queries, key_vectors, value_vectors, segment_ids
):
    shard_rows = activations.shape[0]
    tap_count = conv_taps.shape[0]
    rim_rows = from_behind(activations[shard_rows - (tap_count - 1) :], "seq", 1)
    widened = jnp.concatenate([rim_rows, activations], 0).astype(jnp.float32)
    summed = jnp.zeros(activations.shape, jnp.float32)
    for shift_back in range(tap_count):
        start_row = tap_count - 1 - shift_back
        summed = (
            summed
            + conv_taps[shift_back].astype(jnp.float32)
            * widened[start_row : start_row + shard_rows]
        )
    mixed_rows = summed.astype(jnp.bfloat16)
    partial_hidden = jnp.dot(
        mixed_rows,
        lax.all_gather(gate_in, "seq", axis=1, tiled=True),
        preferred_element_type=jnp.float32,
    )
    kv_local = key_vectors.shape[1] // HEAD_DIM
    group_size = QUERY_HEADS // KV_HEADS
    head_rank = lax.axis_index("heads")
    hidden = jax.nn.silu(lax.psum(partial_hidden, "heads")).astype(jnp.bfloat16)
    logits = jnp.dot(hidden, gate_out, preferred_element_type=jnp.float32)
    retention = lax.dynamic_slice_in_dim(
        jax.nn.log_sigmoid(logits).astype(jnp.bfloat16), head_rank * kv_local, kv_local, 1
    )
    seq_rank = lax.axis_index("seq")
    local_index = jnp.arange(shard_rows, dtype=jnp.int32)
    own_queries, own_keys, own_values, own_bias = (queries, key_vectors, value_vectors, retention)
    query_places = seq_rank * shard_rows + local_index
    query_segments = jnp.take(segment_ids, query_places)
    query_heads = own_queries.reshape(shard_rows, kv_local, group_size, HEAD_DIM)
    score_scale = 1.0 / math.sqrt(HEAD_DIM)

    def visibility(flat_index):
        key_segments = jnp.take(segment_ids, flat_index)
        return (flat_index[None, :] <= query_places[:, None]) & (
            key_segments[None, :] == query_segments[:, None]
        )

    initial = (
        jnp.full((kv_local, group_size, shard_rows), NEG_FILL, jnp.float32),
        jnp.zeros((kv_local, group_size, shard_rows), jnp.float32),
    )
    all_keys, all_values, all_bias = (
        lax.all_gather(own_keys, "seq", axis=0, tiled=True),
        lax.all_gather(own_values, "seq", axis=0, tiled=True),
        lax.all_gather(own_bias, "seq", axis=0, tiled=True),
    )
    piece_rows = all_keys.shape[0]
    stats_block_width = math.gcd(piece_rows, 512)

    def one_block(block_number, state_in):
        offset = block_number * stats_block_width
        key_block = lax.dynamic_slice_in_dim(all_keys, offset, stats_block_width, 0).reshape(
            stats_block_width, kv_local, HEAD_DIM
        )
        bias_block = lax.dynamic_slice_in_dim(all_bias, offset, stats_block_width, 0)
        allowed = visibility(0 + offset + jnp.arange(stats_block_width, dtype=jnp.int32))

        def update(state_old):
            peak_old, mass_old = state_old
            masked = block_scores(query_heads, key_block, bias_block, allowed, score_scale)
            peak_new = jnp.maximum(peak_old, jnp.max(masked, axis=3))
            exponent = jnp.where(allowed[None, None], jnp.exp(masked - peak_new[..., None]), 0.0)
            return (peak_new, mass_old * jnp.exp(peak_old - peak_new) + jnp.sum(exponent, axis=3))

        def keep_state(state_old):
            return state_old

        return lax.cond(jnp.any(allowed), update, keep_state, state_in)

    row_peak, total_mass = lax.fori_loop(0, piece_rows // stats_block_width, one_block, initial)
    total_keys = all_keys.shape[0]
    block_width = math.gcd(total_keys, 512)
    block_count = total_keys // block_width
    key_blocks = all_keys.reshape(block_count, block_width, kv_local, HEAD_DIM)
    value_blocks = all_values.reshape(block_count, block_width, kv_local, HEAD_DIM)
    bias_blocks = all_bias.reshape(block_count, block_width, kv_local)

    def second_pass(accumulated, block_items):
        block_number, key_block, value_block, bias_block = block_items
        allowed = visibility(block_number * block_width + jnp.arange(block_width, dtype=jnp.int32))

        def attend(accum_in):
            masked = block_scores(query_heads, key_block, bias_block, allowed, score_scale)
            weights = (
                jnp.where(allowed[None, None], jnp.exp(masked - row_peak[..., None]), 0.0)
                / total_mass[..., None]
            )
            accum_out = accum_in + jnp.einsum(
                "getk,kgh->tgeh",
                weights.astype(jnp.bfloat16),
                value_block,
                preferred_element_type=jnp.float32,
            )
            return (accum_out, jnp.transpose(jnp.sum(weights, axis=(1, 2))) / group_size)

        def skip_block(accum_in):
            return (accum_in, jnp.zeros((block_width, kv_local), jnp.float32))

        return lax.cond(jnp.any(allowed), attend, skip_block, accumulated)

    accumulated, mass_blocks = lax.scan(
        second_pass,
        jnp.zeros((shard_rows, kv_local, group_size, HEAD_DIM), jnp.float32),
        (jnp.arange(block_count, dtype=jnp.int32), key_blocks, value_blocks, bias_blocks),
    )
    key_term = mass_blocks.reshape(total_keys, kv_local)
    key_mass = lax.psum_scatter(key_term, "seq", scatter_dimension=0, tiled=True).astype(
        jnp.bfloat16
    )
    attended = accumulated.reshape(shard_rows, kv_local * group_size * HEAD_DIM).astype(
        jnp.bfloat16
    )
    return (attended, jnp.transpose(key_mass))


def solution(mesh):
    return jax.shard_map(
        pair_device if mesh.shape["seq"] == 2 else ring_device,
        mesh=mesh,
        in_specs=(
            P(("dp", "seq"), "heads"),
            P(None, "heads"),
            P("heads", "seq"),
            P(),
            P(("dp", "seq"), "heads"),
            P(("dp", "seq"), "heads"),
            P(("dp", "seq"), "heads"),
            P("dp"),
        ),
        out_specs=(P(("dp", "seq"), "heads"), P("heads", ("dp", "seq"))),
        check_vma=False,
    )
```

```python
import functools
import math

import jax
import jax.numpy as jnp
from jax import lax
from jax.experimental import pallas as pl
from jax.experimental.pallas import tpu as pltpu
from jax.sharding import PartitionSpec as P

QUERY_HEADS = 64
KV_HEADS = 8
HEAD_DIM = 128


NEG_FILL = -1e30
RIM_ROWS = 16
PIECE_HEADS = 4
LEAST_RETENTION = -40.0
VMEM_BYTES = 16 * 1024 * 1024


def convolve(widened, taps, lead, rows):
    summed = jnp.zeros((rows, widened.shape[1]), jnp.float32)
    for back in range(taps.shape[0]):
        summed = summed + taps[back : back + 1] * widened[lead - back : lead - back + rows]
    return summed.astype(jnp.bfloat16)


def own_project_kernel(rows_ref, taps_ref, gate_ref, out_ref, held_taps_ref, held_ref, widened):
    rows, features = rows_ref.shape
    held_taps_ref[...] = taps_ref[...]
    held_ref[:features] = gate_ref[...]
    tile = widened.shape[2]
    total = jnp.zeros(out_ref.shape, jnp.float32)
    for step in range(features // tile):
        columns = slice(step * tile, (step + 1) * tile)
        edges = features + step * 2 * RIM_ROWS
        held_ref[edges : edges + RIM_ROWS, :tile] = rows_ref[:RIM_ROWS, columns]
        held_ref[edges + RIM_ROWS : edges + 2 * RIM_ROWS, :tile] = rows_ref[
            rows - RIM_ROWS :, columns
        ]
        wide = widened.at[step % 2]
        wide[...] = rows_ref[:, columns].astype(jnp.float32)
        taps = taps_ref[:, columns]
        mixed = convolve(wide, taps, RIM_ROWS, rows - RIM_ROWS)
        total = total + jnp.dot(mixed, gate_ref[columns, :], preferred_element_type=jnp.float32)
    out_ref[...] = total


def peer_project_kernel(
    peer_ref, taps_ref, held_ref, near_ref, far_ref, widened, own_widened
):
    rows, features = peer_ref.shape
    tile = widened.shape[2]
    first = lax.axis_index("seq") == 0
    half = near_ref.shape[1]
    total = jnp.zeros((near_ref.shape[0], 2 * half), jnp.float32)
    for step in range(features // tile):
        columns = slice(step * tile, (step + 1) * tile)
        wide, own_wide = widened.at[step % 2], own_widened.at[step % 2]
        edges = held_ref.at[
            features + step * 2 * RIM_ROWS : features + (step + 1) * 2 * RIM_ROWS, :tile
        ]
        own_tail = edges[RIM_ROWS:].astype(jnp.float32)
        peer_tail = peer_ref[rows - RIM_ROWS :, columns].astype(jnp.float32)
        wide[:RIM_ROWS] = jnp.where(first, own_tail, 0.0)
        wide[RIM_ROWS:] = peer_ref[:, columns].astype(jnp.float32)
        own_wide[:RIM_ROWS] = jnp.where(first, 0.0, peer_tail)
        own_wide[RIM_ROWS:] = edges[:RIM_ROWS].astype(jnp.float32)
        taps = taps_ref[:, columns]
        mixed = jnp.concatenate(
            [
                convolve(own_wide, taps, RIM_ROWS, RIM_ROWS),
                convolve(wide, taps, RIM_ROWS, rows),
            ],
            axis=0,
        )
        total = total + jnp.dot(mixed, held_ref[columns, :], preferred_element_type=jnp.float32)
    near_ref[...] = total[:, :half]
    far_ref[...] = total[:, half:].astype(jnp.bfloat16)


def own_project(activations, conv_taps, gate_in):
    rows, features = activations.shape
    done = rows - RIM_ROWS
    tile = math.gcd(features, gate_in.shape[1])
    return pl.pallas_call(
        own_project_kernel,
        out_shape=(
            jax.ShapeDtypeStruct((done, gate_in.shape[1]), jnp.float32),
            jax.ShapeDtypeStruct(conv_taps.shape, jnp.float32),
            jax.ShapeDtypeStruct(
                (features + features // tile * 2 * RIM_ROWS, gate_in.shape[1]), gate_in.dtype
            ),
        ),
        scratch_shapes=[pltpu.VMEM((2, rows, tile), jnp.float32)],
        compiler_params=pltpu.CompilerParams(vmem_limit_bytes=VMEM_BYTES),
        cost_estimate=pl.CostEstimate(flops=1, bytes_accessed=1, transcendentals=0),
    )(activations, conv_taps, gate_in)


def peer_project(peer_rows, taps, held):
    rows, features = peer_rows.shape
    done = rows + RIM_ROWS
    tile = math.gcd(features, held.shape[1])
    half = held.shape[1] // 2
    return pl.pallas_call(
        peer_project_kernel,
        out_shape=(
            jax.ShapeDtypeStruct((done, half), jnp.float32),
            jax.ShapeDtypeStruct((done, half), jnp.bfloat16),
        ),
        scratch_shapes=[
            pltpu.VMEM((2, rows + RIM_ROWS, tile), jnp.float32),
            pltpu.VMEM((2, 2 * RIM_ROWS, tile), jnp.float32),
        ],
        compiler_params=pltpu.CompilerParams(vmem_limit_bytes=VMEM_BYTES),
        cost_estimate=pl.CostEstimate(flops=1, bytes_accessed=1, transcendentals=0),
    )(peer_rows, taps, held)


def head_sum(part):
    count = lax.axis_size("heads")
    step = 1
    received = None
    while step < count:
        if received is not None:
            part = part + received.astype(jnp.float32)
        received = exchange_heads(part if step == 1 else part.astype(jnp.bfloat16), step)
        step *= 2
    return part, received


def exchange_heads(block, step):
    count = lax.axis_size("heads")
    return lax.ppermute(block, "heads", [(i, i ^ step) for i in range(count)])


def in_one_piece(work, *given):
    shapes = jax.eval_shape(work, *given)
    return lax.cond(
        lax.axis_index("seq") >= 0,
        work,
        lambda *given: jax.tree.map(lambda like: jnp.zeros(like.shape, like.dtype), shapes),
        *given,
    )


def far_logits(block, gate_out):
    step = lax.axis_size("heads") // 2
    received = exchange_heads(block, step)

    def nearer(block, received, gate_out):
        distance = step
        while distance > 1:
            distance //= 2
            block = block.astype(jnp.float32) + received.astype(jnp.float32)
            received = exchange_heads(block.astype(jnp.bfloat16), distance)
        return partial_logits(block, received, gate_out, block.shape[1])

    return in_one_piece(nearer, block, received, gate_out)


def share_of_logits(pre_ref, in_ref, gate_out_ref, offset):
    pre = pre_ref[...] + in_ref[...].astype(jnp.float32)
    hidden = (pre / (1.0 + jnp.exp(-pre))).astype(jnp.bfloat16)
    share = gate_out_ref.shape[1] // lax.axis_size("seq")
    start = pl.multiple_of(lax.axis_index("seq") * share + offset, HEAD_DIM)
    gate_columns = gate_out_ref[:, pl.ds(start, pre.shape[1])].astype(jnp.bfloat16)
    return lax.dot_general(
        gate_columns, hidden, (((1,), (1,)), ((), ())), preferred_element_type=jnp.float32
    )


def partial_logits_kernel(offset, own_ref, in_ref, gate_out_ref, out_ref):
    out_ref[...] = share_of_logits(own_ref, in_ref, gate_out_ref, offset)


def partial_logits(part, received, gate_out, offset):
    return pl.pallas_call(
        functools.partial(partial_logits_kernel, offset),
        out_shape=jax.ShapeDtypeStruct((gate_out.shape[0], part.shape[0]), jnp.float32),
        compiler_params=pltpu.CompilerParams(vmem_limit_bytes=VMEM_BYTES),
    )(part, received, gate_out)


def logits_kernel(own_ref, far_share_ref, near_ref, near_in_ref, gate_out_ref, out_ref):
    first = lax.axis_index("seq") == 0
    share = share_of_logits(near_ref, near_in_ref, gate_out_ref, 0) + far_share_ref[...]
    own = jnp.concatenate([share[:, :RIM_ROWS], own_ref[...]], axis=1)
    peer = share[:, RIM_ROWS:]
    out_ref[0] = jnp.where(first, own, peer)
    out_ref[1] = jnp.where(first, peer, own)


def logits_share(own_share, far_share, near, near_in, gate_out):
    rows = own_share.shape[1] + RIM_ROWS
    return pl.pallas_call(
        logits_kernel,
        out_shape=jax.ShapeDtypeStruct((2, gate_out.shape[0], rows), jnp.float32),
        compiler_params=pltpu.CompilerParams(vmem_limit_bytes=VMEM_BYTES),
    )(own_share, far_share, near, near_in, gate_out)


def hide_unseen(seq_rank, segments_ref, rows):
    own_segments = segments_ref[pl.ds(seq_rank, 1), :]
    behind_segments = segments_ref[pl.ds(0, 1), :]
    query_segments = jnp.transpose(jnp.broadcast_to(own_segments, (rows, rows)))
    query_at = lax.broadcasted_iota(jnp.int32, (rows, rows), 0)
    key_at = lax.broadcasted_iota(jnp.int32, (rows, rows), 1)
    see_own = (key_at <= query_at) & (query_segments == own_segments)
    see_behind = (query_segments == behind_segments) & (seq_rank > 0)
    return jnp.where(jnp.concatenate([see_behind, see_own], axis=1), 0.0, NEG_FILL)


def head_columns(number):
    return slice(number * HEAD_DIM, (number + 1) * HEAD_DIM)


def scores_of(queries_ref, keys, offset, head):
    scores = lax.dot_general(
        queries_ref[:, head_columns(head)],
        keys,
        (((1,), (1,)), ((), ())),
        preferred_element_type=jnp.float32,
    )
    return scores * (1.0 / math.sqrt(HEAD_DIM)) + offset


def with_behind(ref, behind_ref, number, whole):
    own = ref[:, head_columns(number)]
    if not whole:
        return own
    return jnp.concatenate([behind_ref[:, head_columns(number)], own], axis=0)


def powers_kernel(segments_ref, queries_ref, keys_ref, behind_keys_ref, powers_ref):
    seq_rank = lax.axis_index("seq")
    rows = queries_ref.shape[0]
    kv_local = keys_ref.shape[1] // HEAD_DIM
    group_size = queries_ref.shape[1] // keys_ref.shape[1]
    hide = hide_unseen(seq_rank, segments_ref, rows)

    def fill(whole):
        start = 0 if whole else rows
        for head in range(kv_local * group_size):
            g = head // group_size
            keys = with_behind(keys_ref, behind_keys_ref, g, whole)
            scores = scores_of(queries_ref, keys, hide[:, start:], head)
            powers_ref[head, :, start:] = jnp.exp(
                scores - jnp.max(scores, axis=1, keepdims=True)
            )

    pl.when(seq_rank > 0)(lambda: fill(True))
    pl.when(seq_rank == 0)(lambda: fill(False))


def powers_of(segments, queries, keys, behind_keys):
    rows = queries.shape[0]
    heads = queries.shape[1] // HEAD_DIM
    return pl.pallas_call(
        powers_kernel,
        out_shape=jax.ShapeDtypeStruct((heads, rows, 2 * rows), jnp.float32),
        compiler_params=pltpu.CompilerParams(vmem_limit_bytes=VMEM_BYTES),
        cost_estimate=pl.CostEstimate(
            flops=4 * rows * rows * queries.shape[1],
            bytes_accessed=8 * heads * rows * rows,
            transcendentals=2 * heads * rows * rows,
        ),
    )(segments, queries, keys, behind_keys)


def read_retention(share_refs, retention):
    seq_rank, head_rank = lax.axis_index("seq"), lax.axis_index("heads")
    logits = share_refs[0][...] + share_refs[1][...]
    log_gate = jnp.minimum(logits, 0.0) - jnp.log1p(jnp.exp(-jnp.abs(logits)))
    retention[...] = log_gate.astype(jnp.bfloat16).astype(jnp.float32)
    kv_local = retention.shape[1] // lax.axis_size("heads")
    biases = []
    for g in range(kv_local):
        at = pl.ds(head_rank * kv_local + g, 1)
        biases.append(jnp.concatenate([retention[0, at, :], retention[seq_rank, at, :]], axis=1))
    return biases


def by_group(
    whole,
    biases,
    powers_ref,
    segments_ref,
    queries_ref,
    keys_ref,
    behind_keys_ref,
    group,
    finish=None,
):
    rows = queries_ref.shape[0]
    start = 0 if whole else rows
    moderate = jnp.min(functools.reduce(jnp.minimum, biases)) >= LEAST_RETENTION

    def by_powers(g):
        factor = jnp.exp(biases[g] - jnp.max(biases[g]))[:, start:]
        return lambda head: powers_ref[head, :, start:] * factor

    def by_scores(g):
        hide = hide_unseen(lax.axis_index("seq"), segments_ref, rows)
        offset = (hide + biases[g])[:, start:]
        keys = with_behind(keys_ref, behind_keys_ref, g, whole)

        def terms(head):
            scores = scores_of(queries_ref, keys, offset, head)
            return jnp.exp(scores - jnp.max(scores, axis=1, keepdims=True))

        return terms

    def run(terms_of):
        for g in range(len(biases)):
            group(g, terms_of(g))

        if finish is not None:
            finish()

    pl.when(moderate)(lambda: run(by_powers))
    pl.when(jnp.logical_not(moderate))(lambda: run(by_scores))


def behind_mass_kernel(*refs):
    *share_refs, powers_ref, segments_ref, queries_ref, keys_ref, behind_keys_ref = refs[:7]
    mass_ref, retention = refs[7:]
    rows = queries_ref.shape[0]
    group_size = queries_ref.shape[1] // keys_ref.shape[1]

    def group(g, terms_of):
        mass = jnp.zeros((1, rows), jnp.float32)
        for head in range(g * group_size, (g + 1) * group_size):
            terms = terms_of(head)
            weights = terms[:, :rows] * (1.0 / jnp.sum(terms, axis=1, keepdims=True))
            mass = mass + jnp.sum(weights, axis=0, keepdims=True)
        mass_ref[g : g + 1, :] = mass / group_size

    def fill():
        biases = read_retention(share_refs, retention)
        by_group(
            True, biases, powers_ref, segments_ref, queries_ref, keys_ref, behind_keys_ref, group
        )

    def clear():
        mass_ref[...] = jnp.zeros(mass_ref.shape, jnp.float32)

    pl.when(lax.axis_index("seq") > 0)(fill)
    pl.when(lax.axis_index("seq") == 0)(clear)


def behind_mass_of(shares, powers, segments, queries, keys, behind_keys):
    return pl.pallas_call(
        behind_mass_kernel,
        out_shape=jax.ShapeDtypeStruct(
            (keys.shape[1] // HEAD_DIM, queries.shape[0]), jnp.float32
        ),
        scratch_shapes=[pltpu.VMEM(shares[0].shape, jnp.float32)],
        compiler_params=pltpu.CompilerParams(vmem_limit_bytes=VMEM_BYTES),
    )(*shares, powers, segments, queries, keys, behind_keys)


def attend_kernel(*refs):
    *share_refs, powers_ref, segments_ref, queries_ref, keys_ref, behind_keys_ref = refs[:7]
    values_ref, behind_values_ref, attended_hbm, mass_ref, retention, attended_ref, done = refs[7:]
    rows = queries_ref.shape[0]
    group_size = queries_ref.shape[1] // keys_ref.shape[1]

    def copy_out(piece):
        columns = slice(piece * PIECE_HEADS * HEAD_DIM, (piece + 1) * PIECE_HEADS * HEAD_DIM)
        return pltpu.make_async_copy(
            attended_ref.at[:, columns], attended_hbm.at[:, columns], done.at[piece]
        )

    def finish():
        for piece in range(done.shape[0]):
            copy_out(piece).wait()

    def fill(whole):
        def group(g, terms_of):
            values = with_behind(values_ref, behind_values_ref, g, whole)
            own = values.shape[0] - rows
            mass = jnp.zeros((1, rows), jnp.float32)
            for head in range(g * group_size, (g + 1) * group_size):
                terms = terms_of(head)
                weights = terms * (1.0 / jnp.sum(terms, axis=1, keepdims=True))
                mass = mass + jnp.sum(weights[:, own:], axis=0, keepdims=True)
                attended_ref[:, head_columns(head)] = jnp.dot(
                    weights.astype(jnp.bfloat16), values, preferred_element_type=jnp.float32
                ).astype(jnp.bfloat16)
                if (head + 1) % PIECE_HEADS == 0:
                    copy_out(head // PIECE_HEADS).start()
            mass_ref[g : g + 1, :] = mass / group_size

        biases = read_retention(share_refs, retention)
        by_group(
            whole,
            biases,
            powers_ref,
            segments_ref,
            queries_ref,
            keys_ref,
            behind_keys_ref,
            group,
            finish,
        )

    pl.when(lax.axis_index("seq") > 0)(lambda: fill(True))
    pl.when(lax.axis_index("seq") == 0)(lambda: fill(False))


def attend(shares, powers, segments, queries, keys, behind_keys, values, behind_values, sent):
    rows = queries.shape[0]
    shares, powers, sent = lax.optimization_barrier((shares, powers, sent))
    attended, mass = pl.pallas_call(
        attend_kernel,
        out_specs=(
            pl.BlockSpec(memory_space=pl.ANY),
            pl.BlockSpec(memory_space=pltpu.VMEM),
        ),
        out_shape=(
            jax.ShapeDtypeStruct(queries.shape, jnp.bfloat16),
            jax.ShapeDtypeStruct((keys.shape[1] // HEAD_DIM, rows), jnp.float32),
        ),
        scratch_shapes=[
            pltpu.VMEM(shares[0].shape, jnp.float32),
            pltpu.VMEM(queries.shape, jnp.bfloat16),
            pltpu.SemaphoreType.DMA((queries.shape[1] // HEAD_DIM // PIECE_HEADS,)),
        ],
        compiler_params=pltpu.CompilerParams(vmem_limit_bytes=VMEM_BYTES),
        cost_estimate=pl.CostEstimate(
            flops=4 * rows * rows * queries.shape[1],
            bytes_accessed=4 * queries.size,
            transcendentals=0,
        ),
    )(*shares, powers, segments, queries, keys, behind_keys, values, behind_values)
    return attended, mass, sent


def pair_device(
    activations, conv_taps, gate_in, gate_out, queries, key_vectors, value_vectors, segment_ids
):
    rows = activations.shape[0]
    swap = [(0, 1), (1, 0)]
    segments = segment_ids.reshape(2, rows)
    gate_out = jnp.transpose(gate_out).astype(jnp.float32)
    conv_taps = conv_taps.astype(jnp.float32)

    peer_rows = lax.ppermute(activations, "seq", swap)

    def own_work(activations, conv_taps, gate_in, gate_out):
        part, *held = own_project(activations, conv_taps, gate_in)
        return partial_logits(*head_sum(part), gate_out, 0), held

    own_share, held = in_one_piece(own_work, activations, conv_taps, gate_in, gate_out)
    peer_rows, own_share, held = lax.optimization_barrier((peer_rows, own_share, held))
    near, far = peer_project(peer_rows, *held)
    behind_keys = lax.ppermute(key_vectors, "seq", swap)
    behind_values = lax.ppermute(value_vectors, "seq", swap)
    near, near_in = head_sum(near)
    far_share = far_logits(far, gate_out)
    share = logits_share(own_share, far_share, near, near_in, gate_out)
    share, queries = lax.optimization_barrier((share, queries))
    powers = powers_of(segments, queries, key_vectors, behind_keys)
    count = lax.axis_size("heads")
    across = [
        (seq * count + head, (1 - seq) * count + (head ^ 1))
        for seq in range(2)
        for head in range(count)
    ]
    shares = (share, lax.ppermute(share, ("seq", "heads"), across))
    given = (shares, powers, segments, queries, key_vectors, behind_keys)
    sent = behind_mass_of(*given)
    attended, own_mass, sent = attend(*given, value_vectors, behind_values, sent)
    key_mass = own_mass + lax.ppermute(sent, "seq", swap)
    return (attended, key_mass.astype(jnp.bfloat16))


def from_behind(block, axis, distance):
    devices = range(lax.axis_size(axis))
    route = [(i - distance, i) for i in devices if i - distance in devices]
    return lax.ppermute(block, axis, route)


def block_scores(query_heads, key_block, bias_block, allowed, score_scale):
    scores = (
        jnp.einsum("tgeh,kgh->getk", query_heads, key_block, preferred_element_type=jnp.float32)
        * score_scale
    )
    scores = scores + jnp.transpose(bias_block.astype(jnp.float32))[:, None, None, :]
    return jnp.where(allowed[None, None], scores, NEG_FILL)


def ring_device(
    activations, conv_taps, gate_in, gate_out, queries, key_vectors, value_vectors, segment_ids
):
    shard_rows = activations.shape[0]
    tap_count = conv_taps.shape[0]
    rim_rows = from_behind(activations[shard_rows - (tap_count - 1) :], "seq", 1)
    widened = jnp.concatenate([rim_rows, activations], 0).astype(jnp.float32)
    summed = jnp.zeros(activations.shape, jnp.float32)
    for shift_back in range(tap_count):
        start_row = tap_count - 1 - shift_back
        summed = (
            summed
            + conv_taps[shift_back].astype(jnp.float32)
            * widened[start_row : start_row + shard_rows]
        )
    mixed_rows = summed.astype(jnp.bfloat16)
    partial_hidden = jnp.dot(
        mixed_rows,
        lax.all_gather(gate_in, "seq", axis=1, tiled=True),
        preferred_element_type=jnp.float32,
    )
    kv_local = key_vectors.shape[1] // HEAD_DIM
    group_size = QUERY_HEADS // KV_HEADS
    head_rank = lax.axis_index("heads")
    hidden = jax.nn.silu(lax.psum(partial_hidden, "heads")).astype(jnp.bfloat16)
    logits = jnp.dot(hidden, gate_out, preferred_element_type=jnp.float32)
    retention = lax.dynamic_slice_in_dim(
        jax.nn.log_sigmoid(logits).astype(jnp.bfloat16), head_rank * kv_local, kv_local, 1
    )
    seq_rank = lax.axis_index("seq")
    local_index = jnp.arange(shard_rows, dtype=jnp.int32)
    own_queries, own_keys, own_values, own_bias = (queries, key_vectors, value_vectors, retention)
    query_places = seq_rank * shard_rows + local_index
    query_segments = jnp.take(segment_ids, query_places)
    query_heads = own_queries.reshape(shard_rows, kv_local, group_size, HEAD_DIM)
    score_scale = 1.0 / math.sqrt(HEAD_DIM)

    def visibility(flat_index):
        key_segments = jnp.take(segment_ids, flat_index)
        return (flat_index[None, :] <= query_places[:, None]) & (
            key_segments[None, :] == query_segments[:, None]
        )

    initial = (
        jnp.full((kv_local, group_size, shard_rows), NEG_FILL, jnp.float32),
        jnp.zeros((kv_local, group_size, shard_rows), jnp.float32),
    )
    all_keys, all_values, all_bias = (
        lax.all_gather(own_keys, "seq", axis=0, tiled=True),
        lax.all_gather(own_values, "seq", axis=0, tiled=True),
        lax.all_gather(own_bias, "seq", axis=0, tiled=True),
    )
    piece_rows = all_keys.shape[0]
    stats_block_width = math.gcd(piece_rows, 512)

    def one_block(block_number, state_in):
        offset = block_number * stats_block_width
        key_block = lax.dynamic_slice_in_dim(all_keys, offset, stats_block_width, 0).reshape(
            stats_block_width, kv_local, HEAD_DIM
        )
        bias_block = lax.dynamic_slice_in_dim(all_bias, offset, stats_block_width, 0)
        allowed = visibility(0 + offset + jnp.arange(stats_block_width, dtype=jnp.int32))

        def update(state_old):
            peak_old, mass_old = state_old
            masked = block_scores(query_heads, key_block, bias_block, allowed, score_scale)
            peak_new = jnp.maximum(peak_old, jnp.max(masked, axis=3))
            exponent = jnp.where(allowed[None, None], jnp.exp(masked - peak_new[..., None]), 0.0)
            return (peak_new, mass_old * jnp.exp(peak_old - peak_new) + jnp.sum(exponent, axis=3))

        def keep_state(state_old):
            return state_old

        return lax.cond(jnp.any(allowed), update, keep_state, state_in)

    row_peak, total_mass = lax.fori_loop(0, piece_rows // stats_block_width, one_block, initial)
    total_keys = all_keys.shape[0]
    block_width = math.gcd(total_keys, 512)
    block_count = total_keys // block_width
    key_blocks = all_keys.reshape(block_count, block_width, kv_local, HEAD_DIM)
    value_blocks = all_values.reshape(block_count, block_width, kv_local, HEAD_DIM)
    bias_blocks = all_bias.reshape(block_count, block_width, kv_local)

    def second_pass(accumulated, block_items):
        block_number, key_block, value_block, bias_block = block_items
        allowed = visibility(block_number * block_width + jnp.arange(block_width, dtype=jnp.int32))

        def attend(accum_in):
            masked = block_scores(query_heads, key_block, bias_block, allowed, score_scale)
            weights = (
                jnp.where(allowed[None, None], jnp.exp(masked - row_peak[..., None]), 0.0)
                / total_mass[..., None]
            )
            accum_out = accum_in + jnp.einsum(
                "getk,kgh->tgeh",
                weights.astype(jnp.bfloat16),
                value_block,
                preferred_element_type=jnp.float32,
            )
            return (accum_out, jnp.transpose(jnp.sum(weights, axis=(1, 2))) / group_size)

        def skip_block(accum_in):
            return (accum_in, jnp.zeros((block_width, kv_local), jnp.float32))

        return lax.cond(jnp.any(allowed), attend, skip_block, accumulated)

    accumulated, mass_blocks = lax.scan(
        second_pass,
        jnp.zeros((shard_rows, kv_local, group_size, HEAD_DIM), jnp.float32),
        (jnp.arange(block_count, dtype=jnp.int32), key_blocks, value_blocks, bias_blocks),
    )
    key_term = mass_blocks.reshape(total_keys, kv_local)
    key_mass = lax.psum_scatter(key_term, "seq", scatter_dimension=0, tiled=True).astype(
        jnp.bfloat16
    )
    attended = accumulated.reshape(shard_rows, kv_local * group_size * HEAD_DIM).astype(
        jnp.bfloat16
    )
    return (attended, jnp.transpose(key_mass))


def solution(mesh):
    return jax.shard_map(
        pair_device if mesh.shape["seq"] == 2 else ring_device,
        mesh=mesh,
        in_specs=(
            P(("dp", "seq"), "heads"),
            P(None, "heads"),
            P("heads", "seq"),
            P(),
            P(("dp", "seq"), "heads"),
            P(("dp", "seq"), "heads"),
            P(("dp", "seq"), "heads"),
            P("dp"),
        ),
        out_specs=(P(("dp", "seq"), "heads"), P("heads", ("dp", "seq"))),
        check_vma=False,
    )
```

```python
import functools
import math

import jax
import jax.numpy as jnp
from jax import lax
from jax.experimental import pallas as pl
from jax.experimental.pallas import tpu as pltpu
from jax.sharding import PartitionSpec as P

QUERY_HEADS = 64
KV_HEADS = 8
HEAD_DIM = 128


NEG_FILL = -1e30
RIM_ROWS = 16
PIECE_HEADS = 2
LEAST_RETENTION = -40.0
VMEM_BYTES = 16 * 1024 * 1024


def convolve(widened, taps, lead, rows):
    summed = jnp.zeros((rows, widened.shape[1]), jnp.float32)
    for back in range(taps.shape[0]):
        summed = summed + taps[back : back + 1] * widened[lead - back : lead - back + rows]
    return summed.astype(jnp.bfloat16)


def own_project_kernel(rows_ref, taps_ref, gate_ref, out_ref, held_taps_ref, held_ref, widened):
    rows, features = rows_ref.shape
    held_taps_ref[...] = taps_ref[...].astype(jnp.float32)
    held_ref[:features] = gate_ref[...]
    tile = widened.shape[2]
    total = jnp.zeros(out_ref.shape, jnp.float32)
    for step in range(features // tile):
        columns = slice(step * tile, (step + 1) * tile)
        edges = features + step * 2 * RIM_ROWS
        held_ref[edges : edges + RIM_ROWS, :tile] = rows_ref[:RIM_ROWS, columns]
        held_ref[edges + RIM_ROWS : edges + 2 * RIM_ROWS, :tile] = rows_ref[
            rows - RIM_ROWS :, columns
        ]
        wide = widened.at[step % 2]
        wide[...] = rows_ref[:, columns].astype(jnp.float32)
        taps = taps_ref[:, columns].astype(jnp.float32)
        mixed = convolve(wide, taps, RIM_ROWS, rows - RIM_ROWS)
        total = total + jnp.dot(mixed, gate_ref[columns, :], preferred_element_type=jnp.float32)
    out_ref[...] = total


def peer_project_kernel(
    peer_ref, taps_ref, held_ref, near_ref, far_ref, widened, own_widened
):
    rows, features = peer_ref.shape
    tile = widened.shape[2]
    first = lax.axis_index("seq") == 0
    half = near_ref.shape[1]
    total = jnp.zeros((near_ref.shape[0], 2 * half), jnp.float32)
    for step in range(features // tile):
        columns = slice(step * tile, (step + 1) * tile)
        wide, own_wide = widened.at[step % 2], own_widened.at[step % 2]
        edges = held_ref.at[
            features + step * 2 * RIM_ROWS : features + (step + 1) * 2 * RIM_ROWS, :tile
        ]
        own_tail = edges[RIM_ROWS:].astype(jnp.float32)
        peer_tail = peer_ref[rows - RIM_ROWS :, columns].astype(jnp.float32)
        wide[:RIM_ROWS] = jnp.where(first, own_tail, 0.0)
        wide[RIM_ROWS:] = peer_ref[:, columns].astype(jnp.float32)
        own_wide[:RIM_ROWS] = jnp.where(first, 0.0, peer_tail)
        own_wide[RIM_ROWS:] = edges[:RIM_ROWS].astype(jnp.float32)
        taps = taps_ref[:, columns].astype(jnp.float32)
        mixed = jnp.concatenate(
            [
                convolve(own_wide, taps, RIM_ROWS, RIM_ROWS),
                convolve(wide, taps, RIM_ROWS, rows),
            ],
            axis=0,
        )
        total = total + jnp.dot(mixed, held_ref[columns, :], preferred_element_type=jnp.float32)
    near_ref[...] = total[:, :half]
    far_ref[...] = total[:, half:].astype(jnp.bfloat16)


def own_project(activations, conv_taps, gate_in):
    rows, features = activations.shape
    done = rows - RIM_ROWS
    tile = math.gcd(features, gate_in.shape[1])
    return pl.pallas_call(
        own_project_kernel,
        out_shape=(
            jax.ShapeDtypeStruct((done, gate_in.shape[1]), jnp.float32),
            jax.ShapeDtypeStruct(conv_taps.shape, jnp.float32),
            jax.ShapeDtypeStruct(
                (features + features // tile * 2 * RIM_ROWS, gate_in.shape[1]), gate_in.dtype
            ),
        ),
        scratch_shapes=[pltpu.VMEM((2, rows, tile), jnp.float32)],
        compiler_params=pltpu.CompilerParams(vmem_limit_bytes=VMEM_BYTES),
        cost_estimate=pl.CostEstimate(flops=1, bytes_accessed=1, transcendentals=0),
    )(activations, conv_taps, gate_in)


def peer_project(peer_rows, taps, held):
    rows, features = peer_rows.shape
    done = rows + RIM_ROWS
    tile = math.gcd(features, held.shape[1])
    half = held.shape[1] // 2
    return pl.pallas_call(
        peer_project_kernel,
        out_shape=(
            jax.ShapeDtypeStruct((done, half), jnp.float32),
            jax.ShapeDtypeStruct((done, half), jnp.bfloat16),
        ),
        scratch_shapes=[
            pltpu.VMEM((2, rows + RIM_ROWS, tile), jnp.float32),
            pltpu.VMEM((2, 2 * RIM_ROWS, tile), jnp.float32),
        ],
        compiler_params=pltpu.CompilerParams(vmem_limit_bytes=VMEM_BYTES),
        cost_estimate=pl.CostEstimate(flops=1, bytes_accessed=1, transcendentals=0),
    )(peer_rows, taps, held)


def head_sum(part):
    count = lax.axis_size("heads")
    step = 1
    received = None
    while step < count:
        if received is not None:
            part = part + received.astype(jnp.float32)
        received = exchange_heads(part if step == 1 else part.astype(jnp.bfloat16), step)
        step *= 2
    return part, received


def exchange_heads(block, step):
    count = lax.axis_size("heads")
    return lax.ppermute(block, "heads", [(i, i ^ step) for i in range(count)])


def in_one_piece(work, *given):
    shapes = jax.eval_shape(work, *given)
    return lax.cond(
        lax.axis_index("seq") >= 0,
        work,
        lambda *given: jax.tree.map(lambda like: jnp.zeros(like.shape, like.dtype), shapes),
        *given,
    )


def far_logits(block, gate_out):
    step = lax.axis_size("heads") // 2
    received = exchange_heads(block, step)

    def nearer(block, received, gate_out):
        distance = step
        while distance > 1:
            distance //= 2
            block = block.astype(jnp.float32) + received.astype(jnp.float32)
            received = exchange_heads(block.astype(jnp.bfloat16), distance)
        return partial_logits(block, received, gate_out, block.shape[1])

    return in_one_piece(nearer, block, received, gate_out)


def share_of_logits(pre_ref, in_ref, gate_out_ref, offset):
    pre = pre_ref[...] + in_ref[...].astype(jnp.float32)
    hidden = (pre / (1.0 + jnp.exp(-pre))).astype(jnp.bfloat16)
    share = gate_out_ref.shape[1] // lax.axis_size("seq")
    start = pl.multiple_of(lax.axis_index("seq") * share + offset, HEAD_DIM)
    gate_columns = gate_out_ref[:, pl.ds(start, pre.shape[1])]
    return lax.dot_general(
        gate_columns, hidden, (((1,), (1,)), ((), ())), preferred_element_type=jnp.float32
    )


def partial_logits_kernel(offset, own_ref, in_ref, gate_out_ref, out_ref):
    out_ref[...] = share_of_logits(own_ref, in_ref, gate_out_ref, offset)


def partial_logits(part, received, gate_out, offset):
    return pl.pallas_call(
        functools.partial(partial_logits_kernel, offset),
        out_shape=jax.ShapeDtypeStruct((gate_out.shape[0], part.shape[0]), jnp.float32),
        compiler_params=pltpu.CompilerParams(vmem_limit_bytes=VMEM_BYTES),
    )(part, received, gate_out)


def logits_kernel(own_ref, far_share_ref, near_ref, near_in_ref, gate_out_ref, out_ref):
    first = lax.axis_index("seq") == 0
    share = share_of_logits(near_ref, near_in_ref, gate_out_ref, 0) + far_share_ref[...]
    own = jnp.concatenate([share[:, :RIM_ROWS], own_ref[...]], axis=1)
    peer = share[:, RIM_ROWS:]
    out_ref[0] = jnp.where(first, own, peer)
    out_ref[1] = jnp.where(first, peer, own)


def logits_share(own_share, far_share, near, near_in, gate_out):
    rows = own_share.shape[1] + RIM_ROWS
    return pl.pallas_call(
        logits_kernel,
        out_shape=jax.ShapeDtypeStruct((2, gate_out.shape[0], rows), jnp.float32),
        compiler_params=pltpu.CompilerParams(vmem_limit_bytes=VMEM_BYTES),
    )(own_share, far_share, near, near_in, gate_out)


def hide_unseen(seq_rank, segments_ref, rows):
    own_segments = segments_ref[pl.ds(seq_rank, 1), :]
    behind_segments = segments_ref[pl.ds(0, 1), :]
    query_segments = jnp.transpose(jnp.broadcast_to(own_segments, (rows, rows)))
    query_at = lax.broadcasted_iota(jnp.int32, (rows, rows), 0)
    key_at = lax.broadcasted_iota(jnp.int32, (rows, rows), 1)
    see_own = (key_at <= query_at) & (query_segments == own_segments)
    see_behind = (query_segments == behind_segments) & (seq_rank > 0)
    return jnp.where(jnp.concatenate([see_behind, see_own], axis=1), 0.0, NEG_FILL)


def head_columns(number):
    return slice(number * HEAD_DIM, (number + 1) * HEAD_DIM)


def scores_of(queries_ref, keys, offset, head):
    scores = lax.dot_general(
        queries_ref[:, head_columns(head)],
        keys,
        (((1,), (1,)), ((), ())),
        preferred_element_type=jnp.float32,
    )
    return scores * (1.0 / math.sqrt(HEAD_DIM)) + offset


def with_behind(ref, behind_ref, number, whole):
    own = ref[:, head_columns(number)]
    if not whole:
        return own
    return jnp.concatenate([behind_ref[:, head_columns(number)], own], axis=0)


def powers_kernel(segments_ref, queries_ref, keys_ref, behind_keys_ref, powers_ref):
    seq_rank = lax.axis_index("seq")
    rows = queries_ref.shape[0]
    kv_local = keys_ref.shape[1] // HEAD_DIM
    group_size = queries_ref.shape[1] // keys_ref.shape[1]
    hide = hide_unseen(seq_rank, segments_ref, rows)

    def fill(whole):
        start = 0 if whole else rows
        for head in range(kv_local * group_size):
            g = head // group_size
            keys = with_behind(keys_ref, behind_keys_ref, g, whole)
            scores = scores_of(queries_ref, keys, hide[:, start:], head)
            powers_ref[head, :, start:] = jnp.exp(
                scores - jnp.max(scores, axis=1, keepdims=True)
            )

    pl.when(seq_rank > 0)(lambda: fill(True))
    pl.when(seq_rank == 0)(lambda: fill(False))


def powers_of(segments, queries, keys, behind_keys):
    rows = queries.shape[0]
    heads = queries.shape[1] // HEAD_DIM
    return pl.pallas_call(
        powers_kernel,
        out_shape=jax.ShapeDtypeStruct((heads, rows, 2 * rows), jnp.float32),
        compiler_params=pltpu.CompilerParams(vmem_limit_bytes=VMEM_BYTES),
        cost_estimate=pl.CostEstimate(
            flops=4 * rows * rows * queries.shape[1],
            bytes_accessed=8 * heads * rows * rows,
            transcendentals=2 * heads * rows * rows,
        ),
    )(segments, queries, keys, behind_keys)


def read_retention(share_refs, retention):
    seq_rank, head_rank = lax.axis_index("seq"), lax.axis_index("heads")
    logits = share_refs[0][...] + share_refs[1][...]
    log_gate = jnp.minimum(logits, 0.0) - jnp.log1p(jnp.exp(-jnp.abs(logits)))
    retention[...] = log_gate.astype(jnp.bfloat16).astype(jnp.float32)
    kv_local = retention.shape[1] // lax.axis_size("heads")
    biases = []
    for g in range(kv_local):
        at = pl.ds(head_rank * kv_local + g, 1)
        biases.append(jnp.concatenate([retention[0, at, :], retention[seq_rank, at, :]], axis=1))
    return biases


def by_group(
    whole,
    biases,
    powers_ref,
    segments_ref,
    queries_ref,
    keys_ref,
    behind_keys_ref,
    group,
    finish=None,
):
    rows = queries_ref.shape[0]
    start = 0 if whole else rows
    moderate = jnp.min(functools.reduce(jnp.minimum, biases)) >= LEAST_RETENTION

    def by_powers(g):
        factor = jnp.exp(biases[g] - jnp.max(biases[g]))[:, start:]
        return lambda head: powers_ref[head, :, start:] * factor

    def by_scores(g):
        hide = hide_unseen(lax.axis_index("seq"), segments_ref, rows)
        offset = (hide + biases[g])[:, start:]
        keys = with_behind(keys_ref, behind_keys_ref, g, whole)

        def terms(head):
            scores = scores_of(queries_ref, keys, offset, head)
            return jnp.exp(scores - jnp.max(scores, axis=1, keepdims=True))

        return terms

    def run(terms_of):
        for g in range(len(biases)):
            group(g, terms_of(g))

        if finish is not None:
            finish()

    pl.when(moderate)(lambda: run(by_powers))
    pl.when(jnp.logical_not(moderate))(lambda: run(by_scores))


def behind_mass_kernel(*refs):
    *share_refs, powers_ref, segments_ref, queries_ref, keys_ref, behind_keys_ref = refs[:7]
    mass_ref, retention = refs[7:]
    rows = queries_ref.shape[0]
    group_size = queries_ref.shape[1] // keys_ref.shape[1]

    def group(g, terms_of):
        mass = jnp.zeros((1, rows), jnp.float32)
        for head in range(g * group_size, (g + 1) * group_size):
            terms = terms_of(head)
            weights = terms[:, :rows] * (1.0 / jnp.sum(terms, axis=1, keepdims=True))
            mass = mass + jnp.sum(weights, axis=0, keepdims=True)
        mass_ref[g : g + 1, :] = mass / group_size

    def fill():
        biases = read_retention(share_refs, retention)
        by_group(
            True, biases, powers_ref, segments_ref, queries_ref, keys_ref, behind_keys_ref, group
        )

    def clear():
        mass_ref[...] = jnp.zeros(mass_ref.shape, jnp.float32)

    pl.when(lax.axis_index("seq") > 0)(fill)
    pl.when(lax.axis_index("seq") == 0)(clear)


def behind_mass_of(shares, powers, segments, queries, keys, behind_keys):
    return pl.pallas_call(
        behind_mass_kernel,
        out_shape=jax.ShapeDtypeStruct(
            (keys.shape[1] // HEAD_DIM, queries.shape[0]), jnp.float32
        ),
        scratch_shapes=[pltpu.VMEM(shares[0].shape, jnp.float32)],
        compiler_params=pltpu.CompilerParams(vmem_limit_bytes=VMEM_BYTES),
    )(*shares, powers, segments, queries, keys, behind_keys)


def attend_kernel(*refs):
    *share_refs, powers_ref, segments_ref, queries_ref, keys_ref, behind_keys_ref = refs[:7]
    values_ref, behind_values_ref, attended_hbm, mass_ref, retention, attended_ref, done = refs[7:]
    rows = queries_ref.shape[0]
    group_size = queries_ref.shape[1] // keys_ref.shape[1]

    def copy_out(piece):
        columns = slice(piece * PIECE_HEADS * HEAD_DIM, (piece + 1) * PIECE_HEADS * HEAD_DIM)
        return pltpu.make_async_copy(
            attended_ref.at[:, columns], attended_hbm.at[:, columns], done.at[piece]
        )

    def finish():
        for piece in range(done.shape[0]):
            copy_out(piece).wait()

    def fill(whole):
        def group(g, terms_of):
            values = with_behind(values_ref, behind_values_ref, g, whole)
            own = values.shape[0] - rows
            mass = jnp.zeros((1, rows), jnp.float32)
            for head in range(g * group_size, (g + 1) * group_size):
                terms = terms_of(head)
                weights = terms * (1.0 / jnp.sum(terms, axis=1, keepdims=True))
                mass = mass + jnp.sum(weights[:, own:], axis=0, keepdims=True)
                attended_ref[:, head_columns(head)] = jnp.dot(
                    weights.astype(jnp.bfloat16), values, preferred_element_type=jnp.float32
                ).astype(jnp.bfloat16)
                if (head + 1) % PIECE_HEADS == 0:
                    copy_out(head // PIECE_HEADS).start()
            mass_ref[g : g + 1, :] = mass / group_size

        biases = read_retention(share_refs, retention)
        by_group(
            whole,
            biases,
            powers_ref,
            segments_ref,
            queries_ref,
            keys_ref,
            behind_keys_ref,
            group,
            finish,
        )

    pl.when(lax.axis_index("seq") > 0)(lambda: fill(True))
    pl.when(lax.axis_index("seq") == 0)(lambda: fill(False))


def attend(shares, powers, segments, queries, keys, behind_keys, values, behind_values, sent):
    rows = queries.shape[0]
    shares, powers, sent = lax.optimization_barrier((shares, powers, sent))
    attended, mass = pl.pallas_call(
        attend_kernel,
        out_specs=(
            pl.BlockSpec(memory_space=pl.ANY),
            pl.BlockSpec(memory_space=pltpu.VMEM),
        ),
        out_shape=(
            jax.ShapeDtypeStruct(queries.shape, jnp.bfloat16),
            jax.ShapeDtypeStruct((keys.shape[1] // HEAD_DIM, rows), jnp.float32),
        ),
        scratch_shapes=[
            pltpu.VMEM(shares[0].shape, jnp.float32),
            pltpu.VMEM(queries.shape, jnp.bfloat16),
            pltpu.SemaphoreType.DMA((queries.shape[1] // HEAD_DIM // PIECE_HEADS,)),
        ],
        compiler_params=pltpu.CompilerParams(vmem_limit_bytes=VMEM_BYTES),
        cost_estimate=pl.CostEstimate(
            flops=4 * rows * rows * queries.shape[1],
            bytes_accessed=4 * queries.size,
            transcendentals=0,
        ),
    )(*shares, powers, segments, queries, keys, behind_keys, values, behind_values)
    return attended, mass, sent


def pair_device(
    activations, conv_taps, gate_in, gate_out, queries, key_vectors, value_vectors, segment_ids
):
    rows = activations.shape[0]
    swap = [(0, 1), (1, 0)]
    segments = segment_ids.reshape(2, rows)
    gate_out = jnp.transpose(gate_out)

    peer_rows = lax.ppermute(activations, "seq", swap)

    def own_work(activations, conv_taps, gate_in, gate_out):
        part, *held = own_project(activations, conv_taps, gate_in)
        return partial_logits(*head_sum(part), gate_out, 0), held

    own_share, held = in_one_piece(own_work, activations, conv_taps, gate_in, gate_out)
    peer_rows, own_share, held = lax.optimization_barrier((peer_rows, own_share, held))
    near, far = peer_project(peer_rows, *held)
    behind_keys = lax.ppermute(key_vectors, "seq", swap)
    behind_values = lax.ppermute(value_vectors, "seq", swap)
    near, near_in = head_sum(near)
    far_share = far_logits(far, gate_out)
    share = logits_share(own_share, far_share, near, near_in, gate_out)
    share, queries = lax.optimization_barrier((share, queries))
    powers = powers_of(segments, queries, key_vectors, behind_keys)
    count = lax.axis_size("heads")
    across = [
        (seq * count + head, (1 - seq) * count + (head ^ 1))
        for seq in range(2)
        for head in range(count)
    ]
    shares = (share, lax.ppermute(share, ("seq", "heads"), across))
    given = (shares, powers, segments, queries, key_vectors, behind_keys)
    sent = behind_mass_of(*given)
    attended, own_mass, sent = attend(*given, value_vectors, behind_values, sent)
    key_mass = own_mass + lax.ppermute(sent, "seq", swap)
    return (attended, key_mass.astype(jnp.bfloat16))


def from_behind(block, axis, distance):
    devices = range(lax.axis_size(axis))
    route = [(i - distance, i) for i in devices if i - distance in devices]
    return lax.ppermute(block, axis, route)


def block_scores(query_heads, key_block, bias_block, allowed, score_scale):
    scores = (
        jnp.einsum("tgeh,kgh->getk", query_heads, key_block, preferred_element_type=jnp.float32)
        * score_scale
    )
    scores = scores + jnp.transpose(bias_block.astype(jnp.float32))[:, None, None, :]
    return jnp.where(allowed[None, None], scores, NEG_FILL)


def ring_device(
    activations, conv_taps, gate_in, gate_out, queries, key_vectors, value_vectors, segment_ids
):
    shard_rows = activations.shape[0]
    tap_count = conv_taps.shape[0]
    rim_rows = from_behind(activations[shard_rows - (tap_count - 1) :], "seq", 1)
    widened = jnp.concatenate([rim_rows, activations], 0).astype(jnp.float32)
    summed = jnp.zeros(activations.shape, jnp.float32)
    for shift_back in range(tap_count):
        start_row = tap_count - 1 - shift_back
        summed = (
            summed
            + conv_taps[shift_back].astype(jnp.float32)
            * widened[start_row : start_row + shard_rows]
        )
    mixed_rows = summed.astype(jnp.bfloat16)
    partial_hidden = jnp.dot(
        mixed_rows,
        lax.all_gather(gate_in, "seq", axis=1, tiled=True),
        preferred_element_type=jnp.float32,
    )
    kv_local = key_vectors.shape[1] // HEAD_DIM
    group_size = QUERY_HEADS // KV_HEADS
    head_rank = lax.axis_index("heads")
    hidden = jax.nn.silu(lax.psum(partial_hidden, "heads")).astype(jnp.bfloat16)
    logits = jnp.dot(hidden, gate_out, preferred_element_type=jnp.float32)
    retention = lax.dynamic_slice_in_dim(
        jax.nn.log_sigmoid(logits).astype(jnp.bfloat16), head_rank * kv_local, kv_local, 1
    )
    seq_rank = lax.axis_index("seq")
    local_index = jnp.arange(shard_rows, dtype=jnp.int32)
    own_queries, own_keys, own_values, own_bias = (queries, key_vectors, value_vectors, retention)
    query_places = seq_rank * shard_rows + local_index
    query_segments = jnp.take(segment_ids, query_places)
    query_heads = own_queries.reshape(shard_rows, kv_local, group_size, HEAD_DIM)
    score_scale = 1.0 / math.sqrt(HEAD_DIM)

    def visibility(flat_index):
        key_segments = jnp.take(segment_ids, flat_index)
        return (flat_index[None, :] <= query_places[:, None]) & (
            key_segments[None, :] == query_segments[:, None]
        )

    initial = (
        jnp.full((kv_local, group_size, shard_rows), NEG_FILL, jnp.float32),
        jnp.zeros((kv_local, group_size, shard_rows), jnp.float32),
    )
    all_keys, all_values, all_bias = (
        lax.all_gather(own_keys, "seq", axis=0, tiled=True),
        lax.all_gather(own_values, "seq", axis=0, tiled=True),
        lax.all_gather(own_bias, "seq", axis=0, tiled=True),
    )
    piece_rows = all_keys.shape[0]
    stats_block_width = math.gcd(piece_rows, 512)

    def one_block(block_number, state_in):
        offset = block_number * stats_block_width
        key_block = lax.dynamic_slice_in_dim(all_keys, offset, stats_block_width, 0).reshape(
            stats_block_width, kv_local, HEAD_DIM
        )
        bias_block = lax.dynamic_slice_in_dim(all_bias, offset, stats_block_width, 0)
        allowed = visibility(0 + offset + jnp.arange(stats_block_width, dtype=jnp.int32))

        def update(state_old):
            peak_old, mass_old = state_old
            masked = block_scores(query_heads, key_block, bias_block, allowed, score_scale)
            peak_new = jnp.maximum(peak_old, jnp.max(masked, axis=3))
            exponent = jnp.where(allowed[None, None], jnp.exp(masked - peak_new[..., None]), 0.0)
            return (peak_new, mass_old * jnp.exp(peak_old - peak_new) + jnp.sum(exponent, axis=3))

        def keep_state(state_old):
            return state_old

        return lax.cond(jnp.any(allowed), update, keep_state, state_in)

    row_peak, total_mass = lax.fori_loop(0, piece_rows // stats_block_width, one_block, initial)
    total_keys = all_keys.shape[0]
    block_width = math.gcd(total_keys, 512)
    block_count = total_keys // block_width
    key_blocks = all_keys.reshape(block_count, block_width, kv_local, HEAD_DIM)
    value_blocks = all_values.reshape(block_count, block_width, kv_local, HEAD_DIM)
    bias_blocks = all_bias.reshape(block_count, block_width, kv_local)

    def second_pass(accumulated, block_items):
        block_number, key_block, value_block, bias_block = block_items
        allowed = visibility(block_number * block_width + jnp.arange(block_width, dtype=jnp.int32))

        def attend(accum_in):
            masked = block_scores(query_heads, key_block, bias_block, allowed, score_scale)
            weights = (
                jnp.where(allowed[None, None], jnp.exp(masked - row_peak[..., None]), 0.0)
                / total_mass[..., None]
            )
            accum_out = accum_in + jnp.einsum(
                "getk,kgh->tgeh",
                weights.astype(jnp.bfloat16),
                value_block,
                preferred_element_type=jnp.float32,
            )
            return (accum_out, jnp.transpose(jnp.sum(weights, axis=(1, 2))) / group_size)

        def skip_block(accum_in):
            return (accum_in, jnp.zeros((block_width, kv_local), jnp.float32))

        return lax.cond(jnp.any(allowed), attend, skip_block, accumulated)

    accumulated, mass_blocks = lax.scan(
        second_pass,
        jnp.zeros((shard_rows, kv_local, group_size, HEAD_DIM), jnp.float32),
        (jnp.arange(block_count, dtype=jnp.int32), key_blocks, value_blocks, bias_blocks),
    )
    key_term = mass_blocks.reshape(total_keys, kv_local)
    key_mass = lax.psum_scatter(key_term, "seq", scatter_dimension=0, tiled=True).astype(
        jnp.bfloat16
    )
    attended = accumulated.reshape(shard_rows, kv_local * group_size * HEAD_DIM).astype(
        jnp.bfloat16
    )
    return (attended, jnp.transpose(key_mass))


def solution(mesh):
    return jax.shard_map(
        pair_device if mesh.shape["seq"] == 2 else ring_device,
        mesh=mesh,
        in_specs=(
            P(("dp", "seq"), "heads"),
            P(None, "heads"),
            P("heads", "seq"),
            P(),
            P(("dp", "seq"), "heads"),
            P(("dp", "seq"), "heads"),
            P(("dp", "seq"), "heads"),
            P("dp"),
        ),
        out_specs=(P(("dp", "seq"), "heads"), P("heads", ("dp", "seq"))),
        check_vma=False,
    )
```
